32 devices in a mesh: groups: 2 (over x), blk: 8 (over z, y), head: 2 (over core).
Axes of the slice: x: 2, y: 2, z: 4, core: 2. Of those that a mesh axis runs over, the one named last changes fastest.
Arguments:
- queries: bfloat16 [1024, 36864], P(('groups', 'blk'), 'head'), parts along dimension 0, may hold values from -750 to 750
- latent_cache: bfloat16 [128, 576, 256], P(('groups', 'blk')), parts along dimension 0, may hold values from -6 to 6
- new_latent: bfloat16 [576, 1024], P(None, ('groups', 'blk')), parts along dimension 1, may hold values from -6 to 6
- span_len: int32 [16], P('groups'), parts along dimension 0, may hold values from 2 to 57, as said below
- dec_count: int32 [16], P('groups'), parts along dimension 0, may hold values from 1 to 7, as said below
- span_start: int32 [16], P(('groups', 'blk')), parts along dimension 0, may hold values from 0 to 256, as said below
- cache_len: int32 [16, 7], P(('groups', 'blk')), parts along dimension 0, may hold values from 2 to 256, as said below
- value_weight: bfloat16 [64, 512, 128], P('head'), may hold values from -0.25 to 0.25
- out_weight: bfloat16 [8192, 7168], P('head', 'blk'), may hold values from -0.0625 to 0.0625
- residual: bfloat16 [1024, 7168], P(('groups', 'blk')), parts along dimension 0, may hold values from -34 to 34
- norm_gain: float32 [7168], replicated, may hold values from 0.1 to 1.9
- gate_weight: bfloat16 [7168, 9216], P(None, ('blk', 'head')), may hold values from -0.0625 to 0.0625
- up_weight: bfloat16 [7168, 9216], P(None, ('blk', 'head')), may hold values from -0.0625 to 0.0625
- down_weight: bfloat16 [9216, 7168], P(('blk', 'head')), may hold values from -0.0625 to 0.0625
Outputs:
- mixed: bfloat16 [1024, 7168], P(('groups', 'blk', 'head')), parts along dimension 0
The draws below stay inside these ranges and needn't reach their ends.
There are 2 independent parts, one for each index of `groups`. The reference program is written for one: setup_inputs(seed, part) draws one part's arguments, and reference() takes and returns one part's arrays. A program takes and returns all parts, laid end to end along the dimension named above; an argument that names none is the same for every part. Nothing has to cross between parts.
Inputs may be any that keep to these rules, and one draw needn't show every extreme that they name: span_len + dec_count is at most 64 on every rank, exactly 64 on one rank, at most 32 on every other rank and exactly 32 on some other rank; its sum over all ranks is exactly 256. `dec_count`: decode row j of a rank uses the rank's sequence slot j + 1. `span_start`: the cached positions of a rank's sequence slot 0. `cache_len`: entry j belongs to sequence slot j + 1; entries at or past a rank's dec_count are unused.
All inputs are finite; a program needn't handle non-finite values.
Results may differ from the reference program's by a relative error of at most 0.02.
Values may be sent and summed in bfloat16 or wider, within the bound.
No kernel may reach another device: no remote copies, remote signals or barrier semaphores. Data moves between devices by JAX's collectives and lax.ppermute only.
A program may use at most 128 MiB of HBM per device.

```python
import jax
import jax.numpy as jnp
from jax import lax

D = 7168
FF = 9216
HEADS = 64
KV = 512
VH = 128
ROWS_DEV = 64
SEQ_DEV = 8
CACHE = 256
LAT = 576
RANKS = 8
ROWS = 512
SEQS = 64
SHARDS = 16


def serving_plan(key):
    base_key = jax.random.fold_in(key, 7001)
    keys_all = jax.random.split(base_key, 5)
    ranking = jax.random.permutation(keys_all[0], RANKS)
    busiest = ranking[0]
    lightest = ranking[1]
    fullest = ranking[2]
    half_rows = ROWS_DEV // 2
    rank_ids = jnp.arange(RANKS, dtype=jnp.int32)
    weights_int = jax.random.randint(keys_all[1], (RANKS,), 1, 8)
    weights_int = jnp.where((rank_ids == busiest) | (rank_ids == fullest), 0, weights_int)
    losses = weights_int * half_rows // jnp.sum(weights_int)
    shortfall = half_rows - jnp.sum(losses)
    places = jnp.argsort(ranking)
    losses = losses + ((places >= 3) & (places <= shortfall + 2)).astype(jnp.int32)
    lives = jnp.where(rank_ids == busiest, ROWS_DEV, half_rows - losses)
    decode = jax.random.randint(keys_all[2], (RANKS,), 1, SEQ_DEV)
    decode = jnp.minimum(decode, lives - 2)
    decode = jnp.where(rank_ids == busiest, SEQ_DEV - 1, decode)
    decode = jnp.where(rank_ids == lightest, 1, decode)
    spans = lives - decode
    starts = jax.random.randint(keys_all[3], (RANKS,), 0, CACHE + 1)
    starts = jnp.where(rank_ids == lightest, 0, starts)
    starts = jnp.where(rank_ids == busiest, CACHE, starts)
    lengths = jax.random.randint(keys_all[4], (RANKS, SEQ_DEV - 1), 2, CACHE + 1)
    lengths = lengths.at[busiest, 0].set(CACHE)
    lengths = lengths.at[lightest, 0].set(2)
    return (spans.astype(jnp.int32), decode.astype(jnp.int32), starts.astype(jnp.int32), lengths.astype(jnp.int32))


def float_inputs(key):
    float_key = jax.random.fold_in(key, 9001)
    keys_all = jax.random.split(float_key, 3)
    latent_cache = jnp.clip(jax.random.normal(keys_all[0], (SEQS, LAT, CACHE), jnp.float32), -6.0, 6.0)
    new_latent = jnp.clip(jax.random.normal(keys_all[1], (LAT, ROWS), jnp.float32), -6.0, 6.0)
    queries = jnp.clip(jax.random.normal(keys_all[2], (ROWS, HEADS, LAT), jnp.float32), -6.0, 6.0)
    return (queries.reshape(ROWS, HEADS * LAT), latent_cache, new_latent)


def draw_queries(key, part):
    return float_inputs(key)[0].astype(jnp.bfloat16)


def draw_latent_cache(key, part):
    return float_inputs(key)[1].astype(jnp.bfloat16)


def draw_new_latent(key, part):
    return float_inputs(key)[2].astype(jnp.bfloat16)


def draw_span_len(key, part):
    return serving_plan(key)[0]


def draw_dec_count(key, part):
    return serving_plan(key)[1]


def draw_span_start(key, part):
    return serving_plan(key)[2]


def draw_cache_len(key, part):
    return serving_plan(key)[3]


def draw_residual(key, part):
    keys_all = jax.random.split(jax.random.fold_in(key, 4242), 1)
    values = jnp.clip(jax.random.normal(keys_all[0], (ROWS, D), jnp.float32), -6.0, 6.0) * 0.5
    return values.astype(jnp.bfloat16)


def steps_of(stream_key, dims, cuts, low, largest):
    gain, own = 1.0, jax.random.fold_in(stream_key, 6)
    for dim, blocks in cuts:
        steps = jnp.exp(jax.random.uniform(jax.random.fold_in(own, dim), (blocks,), jnp.float32, low / len(cuts), largest / len(cuts)))
        gain = gain * jnp.repeat(steps, dims[dim] // blocks).reshape([-1 if axis == dim else 1 for axis in range(len(dims))])
    return gain


def scatter_about(key, dims, deviation, limit, cuts=(), held_as=jnp.bfloat16):
    array = jax.random.normal(key, dims, jnp.float32) * deviation
    if len(cuts) > 0:
        array = steps_of(key, dims, cuts, -0.22, 0.18) * array
    return jnp.clip(array, min=-limit, max=limit).astype(held_as)


def setup_inputs(seed: int = 0, part: int = 0) -> dict:
    streams_of = jax.random.split(jax.random.key(seed), 15)
    part_keys = jax.random.split(jax.random.fold_in(streams_of[14], part), 15)
    queries = draw_queries(jax.random.fold_in(jax.random.fold_in(streams_of[14], part), 71), part)
    latent_cache = draw_latent_cache(jax.random.fold_in(jax.random.fold_in(streams_of[14], part), 71), part)
    new_latent = draw_new_latent(jax.random.fold_in(jax.random.fold_in(streams_of[14], part), 71), part)
    span_len = draw_span_len(jax.random.fold_in(jax.random.fold_in(streams_of[14], part), 71), part)
    dec_count = draw_dec_count(jax.random.fold_in(jax.random.fold_in(streams_of[14], part), 71), part)
    span_start = draw_span_start(jax.random.fold_in(jax.random.fold_in(streams_of[14], part), 71), part)
    cache_len = draw_cache_len(jax.random.fold_in(jax.random.fold_in(streams_of[14], part), 71), part)
    value_weight = scatter_about(streams_of[7], (HEADS, KV, VH), KV ** -0.5, 0.25, ((0, 2),))
    out_weight = scatter_about(streams_of[8], (HEADS * VH, D), (HEADS * VH) ** -0.5, 0.0625, ((0, 2), (1, 8)))
    residual = draw_residual(jax.random.fold_in(jax.random.fold_in(streams_of[14], part), 71), part)
    norm_gain = jnp.clip(1.0 + 0.18 * jax.random.normal(streams_of[10], (D,), jnp.float32), 0.1, 1.9)
    gate_weight = scatter_about(streams_of[11], (D, FF), D ** -0.5, 0.0625, ((1, 16),))
    up_weight = scatter_about(streams_of[12], (D, FF), D ** -0.5, 0.0625, ((1, 16),))
    down_weight = scatter_about(streams_of[13], (FF, D), FF ** -0.5, 0.0625, ((0, 16),))
    return dict(queries=queries, latent_cache=latent_cache, new_latent=new_latent, span_len=span_len, dec_count=dec_count, span_start=span_start, cache_len=cache_len, value_weight=value_weight, out_weight=out_weight, residual=residual, norm_gain=norm_gain, gate_weight=gate_weight, up_weight=up_weight, down_weight=down_weight)


score_scale = 192.0 ** (-0.5)
norm_eps = 1e-06
masked_score = -1e+30

def rounded(values):
    return lax.optimization_barrier(values.astype(jnp.bfloat16)).astype(jnp.float32)

def rank_attention(rank_index, queries, latent_cache, new_latent, span_len, dec_count, span_start, cache_len, value_weight):
    row_slots = lax.dynamic_slice_in_dim(queries, (rank_index * ROWS_DEV).astype(jnp.int32), ROWS_DEV, 0)
    query_rows = row_slots.reshape(ROWS_DEV, HEADS, LAT).astype(jnp.float32)
    cache_slots = lax.dynamic_slice_in_dim(latent_cache, (rank_index * SEQ_DEV).astype(jnp.int32), SEQ_DEV, 0).astype(jnp.float32)
    fresh_keys = lax.dynamic_slice_in_dim(new_latent, (rank_index * ROWS_DEV).astype(jnp.int32), ROWS_DEV, 1).astype(jnp.float32)
    span_rows = span_len[rank_index]
    decode_rows = dec_count[rank_index]
    start_pos = span_start[rank_index]
    lengths = cache_len[rank_index]
    positions = jnp.arange(CACHE, dtype=jnp.int32)
    local_rows = jnp.arange(ROWS_DEV, dtype=jnp.int32)
    cached_scores = jnp.einsum('rhl,lt->rht', query_rows, cache_slots[0]) * score_scale
    fresh_scores = jnp.einsum('rhl,lj->rhj', query_rows, fresh_keys) * score_scale
    cached_seen = (positions < start_pos)[None, None, :]
    fresh_seen = (local_rows[None, :] <= local_rows[:, None])[:, None, :]
    cached_scores = jnp.where(cached_seen, cached_scores, masked_score)
    fresh_scores = jnp.where(fresh_seen, fresh_scores, masked_score)
    peak_score = jnp.maximum(lax.optimization_barrier(jnp.max(cached_scores, axis=2)), lax.optimization_barrier(jnp.max(fresh_scores, axis=2)))[:, :, None]
    cached_exp = jnp.where(cached_seen, jnp.exp(cached_scores - peak_score), 0.0)
    fresh_exp = jnp.where(fresh_seen, jnp.exp(fresh_scores - peak_score), 0.0)
    totals = lax.optimization_barrier(jnp.sum(cached_exp, axis=2, keepdims=True)) + lax.optimization_barrier(jnp.sum(fresh_exp, axis=2, keepdims=True))
    span_out = jnp.einsum('rht,lt->rhl', rounded(cached_exp / totals), cache_slots[0, :KV])
    span_out = span_out + jnp.einsum('rhj,lj->rhl', rounded(fresh_exp / totals), fresh_keys[:KV])
    decode_slots = jnp.arange(SEQ_DEV - 1, dtype=jnp.int32)
    decode_index = jnp.clip(span_rows + decode_slots, 0, ROWS_DEV - 1).astype(jnp.int32)
    decode_query = query_rows[decode_index]
    decode_keys = cache_slots[1:]
    own_keys = fresh_keys[:, decode_index]
    slot_scores = jnp.einsum('shl,slt->sht', decode_query, decode_keys) * score_scale
    slot_seen = (positions[None, :] < lengths[:, None])[:, None, :]
    slot_scores = jnp.where(slot_seen, slot_scores, masked_score)
    own_scores = jnp.einsum('shl,ls->sh', decode_query, own_keys) * score_scale
    slot_peak = jnp.maximum(lax.optimization_barrier(jnp.max(slot_scores, axis=2)), own_scores)
    slot_exp = jnp.where(slot_seen, jnp.exp(slot_scores - slot_peak[:, :, None]), 0.0)
    own_exp = jnp.exp(own_scores - slot_peak)
    slot_totals = lax.optimization_barrier(jnp.sum(slot_exp, axis=2)) + own_exp
    decode_out = jnp.einsum('sht,slt->shl', rounded(slot_exp / slot_totals[:, :, None]), decode_keys[:, :KV])
    decode_out = decode_out + rounded(own_exp / slot_totals)[:, :, None] * own_keys[:KV].T[:, None, :]
    placing = ((local_rows[:, None] == span_rows + decode_slots[None, :]) & (decode_slots[None, :] < decode_rows)).astype(jnp.float32)
    latent_out = jnp.where((local_rows < span_rows)[:, None, None], span_out, 0.0)
    latent_out = latent_out + jnp.einsum('is,shl->ihl', placing, decode_out)
    head_values = jnp.einsum('rhl,hlv->rhv', rounded(latent_out), value_weight.astype(jnp.float32))
    return head_values.astype(jnp.bfloat16).reshape(ROWS_DEV, HEADS * VH)

def reference(queries, latent_cache, new_latent, span_len, dec_count, span_start, cache_len, value_weight, out_weight, residual, norm_gain, gate_weight, up_weight, down_weight):
    rank_ids = jnp.arange(RANKS, dtype=jnp.int32)
    head_values = lax.map(lambda rank_index: rank_attention(rank_index, queries, latent_cache, new_latent, span_len, dec_count, span_start, cache_len, value_weight), rank_ids)
    head_values = head_values.reshape(ROWS, HEADS * VH)
    attended = jnp.dot(head_values, out_weight, preferred_element_type=jnp.float32)
    stream = residual.astype(jnp.float32) + attended
    scale_rows = lax.rsqrt(lax.optimization_barrier(jnp.mean(stream * stream, axis=1, keepdims=True)) + norm_eps)
    normed = (stream * scale_rows * norm_gain[None, :]).astype(jnp.bfloat16)
    gate_values = jnp.dot(normed, gate_weight, preferred_element_type=jnp.float32)
    up_values = jnp.dot(normed, up_weight, preferred_element_type=jnp.float32)
    hidden = (jax.nn.silu(gate_values) * up_values).astype(jnp.bfloat16)
    block_width = FF // SHARDS

    def add_block(block_index, running):
        begin = (block_index * block_width).astype(jnp.int32)
        part_hidden = lax.dynamic_slice_in_dim(hidden, begin, block_width, 1)
        part_down = lax.dynamic_slice_in_dim(down_weight, begin, block_width, 0)
        return running + rounded(jnp.dot(part_hidden, part_down, preferred_element_type=jnp.float32))
    projected = lax.fori_loop(0, SHARDS, add_block, jnp.zeros((ROWS, D), jnp.float32))
    lives = span_len + dec_count
    slot_ids = jnp.arange(ROWS, dtype=jnp.int32)
    owners = slot_ids // ROWS_DEV
    live_rows = slot_ids % ROWS_DEV < lives[owners]
    return jnp.where(live_rows[:, None], stream + projected, 0.0).astype(jnp.bfloat16)
```

```python
import jax
import jax.numpy as jnp
from jax import lax
from jax.sharding import PartitionSpec as P

score_scale = 192.0 ** (-0.5)
norm_eps = 1e-06
masked_score = -1e30


def rounded(values):
    return lax.optimization_barrier(values.astype(jnp.bfloat16)).astype(jnp.float32)


def pick_rank(values, rank_index):
    matches = jnp.arange(values.shape[0], dtype=jnp.int32) == rank_index
    return jnp.sum(jnp.where(matches, values, 0))


def ring_order(mesh):
    count = mesh.shape["blk"]
    natural = list(range(count))
    snake = natural[0::2] + natural[1::2][::-1]
    names = list(mesh.axis_names)
    lane = mesh.devices.transpose([names.index("blk")] + [a for a, x in enumerate(names) if x != "blk"])
    firsts = [lane[i].reshape(-1)[0] for i in natural]
    if not all(hasattr(d, "coords") for d in firsts):
        return snake

    def length(order):
        hops = zip(order, order[1:] + order[:1])
        return sum(sum(abs(u - v) for u, v in zip(firsts[a].coords, firsts[b].coords)) for a, b in hops)

    return natural if length(natural) <= length(snake) else snake


def local_attention(
    query_rows, cache_slots, fresh_keys, span_rows, decode_rows, start_pos, lengths, key_width
):
    row_count = query_rows.shape[0]
    slot_count = cache_slots.shape[0]
    positions = jnp.arange(cache_slots.shape[2], dtype=jnp.int32)
    local_rows = jnp.arange(row_count, dtype=jnp.int32)
    cached_scores = (
        jnp.einsum("rhl,lt->rht", query_rows, cache_slots[0], preferred_element_type=jnp.float32)
        * score_scale
    )
    fresh_scores = (
        jnp.einsum("rhl,lj->rhj", query_rows, fresh_keys, preferred_element_type=jnp.float32)
        * score_scale
    )
    cached_seen = (positions < start_pos)[None, None, :]
    fresh_seen = (local_rows[None, :] <= local_rows[:, None])[:, None, :]
    cached_scores = jnp.where(cached_seen, cached_scores, masked_score)
    fresh_scores = jnp.where(fresh_seen, fresh_scores, masked_score)
    peak_score = jnp.maximum(jnp.max(cached_scores, axis=2), jnp.max(fresh_scores, axis=2))[
        :, :, None
    ]
    cached_exp = jnp.where(cached_seen, jnp.exp(cached_scores - peak_score), 0.0)
    fresh_exp = jnp.where(fresh_seen, jnp.exp(fresh_scores - peak_score), 0.0)
    totals = jnp.sum(cached_exp, axis=2, keepdims=True) + jnp.sum(fresh_exp, axis=2, keepdims=True)
    span_out = jnp.einsum(
        "rht,lt->rhl",
        (cached_exp / totals).astype(jnp.bfloat16),
        cache_slots[0, :key_width],
        preferred_element_type=jnp.float32,
    )
    span_out = span_out + jnp.einsum(
        "rhj,lj->rhl",
        (fresh_exp / totals).astype(jnp.bfloat16),
        fresh_keys[:key_width],
        preferred_element_type=jnp.float32,
    )
    decode_slots = jnp.arange(slot_count - 1, dtype=jnp.int32)
    decode_index = jnp.clip(span_rows + decode_slots, 0, row_count - 1)
    decode_query = jnp.take(query_rows, decode_index, axis=0)
    decode_keys = cache_slots[1:]
    own_keys = jnp.take(fresh_keys, decode_index, axis=1)
    slot_scores = (
        jnp.einsum("shl,slt->sht", decode_query, decode_keys, preferred_element_type=jnp.float32)
        * score_scale
    )
    slot_seen = (positions[None, :] < lengths[:, None])[:, None, :]
    slot_scores = jnp.where(slot_seen, slot_scores, masked_score)
    own_scores = (
        jnp.einsum("shl,ls->sh", decode_query, own_keys, preferred_element_type=jnp.float32)
        * score_scale
    )
    slot_peak = jnp.maximum(jnp.max(slot_scores, axis=2), own_scores)
    slot_exp = jnp.where(slot_seen, jnp.exp(slot_scores - slot_peak[:, :, None]), 0.0)
    own_exp = jnp.exp(own_scores - slot_peak)
    slot_totals = jnp.sum(slot_exp, axis=2) + own_exp
    decode_out = jnp.einsum(
        "sht,slt->shl",
        (slot_exp / slot_totals[:, :, None]).astype(jnp.bfloat16),
        decode_keys[:, :key_width],
        preferred_element_type=jnp.float32,
    )
    decode_out = (
        decode_out
        + rounded(own_exp / slot_totals)[:, :, None]
        * own_keys[:key_width].T.astype(jnp.float32)[:, None, :]
    )
    placing = (
        (local_rows[:, None] == span_rows + decode_slots[None, :])
        & (decode_slots[None, :] < decode_rows)
    ).astype(jnp.float32)
    latent_out = jnp.where((local_rows < span_rows)[:, None, None], span_out, 0.0)
    latent_out = latent_out + jnp.einsum("is,shl->ihl", placing, decode_out)
    return latent_out.astype(jnp.bfloat16)


def on_device(
    order,
    queries,
    latent_cache,
    new_latent,
    span_len,
    dec_count,
    span_start,
    cache_len,
    value_weight,
    out_weight,
    residual,
    norm_gain,
    gate_weight,
    up_weight,
    down_weight,
):
    f32, bf16 = jnp.float32, jnp.bfloat16
    ranks = len(order)
    reach = ranks // 2
    rank = lax.axis_index("blk")
    core = lax.axis_index("head")
    cores = lax.axis_size("head")
    rows_dev, width = residual.shape
    block = rows_dev // 2
    half = block // cores
    nodes = ranks + 1
    features = out_weight.shape[1]
    lives = span_len + dec_count
    at = jnp.asarray([order.index(i) for i in range(ranks)], jnp.int32)
    who = jnp.asarray(order, jnp.int32)
    busy_rank = jnp.argmax(lives).astype(jnp.int32)
    place = at[rank]
    busy_place = at[busy_rank]
    busy = rank == busy_rank

    forward = [(order[i], order[(i + 1) % ranks]) for i in range(ranks)]
    backward = [(b, a) for a, b in forward]
    exchange = [(c, cores - 1 - c) for c in range(cores)]

    def send_next(x):
        return lax.ppermute(x, "blk", forward)

    def send_prev(x):
        return lax.ppermute(x, "blk", backward)

    def swap(x):
        return lax.ppermute(x, "head", exchange)

    def node_ahead(k):
        e = (busy_place - place) % ranks
        far = (e > 0) & (k > e + 1)
        slot = who[(place + k - far.astype(jnp.int32)) % ranks]
        return jnp.where((e > 0) & (k == e + 1), ranks, slot)

    def node_behind(k):
        e = (place - busy_place) % ranks
        far = (e > 0) & (k > e)
        slot = who[(place - k + far.astype(jnp.int32)) % ranks]
        return jnp.where((e > 0) & (k == e), ranks, slot)

    res_halves = lax.dynamic_slice_in_dim(
        residual.reshape(2, cores, half, width), core, 1, 1
    ).reshape(2, half, width)

    def res_for(target):
        return lax.dynamic_slice_in_dim(res_halves, target * features, features, 2)

    res_parts = [res_for(rank)]
    for shift in range(1, ranks):
        res_parts.append(
            lax.ppermute(
                res_for((rank + shift) % ranks),
                "blk",
                [(i, (i + shift) % ranks) for i in range(ranks)],
            )
        )

    heads_here = value_weight.shape[0]
    query_rows = queries.reshape(rows_dev, heads_here, queries.shape[1] // heads_here)
    latent_out = local_attention(
        query_rows,
        latent_cache,
        new_latent,
        pick_rank(span_len, rank),
        pick_rank(dec_count, rank),
        span_start[0],
        cache_len[0],
        value_weight.shape[1],
    )
    head_values = jnp.einsum("rhl,hlv->rhv", latent_out, value_weight, preferred_element_type=f32)
    head_values = head_values.astype(bf16).reshape(rows_dev, heads_here * value_weight.shape[2])

    main, extra = head_values[:block], head_values[block:]
    from_behind, from_ahead = [], []
    for step in range(reach):
        if step == 0:
            out_f, out_b = jnp.where(busy, extra, main), main
        elif step == 1:
            out_f = jnp.where(busy, main, from_behind[0])
            out_b = jnp.where(busy, extra, from_ahead[0])
        else:
            out_f = jnp.where(busy, from_behind[step - 2], from_behind[step - 1])
            out_b = jnp.where(busy, from_ahead[step - 2], from_ahead[step - 1])
        from_behind.append(send_next(out_f))
        from_ahead.append(send_prev(out_b))
    blocks = [main] + from_behind + from_ahead[:-1] + [jnp.where(busy, extra, from_ahead[-1])]
    slots = [rank] + [node_behind(k + 1) for k in range(reach)]
    slots += [node_ahead(k + 1) for k in range(reach - 1)]
    slots += [jnp.where(busy, ranks, node_ahead(reach))]
    slots = jnp.stack(slots)
    sources = jnp.argmax(slots[None, :] == jnp.arange(nodes)[:, None], axis=1)

    partial_out = jnp.dot(jnp.concatenate(blocks, 0), out_weight, preferred_element_type=f32)
    partial_out = jnp.take(partial_out.reshape(nodes, cores, half, features), sources, axis=0)
    first, second = partial_out[:, 0], partial_out[:, 1]
    kept = jnp.where(core == 0, first, second)
    given = jnp.where(core == 0, second, first).astype(bf16)
    res_all = jnp.stack(res_parts)
    res_main = jnp.take(res_all[:, 0], (rank - jnp.arange(ranks)) % ranks, axis=0)
    res_extra = lax.dynamic_index_in_dim(res_all[:, 1], (rank - busy_rank) % ranks, 0)
    res_here = jnp.concatenate([res_main, res_extra], 0).astype(f32)
    stream = (kept + swap(given).astype(f32) + res_here).astype(bf16).reshape(nodes * half, features)

    gain_blocks = norm_gain.reshape(ranks, features)

    def chunk(mine, owner):
        both = jnp.concatenate([mine, swap(mine)], 0).astype(f32)
        squares = jnp.sum(both * both, axis=1, keepdims=True)
        scaled = (both * gain_blocks[owner][None, :]).astype(bf16)
        gate_part = lax.dynamic_slice_in_dim(gate_weight, owner * features, features, 0)
        up_part = lax.dynamic_slice_in_dim(up_weight, owner * features, features, 0)
        return (
            squares,
            jnp.dot(scaled, gate_part, preferred_element_type=f32),
            jnp.dot(scaled, up_part, preferred_element_type=f32),
        )

    held = [(stream, rank)]
    ahead, behind = stream, stream
    for step in range(1, reach + 1):
        ahead = send_next(ahead)
        held.append((ahead, who[(place - step) % ranks]))
        if step < reach:
            behind = send_prev(behind)
            held.append((behind, who[(place + step) % ranks]))
    sums = chunk(*held[0])
    for piece in held[1:]:
        sums = tuple(a + b for a, b in zip(sums, chunk(*piece)))
    squares, gate_values, up_values = sums
    scale_rows = lax.rsqrt(squares / width + norm_eps)
    hidden = (jax.nn.silu(gate_values * scale_rows) * (up_values * scale_rows)).astype(bf16)

    own_parts = jnp.stack(
        [
            jnp.stack(
                [
                    lax.dynamic_slice_in_dim(piece, rank * half, half, 0),
                    piece[ranks * half :],
                ]
            )
            for piece, _ in held
        ]
    )
    owners = jnp.stack([owner for _, owner in held])
    arrival = jnp.argmax(owners[None, :] == jnp.arange(ranks)[:, None], axis=1)
    own_stream = jnp.take(own_parts, arrival, axis=0)
    own_stream = own_stream.transpose(1, 2, 0, 3).reshape(2, half, width).astype(f32)

    rows_here = nodes * half
    other = jnp.dot(hidden[rows_here:], down_weight, preferred_element_type=f32).astype(bf16)
    theirs = swap(other).reshape(nodes, half, width)
    mine = jnp.dot(hidden[:rows_here], down_weight, preferred_element_type=f32).astype(bf16)
    mine = mine.reshape(nodes, half, width)

    def share(slot):
        a = lax.dynamic_index_in_dim(mine, slot, 0, keepdims=False).astype(f32)
        b = lax.dynamic_index_in_dim(theirs, slot, 0, keepdims=False).astype(f32)
        return a + b

    got_f, got_b = [], []
    for step in range(1, reach + 1):
        add_f = share(node_ahead(reach + 1 - step))
        add_b = share(node_behind(reach + 1 - step))
        if step == 1:
            add_f = jnp.where(busy, 0.0, add_f)
        elif step == 2:
            add_f = add_f + jnp.where(busy, 0.0, got_f[0].astype(f32))
            add_b = add_b + jnp.where(busy, 0.0, got_b[0].astype(f32))
        else:
            add_f = add_f + jnp.where(busy, got_f[step - 3], got_f[step - 2]).astype(f32)
            add_b = add_b + jnp.where(busy, got_b[step - 3], got_b[step - 2]).astype(f32)
        got_f.append(send_next(add_f.astype(bf16)))
        got_b.append(send_prev(add_b.astype(bf16)))
    main_sum = share(rank) + got_f[-1].astype(f32)
    main_sum = main_sum + jnp.where(busy, got_b[-2], got_b[-1]).astype(f32)
    extra_sum = share(jnp.int32(ranks)) + got_f[-2].astype(f32) + got_b[-1].astype(f32)

    main_out = (own_stream[0] + main_sum).astype(bf16)
    extra_out = (own_stream[1] + extra_sum).astype(bf16)
    kept_out = jnp.where(core == 0, main_out, extra_out)
    swapped = swap(jnp.where(core == 0, extra_out, main_out))
    low = jnp.where(core == 0, kept_out, swapped)
    high = jnp.where(core == 0, swapped, kept_out)
    result = jnp.concatenate([low, high], 0)
    own_rows = core * block + jnp.arange(block, dtype=jnp.int32)
    alive = own_rows < pick_rank(lives, rank)
    return jnp.where(alive[:, None], result, jnp.zeros_like(result))


def solution(mesh):
    placed = (
        P(("groups", "blk"), "head"),
        P(("groups", "blk"), None, None),
        P(None, ("groups", "blk")),
        P("groups"),
        P("groups"),
        P(("groups", "blk")),
        P(("groups", "blk"), None),
        P("head", None, None),
        P("head", "blk"),
        P(("groups", "blk"), None),
        P(),
        P(None, ("blk", "head")),
        P(None, ("blk", "head")),
        P(("blk", "head"), None),
    )
    order = ring_order(mesh)
    return jax.shard_map(
        lambda *args: on_device(order, *args),
        mesh=mesh,
        in_specs=placed,
        out_specs=P(("groups", "blk", "head"), None),
        check_vma=False,
    )
```

```python
import functools

import jax
import jax.numpy as jnp
from jax import lax
from jax.experimental import pallas as pl
from jax.experimental.pallas import tpu as pltpu
from jax.sharding import PartitionSpec as P

score_scale = 192.0 ** (-0.5)
norm_eps = 1e-06
masked_score = -1e30
f32, bf16, i32 = jnp.float32, jnp.bfloat16, jnp.int32
SMEM = pltpu.SMEM
MIB = 1 << 20

RANK, CORE, BUSY, BUSY_RANK, SPAN, DEC, LIVE, START, LENGTHS = range(9)


def mm(a, b):
    return lax.dot_general(a, b, (((1,), (0,)), ((), ())), preferred_element_type=f32)


def mm_nt(a, b):
    return lax.dot_general(a, b, (((1,), (1,)), ((), ())), preferred_element_type=f32)


def smem():
    return pl.BlockSpec(memory_space=SMEM)


def whole():
    return pl.BlockSpec(memory_space=pltpu.VMEM)


def params(mib=32):
    return pltpu.CompilerParams(vmem_limit_bytes=mib * MIB)


def cost(flops, moved, exps=0):
    return pl.CostEstimate(flops=int(flops), bytes_accessed=int(moved), transcendentals=int(exps))


def ring_order(mesh):
    count = mesh.shape["blk"]
    natural = list(range(count))
    snake = natural[0::2] + natural[1::2][::-1]
    names = list(mesh.axis_names)
    axes = [names.index("blk")] + [a for a, x in enumerate(names) if x != "blk"]
    lane = mesh.devices.transpose(axes)
    firsts = [lane[i].reshape(-1)[0] for i in natural]
    if not all(hasattr(d, "coords") for d in firsts):
        return snake

    def length(order):
        hops = zip(order, order[1:] + order[:1])
        return sum(
            sum(abs(u - v) for u, v in zip(firsts[a].coords, firsts[b].coords)) for a, b in hops
        )

    return natural if length(natural) <= length(snake) else snake


class Table:
    def __init__(self, ranks, slots):
        self.reach = ranks // 2
        self.source = LENGTHS + slots
        self.ahead = self.source + ranks + 1
        self.behind = self.ahead + self.reach + 1
        self.owner_back = self.behind + self.reach + 1
        self.owner_fore = self.owner_back + self.reach + 1
        self.size = self.owner_fore + self.reach + 1


def table_kernel(table, ranks, ids, span, dec, start, lengths, at, who, out):
    reach = table.reach
    rank, core = ids[0], ids[1]
    most, busy_rank = span[0] + dec[0], jnp.int32(0)
    for i in range(1, ranks):
        here = span[i] + dec[i]
        busy_rank = jnp.where(here > most, i, busy_rank)
        most = jnp.maximum(here, most)
    busy = rank == busy_rank

    def wrap(x):
        x = jnp.where(x < 0, x + ranks, x)
        return jnp.where(x >= ranks, x - ranks, x)

    place, busy_place = at[rank], at[busy_rank]
    to_busy = wrap(busy_place - place)
    from_busy = wrap(place - busy_place)

    def node_ahead(k):
        far = (to_busy > 0) & (k > to_busy + 1)
        slot = who[wrap(place + k - jnp.where(far, 1, 0))]
        return jnp.where((to_busy > 0) & (k == to_busy + 1), ranks, slot)

    def node_behind(k):
        far = (from_busy > 0) & (k > from_busy)
        slot = who[wrap(place - k + jnp.where(far, 1, 0))]
        return jnp.where((from_busy > 0) & (k == from_busy), ranks, slot)

    out[RANK] = rank
    out[CORE] = core
    out[BUSY] = jnp.where(busy, 1, 0)
    out[BUSY_RANK] = busy_rank
    out[SPAN] = span[rank]
    out[DEC] = dec[rank]
    out[LIVE] = span[rank] + dec[rank]
    out[START] = start[0]
    for j in range(lengths.shape[1]):
        out[LENGTHS + j] = lengths[0, j]
    out[table.source + rank] = 0
    for k in range(1, reach + 1):
        out[table.ahead + k] = node_ahead(k)
        out[table.behind + k] = node_behind(k)
        out[table.owner_back + k] = who[wrap(place - k)]
        out[table.owner_fore + k] = who[wrap(place + k)]
        out[table.source + node_behind(k)] = k
        last = jnp.where(busy, ranks, node_ahead(k)) if k == reach else node_ahead(k)
        out[table.source + last] = reach + k


def attend_kernel(
    heads, group, rows, lat, cached, value, start_step,
    tab, q, cache, fresh, vw, main, extra, k0, k1, kpad, dq, dec,
):
    pair = 2 * lat
    wide = -(-lat // 128) * 128
    shift = wide - lat
    keys = cached + rows
    cols = -(-keys // 128) * 128
    slots = cache.shape[0] - 1
    dr = 8
    span, decs = tab[SPAN], tab[DEC]

    def onehot(shape, row_dim, slot_dim):
        r = lax.broadcasted_iota(i32, shape, row_dim)
        j = lax.broadcasted_iota(i32, shape, slot_dim)
        return jnp.where((r == span + j) & (j < decs), 1.0, 0.0).astype(bf16)

    @pl.when(pl.program_id(0) == 0)
    def _():
        k0[...] = jnp.zeros_like(k0)
        k1[...] = jnp.zeros_like(k1)
        for ref, off in ((k0, 0), (k1, shift)):
            ref[off : off + lat, :cached] = cache[0]
            ref[off : off + lat, cached:keys] = fresh[...]
        kpad[...] = jnp.zeros_like(kpad)
        for s in range(slots):
            kpad[s, :lat] = cache[s + 1]
        pick = onehot((16, rows), 1, 0)
        for p in range(heads // 2):
            got = mm(pick, q[:, pair * p : pair * (p + 1)])[:dr]
            dq[2 * p * dr : (2 * p + 1) * dr] = got[:, :wide]
            dq[(2 * p + 1) * dr : (2 * p + 2) * dr] = pltpu.roll(got[:, pair - wide :], wide - shift, 1)
        n = heads * dr
        queries = dq[...].astype(bf16)
        slot = lax.broadcasted_iota(i32, (n, 1), 0) % dr
        length = jnp.zeros((n, 1), i32)
        scores = jnp.zeros((n, cached), f32)
        for s in range(slots):
            scores = jnp.where(slot == s, mm(queries, kpad[s]), scores)
            length = jnp.where(slot == s, tab[LENGTHS + s], length)
        seen = lax.broadcasted_iota(i32, (n, cached), 1) < length
        scores = jnp.where(seen, scores * score_scale, masked_score)
        own = mm(queries, k0[:, cached:])
        column = lax.broadcasted_iota(i32, own.shape, 1)
        own = jnp.sum(jnp.where(column == span + slot, own, 0.0), axis=1, keepdims=True)
        own = own * score_scale
        peak = jnp.maximum(jnp.max(scores, axis=1, keepdims=True), own)
        e = jnp.where(seen, jnp.exp(scores - peak), 0.0)
        e_own = jnp.exp(own - peak)
        total = jnp.sum(e, axis=1, keepdims=True) + e_own
        w = e / total
        acc = jnp.zeros((n, value), f32)
        for s in range(slots):
            acc = acc + mm_nt(jnp.where(slot == s, w, 0.0).astype(bf16), cache[s + 1, :value])
        own_value = mm_nt(pick, fresh[:value])[:dr]
        own_value = jnp.broadcast_to(own_value[None], (heads, dr, value)).reshape(n, value)
        dec[...] = acc + (e_own / total).astype(bf16).astype(f32) * own_value

    step = pl.program_id(0)
    start = step * (group * lat)
    pairs = group // 2

    def stacked(off):
        return jnp.concatenate(
            [q[:, pl.ds(pl.multiple_of(start + pair * p + off, 128), wide)] for p in range(pairs)], 0
        )

    m = pairs * rows
    row = lax.broadcasted_iota(i32, (m, 1), 0) % rows
    col = lax.broadcasted_iota(i32, (m, cols), 1)
    seen = (col < jnp.where(col < cached, tab[START], cached + 1 + row)) & (col < keys)
    values = k0[:value]

    def latent(lhs, ref):
        s = jnp.where(seen, mm(lhs, ref[...]) * score_scale, masked_score)
        e = jnp.where(seen, jnp.exp(s - jnp.max(s, axis=1, keepdims=True)), 0.0)
        w = (e * (1.0 / jnp.sum(e, axis=1, keepdims=True))).astype(bf16)
        o = mm_nt(w, values)
        return jnp.where(row < span, o, 0.0).astype(bf16)

    even, odd = latent(stacked(0), k0), latent(stacked(pair - wide), k1)
    outs, decoded = [], []
    for p in range(pairs):
        at = pl.multiple_of((step * group + 2 * p) * dr, 16)
        lhs = jnp.concatenate(
            [even[p * rows : (p + 1) * rows], odd[p * rows : (p + 1) * rows], dec[pl.ds(at, 16)].astype(bf16)], 0
        )
        vh = vw.shape[2]
        r = mm(lhs, jnp.concatenate([vw[2 * p], vw[2 * p + 1]], 1))
        outs += [r[:rows, :vh], r[rows : 2 * rows, vh:]]
        decoded += [r[2 * rows : 2 * rows + dr, :vh], r[2 * rows + dr :, vh:]]
    decoded = jnp.concatenate(decoded, 1)
    decoded = jnp.concatenate([decoded, jnp.zeros_like(decoded)], 0).astype(bf16)
    out = jnp.concatenate(outs, 1) + mm(onehot((rows, 16), 0, 1), decoded)
    out = out.astype(bf16)
    main[...] = out[: rows // 2]
    extra[...] = out[rows // 2 :]


def attend(tab, queries, cache, fresh, vw, part, parts):
    rows, heads = queries.shape[0], vw.shape[0] // parts
    lat = queries.shape[1] // vw.shape[0]
    slots, _, cached = cache.shape
    value, vh = vw.shape[1:]
    group = min(8, heads)
    wide, cols = -(-lat // 128) * 128, -(-(cached + rows) // 128) * 128
    steps = heads // group
    half = jax.ShapeDtypeStruct((rows // 2, heads * vh), bf16)
    return pl.pallas_call(
        functools.partial(attend_kernel, heads, group, rows, lat, cached, value, part),
        grid=(steps,),
        in_specs=[
            smem(),
            pl.BlockSpec((rows, heads * lat), lambda i: (0, part)),
            pl.BlockSpec(cache.shape, lambda i: (0, 0, 0)),
            pl.BlockSpec(fresh.shape, lambda i: (0, 0)),
            pl.BlockSpec((group, value, vh), lambda i: (part * steps + i, 0, 0)),
        ],
        out_specs=[pl.BlockSpec((rows // 2, group * vh), lambda i: (0, i))] * 2,
        out_shape=[half, half],
        scratch_shapes=[
            pltpu.VMEM((wide, cols), bf16),
            pltpu.VMEM((wide, cols), bf16),
            pltpu.VMEM((slots - 1, wide, cached), bf16),
            pltpu.VMEM((heads * 8, wide), f32),
            pltpu.VMEM((heads * 8, value), f32),
        ],
        compiler_params=params(40),
        cost_estimate=cost(
            2 * rows * heads * (cached + rows) * (lat + value),
            2 * (queries.size // parts + cache.size + vw.size // parts),
            rows * heads * (cached + rows),
        ),
        name="attend",
    )(tab, queries, cache, fresh, vw)


def pack_kernel(ranks, features, half, tab, res, *outs):
    core, rank = tab[CORE], tab[RANK]
    low = pl.multiple_of(core * half, half)
    high = pl.multiple_of(res.shape[0] // 2 + core * half, half)
    for k in range(ranks):
        target = rank + k
        target = jnp.where(target >= ranks, target - ranks, target)

        def put(columns, k=k):
            outs[k][:half] = res[pl.ds(low, half), columns]
            outs[k][half:] = res[pl.ds(high, half), columns]

        if features % 128 == 0:
            put(pl.ds(pl.multiple_of(target * features, 128), features))
        else:
            for t in range(ranks):
                pl.when(target == t)(functools.partial(put, slice(t * features, (t + 1) * features)))


def pack(tab, residual, ranks, cores):
    rows, width = residual.shape
    half, features = rows // 2 // cores, width // ranks
    return pl.pallas_call(
        functools.partial(pack_kernel, ranks, features, half),
        in_specs=[smem(), whole()],
        out_specs=[whole()] * ranks,
        out_shape=[jax.ShapeDtypeStruct((2 * half, features), bf16)] * ranks,
        compiler_params=params(),
        cost_estimate=cost(0, 4 * residual.size),
        name="pack",
    )(tab, residual)


def route_kernel(tab, *refs):
    count = len(refs) // 3
    busy = tab[BUSY] == 1
    for i in range(count):
        special, usual, out = refs[2 * i], refs[2 * i + 1], refs[2 * count + i]

        @pl.when(busy)
        def _(special=special, out=out):
            out[...] = special[...]

        @pl.when(jnp.logical_not(busy))
        def _(usual=usual, out=out):
            out[...] = usual[...]


def route(tab, *choices):
    flat = [x for pair in choices for x in pair]
    return pl.pallas_call(
        route_kernel,
        in_specs=[smem()] + [whole()] * len(flat),
        out_specs=[whole()] * len(choices),
        out_shape=[jax.ShapeDtypeStruct(b.shape, b.dtype) for _, b in choices],
        compiler_params=params(),
        cost_estimate=cost(0, 3 * sum(2 * b.size for _, b in choices)),
        name="route",
    )(tab, *flat)


def project_kernel(source, nodes, block, half, first, tab, *refs):
    blocks, refs = refs[: nodes + 1], refs[nodes + 1 :]
    before = None if first else refs[0]
    weight, kept, given, acc = refs[-4:]
    step = pl.program_id(0)
    depth = weight.shape[0]
    columns = pl.ds(pl.multiple_of(step * depth, 128), depth)
    last = jnp.where(tab[BUSY] == 1, blocks[nodes][:, columns], blocks[nodes - 1][:, columns])
    lhs = jnp.concatenate([b[:, columns] for b in blocks[: nodes - 1]] + [last], 0)
    got = mm(lhs, weight[...])

    @pl.when(step == 0)
    def _():
        acc[...] = got if first else got + before[...]

    @pl.when(step > 0)
    def _():
        acc[...] += got

    @pl.when(step == pl.num_programs(0) - 1)
    def _():
        core = tab[CORE]
        for k in range(nodes):
            at = tab[source + k] * block
            kept[k * half : (k + 1) * half] = acc[pl.ds(pl.multiple_of(at + core * half, half), half)]
            other = acc[pl.ds(pl.multiple_of(at + (1 - core) * half, half), half)]
            given[k * half : (k + 1) * half] = other.astype(bf16)


def project_part_kernel(nodes, first, tab, *refs):
    blocks, refs = refs[: nodes + 1], refs[nodes + 1 :]
    weight, out = refs[-2:]
    step = pl.program_id(0)
    depth = weight.shape[0]
    columns = pl.ds(pl.multiple_of(step * depth, 128), depth)
    last = jnp.where(tab[BUSY] == 1, blocks[nodes][:, columns], blocks[nodes - 1][:, columns])
    lhs = jnp.concatenate([b[:, columns] for b in blocks[: nodes - 1]] + [last], 0)
    got = mm(lhs, weight[...])

    @pl.when(step == 0)
    def _():
        out[...] = got if first else got + refs[0][...]

    @pl.when(step > 0)
    def _():
        out[...] += got


def project(tab, table, blocks, before, weight, part, parts, cores):
    block, width = blocks[0].shape
    nodes = len(blocks) - 1
    half = block // cores
    features = weight.shape[1]
    depth = 1024 if width % 1024 == 0 else width
    steps = width // depth
    total = jax.ShapeDtypeStruct((nodes * block, features), f32)
    final = part == parts - 1
    first = before is None
    ins = [smem()] + [whole()] * (nodes + 1 + (not first))
    ins += [pl.BlockSpec((depth, features), lambda i: (part * steps + i, 0))]
    args = [tab, *blocks] + ([] if first else [before]) + [weight]
    estimate = cost(
        2 * nodes * block * width * features, 2 * (nodes * block * width + width * features)
    )
    if not final:
        return pl.pallas_call(
            functools.partial(project_part_kernel, nodes, first),
            grid=(steps,),
            in_specs=ins,
            out_specs=pl.BlockSpec(total.shape, lambda i: (0, 0)),
            out_shape=total,
            compiler_params=params(),
            cost_estimate=estimate,
            name="project",
        )(*args)
    return pl.pallas_call(
        functools.partial(project_kernel, table.source, nodes, block, half, first),
        grid=(steps,),
        in_specs=ins,
        out_specs=[pl.BlockSpec((nodes * half, features), lambda i: (0, 0))] * 2,
        out_shape=[
            jax.ShapeDtypeStruct((nodes * half, features), f32),
            jax.ShapeDtypeStruct((nodes * half, features), bf16),
        ],
        scratch_shapes=[pltpu.VMEM(total.shape, f32)],
        compiler_params=params(),
        cost_estimate=estimate,
        name="project",
    )(*args)


def stream_kernel(ranks, half, tab, kept, other, *refs):
    res, out = refs[:-1], refs[-1]
    rank, busy_rank = tab[RANK], tab[BUSY_RANK]

    def put(slot, extra):
        rows = pl.ds(pl.multiple_of(slot * half, half), half)
        total = kept[rows] + other[rows].astype(f32) + extra.astype(f32)
        out[rows] = total.astype(bf16)

    for k in range(ranks):
        owner = rank - k
        owner = jnp.where(owner < 0, owner + ranks, owner)
        put(owner, res[k][:half])

        @pl.when(owner == busy_rank)
        def _(k=k):
            put(ranks, res[k][half:])


def stream_of(tab, kept, other, res):
    half = res[0].shape[0] // 2
    return pl.pallas_call(
        functools.partial(stream_kernel, len(res), half),
        in_specs=[smem()] + [whole()] * (2 + len(res)),
        out_specs=whole(),
        out_shape=jax.ShapeDtypeStruct(other.shape, bf16),
        compiler_params=params(),
        cost_estimate=cost(0, 10 * other.size),
        name="stream",
    )(tab, kept, other, *res)


def expand_kernel(count, first, final, width, tab, *refs):
    mines, theirs = refs[:count], refs[count : 2 * count]
    refs = refs[2 * count :]
    gain, gate, up = refs[:3]
    refs = refs[3:]
    if not first:
        before, refs = refs[:3], refs[3:]
    if final:
        hidden, refs = refs[0], refs[1:]
    gates, ups, squares = refs
    step = pl.program_id(0)
    for i in range(count):

        @pl.when(step == i)
        def _(i=i):
            both = jnp.concatenate([mines[i][...], theirs[i][...]], 0).astype(f32)
            scaled = (both * gain[0]).astype(bf16)
            values = (
                mm(scaled, gate[...]),
                mm(scaled, up[...]),
                jnp.sum(both * both, axis=1, keepdims=True),
            )
            for n, (ref, value) in enumerate(zip((gates, ups, squares), values)):
                if i == 0:
                    ref[...] = value if first else value + before[n][...]
                else:
                    ref[...] += value

    if final:

        @pl.when(step == count - 1)
        def _():
            scale = lax.rsqrt(squares[...] / width + norm_eps)
            g = gates[...] * scale
            hidden[...] = (g / (1.0 + jnp.exp(-g)) * (ups[...] * scale)).astype(bf16)


def expand(tab, mines, theirs, owners, gain, gate, up, before, final):
    count = len(mines)
    rows, features = mines[0].shape
    units = gate.shape[1]
    first = before is None

    def owner(i, tab):
        index = tab[owners[0]]
        for n in range(1, count):
            index = jnp.where(i == n, tab[owners[n]], index)
        return index

    def full(shape):
        return pl.BlockSpec(shape, lambda i, tab: (0,) * len(shape))

    sums = [(2 * rows, units), (2 * rows, units), (2 * rows, 1)]
    ins = [full((rows, features))] * (2 * count)
    ins += [pl.BlockSpec((1, 1, features), lambda i, tab: (owner(i, tab), 0, 0))]
    ins += [pl.BlockSpec((features, units), lambda i, tab: (owner(i, tab), 0))] * 2
    if not first:
        ins += [full(s) for s in sums]
    shapes = [jax.ShapeDtypeStruct(s, f32) for s in sums]
    out_shapes = [jax.ShapeDtypeStruct((2 * rows, units), bf16)] if final else shapes
    return pl.pallas_call(
        functools.partial(expand_kernel, count, first, final, gate.shape[0]),
        grid_spec=pltpu.PrefetchScalarGridSpec(
            num_scalar_prefetch=1,
            grid=(count,),
            in_specs=ins,
            out_specs=[full(s.shape) for s in out_shapes],
            scratch_shapes=[pltpu.VMEM(s, f32) for s in sums] if final else [],
        ),
        out_shape=out_shapes,
        compiler_params=params(),
        cost_estimate=cost(
            8 * count * rows * features * units, count * (4 * features * units + 4 * rows * features)
        ),
        name="expand",
    )(tab, *mines, *theirs, gain, gate, up, *([] if first else before))


def collect_kernel(owners, tab, *refs):
    out = refs[-1]
    half = out.shape[1] // 2
    for i, at in enumerate(owners):
        out[tab[at], :half] = refs[2 * i][...]
        out[tab[at], half:] = refs[2 * i + 1][...]


def collect(tab, blocks, owners, half):
    ranks = len(blocks)
    features = blocks[0].shape[1]
    ins, args = [], []
    for x in blocks:
        ins += [
            pl.BlockSpec((half, features), lambda i, tab: (tab[RANK], 0)),
            pl.BlockSpec((half, features), lambda i, tab: (ranks, 0)),
        ]
        args += [x, x]
    shape = (ranks, 2 * half, features)
    return pl.pallas_call(
        functools.partial(collect_kernel, owners),
        grid_spec=pltpu.PrefetchScalarGridSpec(
            num_scalar_prefetch=1,
            grid=(1,),
            in_specs=ins,
            out_specs=pl.BlockSpec(shape, lambda i, tab: (0, 0, 0)),
        ),
        out_shape=jax.ShapeDtypeStruct(shape, bf16),
        compiler_params=params(),
        cost_estimate=cost(0, 8 * ranks * half * features),
        name="collect",
    )(tab, *args)


def contract_kernel(hidden, weight, mine, given):
    got = mm(hidden[...], weight[...]).astype(bf16)
    rows = mine.shape[0]
    mine[...] = got[:rows]
    given[...] = got[rows:]


def contract(hidden, weight, part, parts):
    rows, units = hidden.shape
    columns = weight.shape[1] // parts
    wide = columns // 2 if columns % 256 == 0 else columns
    steps = columns // wide
    out = jax.ShapeDtypeStruct((rows // 2, columns), bf16)
    return pl.pallas_call(
        contract_kernel,
        grid=(steps,),
        in_specs=[
            pl.BlockSpec((rows, units), lambda i: (0, 0)),
            pl.BlockSpec((units, wide), lambda i: (0, part * steps + i)),
        ],
        out_specs=[pl.BlockSpec((rows // 2, wide), lambda i: (0, i))] * 2,
        out_shape=[out, out],
        compiler_params=params(),
        cost_estimate=cost(2 * rows * units * columns, 2 * (units + rows) * columns),
        name="contract",
    )(hidden, weight)


def add_kernel(step, tab, mine_f, theirs_f, mine_b, theirs_b, *refs):
    got, (out_f, out_b) = refs[:-2], refs[-2:]
    busy = tab[BUSY] == 1
    own_f = mine_f[...].astype(f32) + theirs_f[...].astype(f32)
    own_b = mine_b[...].astype(f32) + theirs_b[...].astype(f32)
    if step == 1:
        out_f[...] = jnp.where(busy, 0.0, own_f).astype(bf16)
        out_b[...] = own_b.astype(bf16)
    elif step == 2:
        out_f[...] = (own_f + jnp.where(busy, 0.0, got[0][...].astype(f32))).astype(bf16)
        out_b[...] = (own_b + jnp.where(busy, 0.0, got[1][...].astype(f32))).astype(bf16)
    else:
        from_f = jnp.where(busy, got[0][...], got[1][...]).astype(f32)
        from_b = jnp.where(busy, got[2][...], got[3][...]).astype(f32)
        out_f[...] = (own_f + from_f).astype(bf16)
        out_b[...] = (own_b + from_b).astype(bf16)


def add(tab, table, step, mine, theirs, got, half):
    columns = mine.shape[1]
    far = table.reach + 1 - step

    def at(where):
        return pl.BlockSpec((half, columns), lambda i, tab: (tab[where + far], 0))

    full = pl.BlockSpec((half, columns), lambda i, tab: (0, 0))
    out = jax.ShapeDtypeStruct((half, columns), bf16)
    return pl.pallas_call(
        functools.partial(add_kernel, step),
        grid_spec=pltpu.PrefetchScalarGridSpec(
            num_scalar_prefetch=1,
            grid=(1,),
            in_specs=[at(table.ahead)] * 2 + [at(table.behind)] * 2 + [full] * len(got),
            out_specs=[full, full],
        ),
        out_shape=[out, out],
        compiler_params=params(),
        cost_estimate=cost(0, 16 * half * columns),
        name="add",
    )(tab, mine, theirs, mine, theirs, *got)


def close_kernel(begin, tab, mm_, tm, me, te, f_last, f_prev, b_last, b_prev, own, kept, given):
    busy, first = tab[BUSY] == 1, tab[CORE] == 0
    half, columns = kept.shape
    features = own.shape[2]

    def total(*refs):
        out = refs[0][...].astype(f32)
        for r in refs[1:]:
            out = out + r[...].astype(f32)
        return out

    main = total(mm_, tm, f_last) + jnp.where(busy, b_prev[...], b_last[...]).astype(f32)
    extra = total(me, te, f_prev, b_last)
    for c in range(columns // features):
        cols = slice(c * features, (c + 1) * features)
        m = (main[:, cols] + own[begin + c, :half].astype(f32)).astype(bf16)
        e = (extra[:, cols] + own[begin + c, half:].astype(f32)).astype(bf16)
        kept[:, cols] = jnp.where(first, m, e)
        given[:, cols] = jnp.where(first, e, m)


def close(tab, mine, theirs, got_f, got_b, own, begin, half):
    columns = mine.shape[1]
    nodes = mine.shape[0] // half
    own_at = pl.BlockSpec((half, columns), lambda i, tab: (tab[RANK], 0))
    extra_at = pl.BlockSpec((half, columns), lambda i, tab: (nodes - 1, 0))
    full = pl.BlockSpec((half, columns), lambda i, tab: (0, 0))
    out = jax.ShapeDtypeStruct((half, columns), bf16)
    return pl.pallas_call(
        functools.partial(close_kernel, begin),
        grid_spec=pltpu.PrefetchScalarGridSpec(
            num_scalar_prefetch=1,
            grid=(1,),
            in_specs=[own_at, own_at, extra_at, extra_at]
            + [full] * 4
            + [pl.BlockSpec(own.shape, lambda i, tab: (0, 0, 0))],
            out_specs=[full, full],
        ),
        out_shape=[out, out],
        compiler_params=params(),
        cost_estimate=cost(0, 24 * half * columns),
        name="close",
    )(tab, mine, theirs, mine, theirs, got_f[-1], got_f[-2], got_b[-1], got_b[-2], own)


def finish_kernel(parts, tab, *refs):
    kept, got, out = refs[:parts], refs[parts : 2 * parts], refs[-1]
    half, columns = kept[0].shape
    first = tab[CORE] == 0
    row = tab[CORE] * (2 * half) + lax.broadcasted_iota(i32, (half, 1), 0)
    for p in range(parts):
        cols = slice(p * columns, (p + 1) * columns)
        low = jnp.where(first, kept[p][...], got[p][...])
        high = jnp.where(first, got[p][...], kept[p][...])
        zero = jnp.zeros_like(low)
        out[:half, cols] = jnp.where(row < tab[LIVE], low, zero)
        out[half:, cols] = jnp.where(row + half < tab[LIVE], high, zero)


def finish(tab, kept, got):
    half, columns = kept[0].shape
    return pl.pallas_call(
        functools.partial(finish_kernel, len(kept)),
        in_specs=[smem()] + [whole()] * (2 * len(kept)),
        out_specs=whole(),
        out_shape=jax.ShapeDtypeStruct((2 * half, columns * len(kept)), bf16),
        compiler_params=params(),
        cost_estimate=cost(0, 8 * half * columns * len(kept)),
        name="finish",
    )(tab, *kept, *got)


attention_parts = 2
contract_parts = 2


def on_device(
    order,
    queries,
    latent_cache,
    new_latent,
    span_len,
    dec_count,
    span_start,
    cache_len,
    value_weight,
    out_weight,
    residual,
    norm_gain,
    gate_weight,
    up_weight,
    down_weight,
):
    ranks = len(order)
    reach = ranks // 2
    cores = lax.axis_size("head")
    rows_dev, width = residual.shape
    half = rows_dev // 2 // cores
    features = out_weight.shape[1]
    table = Table(ranks, cache_len.shape[1])

    forward = [(order[i], order[(i + 1) % ranks]) for i in range(ranks)]
    backward = [(b, a) for a, b in forward]
    exchange = [(c, cores - 1 - c) for c in range(cores)]

    def send_next(x):
        return lax.ppermute(x, "blk", forward)

    def send_prev(x):
        return lax.ppermute(x, "blk", backward)

    def swap(x):
        return lax.ppermute(x, "head", exchange)

    ids = jnp.stack([lax.axis_index("blk"), lax.axis_index("head")]).astype(i32)
    at = jnp.asarray([order.index(i) for i in range(ranks)], i32)
    who = jnp.asarray(order, i32)
    tab = pl.pallas_call(
        functools.partial(table_kernel, table, ranks),
        in_specs=[smem()] * 7,
        out_specs=smem(),
        out_shape=jax.ShapeDtypeStruct((table.size,), i32),
        name="table",
    )(ids, span_len, dec_count, span_start, cache_len, at, who)

    packed = pack(tab, residual, ranks, cores)
    res = [packed[0]]
    for shift in range(1, ranks):
        pairs = [(i, (i + shift) % ranks) for i in range(ranks)]
        res.append(lax.ppermute(packed[shift], "blk", pairs))

    total, halves = None, None
    gathered = []
    for part in range(attention_parts):
        main, extra = attend(
            tab, queries, latent_cache, new_latent, value_weight, part, attention_parts
        )
        behind, ahead = [], []
        for step in range(reach):
            if step == 0:
                (out_f,), out_b = route(tab, (extra, main)), main
            elif step == 1:
                out_f, out_b = route(tab, (main, behind[0]), (extra, ahead[0]))
            else:
                out_f, out_b = route(
                    tab,
                    (behind[step - 2], behind[step - 1]),
                    (ahead[step - 2], ahead[step - 1]),
                )
            behind.append(send_next(out_f))
            ahead.append(send_prev(out_b))
        gathered.append([main] + behind + ahead + [extra])
    for part in range(attention_parts):
        total = project(
            tab, table, gathered[part], total, out_weight, part, attention_parts, cores
        )
    kept, given = total
    stream = stream_of(tab, kept, swap(given), res)

    gain = norm_gain.reshape(ranks, 1, features)
    sums = expand(tab, [stream], [swap(stream)], [RANK], gain, gate_weight, up_weight, None, False)
    blocks, owners = [stream], [RANK]
    fore, back = stream, stream
    for step in range(1, reach + 1):
        back = send_next(back)
        arrived, from_owner = [back], [table.owner_back + step]
        if step < reach:
            fore = send_prev(fore)
            arrived, from_owner = [back, fore], from_owner + [table.owner_fore + step]
        others = [swap(x) for x in arrived]
        sums = expand(
            tab, arrived, others, from_owner, gain, gate_weight, up_weight, sums, step == reach
        )
        blocks += arrived
        owners += from_owner
    (hidden,) = sums
    own = collect(tab, blocks, owners, half)

    parts = contract_parts
    mine, theirs = [], []
    for part in range(parts):
        a, b = contract(hidden, down_weight, part, parts)
        mine.append(a)
        theirs.append(swap(b))
    kept_out, got_out = [], []
    for part in range(parts):
        got_f, got_b = [], []
        for step in range(1, reach + 1):
            if step == 1:
                got = []
            elif step == 2:
                got = [got_f[0], got_b[0]]
            else:
                got = [got_f[step - 3], got_f[step - 2], got_b[step - 3], got_b[step - 2]]
            out_f, out_b = add(tab, table, step, mine[part], theirs[part], got, half)
            got_f.append(send_next(out_f))
            got_b.append(send_prev(out_b))
        a, b = close(
            tab, mine[part], theirs[part], got_f, got_b, own, part * (ranks // parts), half
        )
        kept_out.append(a)
        got_out.append(swap(b))
    return finish(tab, kept_out, got_out)


def solution(mesh):
    placed = (
        P(("groups", "blk"), "head"),
        P(("groups", "blk"), None, None),
        P(None, ("groups", "blk")),
        P("groups"),
        P("groups"),
        P(("groups", "blk")),
        P(("groups", "blk"), None),
        P("head", None, None),
        P("head", "blk"),
        P(("groups", "blk"), None),
        P(),
        P(None, ("blk", "head")),
        P(None, ("blk", "head")),
        P(("blk", "head"), None),
    )
    order = ring_order(mesh)
    return jax.shard_map(
        lambda *args: on_device(order, *args),
        mesh=mesh,
        in_specs=placed,
        out_specs=P(("groups", "blk", "head"), None),
        check_vma=False,
    )
```

```python
import functools

import jax
import jax.numpy as jnp
from jax import lax
from jax.experimental import pallas as pl
from jax.experimental.pallas import tpu as pltpu
from jax.sharding import PartitionSpec as P

score_scale = 192.0 ** (-0.5)
norm_eps = 1e-06
masked_score = -1e30
f32, bf16, i32 = jnp.float32, jnp.bfloat16, jnp.int32
SMEM = pltpu.SMEM
MIB = 1 << 20

RANK, CORE, BUSY, BUSY_RANK, SPAN, DEC, LIVE, START, LENGTHS = range(9)


def mm(a, b):
    return lax.dot_general(a, b, (((1,), (0,)), ((), ())), preferred_element_type=f32)


def mm_nt(a, b):
    return lax.dot_general(a, b, (((1,), (1,)), ((), ())), preferred_element_type=f32)


def smem():
    return pl.BlockSpec(memory_space=SMEM)


def whole():
    return pl.BlockSpec(memory_space=pltpu.VMEM)


def params(mib=32):
    return pltpu.CompilerParams(vmem_limit_bytes=mib * MIB)


def cost(flops, moved, exps=0):
    return pl.CostEstimate(flops=int(flops), bytes_accessed=int(moved), transcendentals=int(exps))


def ring_order(mesh):
    count = mesh.shape["blk"]
    natural = list(range(count))
    snake = natural[0::2] + natural[1::2][::-1]
    names = list(mesh.axis_names)
    axes = [names.index("blk")] + [a for a, x in enumerate(names) if x != "blk"]
    lane = mesh.devices.transpose(axes)
    firsts = [lane[i].reshape(-1)[0] for i in natural]
    if not all(hasattr(d, "coords") for d in firsts):
        return snake

    def length(order):
        hops = zip(order, order[1:] + order[:1])
        return sum(
            sum(abs(u - v) for u, v in zip(firsts[a].coords, firsts[b].coords)) for a, b in hops
        )

    return natural if length(natural) <= length(snake) else snake


class Table:
    def __init__(self, ranks, slots):
        self.reach = ranks // 2
        self.source = LENGTHS + slots
        self.ahead = self.source + ranks + 1
        self.behind = self.ahead + self.reach + 1
        self.owner_back = self.behind + self.reach + 1
        self.owner_fore = self.owner_back + self.reach + 1
        self.size = self.owner_fore + self.reach + 1


def table_kernel(table, ranks, ids, span, dec, start, lengths, at, who, out):
    reach = table.reach
    rank, core = ids[0], ids[1]
    most, busy_rank = span[0] + dec[0], jnp.int32(0)
    for i in range(1, ranks):
        here = span[i] + dec[i]
        busy_rank = jnp.where(here > most, i, busy_rank)
        most = jnp.maximum(here, most)
    busy = rank == busy_rank

    def wrap(x):
        x = jnp.where(x < 0, x + ranks, x)
        return jnp.where(x >= ranks, x - ranks, x)

    place, busy_place = at[rank], at[busy_rank]
    to_busy = wrap(busy_place - place)
    from_busy = wrap(place - busy_place)

    def node_ahead(k):
        far = (to_busy > 0) & (k > to_busy + 1)
        slot = who[wrap(place + k - jnp.where(far, 1, 0))]
        return jnp.where((to_busy > 0) & (k == to_busy + 1), ranks, slot)

    def node_behind(k):
        far = (from_busy > 0) & (k > from_busy)
        slot = who[wrap(place - k + jnp.where(far, 1, 0))]
        return jnp.where((from_busy > 0) & (k == from_busy), ranks, slot)

    out[RANK] = rank
    out[CORE] = core
    out[BUSY] = jnp.where(busy, 1, 0)
    out[BUSY_RANK] = busy_rank
    out[SPAN] = span[rank]
    out[DEC] = dec[rank]
    out[LIVE] = span[rank] + dec[rank]
    out[START] = start[0]
    for j in range(lengths.shape[1]):
        out[LENGTHS + j] = lengths[0, j]
    out[table.source + rank] = 0
    for k in range(1, reach + 1):
        out[table.ahead + k] = node_ahead(k)
        out[table.behind + k] = node_behind(k)
        out[table.owner_back + k] = who[wrap(place - k)]
        out[table.owner_fore + k] = who[wrap(place + k)]
        out[table.source + node_behind(k)] = k
        last = jnp.where(busy, ranks, node_ahead(k)) if k == reach else node_ahead(k)
        out[table.source + last] = reach + k


def attend_kernel(
    heads, group, rows, lat, cached, value, start_step,
    tab, q, cache, fresh, vw, main, extra, k0, k1, kpad, dq, dec, turn,
):
    pair = 2 * lat
    wide = -(-lat // 128) * 128
    shift = wide - lat
    keys = cached + rows
    cols = -(-keys // 128) * 128
    slots = cache.shape[0] - 1
    dr = 8
    span, decs = tab[SPAN], tab[DEC]

    def onehot(shape, row_dim, slot_dim):
        r = lax.broadcasted_iota(i32, shape, row_dim)
        j = lax.broadcasted_iota(i32, shape, slot_dim)
        return jnp.where((r == span + j) & (j < decs), 1.0, 0.0).astype(bf16)

    @pl.when(pl.program_id(0) == 0)
    def _():
        turn[...] = jnp.zeros_like(turn)
        turn[:rows, :lat] = fresh[...].astype(f32)
        turned = turn[...].T.astype(bf16)[:lat]
        k0[...] = jnp.zeros_like(k0)
        k1[...] = jnp.zeros_like(k1)
        for ref, off in ((k0, 0), (k1, shift)):
            ref[off : off + lat, :cached] = cache[0]
            ref[off : off + lat, cached:] = turned
        kpad[...] = jnp.zeros_like(kpad)
        for s in range(slots):
            kpad[s, :lat] = cache[s + 1]
        pick = onehot((16, rows), 1, 0)
        for p in range(heads // 2):
            got = mm(pick, q[:, pair * p : pair * (p + 1)])[:dr]
            dq[2 * p * dr : (2 * p + 1) * dr] = got[:, :wide]
            dq[(2 * p + 1) * dr : (2 * p + 2) * dr] = pltpu.roll(got[:, pair - wide :], wide - shift, 1)
        n = heads * dr
        queries = dq[...].astype(bf16)
        slot = lax.broadcasted_iota(i32, (n, 1), 0) % dr
        length = jnp.zeros((n, 1), i32)
        scores = jnp.zeros((n, cached), f32)
        for s in range(slots):
            scores = jnp.where(slot == s, mm(queries, kpad[s]), scores)
            length = jnp.where(slot == s, tab[LENGTHS + s], length)
        seen = lax.broadcasted_iota(i32, (n, cached), 1) < length
        scores = jnp.where(seen, scores * score_scale, masked_score)
        own = mm(queries, k0[:, cached:])
        column = lax.broadcasted_iota(i32, own.shape, 1)
        own = jnp.sum(jnp.where(column == span + slot, own, 0.0), axis=1, keepdims=True)
        own = own * score_scale
        peak = jnp.maximum(jnp.max(scores, axis=1, keepdims=True), own)
        e = jnp.where(seen, jnp.exp(scores - peak), 0.0)
        e_own = jnp.exp(own - peak)
        total = jnp.sum(e, axis=1, keepdims=True) + e_own
        w = e / total
        acc = jnp.zeros((n, value), f32)
        for s in range(slots):
            acc = acc + mm_nt(jnp.where(slot == s, w, 0.0).astype(bf16), cache[s + 1, :value])
        own_value = mm(pick, fresh[:, :value])[:dr]
        own_value = jnp.broadcast_to(own_value[None], (heads, dr, value)).reshape(n, value)
        dec[...] = acc + (e_own / total).astype(bf16).astype(f32) * own_value

    step = pl.program_id(0)
    start = step * (group * lat)
    pairs = group // 2

    def stacked(off):
        return jnp.concatenate(
            [q[:, pl.ds(pl.multiple_of(start + pair * p + off, 128), wide)] for p in range(pairs)], 0
        )

    m = pairs * rows
    row = lax.broadcasted_iota(i32, (m, 1), 0) % rows
    col = lax.broadcasted_iota(i32, (m, cols), 1)
    seen = (col < jnp.where(col < cached, tab[START], cached + 1 + row)) & (col < keys)
    values = k0[:value]

    def latent(lhs, ref):
        s = jnp.where(seen, mm(lhs, ref[...]) * score_scale, masked_score)
        e = jnp.where(seen, jnp.exp(s - jnp.max(s, axis=1, keepdims=True)), 0.0)
        w = (e * (1.0 / jnp.sum(e, axis=1, keepdims=True))).astype(bf16)
        o = mm_nt(w, values)
        return jnp.where(row < span, o, 0.0).astype(bf16)

    even, odd = latent(stacked(0), k0), latent(stacked(pair - wide), k1)
    outs, decoded = [], []
    for p in range(pairs):
        at = pl.multiple_of((step * group + 2 * p) * dr, 16)
        lhs = jnp.concatenate(
            [even[p * rows : (p + 1) * rows], odd[p * rows : (p + 1) * rows], dec[pl.ds(at, 16)].astype(bf16)], 0
        )
        vh = vw.shape[2]
        r = mm(lhs, jnp.concatenate([vw[2 * p], vw[2 * p + 1]], 1))
        outs += [r[:rows, :vh], r[rows : 2 * rows, vh:]]
        decoded += [r[2 * rows : 2 * rows + dr, :vh], r[2 * rows + dr :, vh:]]
    decoded = jnp.concatenate(decoded, 1)
    decoded = jnp.concatenate([decoded, jnp.zeros_like(decoded)], 0).astype(bf16)
    out = jnp.concatenate(outs, 1) + mm(onehot((rows, 16), 0, 1), decoded)
    out = out.astype(bf16)
    main[...] = out[: rows // 2]
    extra[...] = out[rows // 2 :]


def attend(tab, queries, cache, fresh, vw, part, parts):
    rows, heads = queries.shape[0], vw.shape[0] // parts
    lat = queries.shape[1] // vw.shape[0]
    slots, _, cached = cache.shape
    value, vh = vw.shape[1:]
    group = min(8, heads)
    wide, cols = -(-lat // 128) * 128, -(-(cached + rows) // 128) * 128
    steps = heads // group
    half = jax.ShapeDtypeStruct((rows // 2, heads * vh), bf16)
    return pl.pallas_call(
        functools.partial(attend_kernel, heads, group, rows, lat, cached, value, part),
        grid=(steps,),
        in_specs=[
            smem(),
            pl.BlockSpec((rows, heads * lat), lambda i: (0, part)),
            pl.BlockSpec(cache.shape, lambda i: (0, 0, 0)),
            pl.BlockSpec(fresh.shape[::-1], lambda i: (0, 0)),
            pl.BlockSpec((group, value, vh), lambda i: (part * steps + i, 0, 0)),
        ],
        out_specs=[pl.BlockSpec((rows // 2, group * vh), lambda i: (0, i))] * 2,
        out_shape=[half, half],
        scratch_shapes=[
            pltpu.VMEM((wide, cols), bf16),
            pltpu.VMEM((wide, cols), bf16),
            pltpu.VMEM((slots - 1, wide, cached), bf16),
            pltpu.VMEM((heads * 8, wide), f32),
            pltpu.VMEM((heads * 8, value), f32),
            pltpu.VMEM((cols - cached, wide), f32),
        ],
        compiler_params=params(56),
        cost_estimate=cost(
            2 * rows * heads * (cached + rows) * (lat + value),
            2 * (queries.size // parts + cache.size + vw.size // parts),
            rows * heads * (cached + rows),
        ),
        name="attend",
    )(tab, queries, cache, fresh.T, vw)


def pack_kernel(ranks, features, half, tab, res, *outs):
    core, rank = tab[CORE], tab[RANK]
    low = pl.multiple_of(core * half, half)
    high = pl.multiple_of(res.shape[0] // 2 + core * half, half)
    for k in range(ranks):
        target = rank + k
        target = jnp.where(target >= ranks, target - ranks, target)

        def put(columns, k=k):
            outs[k][:half] = res[pl.ds(low, half), columns]
            outs[k][half:] = res[pl.ds(high, half), columns]

        if features % 128 == 0:
            put(pl.ds(pl.multiple_of(target * features, 128), features))
        else:
            for t in range(ranks):
                pl.when(target == t)(functools.partial(put, slice(t * features, (t + 1) * features)))


def pack(tab, residual, ranks, cores):
    rows, width = residual.shape
    half, features = rows // 2 // cores, width // ranks
    return pl.pallas_call(
        functools.partial(pack_kernel, ranks, features, half),
        in_specs=[smem(), whole()],
        out_specs=[whole()] * ranks,
        out_shape=[jax.ShapeDtypeStruct((2 * half, features), bf16)] * ranks,
        compiler_params=params(),
        cost_estimate=cost(0, 4 * residual.size),
        name="pack",
    )(tab, residual)


def route_kernel(tab, *refs):
    count = len(refs) // 3
    busy = tab[BUSY] == 1
    for i in range(count):
        special, usual, out = refs[2 * i], refs[2 * i + 1], refs[2 * count + i]

        @pl.when(busy)
        def _(special=special, out=out):
            out[...] = special[...]

        @pl.when(jnp.logical_not(busy))
        def _(usual=usual, out=out):
            out[...] = usual[...]


def route(tab, *choices):
    flat = [x for pair in choices for x in pair]
    return pl.pallas_call(
        route_kernel,
        in_specs=[smem()] + [whole()] * len(flat),
        out_specs=[whole()] * len(choices),
        out_shape=[jax.ShapeDtypeStruct(b.shape, b.dtype) for _, b in choices],
        compiler_params=params(),
        cost_estimate=cost(0, 3 * sum(2 * b.size for _, b in choices)),
        name="route",
    )(tab, *flat)


def project_kernel(source, nodes, block, half, first, tab, *refs):
    blocks, refs = refs[: nodes + 1], refs[nodes + 1 :]
    before = None if first else refs[0]
    weight, kept, given, acc = refs[-4:]
    step = pl.program_id(0)
    depth = weight.shape[0]
    columns = pl.ds(pl.multiple_of(step * depth, 128), depth)
    last = jnp.where(tab[BUSY] == 1, blocks[nodes][:, columns], blocks[nodes - 1][:, columns])
    lhs = jnp.concatenate([b[:, columns] for b in blocks[: nodes - 1]] + [last], 0)
    got = mm(lhs, weight[...])

    @pl.when(step == 0)
    def _():
        acc[...] = got if first else got + before[...]

    @pl.when(step > 0)
    def _():
        acc[...] += got

    @pl.when(step == pl.num_programs(0) - 1)
    def _():
        core = tab[CORE]
        for k in range(nodes):
            at = tab[source + k] * block
            kept[k * half : (k + 1) * half] = acc[pl.ds(pl.multiple_of(at + core * half, half), half)]
            other = acc[pl.ds(pl.multiple_of(at + (1 - core) * half, half), half)]
            given[k * half : (k + 1) * half] = other.astype(bf16)


def project_part_kernel(nodes, first, tab, *refs):
    blocks, refs = refs[: nodes + 1], refs[nodes + 1 :]
    weight, out = refs[-2:]
    step = pl.program_id(0)
    depth = weight.shape[0]
    columns = pl.ds(pl.multiple_of(step * depth, 128), depth)
    last = jnp.where(tab[BUSY] == 1, blocks[nodes][:, columns], blocks[nodes - 1][:, columns])
    lhs = jnp.concatenate([b[:, columns] for b in blocks[: nodes - 1]] + [last], 0)
    got = mm(lhs, weight[...])

    @pl.when(step == 0)
    def _():
        out[...] = got if first else got + refs[0][...]

    @pl.when(step > 0)
    def _():
        out[...] += got


def project(tab, table, blocks, before, weight, part, parts, cores):
    block, width = blocks[0].shape
    nodes = len(blocks) - 1
    half = block // cores
    features = weight.shape[1]
    depth = 1024 if width % 1024 == 0 else width
    steps = width // depth
    total = jax.ShapeDtypeStruct((nodes * block, features), f32)
    final = part == parts - 1
    first = before is None
    ins = [smem()] + [whole()] * (nodes + 1 + (not first))
    ins += [pl.BlockSpec((depth, features), lambda i: (part * steps + i, 0))]
    args = [tab, *blocks] + ([] if first else [before]) + [weight]
    estimate = cost(
        2 * nodes * block * width * features, 2 * (nodes * block * width + width * features)
    )
    if not final:
        return pl.pallas_call(
            functools.partial(project_part_kernel, nodes, first),
            grid=(steps,),
            in_specs=ins,
            out_specs=pl.BlockSpec(total.shape, lambda i: (0, 0)),
            out_shape=total,
            compiler_params=params(),
            cost_estimate=estimate,
            name="project",
        )(*args)
    return pl.pallas_call(
        functools.partial(project_kernel, table.source, nodes, block, half, first),
        grid=(steps,),
        in_specs=ins,
        out_specs=[pl.BlockSpec((nodes * half, features), lambda i: (0, 0))] * 2,
        out_shape=[
            jax.ShapeDtypeStruct((nodes * half, features), f32),
            jax.ShapeDtypeStruct((nodes * half, features), bf16),
        ],
        scratch_shapes=[pltpu.VMEM(total.shape, f32)],
        compiler_params=params(),
        cost_estimate=estimate,
        name="project",
    )(*args)


def stream_kernel(ranks, half, tab, kept, other, *refs):
    res, out = refs[:-1], refs[-1]
    rank, busy_rank = tab[RANK], tab[BUSY_RANK]

    def put(slot, extra):
        rows = pl.ds(pl.multiple_of(slot * half, half), half)
        total = kept[rows] + other[rows].astype(f32) + extra.astype(f32)
        out[rows] = total.astype(bf16)

    for k in range(ranks):
        owner = rank - k
        owner = jnp.where(owner < 0, owner + ranks, owner)
        put(owner, res[k][:half])

        @pl.when(owner == busy_rank)
        def _(k=k):
            put(ranks, res[k][half:])


def stream_of(tab, kept, other, res):
    half = res[0].shape[0] // 2
    return pl.pallas_call(
        functools.partial(stream_kernel, len(res), half),
        in_specs=[smem()] + [whole()] * (2 + len(res)),
        out_specs=whole(),
        out_shape=jax.ShapeDtypeStruct(other.shape, bf16),
        compiler_params=params(),
        cost_estimate=cost(0, 10 * other.size),
        name="stream",
    )(tab, kept, other, *res)


def expand_kernel(count, first, final, width, turned, tab, *refs):
    mines, theirs = refs[:count], refs[count : 2 * count]
    refs = refs[2 * count :]
    gain, gate, up = refs[:3]
    refs = refs[3:]
    if not first:
        before, refs = refs[:3], refs[3:]
    if final:
        hidden, refs = refs[0], refs[1:]
    gates, ups, squares = refs
    step = pl.program_id(0)
    for i in range(count):

        @pl.when(step == i)
        def _(i=i):
            both = jnp.concatenate([mines[i][...], theirs[i][...]], 0).astype(f32)
            scaled = (both * gain[0]).astype(bf16)
            times = mm_nt if turned else mm
            values = (
                times(scaled, gate[...]),
                times(scaled, up[...]),
                jnp.sum(both * both, axis=1, keepdims=True),
            )
            for n, (ref, value) in enumerate(zip((gates, ups, squares), values)):
                if i == 0:
                    ref[...] = value if first else value + before[n][...]
                else:
                    ref[...] += value

    if final:

        @pl.when(step == count - 1)
        def _():
            scale = lax.rsqrt(squares[...] / width + norm_eps)
            g = gates[...] * scale
            hidden[...] = (g / (1.0 + jnp.exp(-g)) * (ups[...] * scale)).astype(bf16)


def expand(tab, mines, theirs, owners, gain, gate, up, before, final):
    count = len(mines)
    rows, features = mines[0].shape
    units = gate.shape[1]
    first = before is None
    width = gate.shape[0]

    def owner(i, tab):
        index = tab[owners[0]]
        for n in range(1, count):
            index = jnp.where(i == n, tab[owners[n]], index)
        return index

    def full(shape):
        return pl.BlockSpec(shape, lambda i, tab: (0,) * len(shape))

    sums = [(2 * rows, units), (2 * rows, units), (2 * rows, 1)]
    ins = [full((rows, features))] * (2 * count)
    ins += [pl.BlockSpec((1, 1, features), lambda i, tab: (owner(i, tab), 0, 0))]
    turned = features % 128 == 0
    if turned:
        gate, up = gate.T, up.T
        ins += [pl.BlockSpec((units, features), lambda i, tab: (0, owner(i, tab)))] * 2
    else:
        ins += [pl.BlockSpec((features, units), lambda i, tab: (owner(i, tab), 0))] * 2
    if not first:
        ins += [full(s) for s in sums]
    shapes = [jax.ShapeDtypeStruct(s, f32) for s in sums]
    out_shapes = [jax.ShapeDtypeStruct((2 * rows, units), bf16)] if final else shapes
    return pl.pallas_call(
        functools.partial(expand_kernel, count, first, final, width, turned),
        grid_spec=pltpu.PrefetchScalarGridSpec(
            num_scalar_prefetch=1,
            grid=(count,),
            in_specs=ins,
            out_specs=[full(s.shape) for s in out_shapes],
            scratch_shapes=[pltpu.VMEM(s, f32) for s in sums] if final else [],
        ),
        out_shape=out_shapes,
        compiler_params=params(56),
        cost_estimate=cost(
            8 * count * rows * features * units, count * (4 * features * units + 4 * rows * features)
        ),
        name="expand",
    )(tab, *mines, *theirs, gain, gate, up, *([] if first else before))


def collect_kernel(owners, tab, *refs):
    out = refs[-1]
    half = out.shape[1] // 2
    for i, at in enumerate(owners):
        out[tab[at], :half] = refs[2 * i][...]
        out[tab[at], half:] = refs[2 * i + 1][...]


def collect(tab, blocks, owners, half):
    ranks = len(blocks)
    features = blocks[0].shape[1]
    ins, args = [], []
    for x in blocks:
        ins += [
            pl.BlockSpec((half, features), lambda i, tab: (tab[RANK], 0)),
            pl.BlockSpec((half, features), lambda i, tab: (ranks, 0)),
        ]
        args += [x, x]
    shape = (ranks, 2 * half, features)
    return pl.pallas_call(
        functools.partial(collect_kernel, owners),
        grid_spec=pltpu.PrefetchScalarGridSpec(
            num_scalar_prefetch=1,
            grid=(1,),
            in_specs=ins,
            out_specs=pl.BlockSpec(shape, lambda i, tab: (0, 0, 0)),
        ),
        out_shape=jax.ShapeDtypeStruct(shape, bf16),
        compiler_params=params(),
        cost_estimate=cost(0, 8 * ranks * half * features),
        name="collect",
    )(tab, *args)


def contract_kernel(hidden, weight, mine, given):
    got = mm(hidden[...], weight[...]).astype(bf16)
    rows = mine.shape[0]
    mine[...] = got[:rows]
    given[...] = got[rows:]


def contract(hidden, weight, part, parts):
    rows, units = hidden.shape
    columns = weight.shape[1] // parts
    wide = columns // 2 if columns % 256 == 0 else columns
    steps = columns // wide
    out = jax.ShapeDtypeStruct((rows // 2, columns), bf16)
    return pl.pallas_call(
        contract_kernel,
        grid=(steps,),
        in_specs=[
            pl.BlockSpec((rows, units), lambda i: (0, 0)),
            pl.BlockSpec((units, wide), lambda i: (0, part * steps + i)),
        ],
        out_specs=[pl.BlockSpec((rows // 2, wide), lambda i: (0, i))] * 2,
        out_shape=[out, out],
        compiler_params=params(),
        cost_estimate=cost(2 * rows * units * columns, 2 * (units + rows) * columns),
        name="contract",
    )(hidden, weight)


def add_kernel(step, tab, mine_f, theirs_f, mine_b, theirs_b, *refs):
    got, (out_f, out_b) = refs[:-2], refs[-2:]
    busy = tab[BUSY] == 1
    own_f = mine_f[...].astype(f32) + theirs_f[...].astype(f32)
    own_b = mine_b[...].astype(f32) + theirs_b[...].astype(f32)
    if step == 1:
        out_f[...] = jnp.where(busy, 0.0, own_f).astype(bf16)
        out_b[...] = own_b.astype(bf16)
    elif step == 2:
        out_f[...] = (own_f + jnp.where(busy, 0.0, got[0][...].astype(f32))).astype(bf16)
        out_b[...] = (own_b + jnp.where(busy, 0.0, got[1][...].astype(f32))).astype(bf16)
    else:
        from_f = jnp.where(busy, got[0][...], got[1][...]).astype(f32)
        from_b = jnp.where(busy, got[2][...], got[3][...]).astype(f32)
        out_f[...] = (own_f + from_f).astype(bf16)
        out_b[...] = (own_b + from_b).astype(bf16)


def add(tab, table, step, mine, theirs, got, half):
    columns = mine.shape[1]
    far = table.reach + 1 - step

    def at(where):
        return pl.BlockSpec((half, columns), lambda i, tab: (tab[where + far], 0))

    full = pl.BlockSpec((half, columns), lambda i, tab: (0, 0))
    out = jax.ShapeDtypeStruct((half, columns), bf16)
    return pl.pallas_call(
        functools.partial(add_kernel, step),
        grid_spec=pltpu.PrefetchScalarGridSpec(
            num_scalar_prefetch=1,
            grid=(1,),
            in_specs=[at(table.ahead)] * 2 + [at(table.behind)] * 2 + [full] * len(got),
            out_specs=[full, full],
        ),
        out_shape=[out, out],
        compiler_params=params(),
        cost_estimate=cost(0, 16 * half * columns),
        name="add",
    )(tab, mine, theirs, mine, theirs, *got)


def close_kernel(begin, tab, mm_, tm, me, te, f_last, f_prev, b_last, b_prev, own, kept, given):
    busy, first = tab[BUSY] == 1, tab[CORE] == 0
    half, columns = kept.shape
    features = own.shape[2]

    def total(*refs):
        out = refs[0][...].astype(f32)
        for r in refs[1:]:
            out = out + r[...].astype(f32)
        return out

    main = total(mm_, tm, f_last) + jnp.where(busy, b_prev[...], b_last[...]).astype(f32)
    extra = total(me, te, f_prev, b_last)
    for c in range(columns // features):
        cols = slice(c * features, (c + 1) * features)
        m = (main[:, cols] + own[begin + c, :half].astype(f32)).astype(bf16)
        e = (extra[:, cols] + own[begin + c, half:].astype(f32)).astype(bf16)
        kept[:, cols] = jnp.where(first, m, e)
        given[:, cols] = jnp.where(first, e, m)


def close(tab, mine, theirs, got_f, got_b, own, begin, half):
    columns = mine.shape[1]
    nodes = mine.shape[0] // half
    own_at = pl.BlockSpec((half, columns), lambda i, tab: (tab[RANK], 0))
    extra_at = pl.BlockSpec((half, columns), lambda i, tab: (nodes - 1, 0))
    full = pl.BlockSpec((half, columns), lambda i, tab: (0, 0))
    out = jax.ShapeDtypeStruct((half, columns), bf16)
    return pl.pallas_call(
        functools.partial(close_kernel, begin),
        grid_spec=pltpu.PrefetchScalarGridSpec(
            num_scalar_prefetch=1,
            grid=(1,),
            in_specs=[own_at, own_at, extra_at, extra_at]
            + [full] * 4
            + [pl.BlockSpec(own.shape, lambda i, tab: (0, 0, 0))],
            out_specs=[full, full],
        ),
        out_shape=[out, out],
        compiler_params=params(),
        cost_estimate=cost(0, 24 * half * columns),
        name="close",
    )(tab, mine, theirs, mine, theirs, got_f[-1], got_f[-2], got_b[-1], got_b[-2], own)


def finish_kernel(parts, tab, *refs):
    kept, got, out = refs[:parts], refs[parts : 2 * parts], refs[-1]
    half, columns = kept[0].shape
    first = tab[CORE] == 0
    row = tab[CORE] * (2 * half) + lax.broadcasted_iota(i32, (half, 1), 0)
    for p in range(parts):
        cols = slice(p * columns, (p + 1) * columns)
        low = jnp.where(first, kept[p][...], got[p][...])
        high = jnp.where(first, got[p][...], kept[p][...])
        zero = jnp.zeros_like(low)
        out[:half, cols] = jnp.where(row < tab[LIVE], low, zero)
        out[half:, cols] = jnp.where(row + half < tab[LIVE], high, zero)


def finish(tab, kept, got):
    half, columns = kept[0].shape
    return pl.pallas_call(
        functools.partial(finish_kernel, len(kept)),
        in_specs=[smem()] + [whole()] * (2 * len(kept)),
        out_specs=whole(),
        out_shape=jax.ShapeDtypeStruct((2 * half, columns * len(kept)), bf16),
        compiler_params=params(),
        cost_estimate=cost(0, 8 * half * columns * len(kept)),
        name="finish",
    )(tab, *kept, *got)


attention_parts = 2
contract_parts = 2


def on_device(
    order,
    queries,
    latent_cache,
    new_latent,
    span_len,
    dec_count,
    span_start,
    cache_len,
    value_weight,
    out_weight,
    residual,
    norm_gain,
    gate_weight,
    up_weight,
    down_weight,
):
    ranks = len(order)
    reach = ranks // 2
    cores = lax.axis_size("head")
    rows_dev, width = residual.shape
    half = rows_dev // 2 // cores
    features = out_weight.shape[1]
    table = Table(ranks, cache_len.shape[1])

    forward = [(order[i], order[(i + 1) % ranks]) for i in range(ranks)]
    backward = [(b, a) for a, b in forward]
    exchange = [(c, cores - 1 - c) for c in range(cores)]

    def send_next(x):
        return lax.ppermute(x, "blk", forward)

    def send_prev(x):
        return lax.ppermute(x, "blk", backward)

    def swap(x):
        return lax.ppermute(x, "head", exchange)

    ids = jnp.stack([lax.axis_index("blk"), lax.axis_index("head")]).astype(i32)
    at = jnp.asarray([order.index(i) for i in range(ranks)], i32)
    who = jnp.asarray(order, i32)
    tab = pl.pallas_call(
        functools.partial(table_kernel, table, ranks),
        in_specs=[smem()] * 7,
        out_specs=smem(),
        out_shape=jax.ShapeDtypeStruct((table.size,), i32),
        name="table",
    )(ids, span_len, dec_count, span_start, cache_len, at, who)

    packed = pack(tab, residual, ranks, cores)
    res = [packed[0]]
    for shift in range(1, ranks):
        pairs = [(i, (i + shift) % ranks) for i in range(ranks)]
        res.append(lax.ppermute(packed[shift], "blk", pairs))

    total, halves = None, None
    gathered = []
    for part in range(attention_parts):
        main, extra = attend(
            tab, queries, latent_cache, new_latent, value_weight, part, attention_parts
        )
        behind, ahead = [], []
        for step in range(reach):
            if step == 0:
                (out_f,), out_b = route(tab, (extra, main)), main
            elif step == 1:
                out_f, out_b = route(tab, (main, behind[0]), (extra, ahead[0]))
            else:
                out_f, out_b = route(
                    tab,
                    (behind[step - 2], behind[step - 1]),
                    (ahead[step - 2], ahead[step - 1]),
                )
            behind.append(send_next(out_f))
            ahead.append(send_prev(out_b))
        gathered.append([main] + behind + ahead + [extra])
    tied = lax.optimization_barrier((gathered[0], res))
    gathered[0], res = tied
    for part in range(attention_parts):
        total = project(
            tab, table, gathered[part], total, out_weight, part, attention_parts, cores
        )
    kept, given = total
    stream = stream_of(tab, kept, swap(given), res)

    gain = norm_gain.reshape(ranks, 1, features)
    sums = expand(tab, [stream], [swap(stream)], [RANK], gain, gate_weight, up_weight, None, False)
    blocks, owners = [stream], [RANK]
    fore, back = stream, stream
    cut = -(-stream.shape[0] // 32) * 16
    for step in range(1, reach + 1):
        if step < reach:
            back, fore = send_next(back), send_prev(fore)
            arrived = [back, fore]
            from_owner = [table.owner_back + step, table.owner_fore + step]
        else:
            last = [send_next(back[:cut]), send_prev(fore[cut:])]
            arrived = [jnp.concatenate(last, 0)]
            from_owner = [table.owner_back + step]
        others = [swap(x) for x in arrived]
        sums = expand(
            tab, arrived, others, from_owner, gain, gate_weight, up_weight, sums, step == reach
        )
        blocks += arrived
        owners += from_owner
    (hidden,) = sums
    own = collect(tab, blocks, owners, half)

    parts = contract_parts
    mine, theirs = [], []
    for part in range(parts):
        a, b = contract(hidden, down_weight, part, parts)
        mine.append(a)
        theirs.append(swap(b))
    kept_out, got_out = [], []
    for part in range(parts):
        got_f, got_b = [], []
        for step in range(1, reach + 1):
            if step == 1:
                got = []
            elif step == 2:
                got = [got_f[0], got_b[0]]
            else:
                got = [got_f[step - 3], got_f[step - 2], got_b[step - 3], got_b[step - 2]]
            out_f, out_b = add(tab, table, step, mine[part], theirs[part], got, half)
            got_f.append(send_next(out_f))
            got_b.append(send_prev(out_b))
        a, b = close(
            tab, mine[part], theirs[part], got_f, got_b, own, part * (ranks // parts), half
        )
        kept_out.append(a)
        got_out.append(swap(b))
    return finish(tab, kept_out, got_out)


def solution(mesh):
    placed = (
        P(("groups", "blk"), "head"),
        P(("groups", "blk"), None, None),
        P(None, ("groups", "blk")),
        P("groups"),
        P("groups"),
        P(("groups", "blk")),
        P(("groups", "blk"), None),
        P("head", None, None),
        P("head", "blk"),
        P(("groups", "blk"), None),
        P(),
        P(None, ("blk", "head")),
        P(None, ("blk", "head")),
        P(("blk", "head"), None),
    )
    order = ring_order(mesh)
    return jax.shard_map(
        lambda *args: on_device(order, *args),
        mesh=mesh,
        in_specs=placed,
        out_specs=P(("groups", "blk", "head"), None),
        check_vma=False,
    )
```

```python
import functools

import jax
import jax.numpy as jnp
from jax import lax
from jax.experimental import pallas as pl
from jax.experimental.pallas import tpu as pltpu
from jax.sharding import PartitionSpec as P

score_scale = 192.0 ** (-0.5)
norm_eps = 1e-06
masked_score = -1e30
f32, bf16, i32 = jnp.float32, jnp.bfloat16, jnp.int32
SMEM = pltpu.SMEM
MIB = 1 << 20

RANK, CORE, BUSY, BUSY_RANK, SPAN, DEC, LIVE, START, LENGTHS = range(9)


def mm(a, b):
    return lax.dot_general(a, b, (((1,), (0,)), ((), ())), preferred_element_type=f32)


def mm_nt(a, b):
    return lax.dot_general(a, b, (((1,), (1,)), ((), ())), preferred_element_type=f32)


def smem():
    return pl.BlockSpec(memory_space=SMEM)


def whole():
    return pl.BlockSpec(memory_space=pltpu.VMEM)


def params(mib=32):
    return pltpu.CompilerParams(vmem_limit_bytes=mib * MIB)


def cost(flops, moved, exps=0):
    return pl.CostEstimate(flops=int(flops), bytes_accessed=int(moved), transcendentals=int(exps))


def ring_order(mesh):
    count = mesh.shape["blk"]
    natural = list(range(count))
    snake = natural[0::2] + natural[1::2][::-1]
    names = list(mesh.axis_names)
    axes = [names.index("blk")] + [a for a, x in enumerate(names) if x != "blk"]
    lane = mesh.devices.transpose(axes)
    firsts = [lane[i].reshape(-1)[0] for i in natural]
    if not all(hasattr(d, "coords") for d in firsts):
        return snake

    def length(order):
        hops = zip(order, order[1:] + order[:1])
        return sum(
            sum(abs(u - v) for u, v in zip(firsts[a].coords, firsts[b].coords)) for a, b in hops
        )

    return natural if length(natural) <= length(snake) else snake


class Table:
    def __init__(self, ranks, slots):
        self.reach = ranks // 2
        self.source = LENGTHS + slots
        self.ahead = self.source + ranks + 1
        self.behind = self.ahead + self.reach + 1
        self.owner_back = self.behind + self.reach + 1
        self.owner_fore = self.owner_back + self.reach + 1
        self.size = self.owner_fore + self.reach + 1


def table_kernel(table, ranks, ids, span, dec, start, lengths, at, who, out):
    reach = table.reach
    rank, core = ids[0], ids[1]
    most, busy_rank = span[0] + dec[0], jnp.int32(0)
    for i in range(1, ranks):
        here = span[i] + dec[i]
        busy_rank = jnp.where(here > most, i, busy_rank)
        most = jnp.maximum(here, most)
    busy = rank == busy_rank

    def wrap(x):
        x = jnp.where(x < 0, x + ranks, x)
        return jnp.where(x >= ranks, x - ranks, x)

    place, busy_place = at[rank], at[busy_rank]
    to_busy = wrap(busy_place - place)
    from_busy = wrap(place - busy_place)

    def node_ahead(k):
        far = (to_busy > 0) & (k > to_busy + 1)
        slot = who[wrap(place + k - jnp.where(far, 1, 0))]
        return jnp.where((to_busy > 0) & (k == to_busy + 1), ranks, slot)

    def node_behind(k):
        far = (from_busy > 0) & (k > from_busy)
        slot = who[wrap(place - k + jnp.where(far, 1, 0))]
        return jnp.where((from_busy > 0) & (k == from_busy), ranks, slot)

    out[RANK] = rank
    out[CORE] = core
    out[BUSY] = jnp.where(busy, 1, 0)
    out[BUSY_RANK] = busy_rank
    out[SPAN] = span[rank]
    out[DEC] = dec[rank]
    out[LIVE] = span[rank] + dec[rank]
    out[START] = start[0]
    for j in range(lengths.shape[1]):
        out[LENGTHS + j] = lengths[0, j]
    out[table.source + rank] = 0
    for k in range(1, reach + 1):
        out[table.ahead + k] = node_ahead(k)
        out[table.behind + k] = node_behind(k)
        out[table.owner_back + k] = who[wrap(place - k)]
        out[table.owner_fore + k] = who[wrap(place + k)]
        out[table.source + node_behind(k)] = k
        last = jnp.where(busy, ranks, node_ahead(k)) if k == reach else node_ahead(k)
        out[table.source + last] = reach + k


def attend_kernel(
    heads, group, rows, lat, cached, value, start_step,
    tab, q, cache, fresh, vw, main, extra, k0, k1, kpad, dq, dec, turn,
):
    pair = 2 * lat
    wide = -(-lat // 128) * 128
    shift = wide - lat
    keys = cached + rows
    cols = -(-keys // 128) * 128
    slots = cache.shape[0] - 1
    dr = 8
    span, decs = tab[SPAN], tab[DEC]

    def onehot(shape, row_dim, slot_dim):
        r = lax.broadcasted_iota(i32, shape, row_dim)
        j = lax.broadcasted_iota(i32, shape, slot_dim)
        return jnp.where((r == span + j) & (j < decs), 1.0, 0.0).astype(bf16)

    @pl.when(pl.program_id(0) == 0)
    def _():
        turn[...] = jnp.zeros_like(turn)
        turn[:rows, :lat] = fresh[...].astype(f32)
        turned = turn[...].T.astype(bf16)[:lat]
        k0[...] = jnp.zeros_like(k0)
        k1[...] = jnp.zeros_like(k1)
        for ref, off in ((k0, 0), (k1, shift)):
            ref[off : off + lat, :cached] = cache[0]
            ref[off : off + lat, cached:] = turned
        kpad[...] = jnp.zeros_like(kpad)
        for s in range(slots):
            kpad[s, :lat] = cache[s + 1]
        pick = onehot((16, rows), 1, 0)
        for p in range(heads // 2):
            got = mm(pick, q[:, pair * p : pair * (p + 1)])[:dr]
            dq[2 * p * dr : (2 * p + 1) * dr] = got[:, :wide]
            dq[(2 * p + 1) * dr : (2 * p + 2) * dr] = pltpu.roll(got[:, pair - wide :], wide - shift, 1)
        n = heads * dr
        queries = dq[...].astype(bf16)
        slot = lax.broadcasted_iota(i32, (n, 1), 0) % dr
        length = jnp.zeros((n, 1), i32)
        scores = jnp.zeros((n, cached), f32)
        for s in range(slots):
            scores = jnp.where(slot == s, mm(queries, kpad[s]), scores)
            length = jnp.where(slot == s, tab[LENGTHS + s], length)
        seen = lax.broadcasted_iota(i32, (n, cached), 1) < length
        scores = jnp.where(seen, scores * score_scale, masked_score)
        own = mm(queries, k0[:, cached:])
        column = lax.broadcasted_iota(i32, own.shape, 1)
        own = jnp.sum(jnp.where(column == span + slot, own, 0.0), axis=1, keepdims=True)
        own = own * score_scale
        peak = jnp.maximum(jnp.max(scores, axis=1, keepdims=True), own)
        e = jnp.where(seen, jnp.exp(scores - peak), 0.0)
        e_own = jnp.exp(own - peak)
        total = jnp.sum(e, axis=1, keepdims=True) + e_own
        w = e / total
        acc = jnp.zeros((n, value), f32)
        for s in range(slots):
            acc = acc + mm_nt(jnp.where(slot == s, w, 0.0).astype(bf16), cache[s + 1, :value])
        own_value = mm(pick, fresh[:, :value])[:dr]
        own_value = jnp.broadcast_to(own_value[None], (heads, dr, value)).reshape(n, value)
        dec[...] = acc + (e_own / total).astype(bf16).astype(f32) * own_value

    step = pl.program_id(0)
    start = step * (group * lat)
    pairs = group // 2

    def stacked(off):
        return jnp.concatenate(
            [q[:, pl.ds(pl.multiple_of(start + pair * p + off, 128), wide)] for p in range(pairs)], 0
        )

    m = pairs * rows
    row = lax.broadcasted_iota(i32, (m, 1), 0) % rows
    col = lax.broadcasted_iota(i32, (m, cols), 1)
    seen = (col < jnp.where(col < cached, tab[START], cached + 1 + row)) & (col < keys)
    values = k0[:value]

    def latent(lhs, ref):
        s = jnp.where(seen, mm(lhs, ref[...]) * score_scale, masked_score)
        e = jnp.where(seen, jnp.exp(s - jnp.max(s, axis=1, keepdims=True)), 0.0)
        w = (e * (1.0 / jnp.sum(e, axis=1, keepdims=True))).astype(bf16)
        o = mm_nt(w, values)
        return jnp.where(row < span, o, 0.0).astype(bf16)

    even, odd = latent(stacked(0), k0), latent(stacked(pair - wide), k1)
    outs, decoded = [], []
    for p in range(pairs):
        at = pl.multiple_of((step * group + 2 * p) * dr, 16)
        lhs = jnp.concatenate(
            [even[p * rows : (p + 1) * rows], odd[p * rows : (p + 1) * rows], dec[pl.ds(at, 16)].astype(bf16)], 0
        )
        vh = vw.shape[2]
        r = mm(lhs, jnp.concatenate([vw[2 * p], vw[2 * p + 1]], 1))
        outs += [r[:rows, :vh], r[rows : 2 * rows, vh:]]
        decoded += [r[2 * rows : 2 * rows + dr, :vh], r[2 * rows + dr :, vh:]]
    decoded = jnp.concatenate(decoded, 1)
    decoded = jnp.concatenate([decoded, jnp.zeros_like(decoded)], 0).astype(bf16)
    out = jnp.concatenate(outs, 1) + mm(onehot((rows, 16), 0, 1), decoded)
    out = out.astype(bf16)
    at = pl.ds(pl.multiple_of(step * out.shape[1], out.shape[1]), out.shape[1])
    main[:, at] = out[: rows // 2]
    extra[:, at] = out[rows // 2 :]


def attend(tab, queries, cache, fresh, vw, part, parts):
    rows, heads = queries.shape[0], vw.shape[0] // parts
    lat = queries.shape[1] // vw.shape[0]
    slots, _, cached = cache.shape
    value, vh = vw.shape[1:]
    group = min(8, heads)
    wide, cols = -(-lat // 128) * 128, -(-(cached + rows) // 128) * 128
    steps = heads // group
    half = jax.ShapeDtypeStruct((rows // 2, heads * vh), bf16)
    return pl.pallas_call(
        functools.partial(attend_kernel, heads, group, rows, lat, cached, value, part),
        grid=(steps,),
        in_specs=[
            smem(),
            pl.BlockSpec((rows, heads * lat), lambda i: (0, part)),
            pl.BlockSpec(cache.shape, lambda i: (0, 0, 0)),
            pl.BlockSpec(fresh.shape[::-1], lambda i: (0, 0)),
            pl.BlockSpec((group, value, vh), lambda i: (part * steps + i, 0, 0)),
        ],
        out_specs=[whole()] * 2,
        out_shape=[half, half],
        scratch_shapes=[
            pltpu.VMEM((wide, cols), bf16),
            pltpu.VMEM((wide, cols), bf16),
            pltpu.VMEM((slots - 1, wide, cached), bf16),
            pltpu.VMEM((heads * 8, wide), f32),
            pltpu.VMEM((heads * 8, value), f32),
            pltpu.VMEM((cols - cached, wide), f32),
        ],
        compiler_params=params(56),
        cost_estimate=cost(
            2 * rows * heads * (cached + rows) * (lat + value),
            2 * (queries.size // parts + cache.size + vw.size // parts),
            rows * heads * (cached + rows),
        ),
        name="attend",
    )(tab, queries, cache, fresh.T, vw)


def pack_kernel(ranks, features, half, tab, res, *outs):
    core, rank = tab[CORE], tab[RANK]
    low = pl.multiple_of(core * half, half)
    high = pl.multiple_of(res.shape[0] // 2 + core * half, half)
    for k in range(ranks):
        target = rank + k
        target = jnp.where(target >= ranks, target - ranks, target)

        def put(columns, k=k):
            outs[k][:half] = res[pl.ds(low, half), columns]
            outs[k][half:] = res[pl.ds(high, half), columns]

        if features % 128 == 0:
            put(pl.ds(pl.multiple_of(target * features, 128), features))
        else:
            for t in range(ranks):
                pl.when(target == t)(functools.partial(put, slice(t * features, (t + 1) * features)))


def pack(tab, residual, ranks, cores):
    rows, width = residual.shape
    half, features = rows // 2 // cores, width // ranks
    return pl.pallas_call(
        functools.partial(pack_kernel, ranks, features, half),
        in_specs=[smem(), whole()],
        out_specs=[whole()] * ranks,
        out_shape=[jax.ShapeDtypeStruct((2 * half, features), bf16)] * ranks,
        compiler_params=params(8),
        cost_estimate=cost(0, 4 * residual.size),
        name="pack",
    )(tab, residual)


def route_kernel(tab, *refs):
    count = len(refs) // 3
    busy = tab[BUSY] == 1
    for i in range(count):
        special, usual, out = refs[2 * i], refs[2 * i + 1], refs[2 * count + i]

        @pl.when(busy)
        def _(special=special, out=out):
            out[...] = special[...]

        @pl.when(jnp.logical_not(busy))
        def _(usual=usual, out=out):
            out[...] = usual[...]


def route(tab, *choices):
    flat = [x for pair in choices for x in pair]
    return pl.pallas_call(
        route_kernel,
        in_specs=[smem()] + [whole()] * len(flat),
        out_specs=[whole()] * len(choices),
        out_shape=[jax.ShapeDtypeStruct(b.shape, b.dtype) for _, b in choices],
        compiler_params=params(6),
        cost_estimate=cost(0, 3 * sum(2 * b.size for _, b in choices)),
        name="route",
    )(tab, *flat)


def project_kernel(source, nodes, block, half, part, first, tab, *refs):
    blocks, refs = refs[: nodes + 1], refs[nodes + 1 :]
    before = None if first else refs[0]
    weight, kept, given, acc = refs[-4:]
    step = pl.program_id(0)
    depth = blocks[0].shape[1] // pl.num_programs(0)
    columns = pl.ds(pl.multiple_of(step * depth, 128), depth)
    last = jnp.where(tab[BUSY] == 1, blocks[nodes][:, columns], blocks[nodes - 1][:, columns])
    lhs = jnp.concatenate([b[:, columns] for b in blocks[: nodes - 1]] + [last], 0)
    got = mm(lhs, weight[pl.ds(pl.multiple_of(part * blocks[0].shape[1] + step * depth, 128), depth)])

    @pl.when(step == 0)
    def _():
        acc[...] = got if first else got + before[...]

    @pl.when(step > 0)
    def _():
        acc[...] += got

    @pl.when(step == pl.num_programs(0) - 1)
    def _():
        core = tab[CORE]
        for k in range(nodes):
            at = tab[source + k] * block
            kept[k * half : (k + 1) * half] = acc[pl.ds(pl.multiple_of(at + core * half, half), half)]
            other = acc[pl.ds(pl.multiple_of(at + (1 - core) * half, half), half)]
            given[k * half : (k + 1) * half] = other.astype(bf16)


def project_part_kernel(nodes, part, first, tab, *refs):
    blocks, refs = refs[: nodes + 1], refs[nodes + 1 :]
    weight, out = refs[-2:]
    step = pl.program_id(0)
    depth = blocks[0].shape[1] // pl.num_programs(0)
    columns = pl.ds(pl.multiple_of(step * depth, 128), depth)
    last = jnp.where(tab[BUSY] == 1, blocks[nodes][:, columns], blocks[nodes - 1][:, columns])
    lhs = jnp.concatenate([b[:, columns] for b in blocks[: nodes - 1]] + [last], 0)
    got = mm(lhs, weight[pl.ds(pl.multiple_of(part * blocks[0].shape[1] + step * depth, 128), depth)])

    @pl.when(step == 0)
    def _():
        out[...] = got if first else got + refs[0][...]

    @pl.when(step > 0)
    def _():
        out[...] += got


def project(tab, table, blocks, before, weight, part, parts, cores):
    block, width = blocks[0].shape
    nodes = len(blocks) - 1
    half = block // cores
    features = weight.shape[1]
    depth = 1024 if width % 1024 == 0 else width
    steps = width // depth
    total = jax.ShapeDtypeStruct((nodes * block, features), f32)
    final = part == parts - 1
    first = before is None
    ins = [smem()] + [whole()] * (nodes + 2 + (not first))
    args = [tab, *blocks] + ([] if first else [before]) + [weight]
    estimate = cost(
        2 * nodes * block * width * features, 2 * (nodes * block * width + width * features)
    )
    if not final:
        return pl.pallas_call(
            functools.partial(project_part_kernel, nodes, part, first),
            grid=(steps,),
            in_specs=ins,
            out_specs=pl.BlockSpec(total.shape, lambda i: (0, 0)),
            out_shape=total,
            compiler_params=params(16),
            cost_estimate=estimate,
            name="project",
        )(*args)
    return pl.pallas_call(
        functools.partial(project_kernel, table.source, nodes, block, half, part, first),
        grid=(steps,),
        in_specs=ins,
        out_specs=[pl.BlockSpec((nodes * half, features), lambda i: (0, 0))] * 2,
        out_shape=[
            jax.ShapeDtypeStruct((nodes * half, features), f32),
            jax.ShapeDtypeStruct((nodes * half, features), bf16),
        ],
        scratch_shapes=[pltpu.VMEM(total.shape, f32)],
        compiler_params=params(16),
        cost_estimate=estimate,
        name="project",
    )(*args)


def stream_kernel(ranks, half, tab, kept, other, *refs):
    res, out = refs[:-1], refs[-1]
    rank, busy_rank = tab[RANK], tab[BUSY_RANK]

    def put(slot, extra):
        rows = pl.ds(pl.multiple_of(slot * half, half), half)
        total = kept[rows] + other[rows].astype(f32) + extra.astype(f32)
        out[rows] = total.astype(bf16)

    for k in range(ranks):
        owner = rank - k
        owner = jnp.where(owner < 0, owner + ranks, owner)
        put(owner, res[k][:half])

        @pl.when(owner == busy_rank)
        def _(k=k):
            put(ranks, res[k][half:])


def stream_of(tab, kept, other, res):
    half = res[0].shape[0] // 2
    return pl.pallas_call(
        functools.partial(stream_kernel, len(res), half),
        in_specs=[smem()] + [whole()] * (2 + len(res)),
        out_specs=whole(),
        out_shape=jax.ShapeDtypeStruct(other.shape, bf16),
        compiler_params=params(8),
        cost_estimate=cost(0, 10 * other.size),
        name="stream",
    )(tab, kept, other, *res)


def expand_kernel(pieces, first, final, width, turned, owners, tab, *refs):
    count = len(pieces)
    blocks = []
    for number in pieces:
        blocks.append(refs[: 2 * number])
        refs = refs[2 * number :]
    gain, gate, up = refs[:3]
    refs = refs[3:]
    if not first:
        before, refs = refs[:3], refs[3:]
    if final:
        hidden, refs = refs[0], refs[1:]
    gates, ups, squares = refs
    step = pl.program_id(0)
    for i in range(count):

        @pl.when(step == i)
        def _(i=i):
            both = jnp.concatenate([x[...] for x in blocks[i]], 0).astype(f32)
            rows_of = both.shape[1]
            scaled = (both * gain[0]).astype(bf16)
            if turned:
                at = pl.ds(pl.multiple_of(tab[owners[i]] * rows_of, 128), rows_of)
                products = mm_nt(scaled, gate[:, at]), mm_nt(scaled, up[:, at])
            else:
                products = mm(scaled, gate[...]), mm(scaled, up[...])
            values = (
                *products,
                jnp.sum(both * both, axis=1, keepdims=True),
            )
            for n, (ref, value) in enumerate(zip((gates, ups, squares), values)):
                if i == 0:
                    ref[...] = value if first else value + before[n][...]
                else:
                    ref[...] += value

    if final:

        @pl.when(step == count - 1)
        def _():
            scale = lax.rsqrt(squares[...] / width + norm_eps)
            g = gates[...] * scale
            hidden[...] = (g / (1.0 + jnp.exp(-g)) * (ups[...] * scale)).astype(bf16)


def expand(tab, mines, theirs, owners, gain, gate, up, before, final):
    count = len(mines)
    pieces = tuple(len(x) for x in mines)
    rows, features = sum(x.shape[0] for x in mines[0]), mines[0][0].shape[1]
    arrays = [x for own, other in zip(mines, theirs) for x in (*own, *other)]
    units = gate.shape[1]
    first = before is None
    width = gate.shape[0]

    def owner(i, tab):
        index = tab[owners[0]]
        for n in range(1, count):
            index = jnp.where(i == n, tab[owners[n]], index)
        return index

    def full(shape):
        return pl.BlockSpec(shape, lambda i, tab: (0,) * len(shape))

    sums = [(2 * rows, units), (2 * rows, units), (2 * rows, 1)]
    ins = [full(x.shape) for x in arrays]
    ins += [pl.BlockSpec((1, 1, features), lambda i, tab: (owner(i, tab), 0, 0))]
    turned = features % 128 == 0
    if turned:
        gate, up = gate.T, up.T
        ins += [pl.BlockSpec(memory_space=pltpu.VMEM)] * 2
    else:
        ins += [pl.BlockSpec((features, units), lambda i, tab: (owner(i, tab), 0))] * 2
    if not first:
        ins += [full(s) for s in sums]
    shapes = [jax.ShapeDtypeStruct(s, f32) for s in sums]
    out_shapes = [jax.ShapeDtypeStruct((2 * rows, units), bf16)] if final else shapes
    return pl.pallas_call(
        functools.partial(expand_kernel, pieces, first, final, width, turned, owners),
        grid_spec=pltpu.PrefetchScalarGridSpec(
            num_scalar_prefetch=1,
            grid=(count,),
            in_specs=ins,
            out_specs=[full(s.shape) for s in out_shapes],
            scratch_shapes=[pltpu.VMEM(s, f32) for s in sums] if final else [],
        ),
        out_shape=out_shapes,
        compiler_params=params(20),
        cost_estimate=cost(
            8 * count * rows * features * units, count * (4 * features * units + 4 * rows * features)
        ),
        name="expand",
    )(tab, *arrays, gain, gate, up, *([] if first else before))


def collect_kernel(owners, tab, *refs):
    out = refs[-1]
    half = out.shape[1] // 2
    for i, at in enumerate(owners):
        out[tab[at], :half] = refs[2 * i][...]
        out[tab[at], half:] = refs[2 * i + 1][...]


def collect(tab, blocks, owners, half):
    ranks = len(blocks)
    features = blocks[0].shape[1]
    ins, args = [], []
    for x in blocks:
        ins += [
            pl.BlockSpec((half, features), lambda i, tab: (tab[RANK], 0)),
            pl.BlockSpec((half, features), lambda i, tab: (ranks, 0)),
        ]
        args += [x, x]
    shape = (ranks, 2 * half, features)
    return pl.pallas_call(
        functools.partial(collect_kernel, owners),
        grid_spec=pltpu.PrefetchScalarGridSpec(
            num_scalar_prefetch=1,
            grid=(1,),
            in_specs=ins,
            out_specs=pl.BlockSpec(shape, lambda i, tab: (0, 0, 0)),
        ),
        out_shape=jax.ShapeDtypeStruct(shape, bf16),
        compiler_params=params(10),
        cost_estimate=cost(0, 8 * ranks * half * features),
        name="collect",
    )(tab, *args)


def contract_kernel(begin, hidden, weight, mine, given):
    rows, wide = mine.shape
    at = pl.ds(pl.multiple_of(begin + pl.program_id(0) * wide, 128), wide)
    got = mm(hidden[...], weight[:, at]).astype(bf16)
    mine[...] = got[:rows]
    given[...] = got[rows:]


def contract(hidden, weight, part, parts):
    rows, units = hidden.shape
    columns = weight.shape[1] // parts
    wide = columns // 2 if columns % 256 == 0 else columns
    steps = columns // wide
    out = jax.ShapeDtypeStruct((rows // 2, columns), bf16)
    return pl.pallas_call(
        functools.partial(contract_kernel, part * columns),
        grid=(steps,),
        in_specs=[
            pl.BlockSpec((rows, units), lambda i: (0, 0)),
            whole(),
        ],
        out_specs=[pl.BlockSpec((rows // 2, wide), lambda i: (0, i))] * 2,
        out_shape=[out, out],
        compiler_params=params(16),
        cost_estimate=cost(2 * rows * units * columns, 2 * (units + rows) * columns),
        name="contract",
    )(hidden, weight)


def add_kernel(step, tab, mine_f, theirs_f, mine_b, theirs_b, *refs):
    got, (out_f, out_b) = refs[:-2], refs[-2:]
    busy = tab[BUSY] == 1
    own_f = mine_f[...].astype(f32) + theirs_f[...].astype(f32)
    own_b = mine_b[...].astype(f32) + theirs_b[...].astype(f32)
    if step == 1:
        out_f[...] = jnp.where(busy, 0.0, own_f).astype(bf16)
        out_b[...] = own_b.astype(bf16)
    elif step == 2:
        out_f[...] = (own_f + jnp.where(busy, 0.0, got[0][...].astype(f32))).astype(bf16)
        out_b[...] = (own_b + jnp.where(busy, 0.0, got[1][...].astype(f32))).astype(bf16)
    else:
        from_f = jnp.where(busy, got[0][...], got[1][...]).astype(f32)
        from_b = jnp.where(busy, got[2][...], got[3][...]).astype(f32)
        out_f[...] = (own_f + from_f).astype(bf16)
        out_b[...] = (own_b + from_b).astype(bf16)


def add(tab, table, step, mine, theirs, got, half):
    columns = mine.shape[1]
    far = table.reach + 1 - step

    def at(where):
        return pl.BlockSpec((half, columns), lambda i, tab: (tab[where + far], 0))

    full = pl.BlockSpec((half, columns), lambda i, tab: (0, 0))
    out = jax.ShapeDtypeStruct((half, columns), bf16)
    return pl.pallas_call(
        functools.partial(add_kernel, step),
        grid_spec=pltpu.PrefetchScalarGridSpec(
            num_scalar_prefetch=1,
            grid=(1,),
            in_specs=[at(table.ahead)] * 2 + [at(table.behind)] * 2 + [full] * len(got),
            out_specs=[full, full],
        ),
        out_shape=[out, out],
        compiler_params=params(8),
        cost_estimate=cost(0, 16 * half * columns),
        name="add",
    )(tab, mine, theirs, mine, theirs, *got)


def close_kernel(begin, tab, mm_, tm, me, te, f_last, f_prev, b_last, b_prev, own, kept, given):
    busy, first = tab[BUSY] == 1, tab[CORE] == 0
    half, columns = kept.shape
    features = own.shape[2]

    def total(*refs):
        out = refs[0][...].astype(f32)
        for r in refs[1:]:
            out = out + r[...].astype(f32)
        return out

    main = total(mm_, tm, f_last) + jnp.where(busy, b_prev[...], b_last[...]).astype(f32)
    extra = total(me, te, f_prev, b_last)
    for c in range(columns // features):
        cols = slice(c * features, (c + 1) * features)
        m = (main[:, cols] + own[begin + c, :half].astype(f32)).astype(bf16)
        e = (extra[:, cols] + own[begin + c, half:].astype(f32)).astype(bf16)
        kept[:, cols] = jnp.where(first, m, e)
        given[:, cols] = jnp.where(first, e, m)


def close(tab, mine, theirs, got_f, got_b, own, begin, half):
    columns = mine.shape[1]
    nodes = mine.shape[0] // half
    own_at = pl.BlockSpec((half, columns), lambda i, tab: (tab[RANK], 0))
    extra_at = pl.BlockSpec((half, columns), lambda i, tab: (nodes - 1, 0))
    full = pl.BlockSpec((half, columns), lambda i, tab: (0, 0))
    out = jax.ShapeDtypeStruct((half, columns), bf16)
    return pl.pallas_call(
        functools.partial(close_kernel, begin),
        grid_spec=pltpu.PrefetchScalarGridSpec(
            num_scalar_prefetch=1,
            grid=(1,),
            in_specs=[own_at, own_at, extra_at, extra_at]
            + [full] * 4
            + [pl.BlockSpec(own.shape, lambda i, tab: (0, 0, 0))],
            out_specs=[full, full],
        ),
        out_shape=[out, out],
        compiler_params=params(12),
        cost_estimate=cost(0, 24 * half * columns),
        name="close",
    )(tab, mine, theirs, mine, theirs, got_f[-1], got_f[-2], got_b[-1], got_b[-2], own)


def finish_kernel(parts, tab, *refs):
    kept, got, out = refs[:parts], refs[parts : 2 * parts], refs[-1]
    half, columns = kept[0].shape
    first = tab[CORE] == 0
    row = tab[CORE] * (2 * half) + lax.broadcasted_iota(i32, (half, 1), 0)
    for p in range(parts):
        cols = slice(p * columns, (p + 1) * columns)
        low = jnp.where(first, kept[p][...], got[p][...])
        high = jnp.where(first, got[p][...], kept[p][...])
        zero = jnp.zeros_like(low)
        out[:half, cols] = jnp.where(row < tab[LIVE], low, zero)
        out[half:, cols] = jnp.where(row + half < tab[LIVE], high, zero)


def finish(tab, kept, got):
    half, columns = kept[0].shape
    return pl.pallas_call(
        functools.partial(finish_kernel, len(kept)),
        in_specs=[smem()] + [whole()] * (2 * len(kept)),
        out_specs=whole(),
        out_shape=jax.ShapeDtypeStruct((2 * half, columns * len(kept)), bf16),
        compiler_params=params(8),
        cost_estimate=cost(0, 8 * half * columns * len(kept)),
        name="finish",
    )(tab, *kept, *got)


attention_parts = 2
contract_parts = 2


def on_device(
    order,
    queries,
    latent_cache,
    new_latent,
    span_len,
    dec_count,
    span_start,
    cache_len,
    value_weight,
    out_weight,
    residual,
    norm_gain,
    gate_weight,
    up_weight,
    down_weight,
):
    ranks = len(order)
    reach = ranks // 2
    cores = lax.axis_size("head")
    rows_dev, width = residual.shape
    half = rows_dev // 2 // cores
    features = out_weight.shape[1]
    table = Table(ranks, cache_len.shape[1])

    forward = [(order[i], order[(i + 1) % ranks]) for i in range(ranks)]
    backward = [(b, a) for a, b in forward]
    exchange = [(c, cores - 1 - c) for c in range(cores)]

    def send_next(x):
        return lax.ppermute(x, "blk", forward)

    def send_prev(x):
        return lax.ppermute(x, "blk", backward)

    def swap(x):
        return lax.ppermute(x, "head", exchange)

    ids = jnp.stack([lax.axis_index("blk"), lax.axis_index("head")]).astype(i32)
    at = jnp.asarray([order.index(i) for i in range(ranks)], i32)
    who = jnp.asarray(order, i32)
    tab = pl.pallas_call(
        functools.partial(table_kernel, table, ranks),
        in_specs=[smem()] * 7,
        out_specs=smem(),
        out_shape=jax.ShapeDtypeStruct((table.size,), i32),
        name="table",
    )(ids, span_len, dec_count, span_start, cache_len, at, who)

    packed = pack(tab, residual, ranks, cores)
    res = [packed[0]]
    for shift in range(1, ranks):
        pairs = [(i, (i + shift) % ranks) for i in range(ranks)]
        res.append(lax.ppermute(packed[shift], "blk", pairs))

    total, halves = None, None
    gathered = []
    for part in range(attention_parts):
        main, extra = attend(
            tab, queries, latent_cache, new_latent, value_weight, part, attention_parts
        )
        if part == attention_parts - 1:
            main, extra, res = lax.optimization_barrier((main, extra, res))
        behind, ahead = [], []
        for step in range(reach):
            if step == 0:
                (out_f,), out_b = route(tab, (extra, main)), main
            elif step == 1:
                out_f, out_b = route(tab, (main, behind[0]), (extra, ahead[0]))
            else:
                out_f, out_b = route(
                    tab,
                    (behind[step - 2], behind[step - 1]),
                    (ahead[step - 2], ahead[step - 1]),
                )
            behind.append(send_next(out_f))
            ahead.append(send_prev(out_b))
        gathered.append([main] + behind + ahead + [extra])
    for part in range(attention_parts):
        total = project(
            tab, table, gathered[part], total, out_weight, part, attention_parts, cores
        )
    kept, given = total
    stream = stream_of(tab, kept, swap(given), res)

    gain = norm_gain.reshape(ranks, 1, features)
    sums = expand(tab, [[stream]], [[swap(stream)]], [RANK], gain, gate_weight, up_weight, None, False)
    blocks, owners = [stream], [RANK]
    fore, back = stream, stream
    cut = -(-stream.shape[0] // 32) * 16
    done = None
    for step in range(1, reach + 1):
        if done is not None:
            back, fore, done = lax.optimization_barrier((back, fore, done))
        done = sums
        if step < reach:
            back, fore = send_next(back), send_prev(fore)
            arrived = [[back], [fore]]
            from_owner = [table.owner_back + step, table.owner_fore + step]
        else:
            arrived = [[send_next(back[:cut]), send_prev(fore[cut:])]]
            from_owner = [table.owner_back + step]
        tied, sums = lax.optimization_barrier((arrived, sums))
        others = [[swap(x) for x in pieces] for pieces in tied]
        sums = expand(
            tab, arrived, others, from_owner, gain, gate_weight, up_weight, sums, step == reach
        )
        blocks += [x[0] if len(x) == 1 else jnp.concatenate(x, 0) for x in arrived]
        owners += from_owner
    (hidden,) = sums
    own = collect(tab, blocks, owners, half)

    parts = contract_parts
    mine, theirs = [], []
    for part in range(parts):
        a, b = contract(hidden, down_weight, part, parts)
        mine.append(a)
        theirs.append(swap(b))
    kept_out, got_out = [], []
    for part in range(parts):
        got_f, got_b = [], []
        for step in range(1, reach + 1):
            if step == 1:
                got = []
            elif step == 2:
                got = [got_f[0], got_b[0]]
            else:
                got = [got_f[step - 3], got_f[step - 2], got_b[step - 3], got_b[step - 2]]
            out_f, out_b = add(tab, table, step, mine[part], theirs[part], got, half)
            got_f.append(send_next(out_f))
            got_b.append(send_prev(out_b))
        a, b = close(
            tab, mine[part], theirs[part], got_f, got_b, own, part * (ranks // parts), half
        )
        kept_out.append(a)
        got_out.append(swap(b))
    return finish(tab, kept_out, got_out)


def solution(mesh):
    placed = (
        P(("groups", "blk"), "head"),
        P(("groups", "blk"), None, None),
        P(None, ("groups", "blk")),
        P("groups"),
        P("groups"),
        P(("groups", "blk")),
        P(("groups", "blk"), None),
        P("head", None, None),
        P("head", "blk"),
        P(("groups", "blk"), None),
        P(),
        P(None, ("blk", "head")),
        P(None, ("blk", "head")),
        P(("blk", "head"), None),
    )
    order = ring_order(mesh)
    return jax.shard_map(
        lambda *args: on_device(order, *args),
        mesh=mesh,
        in_specs=placed,
        out_specs=P(("groups", "blk", "head"), None),
        check_vma=False,
    )
```

```python
import functools

import jax
import jax.numpy as jnp
from jax import lax
from jax.experimental import pallas as pl
from jax.experimental.pallas import tpu as pltpu
from jax.sharding import PartitionSpec as P

score_scale = 192.0 ** (-0.5)
norm_eps = 1e-06
masked_score = -1e30
f32, bf16, i32 = jnp.float32, jnp.bfloat16, jnp.int32
SMEM = pltpu.SMEM
MIB = 1 << 20

RANK, CORE, BUSY, BUSY_RANK, SPAN, DEC, LIVE, START, LENGTHS = range(9)


def mm(a, b):
    return lax.dot_general(a, b, (((1,), (0,)), ((), ())), preferred_element_type=f32)


def mm_nt(a, b):
    return lax.dot_general(a, b, (((1,), (1,)), ((), ())), preferred_element_type=f32)


def in_hbm(x):
    return pltpu.with_memory_space_constraint(x, pltpu.HBM)


def smem():
    return pl.BlockSpec(memory_space=SMEM)


def whole():
    return pl.BlockSpec(memory_space=pltpu.VMEM)


def params(mib=32):
    return pltpu.CompilerParams(vmem_limit_bytes=mib * MIB)


def cost(flops, moved, exps=0):
    return pl.CostEstimate(flops=int(flops), bytes_accessed=int(moved), transcendentals=int(exps))


def ring_order(mesh):
    count = mesh.shape["blk"]
    natural = list(range(count))
    snake = natural[0::2] + natural[1::2][::-1]
    names = list(mesh.axis_names)
    axes = [names.index("blk")] + [a for a, x in enumerate(names) if x != "blk"]
    lane = mesh.devices.transpose(axes)
    firsts = [lane[i].reshape(-1)[0] for i in natural]
    if not all(hasattr(d, "coords") for d in firsts):
        return snake

    def length(order):
        hops = zip(order, order[1:] + order[:1])
        return sum(
            sum(abs(u - v) for u, v in zip(firsts[a].coords, firsts[b].coords)) for a, b in hops
        )

    return natural if length(natural) <= length(snake) else snake


class Table:
    def __init__(self, ranks, slots):
        self.reach = ranks // 2
        self.source = LENGTHS + slots
        self.ahead = self.source + ranks + 1
        self.behind = self.ahead + self.reach + 1
        self.owner_back = self.behind + self.reach + 1
        self.owner_fore = self.owner_back + self.reach + 1
        self.who = self.owner_fore + self.reach + 1
        self.at = self.who + ranks
        self.size = self.at + ranks


def table_kernel(table, order, ids, span, dec, start, lengths, out):
    reach, ranks = table.reach, len(order)
    for i, r in enumerate(order):
        out[table.who + i] = r
        out[table.at + r] = i
    rank, core = ids[0], ids[1]
    most, busy_rank = span[0] + dec[0], jnp.int32(0)
    for i in range(1, ranks):
        here = span[i] + dec[i]
        busy_rank = jnp.where(here > most, i, busy_rank)
        most = jnp.maximum(here, most)
    busy = rank == busy_rank

    def wrap(x):
        x = jnp.where(x < 0, x + ranks, x)
        return jnp.where(x >= ranks, x - ranks, x)

    place, busy_place = out[table.at + rank], out[table.at + busy_rank]
    to_busy = wrap(busy_place - place)
    from_busy = wrap(place - busy_place)

    def node_ahead(k):
        far = (to_busy > 0) & (k > to_busy + 1)
        slot = out[table.who + wrap(place + k - jnp.where(far, 1, 0))]
        return jnp.where((to_busy > 0) & (k == to_busy + 1), ranks, slot)

    def node_behind(k):
        far = (from_busy > 0) & (k > from_busy)
        slot = out[table.who + wrap(place - k + jnp.where(far, 1, 0))]
        return jnp.where((from_busy > 0) & (k == from_busy), ranks, slot)

    out[RANK] = rank
    out[CORE] = core
    out[BUSY] = jnp.where(busy, 1, 0)
    out[BUSY_RANK] = busy_rank
    out[SPAN] = span[rank]
    out[DEC] = dec[rank]
    out[LIVE] = span[rank] + dec[rank]
    out[START] = start[0]
    for j in range(lengths.shape[1]):
        out[LENGTHS + j] = lengths[0, j]
    out[table.source + rank] = 0
    for k in range(1, reach + 1):
        out[table.ahead + k] = node_ahead(k)
        out[table.behind + k] = node_behind(k)
        out[table.owner_back + k] = out[table.who + wrap(place - k)]
        out[table.owner_fore + k] = out[table.who + wrap(place + k)]
        out[table.source + node_behind(k)] = k
        last = jnp.where(busy, ranks, node_ahead(k)) if k == reach else node_ahead(k)
        out[table.source + last] = reach + k


def attend_kernel(
    heads, group, rows, lat, value, parts, tab, q_hbm, cache_hbm, fresh, vw_hbm, *refs
):
    outs, refs = refs[: 2 * parts], refs[2 * parts :]
    q, keys, vw, dq, latent, fz, q_sem, key_sem, vw_sem = refs
    slots = keys.shape[0] - 2
    cached = keys.shape[2]
    wide = keys.shape[1]
    shift, pair, dr = wide - lat, 2 * lat, 8
    groups, pairs = heads // group, group // 2
    span, decs = tab[SPAN], tab[DEC]

    def q_copy(g):
        at = pl.ds(g * group * lat, group * lat)
        return pltpu.make_async_copy(q_hbm.at[:, at], q.at[:, at], q_sem.at[g])

    def vw_copy(g):
        at = pl.ds(g * group, group)
        return pltpu.make_async_copy(vw_hbm.at[at], vw.at[at], vw_sem.at[g])

    even_copy = pltpu.make_async_copy(cache_hbm.at[0], keys.at[0, pl.ds(0, lat)], key_sem.at[0])
    odd_copy = pltpu.make_async_copy(
        cache_hbm.at[0], keys.at[slots + 1, pl.ds(shift, lat)], key_sem.at[1]
    )
    rest_copy = pltpu.make_async_copy(
        cache_hbm.at[pl.ds(1, slots)], keys.at[pl.ds(1, slots), pl.ds(0, lat)], key_sem.at[2]
    )
    even_copy.start()
    odd_copy.start()
    for g in range(groups):
        q_copy(g).start()
    rest_copy.start()
    for g in range(groups):
        vw_copy(g).start()

    def onehot(shape, row_dim, slot_dim):
        r = lax.broadcasted_iota(i32, shape, row_dim)
        j = lax.broadcasted_iota(i32, shape, slot_dim)
        return jnp.where((r == span + j) & (j < decs), 1.0, 0.0).astype(bf16)

    tail = jnp.zeros((shift, cached), bf16)
    for s in range(slots + 1):
        keys[s, lat:] = tail
    keys[slots + 1, :shift] = tail
    fz[...] = jnp.zeros_like(fz)
    fz[:rows, :lat] = fresh[...].astype(f32)
    fresh_even = fz[...].astype(bf16)
    fresh_odd = pltpu.roll(fz[...], shift, 1).astype(bf16)

    m = pairs * rows
    cols = cached + fz.shape[0]
    row = lax.broadcasted_iota(i32, (m, 1), 0) % rows
    col = lax.broadcasted_iota(i32, (m, cols), 1)
    seen = col < jnp.where(col < cached, tab[START], cached + 1 + row)

    def span_latent(lhs, slot, fresh_keys):
        s = jnp.concatenate([mm(lhs, keys[slot]), mm_nt(lhs, fresh_keys)], 1)
        s = jnp.where(seen, s * score_scale, masked_score)
        e = jnp.where(seen, jnp.exp(s - jnp.max(s, axis=1, keepdims=True)), 0.0)
        w = (e * (1.0 / jnp.sum(e, axis=1, keepdims=True))).astype(bf16)
        o = mm_nt(w[:, :cached], keys[0, :value]) + mm(w[:, cached:], fresh_even[:, :value])
        return jnp.where(row < span, o, 0.0).astype(bf16)

    even_copy.wait()
    odd_copy.wait()
    for g in range(groups):
        q_copy(g).wait()
        start = g * group * lat
        for odd in range(2):
            off = start + odd * (pair - wide)
            lhs = jnp.concatenate(
                [q[:, off + pair * p : off + pair * p + wide] for p in range(pairs)], 0
            )
            o = span_latent(lhs, (slots + 1) * odd, fresh_odd if odd else fresh_even)
            latent[g, odd] = o

    pick = onehot((16, rows), 1, 0)
    for p in range(heads // 2):
        got = mm(pick, q[:, pair * p : pair * (p + 1)])[:dr]
        dq[2 * p * dr : (2 * p + 1) * dr] = got[:, :wide]
        dq[(2 * p + 1) * dr : (2 * p + 2) * dr] = pltpu.roll(got[:, pair - wide :], wide - shift, 1)
    n = heads * dr
    queries = dq[...].astype(bf16)
    slot = lax.broadcasted_iota(i32, (n, 1), 0) % dr
    rest_copy.wait()
    length = jnp.zeros((n, 1), i32)
    scores = jnp.zeros((n, cached), f32)
    for s in range(slots):
        scores = jnp.where(slot == s, mm(queries, keys[s + 1]), scores)
        length = jnp.where(slot == s, tab[LENGTHS + s], length)
    unmasked = lax.broadcasted_iota(i32, (n, cached), 1) < length
    scores = jnp.where(unmasked, scores * score_scale, masked_score)
    own = mm_nt(queries, fresh_even)
    column = lax.broadcasted_iota(i32, own.shape, 1)
    own = jnp.sum(jnp.where(column == span + slot, own, 0.0), axis=1, keepdims=True)
    own = own * score_scale
    peak = jnp.maximum(jnp.max(scores, axis=1, keepdims=True), own)
    e = jnp.where(unmasked, jnp.exp(scores - peak), 0.0)
    e_own = jnp.exp(own - peak)
    total = jnp.sum(e, axis=1, keepdims=True) + e_own
    w = e / total
    acc = jnp.zeros((n, value), f32)
    for s in range(slots):
        acc = acc + mm_nt(jnp.where(slot == s, w, 0.0).astype(bf16), keys[s + 1, :value])
    own_value = mm(pick, fresh[:, :value])[:dr]
    own_value = jnp.broadcast_to(own_value[None], (heads, dr, value)).reshape(n, value)
    dec = (acc + (e_own / total).astype(bf16).astype(f32) * own_value).astype(bf16)

    place = onehot((rows, 16), 0, 1)
    vh = vw.shape[2]
    block = rows // 2
    per_part = groups // parts
    for g in range(groups):
        vw_copy(g).wait()
        values, decoded = [], []
        for p in range(pairs):
            h = g * group + 2 * p
            lhs = jnp.concatenate(
                [
                    latent[g, 0, p * rows : (p + 1) * rows],
                    latent[g, 1, p * rows : (p + 1) * rows],
                    dec[h * dr : (h + 2) * dr],
                ],
                0,
            )
            r = mm(lhs, jnp.concatenate([vw[h], vw[h + 1]], 1))
            values += [r[:rows, :vh], r[rows : 2 * rows, vh:]]
            decoded += [r[2 * rows : 2 * rows + dr, :vh], r[2 * rows + dr :, vh:]]
        decoded = jnp.concatenate(decoded, 1)
        decoded = jnp.concatenate([decoded, jnp.zeros_like(decoded)], 0).astype(bf16)
        out = (jnp.concatenate(values, 1) + mm(place, decoded)).astype(bf16)
        part, at = g // per_part, (g % per_part) * group * vh
        outs[2 * part][:, at : at + group * vh] = out[:block]
        outs[2 * part + 1][:, at : at + group * vh] = out[block:]


def attend(tab, queries, cache, fresh, vw, parts):
    rows, heads = queries.shape[0], vw.shape[0]
    lat = queries.shape[1] // heads
    slots, _, cached = cache.shape
    value, vh = vw.shape[1:]
    group = min(8, heads // parts)
    groups = heads // group
    wide = -(-lat // 128) * 128
    half = jax.ShapeDtypeStruct((rows // 2, heads // parts * vh), bf16)
    hbm = pl.BlockSpec(memory_space=pltpu.HBM)
    return pl.pallas_call(
        functools.partial(attend_kernel, heads, group, rows, lat, value, parts),
        in_specs=[smem(), hbm, hbm, whole(), hbm],
        out_specs=[whole()] * (2 * parts),
        out_shape=[half] * (2 * parts),
        scratch_shapes=[
            pltpu.VMEM(queries.shape, bf16),
            pltpu.VMEM((slots + 1, wide, cached), bf16),
            pltpu.VMEM(vw.shape, bf16),
            pltpu.VMEM((heads * 8, wide), f32),
            pltpu.VMEM((groups, 2, group // 2 * rows, value), bf16),
            pltpu.VMEM((-(-rows // 128) * 128, wide), f32),
            pltpu.SemaphoreType.DMA((groups,)),
            pltpu.SemaphoreType.DMA((3,)),
            pltpu.SemaphoreType.DMA((groups,)),
        ],
        compiler_params=params(28),
        cost_estimate=cost(
            2 * rows * heads * (cached + rows) * (lat + value),
            2 * (queries.size + cache.size + vw.size),
            rows * heads * (cached + rows),
        ),
        name="attend",
    )(tab, in_hbm(queries), in_hbm(cache), fresh.T, in_hbm(vw))


def pack_kernel(ranks, cores, features, tab, res, *outs):
    for k in range(ranks // cores):
        target = tab[RANK] + k + (ranks // cores) * tab[CORE]
        target = jnp.where(target >= ranks, target - ranks, target)

        def put(columns, k=k):
            outs[k][...] = res[:, columns]

        if features % 128 == 0:
            put(pl.ds(pl.multiple_of(target * features, 128), features))
        else:
            for t in range(ranks):
                pl.when(target == t)(functools.partial(put, slice(t * features, (t + 1) * features)))


def pack(tab, residual, ranks, cores):
    rows, width = residual.shape
    features = width // ranks
    count = ranks // cores
    return pl.pallas_call(
        functools.partial(pack_kernel, ranks, cores, features),
        in_specs=[smem(), whole()],
        out_specs=[whole()] * count,
        out_shape=[jax.ShapeDtypeStruct((rows, features), bf16)] * count,
        compiler_params=params(8),
        cost_estimate=cost(0, 4 * residual.size),
        name="pack",
    )(tab, residual)


def share_kernel(half, tab, own, *refs):
    pieces, out = refs[:-1], refs[-1]
    other = 1 - tab[CORE]
    block = own.shape[0] // 2
    low = pl.multiple_of(other * half, half)
    high = pl.multiple_of(block + other * half, half)

    def put(k, piece):
        out[2 * k * half : (2 * k + 1) * half] = piece[pl.ds(low, half)]
        out[(2 * k + 1) * half : (2 * k + 2) * half] = piece[pl.ds(high, half)]

    for k, piece in enumerate(pieces):
        if k > 0:
            put(k, piece)
        else:
            pl.when(tab[CORE] == 0)(functools.partial(put, k, own))
            pl.when(tab[CORE] != 0)(functools.partial(put, k, piece))


def share(tab, own, pieces, cores):
    rows, features = own.shape
    half = rows // 2 // cores
    return pl.pallas_call(
        functools.partial(share_kernel, half),
        in_specs=[smem()] + [whole()] * (1 + len(pieces)),
        out_specs=whole(),
        out_shape=jax.ShapeDtypeStruct((2 * half * len(pieces), features), bf16),
        compiler_params=params(8),
        cost_estimate=cost(0, 4 * own.size * len(pieces)),
        name="share",
    )(tab, own, *pieces)


def route_kernel(tab, *refs):
    count = len(refs) // 3
    busy = tab[BUSY] == 1
    for i in range(count):
        special, usual, out = refs[2 * i], refs[2 * i + 1], refs[2 * count + i]

        @pl.when(busy)
        def _(special=special, out=out):
            out[...] = special[...]

        @pl.when(jnp.logical_not(busy))
        def _(usual=usual, out=out):
            out[...] = usual[...]


def route(tab, *choices):
    flat = [x for pair in choices for x in pair]
    return pl.pallas_call(
        route_kernel,
        in_specs=[smem()] + [whole()] * len(flat),
        out_specs=[whole()] * len(choices),
        out_shape=[jax.ShapeDtypeStruct(b.shape, b.dtype) for _, b in choices],
        compiler_params=params(6),
        cost_estimate=cost(0, 3 * sum(2 * b.size for _, b in choices)),
        name="route",
    )(tab, *flat)


def project_kernel(source, nodes, block, half, part, first, tab, *refs):
    blocks, refs = refs[: nodes + 1], refs[nodes + 1 :]
    before = None if first else refs[0]
    weight, kept, given, acc = refs[-4:]
    step = pl.program_id(0)
    depth = blocks[0].shape[1] // pl.num_programs(0)
    columns = pl.ds(pl.multiple_of(step * depth, 128), depth)
    last = jnp.where(tab[BUSY] == 1, blocks[nodes][:, columns], blocks[nodes - 1][:, columns])
    lhs = jnp.concatenate([b[:, columns] for b in blocks[: nodes - 1]] + [last], 0)
    got = mm(lhs, weight[pl.ds(pl.multiple_of(part * blocks[0].shape[1] + step * depth, 128), depth)])

    @pl.when(step == 0)
    def _():
        acc[...] = got if first else got + before[...]

    @pl.when(step > 0)
    def _():
        acc[...] += got

    @pl.when(step == pl.num_programs(0) - 1)
    def _():
        core = tab[CORE]
        for k in range(nodes):
            at = tab[source + k] * block
            kept[k * half : (k + 1) * half] = acc[pl.ds(pl.multiple_of(at + core * half, half), half)]
            other = acc[pl.ds(pl.multiple_of(at + (1 - core) * half, half), half)]
            given[k * half : (k + 1) * half] = other.astype(bf16)


def project_part_kernel(nodes, part, first, tab, *refs):
    blocks, refs = refs[: nodes + 1], refs[nodes + 1 :]
    weight, out = refs[-2:]
    step = pl.program_id(0)
    depth = blocks[0].shape[1] // pl.num_programs(0)
    columns = pl.ds(pl.multiple_of(step * depth, 128), depth)
    last = jnp.where(tab[BUSY] == 1, blocks[nodes][:, columns], blocks[nodes - 1][:, columns])
    lhs = jnp.concatenate([b[:, columns] for b in blocks[: nodes - 1]] + [last], 0)
    got = mm(lhs, weight[pl.ds(pl.multiple_of(part * blocks[0].shape[1] + step * depth, 128), depth)])

    @pl.when(step == 0)
    def _():
        out[...] = got if first else got + refs[0][...]

    @pl.when(step > 0)
    def _():
        out[...] += got


def project(tab, table, blocks, before, weight, part, parts, cores):
    block, width = blocks[0].shape
    nodes = len(blocks) - 1
    half = block // cores
    features = weight.shape[1]
    depth = width
    steps = width // depth
    total = jax.ShapeDtypeStruct((nodes * block, features), f32)
    final = part == parts - 1
    first = before is None
    ins = [smem()] + [whole()] * (nodes + 2 + (not first))
    args = [tab, *blocks] + ([] if first else [before]) + [weight]
    estimate = cost(
        2 * nodes * block * width * features, 2 * (nodes * block * width + width * features)
    )
    if not final:
        return pl.pallas_call(
            functools.partial(project_part_kernel, nodes, part, first),
            grid=(steps,),
            in_specs=ins,
            out_specs=pl.BlockSpec(total.shape, lambda i: (0, 0)),
            out_shape=total,
            compiler_params=params(16),
            cost_estimate=estimate,
            name="project",
        )(*args)
    return pl.pallas_call(
        functools.partial(project_kernel, table.source, nodes, block, half, part, first),
        grid=(steps,),
        in_specs=ins,
        out_specs=[pl.BlockSpec((nodes * half, features), lambda i: (0, 0))] * 2,
        out_shape=[
            jax.ShapeDtypeStruct((nodes * half, features), f32),
            jax.ShapeDtypeStruct((nodes * half, features), bf16),
        ],
        scratch_shapes=[pltpu.VMEM(total.shape, f32)],
        compiler_params=params(16),
        cost_estimate=estimate,
        name="project",
    )(*args)


def stream_kernel(ranks, half, tab, kept, other, own, shared, *refs):
    pieces, out = refs[:-1], refs[-1]
    rank, core, busy_rank = tab[RANK], tab[CORE], tab[BUSY_RANK]
    count = len(pieces)
    block = own.shape[0] // 2

    def put(slot, extra):
        rows = pl.ds(pl.multiple_of(slot * half, half), half)
        total = kept[rows] + other[rows].astype(f32) + extra.astype(f32)
        out[rows] = total.astype(bf16)

    def put_both(owner, main, extra):
        put(owner, main())

        @pl.when(owner == busy_rank)
        def _():
            put(ranks, extra())

    def owner_of(k, c):
        owner = rank - k - count * c
        return jnp.where(owner < 0, owner + ranks, owner)

    low = pl.ds(pl.multiple_of(core * half, half), half)
    high = pl.ds(pl.multiple_of(block + core * half, half), half)
    for k, piece in enumerate(pieces):

        def received(piece=piece, k=k):
            put_both(owner_of(k, core), lambda: piece[low], lambda: piece[high])

        if k > 0:
            received()
        else:
            pl.when(core == 0)(functools.partial(received, own))
            pl.when(core != 0)(received)
        at = 2 * k * half
        put_both(
            owner_of(k, 1 - core),
            lambda at=at: shared[at : at + half],
            lambda at=at: shared[at + half : at + 2 * half],
        )


def stream_of(tab, kept, other, own, shared, pieces, cores):
    half = own.shape[0] // 2 // cores
    return pl.pallas_call(
        functools.partial(stream_kernel, cores * len(pieces), half),
        in_specs=[smem()] + [whole()] * (4 + len(pieces)),
        out_specs=whole(),
        out_shape=jax.ShapeDtypeStruct(other.shape, bf16),
        compiler_params=params(8),
        cost_estimate=cost(0, 10 * other.size),
        name="stream",
    )(tab, kept, other, own, shared, *pieces)


def expand_kernel(pieces, first, final, width, turned, owners, tab, *refs):
    count = len(pieces)
    blocks = []
    for number in pieces:
        blocks.append(refs[: 2 * number])
        refs = refs[2 * number :]
    gain, gate, up = refs[:3]
    refs = refs[3:]
    if not first:
        before, refs = refs[:3], refs[3:]
    if final:
        hidden, refs = refs[0], refs[1:]
    gates, ups, squares = refs
    step = pl.program_id(0)
    for i in range(count):

        @pl.when(step == i)
        def _(i=i):
            both = jnp.concatenate([x[...] for x in blocks[i]], 0).astype(f32)
            rows_of = both.shape[1]
            scaled = (both * gain[0]).astype(bf16)
            if turned:
                at = pl.ds(pl.multiple_of(tab[owners[i]] * rows_of, 128), rows_of)
                products = mm_nt(scaled, gate[:, at]), mm_nt(scaled, up[:, at])
            else:
                products = mm(scaled, gate[...]), mm(scaled, up[...])
            values = (
                *products,
                jnp.sum(both * both, axis=1, keepdims=True),
            )
            for n, (ref, value) in enumerate(zip((gates, ups, squares), values)):
                if i == 0:
                    ref[...] = value if first else value + before[n][...]
                else:
                    ref[...] += value

    if final:

        @pl.when(step == count - 1)
        def _():
            scale = lax.rsqrt(squares[...] / width + norm_eps)
            g = gates[...] * scale
            hidden[...] = (g / (1.0 + jnp.exp(-g)) * (ups[...] * scale)).astype(bf16)


def expand(tab, mines, theirs, owners, gain, gate, up, before, final):
    count = len(mines)
    pieces = tuple(len(x) for x in mines)
    rows, features = sum(x.shape[0] for x in mines[0]), mines[0][0].shape[1]
    arrays = [x for own, other in zip(mines, theirs) for x in (*own, *other)]
    units = gate.shape[1]
    first = before is None
    width = gate.shape[0]

    def owner(i, tab):
        index = tab[owners[0]]
        for n in range(1, count):
            index = jnp.where(i == n, tab[owners[n]], index)
        return index

    def full(shape):
        return pl.BlockSpec(shape, lambda i, tab: (0,) * len(shape))

    sums = [(2 * rows, units), (2 * rows, units), (2 * rows, 1)]
    ins = [full(x.shape) for x in arrays]
    ins += [pl.BlockSpec((1, 1, features), lambda i, tab: (owner(i, tab), 0, 0))]
    turned = features % 128 == 0
    if turned:
        gate, up = gate.T, up.T
        ins += [pl.BlockSpec(memory_space=pltpu.VMEM)] * 2
    else:
        ins += [pl.BlockSpec((features, units), lambda i, tab: (owner(i, tab), 0))] * 2
    if not first:
        ins += [full(s) for s in sums]
    shapes = [jax.ShapeDtypeStruct(s, f32) for s in sums]
    out_shapes = [jax.ShapeDtypeStruct((2 * rows, units), bf16)] if final else shapes
    return pl.pallas_call(
        functools.partial(expand_kernel, pieces, first, final, width, turned, owners),
        grid_spec=pltpu.PrefetchScalarGridSpec(
            num_scalar_prefetch=1,
            grid=(count,),
            in_specs=ins,
            out_specs=[full(s.shape) for s in out_shapes],
            scratch_shapes=[pltpu.VMEM(s, f32) for s in sums] if final else [],
        ),
        out_shape=out_shapes,
        compiler_params=params(20),
        cost_estimate=cost(
            8 * count * rows * features * units, count * (4 * features * units + 4 * rows * features)
        ),
        name="expand",
    )(tab, *arrays, gain, gate, up, *([] if first else before))


def collect_kernel(owners, tab, *refs):
    out = refs[-1]
    half = out.shape[1] // 2
    for i, at in enumerate(owners):
        out[tab[at], :half] = refs[2 * i][...]
        out[tab[at], half:] = refs[2 * i + 1][...]


def collect(tab, blocks, owners, half):
    ranks = len(blocks)
    features = blocks[0].shape[1]
    ins, args = [], []
    for x in blocks:
        ins += [
            pl.BlockSpec((half, features), lambda i, tab: (tab[RANK], 0)),
            pl.BlockSpec((half, features), lambda i, tab: (ranks, 0)),
        ]
        args += [x, x]
    shape = (ranks, 2 * half, features)
    return pl.pallas_call(
        functools.partial(collect_kernel, owners),
        grid_spec=pltpu.PrefetchScalarGridSpec(
            num_scalar_prefetch=1,
            grid=(1,),
            in_specs=ins,
            out_specs=pl.BlockSpec(shape, lambda i, tab: (0, 0, 0)),
        ),
        out_shape=jax.ShapeDtypeStruct(shape, bf16),
        compiler_params=params(10),
        cost_estimate=cost(0, 8 * ranks * half * features),
        name="collect",
    )(tab, *args)


def contract_kernel(begin, hidden, weight, mine, given):
    rows, wide = mine.shape
    at = pl.ds(pl.multiple_of(begin + pl.program_id(0) * wide, 128), wide)
    got = mm(hidden[...], weight[:, at]).astype(bf16)
    mine[...] = got[:rows]
    given[...] = got[rows:]


def contract(hidden, weight, part, parts):
    rows, units = hidden.shape
    columns = weight.shape[1] // parts
    wide = columns // 2 if columns % 256 == 0 else columns
    steps = columns // wide
    out = jax.ShapeDtypeStruct((rows // 2, columns), bf16)
    return pl.pallas_call(
        functools.partial(contract_kernel, part * columns),
        grid=(steps,),
        in_specs=[
            pl.BlockSpec((rows, units), lambda i: (0, 0)),
            whole(),
        ],
        out_specs=[pl.BlockSpec((rows // 2, wide), lambda i: (0, i))] * 2,
        out_shape=[out, out],
        compiler_params=params(16),
        cost_estimate=cost(2 * rows * units * columns, 2 * (units + rows) * columns),
        name="contract",
    )(hidden, weight)


def add_kernel(step, tab, mine_f, theirs_f, mine_b, theirs_b, *refs):
    got, (out_f, out_b) = refs[:-2], refs[-2:]
    busy = tab[BUSY] == 1
    own_f = mine_f[...].astype(f32) + theirs_f[...].astype(f32)
    own_b = mine_b[...].astype(f32) + theirs_b[...].astype(f32)
    if step == 1:
        out_f[...] = jnp.where(busy, 0.0, own_f).astype(bf16)
        out_b[...] = own_b.astype(bf16)
    elif step == 2:
        out_f[...] = (own_f + jnp.where(busy, 0.0, got[0][...].astype(f32))).astype(bf16)
        out_b[...] = (own_b + jnp.where(busy, 0.0, got[1][...].astype(f32))).astype(bf16)
    else:
        from_f = jnp.where(busy, got[0][...], got[1][...]).astype(f32)
        from_b = jnp.where(busy, got[2][...], got[3][...]).astype(f32)
        out_f[...] = (own_f + from_f).astype(bf16)
        out_b[...] = (own_b + from_b).astype(bf16)


def add(tab, table, step, mine, theirs, got, half):
    columns = mine.shape[1]
    far = table.reach + 1 - step

    def at(where):
        return pl.BlockSpec((half, columns), lambda i, tab: (tab[where + far], 0))

    full = pl.BlockSpec((half, columns), lambda i, tab: (0, 0))
    out = jax.ShapeDtypeStruct((half, columns), bf16)
    return pl.pallas_call(
        functools.partial(add_kernel, step),
        grid_spec=pltpu.PrefetchScalarGridSpec(
            num_scalar_prefetch=1,
            grid=(1,),
            in_specs=[at(table.ahead)] * 2 + [at(table.behind)] * 2 + [full] * len(got),
            out_specs=[full, full],
        ),
        out_shape=[out, out],
        compiler_params=params(8),
        cost_estimate=cost(0, 16 * half * columns),
        name="add",
    )(tab, mine, theirs, mine, theirs, *got)


def close_kernel(begin, tab, mm_, tm, me, te, f_last, f_prev, b_last, b_prev, own, kept, given):
    busy, first = tab[BUSY] == 1, tab[CORE] == 0
    half, columns = kept.shape
    features = own.shape[2]

    def total(*refs):
        out = refs[0][...].astype(f32)
        for r in refs[1:]:
            out = out + r[...].astype(f32)
        return out

    main = total(mm_, tm, f_last) + jnp.where(busy, b_prev[...], b_last[...]).astype(f32)
    extra = total(me, te, f_prev, b_last)
    for c in range(columns // features):
        cols = slice(c * features, (c + 1) * features)
        m = (main[:, cols] + own[begin + c, :half].astype(f32)).astype(bf16)
        e = (extra[:, cols] + own[begin + c, half:].astype(f32)).astype(bf16)
        kept[:, cols] = jnp.where(first, m, e)
        given[:, cols] = jnp.where(first, e, m)


def close(tab, mine, theirs, got_f, got_b, own, begin, half):
    columns = mine.shape[1]
    nodes = mine.shape[0] // half
    own_at = pl.BlockSpec((half, columns), lambda i, tab: (tab[RANK], 0))
    extra_at = pl.BlockSpec((half, columns), lambda i, tab: (nodes - 1, 0))
    full = pl.BlockSpec((half, columns), lambda i, tab: (0, 0))
    out = jax.ShapeDtypeStruct((half, columns), bf16)
    return pl.pallas_call(
        functools.partial(close_kernel, begin),
        grid_spec=pltpu.PrefetchScalarGridSpec(
            num_scalar_prefetch=1,
            grid=(1,),
            in_specs=[own_at, own_at, extra_at, extra_at]
            + [full] * 4
            + [pl.BlockSpec(own.shape, lambda i, tab: (0, 0, 0))],
            out_specs=[full, full],
        ),
        out_shape=[out, out],
        compiler_params=params(12),
        cost_estimate=cost(0, 24 * half * columns),
        name="close",
    )(tab, mine, theirs, mine, theirs, got_f[-1], got_f[-2], got_b[-1], got_b[-2], own)


def finish_kernel(parts, tab, *refs):
    kept, got, out = refs[:parts], refs[parts : 2 * parts], refs[-1]
    half, columns = kept[0].shape
    first = tab[CORE] == 0
    row = tab[CORE] * (2 * half) + lax.broadcasted_iota(i32, (half, 1), 0)
    for p in range(parts):
        cols = slice(p * columns, (p + 1) * columns)
        low = jnp.where(first, kept[p][...], got[p][...])
        high = jnp.where(first, got[p][...], kept[p][...])
        zero = jnp.zeros_like(low)
        out[:half, cols] = jnp.where(row < tab[LIVE], low, zero)
        out[half:, cols] = jnp.where(row + half < tab[LIVE], high, zero)


def finish(tab, kept, got):
    half, columns = kept[0].shape
    return pl.pallas_call(
        functools.partial(finish_kernel, len(kept)),
        in_specs=[smem()] + [whole()] * (2 * len(kept)),
        out_specs=whole(),
        out_shape=jax.ShapeDtypeStruct((2 * half, columns * len(kept)), bf16),
        compiler_params=params(8),
        cost_estimate=cost(0, 8 * half * columns * len(kept)),
        name="finish",
    )(tab, *kept, *got)


attention_parts = 2
contract_parts = 2


def on_device(
    order,
    queries,
    latent_cache,
    new_latent,
    span_len,
    dec_count,
    span_start,
    cache_len,
    value_weight,
    out_weight,
    residual,
    norm_gain,
    gate_weight,
    up_weight,
    down_weight,
):
    ranks = len(order)
    reach = ranks // 2
    cores = lax.axis_size("head")
    rows_dev, width = residual.shape
    half = rows_dev // 2 // cores
    features = out_weight.shape[1]
    table = Table(ranks, cache_len.shape[1])

    forward = [(order[i], order[(i + 1) % ranks]) for i in range(ranks)]
    backward = [(b, a) for a, b in forward]
    exchange = [(c, cores - 1 - c) for c in range(cores)]

    def send_next(x):
        return lax.ppermute(x, "blk", forward)

    def send_prev(x):
        return lax.ppermute(x, "blk", backward)

    def swap(x):
        return lax.ppermute(x, "head", exchange)

    ids = jnp.stack([lax.axis_index("blk"), lax.axis_index("head")]).astype(i32)
    tab = pl.pallas_call(
        functools.partial(table_kernel, table, order),
        in_specs=[smem()] * 5,
        out_specs=smem(),
        out_shape=jax.ShapeDtypeStruct((table.size,), i32),
        name="table",
    )(ids, span_len, dec_count, span_start, cache_len)

    packed = pack(tab, residual, ranks, cores)
    pieces = []
    for k, x in enumerate(packed):
        pairs = [
            (i * cores + c, (i + k + len(packed) * c) % ranks * cores + c)
            for i in range(ranks)
            for c in range(cores)
            if k + c > 0
        ]
        pieces.append(lax.ppermute(x, ("blk", "head"), pairs))

    values = attend(tab, queries, latent_cache, new_latent, value_weight, attention_parts)
    values, pieces = lax.optimization_barrier((values, pieces))
    shared = swap(share(tab, packed[0], pieces, cores))
    total = None
    gathered = []
    for part in range(attention_parts):
        main, extra = values[2 * part], values[2 * part + 1]
        behind, ahead = [], []
        for step in range(reach):
            if step == 0:
                (out_f,), out_b = route(tab, (extra, main)), main
            elif step == 1:
                out_f, out_b = route(tab, (main, behind[0]), (extra, ahead[0]))
            else:
                out_f, out_b = route(
                    tab,
                    (behind[step - 2], behind[step - 1]),
                    (ahead[step - 2], ahead[step - 1]),
                )
            behind.append(send_next(out_f))
            ahead.append(send_prev(out_b))
        gathered.append([main] + behind + ahead + [extra])
    gathered[0], shared = lax.optimization_barrier((gathered[0], shared))
    for part in range(attention_parts):
        total = project(
            tab, table, gathered[part], total, out_weight, part, attention_parts, cores
        )
    kept, given = total
    stream = stream_of(tab, kept, swap(given), packed[0], shared, pieces, cores)

    gain = norm_gain.reshape(ranks, 1, features)
    sums = expand(tab, [[stream]], [[swap(stream)]], [RANK], gain, gate_weight, up_weight, None, False)
    blocks, owners = [stream], [RANK]
    fore, back = stream, stream
    cut = -(-stream.shape[0] // 32) * 16
    done = None
    for step in range(1, reach + 1):
        if done is not None:
            back, fore, done = lax.optimization_barrier((back, fore, done))
        done = sums
        if step < reach:
            back, fore = send_next(back), send_prev(fore)
            arrived = [[back], [fore]]
            from_owner = [table.owner_back + step, table.owner_fore + step]
        else:
            arrived = [[send_next(back[:cut]), send_prev(fore[cut:])]]
            from_owner = [table.owner_back + step]
        tied, sums = lax.optimization_barrier((arrived, sums))
        others = [[swap(x) for x in pieces] for pieces in tied]
        sums = expand(
            tab, arrived, others, from_owner, gain, gate_weight, up_weight, sums, step == reach
        )
        blocks += [x[0] if len(x) == 1 else jnp.concatenate(x, 0) for x in arrived]
        owners += from_owner
    (hidden,) = sums
    own = collect(tab, blocks, owners, half)

    parts = contract_parts
    mine, theirs = [], []
    for part in range(parts):
        a, b = contract(hidden, down_weight, part, parts)
        mine.append(a)
        theirs.append(swap(b))
    kept_out, got_out = [], []
    for part in range(parts):
        got_f, got_b = [], []
        for step in range(1, reach + 1):
            if step == 1:
                got = []
            elif step == 2:
                got = [got_f[0], got_b[0]]
            else:
                got = [got_f[step - 3], got_f[step - 2], got_b[step - 3], got_b[step - 2]]
            out_f, out_b = add(tab, table, step, mine[part], theirs[part], got, half)
            got_f.append(send_next(out_f))
            got_b.append(send_prev(out_b))
        a, b = close(
            tab, mine[part], theirs[part], got_f, got_b, own, part * (ranks // parts), half
        )
        kept_out.append(a)
        got_out.append(swap(b))
    return finish(tab, kept_out, got_out)


def solution(mesh):
    placed = (
        P(("groups", "blk"), "head"),
        P(("groups", "blk"), None, None),
        P(None, ("groups", "blk")),
        P("groups"),
        P("groups"),
        P(("groups", "blk")),
        P(("groups", "blk"), None),
        P("head", None, None),
        P("head", "blk"),
        P(("groups", "blk"), None),
        P(),
        P(None, ("blk", "head")),
        P(None, ("blk", "head")),
        P(("blk", "head"), None),
    )
    order = ring_order(mesh)
    return jax.shard_map(
        lambda *args: on_device(order, *args),
        mesh=mesh,
        in_specs=placed,
        out_specs=P(("groups", "blk", "head"), None),
        check_vma=False,
    )
```

```python
import functools

import jax
import jax.numpy as jnp
from jax import lax
from jax.experimental import pallas as pl
from jax.experimental.pallas import tpu as pltpu
from jax.sharding import PartitionSpec as P

score_scale = 192.0 ** (-0.5)
norm_eps = 1e-06
masked_score = -1e30
f32, bf16, i32 = jnp.float32, jnp.bfloat16, jnp.int32
SMEM = pltpu.SMEM
MIB = 1 << 20

RANK, CORE, BUSY, BUSY_RANK, SPAN, DEC, LIVE, START, LENGTHS = range(9)


def mm(a, b):
    return lax.dot_general(a, b, (((1,), (0,)), ((), ())), preferred_element_type=f32)


def mm_nt(a, b):
    return lax.dot_general(a, b, (((1,), (1,)), ((), ())), preferred_element_type=f32)


def in_hbm(x):
    return pltpu.with_memory_space_constraint(x, pltpu.HBM)


def smem():
    return pl.BlockSpec(memory_space=SMEM)


def whole():
    return pl.BlockSpec(memory_space=pltpu.VMEM)


def params(mib=32):
    return pltpu.CompilerParams(vmem_limit_bytes=mib * MIB)


def cost(flops, moved, exps=0):
    return pl.CostEstimate(flops=int(flops), bytes_accessed=int(moved), transcendentals=int(exps))


def ring_order(mesh):
    count = mesh.shape["blk"]
    natural = list(range(count))
    snake = natural[0::2] + natural[1::2][::-1]
    names = list(mesh.axis_names)
    axes = [names.index("blk")] + [a for a, x in enumerate(names) if x != "blk"]
    lane = mesh.devices.transpose(axes)
    firsts = [lane[i].reshape(-1)[0] for i in natural]
    if not all(hasattr(d, "coords") for d in firsts):
        return snake

    def length(order):
        hops = zip(order, order[1:] + order[:1])
        return sum(
            sum(abs(u - v) for u, v in zip(firsts[a].coords, firsts[b].coords)) for a, b in hops
        )

    return natural if length(natural) <= length(snake) else snake


class Table:
    def __init__(self, ranks, slots):
        self.reach = ranks // 2
        self.source = LENGTHS + slots
        self.ahead = self.source + ranks + 1
        self.behind = self.ahead + self.reach + 1
        self.owner_back = self.behind + self.reach + 1
        self.owner_fore = self.owner_back + self.reach + 1
        self.who = self.owner_fore + self.reach + 1
        self.at = self.who + ranks
        self.size = self.at + ranks


def table_kernel(table, order, ids, span, dec, start, lengths, out):
    reach, ranks = table.reach, len(order)
    for i, r in enumerate(order):
        out[table.who + i] = r
        out[table.at + r] = i
    rank, core = ids[0], ids[1]
    most, busy_rank = span[0] + dec[0], jnp.int32(0)
    for i in range(1, ranks):
        here = span[i] + dec[i]
        busy_rank = jnp.where(here > most, i, busy_rank)
        most = jnp.maximum(here, most)
    busy = rank == busy_rank

    def wrap(x):
        x = jnp.where(x < 0, x + ranks, x)
        return jnp.where(x >= ranks, x - ranks, x)

    place, busy_place = out[table.at + rank], out[table.at + busy_rank]
    to_busy = wrap(busy_place - place)
    from_busy = wrap(place - busy_place)

    def node_ahead(k):
        far = (to_busy > 0) & (k > to_busy + 1)
        slot = out[table.who + wrap(place + k - jnp.where(far, 1, 0))]
        return jnp.where((to_busy > 0) & (k == to_busy + 1), ranks, slot)

    def node_behind(k):
        far = (from_busy > 0) & (k > from_busy)
        slot = out[table.who + wrap(place - k + jnp.where(far, 1, 0))]
        return jnp.where((from_busy > 0) & (k == from_busy), ranks, slot)

    out[RANK] = rank
    out[CORE] = core
    out[BUSY] = jnp.where(busy, 1, 0)
    out[BUSY_RANK] = busy_rank
    out[SPAN] = span[rank]
    out[DEC] = dec[rank]
    out[LIVE] = span[rank] + dec[rank]
    out[START] = start[0]
    for j in range(lengths.shape[1]):
        out[LENGTHS + j] = lengths[0, j]
    out[table.source + rank] = 0
    for k in range(1, reach + 1):
        out[table.ahead + k] = node_ahead(k)
        out[table.behind + k] = node_behind(k)
        out[table.owner_back + k] = out[table.who + wrap(place - k)]
        out[table.owner_fore + k] = out[table.who + wrap(place + k)]
        out[table.source + node_behind(k)] = k
        last = jnp.where(busy, ranks, node_ahead(k)) if k == reach else node_ahead(k)
        out[table.source + last] = reach + k


def attend_kernel(
    table, order, heads, first, count, group, rows, lat, value, lead, *refs
):
    if lead:
        scalars, refs = refs[:5], refs[5:]
        q_hbm, cache_hbm, fresh, vw_hbm, tab, head, main, extra, later = refs[:9]
        refs = refs[9:]
        q, keys, vw, latent, fz, q_sem, key_sem, vw_sem, dq = refs
        loaded, base = heads, 0
    else:
        tab, q_hbm, cache_hbm, fresh, vw_hbm, decoded_here, head, main, extra = refs[:9]
        q, keys, vw, latent, fz, q_sem, key_sem, vw_sem = refs[9:]
        loaded, base = count, first
    cached, wide = keys.shape[2], keys.shape[1]
    slots = cache_hbm.shape[0] - 1
    odd_slot = keys.shape[0] - 1
    shift, pair, dr = wide - lat, 2 * lat, 8
    groups, pairs = count // group, group // 2
    loads = loaded // group

    def q_copy(g):
        source = pl.ds((base + g * group) * lat, group * lat)
        return pltpu.make_async_copy(
            q_hbm.at[:, source], q.at[:, pl.ds(g * group * lat, group * lat)], q_sem.at[g]
        )

    def vw_copy(g):
        source = pl.ds(first + g * group, group)
        return pltpu.make_async_copy(vw_hbm.at[source], vw.at[pl.ds(g * group, group)], vw_sem.at[g])

    even_copy = pltpu.make_async_copy(cache_hbm.at[0], keys.at[0, pl.ds(0, lat)], key_sem.at[0])
    odd_copy = pltpu.make_async_copy(
        cache_hbm.at[0], keys.at[odd_slot, pl.ds(shift, lat)], key_sem.at[1]
    )
    waiting = [q_copy(g) for g in range(1, loads)]
    if lead:
        rest_copy = pltpu.make_async_copy(
            cache_hbm.at[pl.ds(1, slots)], keys.at[pl.ds(1, slots), pl.ds(0, lat)], key_sem.at[2]
        )
        waiting.append(rest_copy)
    waiting += [vw_copy(g) for g in range(groups)]

    def start_next(number):
        for _ in range(min(number, len(waiting))):
            waiting.pop(0).start()

    even_copy.start()
    q_copy(0).start()
    odd_copy.start()
    start_next(1)
    if lead:
        table_kernel(table, order, *scalars, tab)
    span, decs = tab[SPAN], tab[DEC]

    def onehot(shape, row_dim, slot_dim):
        r = lax.broadcasted_iota(i32, shape, row_dim)
        j = lax.broadcasted_iota(i32, shape, slot_dim)
        return jnp.where((r == span + j) & (j < decs), 1.0, 0.0).astype(bf16)

    tail = jnp.zeros((shift, cached), bf16)
    for s in range(odd_slot):
        keys[s, lat:] = tail
    keys[odd_slot, :shift] = tail
    fz[...] = jnp.zeros_like(fz)
    fz[:rows, :lat] = fresh[...].astype(f32)
    fresh_even = fz[...].astype(bf16)
    fresh_odd = pltpu.roll(fz[...], shift, 1).astype(bf16)

    m = pairs * rows
    cols = cached + fz.shape[0]
    row = lax.broadcasted_iota(i32, (m, 1), 0) % rows
    col = lax.broadcasted_iota(i32, (m, cols), 1)
    seen = col < jnp.where(col < cached, tab[START], cached + 1 + row)

    def span_latent(lhs, slot, fresh_keys):
        s = jnp.concatenate([mm(lhs, keys[slot]), mm_nt(lhs, fresh_keys)], 1)
        s = jnp.where(seen, s * score_scale, masked_score)
        e = jnp.where(seen, jnp.exp(s - jnp.max(s, axis=1, keepdims=True)), 0.0)
        w = (e * (1.0 / jnp.sum(e, axis=1, keepdims=True))).astype(bf16)
        o = mm_nt(w[:, :cached], keys[0, :value]) + mm(w[:, cached:], fresh_even[:, :value])
        return jnp.where(row < span, o, 0.0).astype(bf16)

    even_copy.wait()
    odd_copy.wait()
    for g in range(groups):
        q_copy(g).wait()
        start_next(2)
        start = g * group * lat
        for odd in range(2):
            off = start + odd * (pair - wide)
            lhs = jnp.concatenate(
                [q[:, off + pair * p : off + pair * p + wide] for p in range(pairs)], 0
            )
            latent[g, odd] = span_latent(lhs, odd_slot * odd, fresh_odd if odd else fresh_even)
    start_next(len(waiting))

    if lead:
        for g in range(groups, loads):
            q_copy(g).wait()
        pick = onehot((16, rows), 1, 0)
        for p in range(heads // 2):
            got = mm(pick, q[:, pair * p : pair * (p + 1)])[:dr]
            dq[2 * p * dr : (2 * p + 1) * dr] = got[:, :wide]
            dq[(2 * p + 1) * dr : (2 * p + 2) * dr] = pltpu.roll(
                got[:, pair - wide :], wide - shift, 1
            )
        n = heads * dr
        queries = dq[...].astype(bf16)
        slot = lax.broadcasted_iota(i32, (n, 1), 0) % dr
        rest_copy.wait()
        length = jnp.zeros((n, 1), i32)
        scores = jnp.zeros((n, cached), f32)
        for s in range(slots):
            scores = jnp.where(slot == s, mm(queries, keys[s + 1]), scores)
            length = jnp.where(slot == s, tab[LENGTHS + s], length)
        unmasked = lax.broadcasted_iota(i32, (n, cached), 1) < length
        scores = jnp.where(unmasked, scores * score_scale, masked_score)
        own = mm_nt(queries, fresh_even)
        column = lax.broadcasted_iota(i32, own.shape, 1)
        own = jnp.sum(jnp.where(column == span + slot, own, 0.0), axis=1, keepdims=True)
        own = own * score_scale
        peak = jnp.maximum(jnp.max(scores, axis=1, keepdims=True), own)
        e = jnp.where(unmasked, jnp.exp(scores - peak), 0.0)
        e_own = jnp.exp(own - peak)
        total = jnp.sum(e, axis=1, keepdims=True) + e_own
        w = e / total
        acc = jnp.zeros((n, value), f32)
        for s in range(slots):
            acc = acc + mm_nt(jnp.where(slot == s, w, 0.0).astype(bf16), keys[s + 1, :value])
        own_value = mm(pick, fresh[:, :value])[:dr]
        own_value = jnp.broadcast_to(own_value[None], (heads, dr, value)).reshape(n, value)
        dec = (acc + (e_own / total).astype(bf16).astype(f32) * own_value).astype(bf16)
        later[...] = dec[count * dr :]
        dec = dec[: count * dr]
    else:
        dec = decoded_here[...]

    place = onehot((rows, 16), 0, 1)
    vh = vw.shape[2]
    block = rows // 2
    for g in range(groups):
        vw_copy(g).wait()
        values, decoded = [], []
        for p in range(pairs):
            h = g * group + 2 * p
            lhs = jnp.concatenate(
                [
                    latent[g, 0, p * rows : (p + 1) * rows],
                    latent[g, 1, p * rows : (p + 1) * rows],
                    dec[h * dr : (h + 2) * dr],
                ],
                0,
            )
            r = mm(lhs, jnp.concatenate([vw[h], vw[h + 1]], 1))
            values += [r[:rows, :vh], r[rows : 2 * rows, vh:]]
            decoded += [r[2 * rows : 2 * rows + dr, :vh], r[2 * rows + dr :, vh:]]
        decoded = jnp.concatenate(decoded, 1)
        decoded = jnp.concatenate([decoded, jnp.zeros_like(decoded)], 0).astype(bf16)
        out = (jnp.concatenate(values, 1) + mm(place, decoded)).astype(bf16)
        at = slice(g * group * vh, (g + 1) * group * vh)
        main[:, at] = out[:block]
        extra[:, at] = out[block:]
        head[:, at] = jnp.where(tab[BUSY] == 1, out[block:], out[:block])


def attend(table, order, scalars, queries, cache, fresh, vw, part, parts, decoded):
    rows, heads = queries.shape[0], vw.shape[0]
    lat = queries.shape[1] // heads
    slots, _, cached = cache.shape
    value, vh = vw.shape[1:]
    count = heads // parts
    group = min(8, count)
    lead = decoded is None
    loaded = heads if lead else count
    wide = -(-lat // 128) * 128
    half = jax.ShapeDtypeStruct((rows // 2, count * vh), bf16)
    hbm = pl.BlockSpec(memory_space=pltpu.HBM)
    scratch = [
        pltpu.VMEM((rows, loaded * lat), bf16),
        pltpu.VMEM((slots + 1 if lead else 2, wide, cached), bf16),
        pltpu.VMEM((count, value, vh), bf16),
        pltpu.VMEM((count // group, 2, group // 2 * rows, value), bf16),
        pltpu.VMEM((-(-rows // 128) * 128, wide), f32),
        pltpu.SemaphoreType.DMA((loaded // group,)),
        pltpu.SemaphoreType.DMA((3,)),
        pltpu.SemaphoreType.DMA((count // group,)),
    ]
    out_shape, out_specs = [half] * 3, [whole()] * 3
    ins = [smem()] * len(scalars) + [hbm, hbm, whole(), hbm]
    args = [*scalars, in_hbm(queries), in_hbm(cache), fresh.T, in_hbm(vw)]
    if lead:
        scratch.append(pltpu.VMEM((heads * 8, wide), f32))
        out_shape = [jax.ShapeDtypeStruct((table.size,), i32)] + out_shape
        out_shape += [jax.ShapeDtypeStruct(((heads - count) * 8, value), bf16)]
        out_specs = [smem()] + out_specs + [whole()]
    else:
        ins.append(whole())
        args.append(decoded)
    return pl.pallas_call(
        functools.partial(
            attend_kernel, table, order, heads, part * count, count, group, rows, lat, value, lead
        ),
        in_specs=ins,
        out_specs=out_specs,
        out_shape=out_shape,
        scratch_shapes=scratch,
        compiler_params=params(24),
        cost_estimate=cost(
            2 * rows * count * (cached + rows) * (lat + value),
            2 * (queries.size + cache.size + vw.size) // parts,
            rows * count * (cached + rows),
        ),
        name="attend",
    )(*args)


def pack_kernel(ranks, cores, features, tab, res, *outs):
    for k in range(ranks // cores):
        target = tab[RANK] + k + (ranks // cores) * tab[CORE]
        target = jnp.where(target >= ranks, target - ranks, target)

        def put(columns, k=k):
            outs[k][...] = res[:, columns]

        if features % 128 == 0:
            put(pl.ds(pl.multiple_of(target * features, 128), features))
        else:
            for t in range(ranks):
                pl.when(target == t)(functools.partial(put, slice(t * features, (t + 1) * features)))


def pack(tab, residual, ranks, cores):
    rows, width = residual.shape
    features = width // ranks
    count = ranks // cores
    return pl.pallas_call(
        functools.partial(pack_kernel, ranks, cores, features),
        in_specs=[smem(), whole()],
        out_specs=[whole()] * count,
        out_shape=[jax.ShapeDtypeStruct((rows, features), bf16)] * count,
        compiler_params=params(8),
        cost_estimate=cost(0, 4 * residual.size),
        name="pack",
    )(tab, residual)


def share_kernel(half, tab, own, *refs):
    pieces, out = refs[:-1], refs[-1]
    other = 1 - tab[CORE]
    block = own.shape[0] // 2
    low = pl.multiple_of(other * half, half)
    high = pl.multiple_of(block + other * half, half)

    def put(k, piece):
        out[2 * k * half : (2 * k + 1) * half] = piece[pl.ds(low, half)]
        out[(2 * k + 1) * half : (2 * k + 2) * half] = piece[pl.ds(high, half)]

    for k, piece in enumerate(pieces):
        if k > 0:
            put(k, piece)
        else:
            pl.when(tab[CORE] == 0)(functools.partial(put, k, own))
            pl.when(tab[CORE] != 0)(functools.partial(put, k, piece))


def share(tab, own, pieces, cores):
    rows, features = own.shape
    half = rows // 2 // cores
    return pl.pallas_call(
        functools.partial(share_kernel, half),
        in_specs=[smem()] + [whole()] * (1 + len(pieces)),
        out_specs=whole(),
        out_shape=jax.ShapeDtypeStruct((2 * half * len(pieces), features), bf16),
        compiler_params=params(8),
        cost_estimate=cost(0, 4 * own.size * len(pieces)),
        name="share",
    )(tab, own, *pieces)


def route_kernel(tab, *refs):
    count = len(refs) // 3
    busy = tab[BUSY] == 1
    for i in range(count):
        special, usual, out = refs[2 * i], refs[2 * i + 1], refs[2 * count + i]

        @pl.when(busy)
        def _(special=special, out=out):
            out[...] = special[...]

        @pl.when(jnp.logical_not(busy))
        def _(usual=usual, out=out):
            out[...] = usual[...]


def route(tab, *choices):
    flat = [x for pair in choices for x in pair]
    return pl.pallas_call(
        route_kernel,
        in_specs=[smem()] + [whole()] * len(flat),
        out_specs=[whole()] * len(choices),
        out_shape=[jax.ShapeDtypeStruct(b.shape, b.dtype) for _, b in choices],
        compiler_params=params(6),
        cost_estimate=cost(0, 3 * sum(2 * b.size for _, b in choices)),
        name="route",
    )(tab, *flat)


def project_kernel(source, nodes, block, half, part, first, tab, *refs):
    blocks, refs = refs[: nodes + 1], refs[nodes + 1 :]
    before = None if first else refs[0]
    weight, kept, given, acc = refs[-4:]
    step = pl.program_id(0)
    depth = blocks[0].shape[1] // pl.num_programs(0)
    columns = pl.ds(pl.multiple_of(step * depth, 128), depth)
    last = jnp.where(tab[BUSY] == 1, blocks[nodes][:, columns], blocks[nodes - 1][:, columns])
    lhs = jnp.concatenate([b[:, columns] for b in blocks[: nodes - 1]] + [last], 0)
    got = mm(lhs, weight[pl.ds(pl.multiple_of(part * blocks[0].shape[1] + step * depth, 128), depth)])

    @pl.when(step == 0)
    def _():
        acc[...] = got if first else got + before[...]

    @pl.when(step > 0)
    def _():
        acc[...] += got

    @pl.when(step == pl.num_programs(0) - 1)
    def _():
        core = tab[CORE]
        for k in range(nodes):
            at = tab[source + k] * block
            kept[k * half : (k + 1) * half] = acc[pl.ds(pl.multiple_of(at + core * half, half), half)]
            other = acc[pl.ds(pl.multiple_of(at + (1 - core) * half, half), half)]
            given[k * half : (k + 1) * half] = other.astype(bf16)


def project_part_kernel(nodes, part, first, tab, *refs):
    blocks, refs = refs[: nodes + 1], refs[nodes + 1 :]
    weight, out = refs[-2:]
    step = pl.program_id(0)
    depth = blocks[0].shape[1] // pl.num_programs(0)
    columns = pl.ds(pl.multiple_of(step * depth, 128), depth)
    last = jnp.where(tab[BUSY] == 1, blocks[nodes][:, columns], blocks[nodes - 1][:, columns])
    lhs = jnp.concatenate([b[:, columns] for b in blocks[: nodes - 1]] + [last], 0)
    got = mm(lhs, weight[pl.ds(pl.multiple_of(part * blocks[0].shape[1] + step * depth, 128), depth)])

    @pl.when(step == 0)
    def _():
        out[...] = got if first else got + refs[0][...]

    @pl.when(step > 0)
    def _():
        out[...] += got


def project(tab, table, blocks, before, weight, part, parts, cores):
    block, width = blocks[0].shape
    nodes = len(blocks) - 1
    half = block // cores
    features = weight.shape[1]
    depth = width
    steps = width // depth
    total = jax.ShapeDtypeStruct((nodes * block, features), f32)
    final = part == parts - 1
    first = before is None
    ins = [smem()] + [whole()] * (nodes + 2 + (not first))
    args = [tab, *blocks] + ([] if first else [before]) + [weight]
    estimate = cost(
        2 * nodes * block * width * features, 2 * (nodes * block * width + width * features)
    )
    if not final:
        return pl.pallas_call(
            functools.partial(project_part_kernel, nodes, part, first),
            grid=(steps,),
            in_specs=ins,
            out_specs=pl.BlockSpec(total.shape, lambda i: (0, 0)),
            out_shape=total,
            compiler_params=params(16),
            cost_estimate=estimate,
            name="project",
        )(*args)
    return pl.pallas_call(
        functools.partial(project_kernel, table.source, nodes, block, half, part, first),
        grid=(steps,),
        in_specs=ins,
        out_specs=[pl.BlockSpec((nodes * half, features), lambda i: (0, 0))] * 2,
        out_shape=[
            jax.ShapeDtypeStruct((nodes * half, features), f32),
            jax.ShapeDtypeStruct((nodes * half, features), bf16),
        ],
        scratch_shapes=[pltpu.VMEM(total.shape, f32)],
        compiler_params=params(16),
        cost_estimate=estimate,
        name="project",
    )(*args)


def stream_kernel(ranks, half, tab, kept, other, own, shared, *refs):
    pieces, out = refs[:-1], refs[-1]
    rank, core, busy_rank = tab[RANK], tab[CORE], tab[BUSY_RANK]
    count = len(pieces)
    block = own.shape[0] // 2

    def put(slot, extra):
        rows = pl.ds(pl.multiple_of(slot * half, half), half)
        total = kept[rows] + other[rows].astype(f32) + extra.astype(f32)
        out[rows] = total.astype(bf16)

    def put_both(owner, main, extra):
        put(owner, main())

        @pl.when(owner == busy_rank)
        def _():
            put(ranks, extra())

    def owner_of(k, c):
        owner = rank - k - count * c
        return jnp.where(owner < 0, owner + ranks, owner)

    low = pl.ds(pl.multiple_of(core * half, half), half)
    high = pl.ds(pl.multiple_of(block + core * half, half), half)
    for k, piece in enumerate(pieces):

        def received(piece=piece, k=k):
            put_both(owner_of(k, core), lambda: piece[low], lambda: piece[high])

        if k > 0:
            received()
        else:
            pl.when(core == 0)(functools.partial(received, own))
            pl.when(core != 0)(received)
        at = 2 * k * half
        put_both(
            owner_of(k, 1 - core),
            lambda at=at: shared[at : at + half],
            lambda at=at: shared[at + half : at + 2 * half],
        )


def stream_of(tab, kept, other, own, shared, pieces, cores):
    half = own.shape[0] // 2 // cores
    return pl.pallas_call(
        functools.partial(stream_kernel, cores * len(pieces), half),
        in_specs=[smem()] + [whole()] * (4 + len(pieces)),
        out_specs=whole(),
        out_shape=jax.ShapeDtypeStruct(other.shape, bf16),
        compiler_params=params(8),
        cost_estimate=cost(0, 10 * other.size),
        name="stream",
    )(tab, kept, other, own, shared, *pieces)


def expand_kernel(pieces, first, final, width, turned, owners, tab, *refs):
    count = len(pieces)
    blocks = []
    for number in pieces:
        blocks.append(refs[: 2 * number])
        refs = refs[2 * number :]
    gain, gate, up = refs[:3]
    refs = refs[3:]
    if not first:
        before, refs = refs[:3], refs[3:]
    if final:
        hidden, refs = refs[0], refs[1:]
    gates, ups, squares = refs
    step = pl.program_id(0)
    for i in range(count):

        @pl.when(step == i)
        def _(i=i):
            both = jnp.concatenate([x[...] for x in blocks[i]], 0).astype(f32)
            rows_of = both.shape[1]
            scaled = (both * gain[0]).astype(bf16)
            if turned:
                at = pl.ds(pl.multiple_of(tab[owners[i]] * rows_of, 128), rows_of)
                products = mm_nt(scaled, gate[:, at]), mm_nt(scaled, up[:, at])
            else:
                products = mm(scaled, gate[...]), mm(scaled, up[...])
            values = (
                *products,
                jnp.sum(both * both, axis=1, keepdims=True),
            )
            for n, (ref, value) in enumerate(zip((gates, ups, squares), values)):
                if i == 0:
                    ref[...] = value if first else value + before[n][...]
                else:
                    ref[...] += value

    if final:

        @pl.when(step == count - 1)
        def _():
            scale = lax.rsqrt(squares[...] / width + norm_eps)
            g = gates[...] * scale
            hidden[...] = (g / (1.0 + jnp.exp(-g)) * (ups[...] * scale)).astype(bf16)


def expand(tab, mines, theirs, owners, gain, gate, up, before, final):
    count = len(mines)
    pieces = tuple(len(x) for x in mines)
    rows, features = sum(x.shape[0] for x in mines[0]), mines[0][0].shape[1]
    arrays = [x for own, other in zip(mines, theirs) for x in (*own, *other)]
    units = gate.shape[1]
    first = before is None
    width = gate.shape[0]

    def owner(i, tab):
        index = tab[owners[0]]
        for n in range(1, count):
            index = jnp.where(i == n, tab[owners[n]], index)
        return index

    def full(shape):
        return pl.BlockSpec(shape, lambda i, tab: (0,) * len(shape))

    sums = [(2 * rows, units), (2 * rows, units), (2 * rows, 1)]
    ins = [full(x.shape) for x in arrays]
    ins += [pl.BlockSpec((1, 1, features), lambda i, tab: (owner(i, tab), 0, 0))]
    turned = features % 128 == 0
    if turned:
        gate, up = gate.T, up.T
        ins += [pl.BlockSpec(memory_space=pltpu.VMEM)] * 2
    else:
        ins += [pl.BlockSpec((features, units), lambda i, tab: (owner(i, tab), 0))] * 2
    if not first:
        ins += [full(s) for s in sums]
    shapes = [jax.ShapeDtypeStruct(s, f32) for s in sums]
    out_shapes = [jax.ShapeDtypeStruct((2 * rows, units), bf16)] if final else shapes
    return pl.pallas_call(
        functools.partial(expand_kernel, pieces, first, final, width, turned, owners),
        grid_spec=pltpu.PrefetchScalarGridSpec(
            num_scalar_prefetch=1,
            grid=(count,),
            in_specs=ins,
            out_specs=[full(s.shape) for s in out_shapes],
            scratch_shapes=[pltpu.VMEM(s, f32) for s in sums] if final else [],
        ),
        out_shape=out_shapes,
        compiler_params=params(20),
        cost_estimate=cost(
            8 * count * rows * features * units, count * (4 * features * units + 4 * rows * features)
        ),
        name="expand",
    )(tab, *arrays, gain, gate, up, *([] if first else before))


def collect_kernel(owners, tab, *refs):
    out = refs[-1]
    half = out.shape[1] // 2
    for i, at in enumerate(owners):
        out[tab[at], :half] = refs[2 * i][...]
        out[tab[at], half:] = refs[2 * i + 1][...]


def collect(tab, blocks, owners, half):
    ranks = len(blocks)
    features = blocks[0].shape[1]
    ins, args = [], []
    for x in blocks:
        ins += [
            pl.BlockSpec((half, features), lambda i, tab: (tab[RANK], 0)),
            pl.BlockSpec((half, features), lambda i, tab: (ranks, 0)),
        ]
        args += [x, x]
    shape = (ranks, 2 * half, features)
    return pl.pallas_call(
        functools.partial(collect_kernel, owners),
        grid_spec=pltpu.PrefetchScalarGridSpec(
            num_scalar_prefetch=1,
            grid=(1,),
            in_specs=ins,
            out_specs=pl.BlockSpec(shape, lambda i, tab: (0, 0, 0)),
        ),
        out_shape=jax.ShapeDtypeStruct(shape, bf16),
        compiler_params=params(10),
        cost_estimate=cost(0, 8 * ranks * half * features),
        name="collect",
    )(tab, *args)


def contract_kernel(begin, hidden, weight, mine, given):
    rows, wide = mine.shape
    at = pl.ds(pl.multiple_of(begin + pl.program_id(0) * wide, 128), wide)
    got = mm(hidden[...], weight[:, at]).astype(bf16)
    mine[...] = got[:rows]
    given[...] = got[rows:]


def contract(hidden, weight, part, parts):
    rows, units = hidden.shape
    columns = weight.shape[1] // parts
    wide = columns // 2 if columns % 256 == 0 else columns
    steps = columns // wide
    out = jax.ShapeDtypeStruct((rows // 2, columns), bf16)
    return pl.pallas_call(
        functools.partial(contract_kernel, part * columns),
        grid=(steps,),
        in_specs=[
            pl.BlockSpec((rows, units), lambda i: (0, 0)),
            whole(),
        ],
        out_specs=[pl.BlockSpec((rows // 2, wide), lambda i: (0, i))] * 2,
        out_shape=[out, out],
        compiler_params=params(16),
        cost_estimate=cost(2 * rows * units * columns, 2 * (units + rows) * columns),
        name="contract",
    )(hidden, weight)


def add_kernel(step, tab, mine_f, theirs_f, mine_b, theirs_b, *refs):
    got, (out_f, out_b) = refs[:-2], refs[-2:]
    busy = tab[BUSY] == 1
    own_f = mine_f[...].astype(f32) + theirs_f[...].astype(f32)
    own_b = mine_b[...].astype(f32) + theirs_b[...].astype(f32)
    if step == 1:
        out_f[...] = jnp.where(busy, 0.0, own_f).astype(bf16)
        out_b[...] = own_b.astype(bf16)
    elif step == 2:
        out_f[...] = (own_f + jnp.where(busy, 0.0, got[0][...].astype(f32))).astype(bf16)
        out_b[...] = (own_b + jnp.where(busy, 0.0, got[1][...].astype(f32))).astype(bf16)
    else:
        from_f = jnp.where(busy, got[0][...], got[1][...]).astype(f32)
        from_b = jnp.where(busy, got[2][...], got[3][...]).astype(f32)
        out_f[...] = (own_f + from_f).astype(bf16)
        out_b[...] = (own_b + from_b).astype(bf16)


def add(tab, table, step, mine, theirs, got, half):
    columns = mine.shape[1]
    far = table.reach + 1 - step

    def at(where):
        return pl.BlockSpec((half, columns), lambda i, tab: (tab[where + far], 0))

    full = pl.BlockSpec((half, columns), lambda i, tab: (0, 0))
    out = jax.ShapeDtypeStruct((half, columns), bf16)
    return pl.pallas_call(
        functools.partial(add_kernel, step),
        grid_spec=pltpu.PrefetchScalarGridSpec(
            num_scalar_prefetch=1,
            grid=(1,),
            in_specs=[at(table.ahead)] * 2 + [at(table.behind)] * 2 + [full] * len(got),
            out_specs=[full, full],
        ),
        out_shape=[out, out],
        compiler_params=params(8),
        cost_estimate=cost(0, 16 * half * columns),
        name="add",
    )(tab, mine, theirs, mine, theirs, *got)


def close_kernel(begin, tab, mm_, tm, me, te, f_last, f_prev, b_last, b_prev, own, kept, given):
    busy, first = tab[BUSY] == 1, tab[CORE] == 0
    half, columns = kept.shape
    features = own.shape[2]

    def total(*refs):
        out = refs[0][...].astype(f32)
        for r in refs[1:]:
            out = out + r[...].astype(f32)
        return out

    main = total(mm_, tm, f_last) + jnp.where(busy, b_prev[...], b_last[...]).astype(f32)
    extra = total(me, te, f_prev, b_last)
    for c in range(columns // features):
        cols = slice(c * features, (c + 1) * features)
        m = (main[:, cols] + own[begin + c, :half].astype(f32)).astype(bf16)
        e = (extra[:, cols] + own[begin + c, half:].astype(f32)).astype(bf16)
        kept[:, cols] = jnp.where(first, m, e)
        given[:, cols] = jnp.where(first, e, m)


def close(tab, mine, theirs, got_f, got_b, own, begin, half):
    columns = mine.shape[1]
    nodes = mine.shape[0] // half
    own_at = pl.BlockSpec((half, columns), lambda i, tab: (tab[RANK], 0))
    extra_at = pl.BlockSpec((half, columns), lambda i, tab: (nodes - 1, 0))
    full = pl.BlockSpec((half, columns), lambda i, tab: (0, 0))
    out = jax.ShapeDtypeStruct((half, columns), bf16)
    return pl.pallas_call(
        functools.partial(close_kernel, begin),
        grid_spec=pltpu.PrefetchScalarGridSpec(
            num_scalar_prefetch=1,
            grid=(1,),
            in_specs=[own_at, own_at, extra_at, extra_at]
            + [full] * 4
            + [pl.BlockSpec(own.shape, lambda i, tab: (0, 0, 0))],
            out_specs=[full, full],
        ),
        out_shape=[out, out],
        compiler_params=params(12),
        cost_estimate=cost(0, 24 * half * columns),
        name="close",
    )(tab, mine, theirs, mine, theirs, got_f[-1], got_f[-2], got_b[-1], got_b[-2], own)


def finish_kernel(parts, tab, *refs):
    kept, got, out = refs[:parts], refs[parts : 2 * parts], refs[-1]
    half, columns = kept[0].shape
    first = tab[CORE] == 0
    row = tab[CORE] * (2 * half) + lax.broadcasted_iota(i32, (half, 1), 0)
    for p in range(parts):
        cols = slice(p * columns, (p + 1) * columns)
        low = jnp.where(first, kept[p][...], got[p][...])
        high = jnp.where(first, got[p][...], kept[p][...])
        zero = jnp.zeros_like(low)
        out[:half, cols] = jnp.where(row < tab[LIVE], low, zero)
        out[half:, cols] = jnp.where(row + half < tab[LIVE], high, zero)


def finish(tab, kept, got):
    half, columns = kept[0].shape
    return pl.pallas_call(
        functools.partial(finish_kernel, len(kept)),
        in_specs=[smem()] + [whole()] * (2 * len(kept)),
        out_specs=whole(),
        out_shape=jax.ShapeDtypeStruct((2 * half, columns * len(kept)), bf16),
        compiler_params=params(8),
        cost_estimate=cost(0, 8 * half * columns * len(kept)),
        name="finish",
    )(tab, *kept, *got)


contract_parts = 2


def on_device(
    order,
    queries,
    latent_cache,
    new_latent,
    span_len,
    dec_count,
    span_start,
    cache_len,
    value_weight,
    out_weight,
    residual,
    norm_gain,
    gate_weight,
    up_weight,
    down_weight,
):
    ranks = len(order)
    reach = ranks // 2
    cores = lax.axis_size("head")
    rows_dev, width = residual.shape
    half = rows_dev // 2 // cores
    features = out_weight.shape[1]
    table = Table(ranks, cache_len.shape[1])

    forward = [(order[i], order[(i + 1) % ranks]) for i in range(ranks)]
    backward = [(b, a) for a, b in forward]
    exchange = [(c, cores - 1 - c) for c in range(cores)]

    def send_next(x):
        return lax.ppermute(x, "blk", forward)

    def send_prev(x):
        return lax.ppermute(x, "blk", backward)

    def swap(x):
        return lax.ppermute(x, "head", exchange)

    ids = jnp.stack([lax.axis_index("blk"), lax.axis_index("head")]).astype(i32)
    scalars = [ids, span_len, dec_count, span_start, cache_len]
    caches = (queries, latent_cache, new_latent, value_weight)
    tab, *lead, decoded = attend(table, order, scalars, *caches, 0, 2, None)

    packed = pack(tab, residual, ranks, cores)
    pieces = []
    for k, x in enumerate(packed):
        pairs = [
            (i * cores + c, (i + k + len(packed) * c) % ranks * cores + c)
            for i in range(ranks)
            for c in range(cores)
            if k + c > 0
        ]
        pieces.append(lax.ppermute(x, ("blk", "head"), pairs))

    decoded, packed = lax.optimization_barrier((decoded, packed))
    follow = attend(table, order, [tab], *caches, 1, 2, decoded)
    follow, pieces = lax.optimization_barrier((follow, pieces))
    shared = swap(share(tab, packed[0], pieces, cores))

    total = None
    gathered = []
    for head, main, extra in (lead, follow):
        behind, ahead = [], []
        for step in range(reach):
            if step == 0:
                out_f, out_b = head, main
            elif step == 1:
                out_f, out_b = route(tab, (main, behind[0]), (extra, ahead[0]))
            else:
                out_f, out_b = route(
                    tab,
                    (behind[step - 2], behind[step - 1]),
                    (ahead[step - 2], ahead[step - 1]),
                )
            behind.append(send_next(out_f))
            ahead.append(send_prev(out_b))
        gathered.append([main] + behind + ahead + [extra])
    gathered[0], shared = lax.optimization_barrier((gathered[0], shared))
    for part in range(2):
        total = project(tab, table, gathered[part], total, out_weight, part, 2, cores)
    kept, given = total
    stream = stream_of(tab, kept, swap(given), packed[0], shared, pieces, cores)

    gain = norm_gain.reshape(ranks, 1, features)
    sums = expand(tab, [[stream]], [[swap(stream)]], [RANK], gain, gate_weight, up_weight, None, False)
    blocks, owners = [stream], [RANK]
    fore, back = stream, stream
    cut = -(-stream.shape[0] // 32) * 16
    done = None
    for step in range(1, reach + 1):
        if done is not None:
            back, fore, done = lax.optimization_barrier((back, fore, done))
        done = sums
        if step < reach:
            back, fore = send_next(back), send_prev(fore)
            arrived = [[back], [fore]]
            from_owner = [table.owner_back + step, table.owner_fore + step]
        else:
            arrived = [[send_next(back[:cut]), send_prev(fore[cut:])]]
            from_owner = [table.owner_back + step]
        tied, sums = lax.optimization_barrier((arrived, sums))
        others = [[swap(x) for x in pieces] for pieces in tied]
        sums = expand(
            tab, arrived, others, from_owner, gain, gate_weight, up_weight, sums, step == reach
        )
        blocks += [x[0] if len(x) == 1 else jnp.concatenate(x, 0) for x in arrived]
        owners += from_owner
    (hidden,) = sums
    own = collect(tab, blocks, owners, half)

    parts = contract_parts
    mine, theirs = [], []
    for part in range(parts):
        a, b = contract(hidden, down_weight, part, parts)
        mine.append(a)
        theirs.append(swap(b))
    kept_out, got_out = [], []
    for part in range(parts):
        got_f, got_b = [], []
        for step in range(1, reach + 1):
            if step == 1:
                got = []
            elif step == 2:
                got = [got_f[0], got_b[0]]
            else:
                got = [got_f[step - 3], got_f[step - 2], got_b[step - 3], got_b[step - 2]]
            out_f, out_b = add(tab, table, step, mine[part], theirs[part], got, half)
            got_f.append(send_next(out_f))
            got_b.append(send_prev(out_b))
        a, b = close(
            tab, mine[part], theirs[part], got_f, got_b, own, part * (ranks // parts), half
        )
        kept_out.append(a)
        got_out.append(swap(b))
    return finish(tab, kept_out, got_out)


def solution(mesh):
    placed = (
        P(("groups", "blk"), "head"),
        P(("groups", "blk"), None, None),
        P(None, ("groups", "blk")),
        P("groups"),
        P("groups"),
        P(("groups", "blk")),
        P(("groups", "blk"), None),
        P("head", None, None),
        P("head", "blk"),
        P(("groups", "blk"), None),
        P(),
        P(None, ("blk", "head")),
        P(None, ("blk", "head")),
        P(("blk", "head"), None),
    )
    order = ring_order(mesh)
    return jax.shard_map(
        lambda *args: on_device(order, *args),
        mesh=mesh,
        in_specs=placed,
        out_specs=P(("groups", "blk", "head"), None),
        check_vma=False,
    )
```

```python
import functools

import jax
import jax.numpy as jnp
from jax import lax
from jax.experimental import pallas as pl
from jax.experimental.pallas import tpu as pltpu
from jax.sharding import PartitionSpec as P

score_scale = 192.0 ** (-0.5)
norm_eps = 1e-06
masked_score = -1e30
f32, bf16, i32 = jnp.float32, jnp.bfloat16, jnp.int32
SMEM = pltpu.SMEM
MIB = 1 << 20

RANK, CORE, BUSY, BUSY_RANK, SPAN, DEC, LIVE, START, LENGTHS = range(9)


def mm(a, b):
    return lax.dot_general(a, b, (((1,), (0,)), ((), ())), preferred_element_type=f32)


def mm_nt(a, b):
    return lax.dot_general(a, b, (((1,), (1,)), ((), ())), preferred_element_type=f32)


def in_hbm(x):
    return pltpu.with_memory_space_constraint(x, pltpu.HBM)


def smem():
    return pl.BlockSpec(memory_space=SMEM)


def whole():
    return pl.BlockSpec(memory_space=pltpu.VMEM)


def params(mib=32):
    return pltpu.CompilerParams(vmem_limit_bytes=mib * MIB)


def cost(flops, moved, exps=0):
    return pl.CostEstimate(flops=int(flops), bytes_accessed=int(moved), transcendentals=int(exps))


def ring_order(mesh):
    count = mesh.shape["blk"]
    natural = list(range(count))
    snake = natural[0::2] + natural[1::2][::-1]
    names = list(mesh.axis_names)
    axes = [names.index("blk")] + [a for a, x in enumerate(names) if x != "blk"]
    lane = mesh.devices.transpose(axes)
    firsts = [lane[i].reshape(-1)[0] for i in natural]
    if not all(hasattr(d, "coords") for d in firsts):
        return snake

    def length(order):
        hops = zip(order, order[1:] + order[:1])
        return sum(
            sum(abs(u - v) for u, v in zip(firsts[a].coords, firsts[b].coords)) for a, b in hops
        )

    return natural if length(natural) <= length(snake) else snake


class Table:
    def __init__(self, ranks, slots):
        self.reach = ranks // 2
        self.source = LENGTHS + slots
        self.ahead = self.source + ranks + 1
        self.behind = self.ahead + self.reach + 1
        self.owner_back = self.behind + self.reach + 1
        self.owner_fore = self.owner_back + self.reach + 1
        self.who = self.owner_fore + self.reach + 1
        self.at = self.who + ranks
        self.size = self.at + ranks


def table_kernel(table, order, ids, span, dec, start, lengths, out):
    reach, ranks = table.reach, len(order)
    for i, r in enumerate(order):
        out[table.who + i] = r
        out[table.at + r] = i
    rank, core = ids[0], ids[1]
    most, busy_rank = span[0] + dec[0], jnp.int32(0)
    for i in range(1, ranks):
        here = span[i] + dec[i]
        busy_rank = jnp.where(here > most, i, busy_rank)
        most = jnp.maximum(here, most)
    busy = rank == busy_rank

    def wrap(x):
        x = jnp.where(x < 0, x + ranks, x)
        return jnp.where(x >= ranks, x - ranks, x)

    place, busy_place = out[table.at + rank], out[table.at + busy_rank]
    to_busy = wrap(busy_place - place)
    from_busy = wrap(place - busy_place)

    def node_ahead(k):
        far = (to_busy > 0) & (k > to_busy + 1)
        slot = out[table.who + wrap(place + k - jnp.where(far, 1, 0))]
        return jnp.where((to_busy > 0) & (k == to_busy + 1), ranks, slot)

    def node_behind(k):
        far = (from_busy > 0) & (k > from_busy)
        slot = out[table.who + wrap(place - k + jnp.where(far, 1, 0))]
        return jnp.where((from_busy > 0) & (k == from_busy), ranks, slot)

    out[RANK] = rank
    out[CORE] = core
    out[BUSY] = jnp.where(busy, 1, 0)
    out[BUSY_RANK] = busy_rank
    out[SPAN] = span[rank]
    out[DEC] = dec[rank]
    out[LIVE] = span[rank] + dec[rank]
    out[START] = start[0]
    for j in range(lengths.shape[1]):
        out[LENGTHS + j] = lengths[0, j]
    out[table.source + rank] = 0
    for k in range(1, reach + 1):
        out[table.ahead + k] = node_ahead(k)
        out[table.behind + k] = node_behind(k)
        out[table.owner_back + k] = out[table.who + wrap(place - k)]
        out[table.owner_fore + k] = out[table.who + wrap(place + k)]
        out[table.source + node_behind(k)] = k
        last = jnp.where(busy, ranks, node_ahead(k)) if k == reach else node_ahead(k)
        out[table.source + last] = reach + k


def attend_kernel(
    table, order, heads, first, count, group, rows, lat, value, lead, *refs
):
    if lead:
        scalars, refs = refs[:5], refs[5:]
        q_hbm, cache_hbm, fresh, vw_hbm, tab, head, main, extra, later, mask = refs[:10]
        refs = refs[10:]
        q, keys, vw, latent, fz, q_sem, key_sem, vw_sem, dq = refs
        loaded, base = heads, 0
    else:
        tab, q_hbm, cache_hbm, fresh, vw_hbm, decoded_here, head, main, extra = refs[:9]
        q, keys, vw, latent, fz, q_sem, key_sem, vw_sem = refs[9:]
        loaded, base = count, first
    cached, wide = keys.shape[2], keys.shape[1]
    slots = cache_hbm.shape[0] - 1
    odd_slot = keys.shape[0] - 1
    shift, pair, dr = wide - lat, 2 * lat, 8
    groups, pairs = count // group, group // 2
    loads = loaded // group

    def q_copy(g):
        source = pl.ds((base + g * group) * lat, group * lat)
        return pltpu.make_async_copy(
            q_hbm.at[:, source], q.at[:, pl.ds(g * group * lat, group * lat)], q_sem.at[g]
        )

    def vw_copy(g):
        source = pl.ds(first + g * group, group)
        return pltpu.make_async_copy(vw_hbm.at[source], vw.at[pl.ds(g * group, group)], vw_sem.at[g])

    even_copy = pltpu.make_async_copy(cache_hbm.at[0], keys.at[0, pl.ds(0, lat)], key_sem.at[0])
    odd_copy = pltpu.make_async_copy(
        cache_hbm.at[0], keys.at[odd_slot, pl.ds(shift, lat)], key_sem.at[1]
    )
    waiting = [q_copy(g) for g in range(1, loads)]
    if lead:
        rest_copy = pltpu.make_async_copy(
            cache_hbm.at[pl.ds(1, slots)], keys.at[pl.ds(1, slots), pl.ds(0, lat)], key_sem.at[2]
        )
        waiting.append(rest_copy)
    waiting += [vw_copy(g) for g in range(groups)]

    def start_next(number):
        for _ in range(min(number, len(waiting))):
            waiting.pop(0).start()

    even_copy.start()
    q_copy(0).start()
    odd_copy.start()
    start_next(1)
    if lead:
        table_kernel(table, order, *scalars, tab)
    span, decs = tab[SPAN], tab[DEC]

    def onehot(shape, row_dim, slot_dim):
        r = lax.broadcasted_iota(i32, shape, row_dim)
        j = lax.broadcasted_iota(i32, shape, slot_dim)
        return jnp.where((r == span + j) & (j < decs), 1.0, 0.0).astype(bf16)

    tail = jnp.zeros((shift, cached), bf16)
    for s in range(odd_slot):
        keys[s, lat:] = tail
    keys[odd_slot, :shift] = tail
    fz[...] = jnp.zeros_like(fz)
    fz[:rows, :lat] = fresh[...].astype(f32)
    fresh_even = fz[...].astype(bf16)
    fresh_odd = pltpu.roll(fz[...], shift, 1).astype(bf16)

    m = pairs * rows
    cols = cached + fz.shape[0]
    row = lax.broadcasted_iota(i32, (m, 1), 0) % rows
    col = lax.broadcasted_iota(i32, (m, cols), 1)
    seen = col < jnp.where(col < cached, tab[START], cached + 1 + row)

    def span_latent(lhs, slot, fresh_keys):
        s = jnp.concatenate([mm(lhs, keys[slot]), mm_nt(lhs, fresh_keys)], 1)
        s = jnp.where(seen, s * score_scale, masked_score)
        e = jnp.exp(s - jnp.max(s, axis=1, keepdims=True))
        w = (e * (1.0 / jnp.sum(e, axis=1, keepdims=True))).astype(bf16)
        o = mm_nt(w[:, :cached], keys[0, :value]) + mm(w[:, cached:], fresh_even[:, :value])
        return jnp.where(row < span, o, 0.0).astype(bf16)

    even_copy.wait()
    odd_copy.wait()
    for g in range(groups):
        q_copy(g).wait()
        start_next(2)
        start = g * group * lat
        for odd in range(2):
            off = start + odd * (pair - wide)
            lhs = jnp.concatenate(
                [q[:, off + pair * p : off + pair * p + wide] for p in range(pairs)], 0
            )
            latent[g, odd] = span_latent(lhs, odd_slot * odd, fresh_odd if odd else fresh_even)
    start_next(len(waiting))

    if lead:
        for g in range(groups, loads):
            q_copy(g).wait()
        pick = onehot((16, rows), 1, 0)
        for p in range(heads // 2):
            got = mm(pick, q[:, pair * p : pair * (p + 1)])[:dr]
            dq[2 * p * dr : (2 * p + 1) * dr] = got[:, :wide]
            dq[(2 * p + 1) * dr : (2 * p + 2) * dr] = pltpu.roll(
                got[:, pair - wide :], wide - shift, 1
            )
        n = heads * dr
        queries = dq[...].astype(bf16)
        slot = lax.broadcasted_iota(i32, (n, 1), 0) % dr
        rest_copy.wait()
        length = jnp.zeros((n, 1), i32)
        scores = jnp.zeros((n, cached), f32)
        for s in range(slots):
            scores = jnp.where(slot == s, mm(queries, keys[s + 1]), scores)
            length = jnp.where(slot == s, tab[LENGTHS + s], length)
        unmasked = lax.broadcasted_iota(i32, (n, cached), 1) < length
        scores = jnp.where(unmasked, scores * score_scale, masked_score)
        own = mm_nt(queries, fresh_even)
        column = lax.broadcasted_iota(i32, own.shape, 1)
        own = jnp.sum(jnp.where(column == span + slot, own, 0.0), axis=1, keepdims=True)
        own = own * score_scale
        peak = jnp.maximum(jnp.max(scores, axis=1, keepdims=True), own)
        e = jnp.exp(scores - peak)
        e_own = jnp.exp(own - peak)
        total = jnp.sum(e, axis=1, keepdims=True) + e_own
        w = e / total
        acc = jnp.zeros((n, value), f32)
        for s in range(slots):
            acc = acc + mm_nt(jnp.where(slot == s, w, 0.0).astype(bf16), keys[s + 1, :value])
        own_value = mm(pick, fresh[:, :value])[:dr]
        own_value = jnp.broadcast_to(own_value[None], (heads, dr, value)).reshape(n, value)
        dec = (acc + (e_own / total).astype(bf16).astype(f32) * own_value).astype(bf16)
        later[...] = dec[count * dr :]
        mask[...] = jnp.full(mask.shape, tab[BUSY].astype(f32))
        dec = dec[: count * dr]
    else:
        dec = decoded_here[...]

    place = onehot((rows, 16), 0, 1)
    vh = vw.shape[2]
    block = rows // 2
    for g in range(groups):
        vw_copy(g).wait()
        values, decoded = [], []
        for p in range(pairs):
            h = g * group + 2 * p
            lhs = jnp.concatenate(
                [
                    latent[g, 0, p * rows : (p + 1) * rows],
                    latent[g, 1, p * rows : (p + 1) * rows],
                    dec[h * dr : (h + 2) * dr],
                ],
                0,
            )
            r = mm(lhs, jnp.concatenate([vw[h], vw[h + 1]], 1))
            values += [r[:rows, :vh], r[rows : 2 * rows, vh:]]
            decoded += [r[2 * rows : 2 * rows + dr, :vh], r[2 * rows + dr :, vh:]]
        decoded = jnp.concatenate(decoded, 1)
        decoded = jnp.concatenate([decoded, jnp.zeros_like(decoded)], 0).astype(bf16)
        out = (jnp.concatenate(values, 1) + mm(place, decoded)).astype(bf16)
        at = slice(g * group * vh, (g + 1) * group * vh)
        main[:, at] = out[:block]
        extra[:, at] = out[block:]
        head[:, at] = jnp.where(tab[BUSY] == 1, out[block:], out[:block])


def attend(table, order, scalars, queries, cache, fresh, vw, part, parts, decoded):
    rows, heads = queries.shape[0], vw.shape[0]
    lat = queries.shape[1] // heads
    slots, _, cached = cache.shape
    value, vh = vw.shape[1:]
    count = heads // parts
    group = min(8, count)
    lead = decoded is None
    loaded = heads if lead else count
    wide = -(-lat // 128) * 128
    half = jax.ShapeDtypeStruct((rows // 2, count * vh), bf16)
    hbm = pl.BlockSpec(memory_space=pltpu.HBM)
    scratch = [
        pltpu.VMEM((rows, loaded * lat), bf16),
        pltpu.VMEM((slots + 1 if lead else 2, wide, cached), bf16),
        pltpu.VMEM((count, value, vh), bf16),
        pltpu.VMEM((count // group, 2, group // 2 * rows, value), bf16),
        pltpu.VMEM((-(-rows // 128) * 128, wide), f32),
        pltpu.SemaphoreType.DMA((loaded // group,)),
        pltpu.SemaphoreType.DMA((3,)),
        pltpu.SemaphoreType.DMA((count // group,)),
    ]
    out_shape, out_specs = [half] * 3, [whole()] * 3
    ins = [smem()] * len(scalars) + [hbm, hbm, whole(), hbm]
    args = [*scalars, in_hbm(queries), in_hbm(cache), fresh.T, in_hbm(vw)]
    if lead:
        scratch.append(pltpu.VMEM((heads * 8, wide), f32))
        out_shape = [jax.ShapeDtypeStruct((table.size,), i32)] + out_shape
        out_shape += [jax.ShapeDtypeStruct(((heads - count) * 8, value), bf16)]
        out_shape += [jax.ShapeDtypeStruct((8, 128), f32)]
        out_specs = [smem()] + out_specs + [whole()] * 2
    else:
        ins.append(whole())
        args.append(decoded)
    return pl.pallas_call(
        functools.partial(
            attend_kernel, table, order, heads, part * count, count, group, rows, lat, value, lead
        ),
        in_specs=ins,
        out_specs=out_specs,
        out_shape=out_shape,
        scratch_shapes=scratch,
        compiler_params=params(24),
        cost_estimate=cost(
            2 * rows * count * (cached + rows) * (lat + value),
            2 * (queries.size + cache.size + vw.size) // parts,
            rows * count * (cached + rows),
        ),
        name="attend",
    )(*args)


def pack_kernel(ranks, cores, features, tab, res, *outs):
    for k in range(ranks // cores):
        target = tab[RANK] + k + (ranks // cores) * tab[CORE]
        target = jnp.where(target >= ranks, target - ranks, target)

        def put(columns, k=k):
            outs[k][...] = res[:, columns]

        if features % 128 == 0:
            put(pl.ds(pl.multiple_of(target * features, 128), features))
        else:
            for t in range(ranks):
                pl.when(target == t)(functools.partial(put, slice(t * features, (t + 1) * features)))


def pack(tab, residual, ranks, cores):
    rows, width = residual.shape
    features = width // ranks
    count = ranks // cores
    return pl.pallas_call(
        functools.partial(pack_kernel, ranks, cores, features),
        in_specs=[smem(), whole()],
        out_specs=[whole()] * count,
        out_shape=[jax.ShapeDtypeStruct((rows, features), bf16)] * count,
        compiler_params=params(8),
        cost_estimate=cost(0, 4 * residual.size),
        name="pack",
    )(tab, residual)


def share_kernel(half, tab, own, *refs):
    pieces, out = refs[:-1], refs[-1]
    other = 1 - tab[CORE]
    block = own.shape[0] // 2
    low = pl.multiple_of(other * half, half)
    high = pl.multiple_of(block + other * half, half)

    def put(k, piece):
        out[2 * k * half : (2 * k + 1) * half] = piece[pl.ds(low, half)]
        out[(2 * k + 1) * half : (2 * k + 2) * half] = piece[pl.ds(high, half)]

    for k, piece in enumerate(pieces):
        if k > 0:
            put(k, piece)
        else:
            pl.when(tab[CORE] == 0)(functools.partial(put, k, own))
            pl.when(tab[CORE] != 0)(functools.partial(put, k, piece))


def share(tab, own, pieces, cores):
    rows, features = own.shape
    half = rows // 2 // cores
    return pl.pallas_call(
        functools.partial(share_kernel, half),
        in_specs=[smem()] + [whole()] * (1 + len(pieces)),
        out_specs=whole(),
        out_shape=jax.ShapeDtypeStruct((2 * half * len(pieces), features), bf16),
        compiler_params=params(8),
        cost_estimate=cost(0, 4 * own.size * len(pieces)),
        name="share",
    )(tab, own, *pieces)


def project_kernel(source, nodes, block, half, part, first, tab, *refs):
    blocks, refs = refs[: nodes + 1], refs[nodes + 1 :]
    before = None if first else refs[0]
    weight, kept, given, acc = refs[-4:]
    step = pl.program_id(0)
    depth = blocks[0].shape[1] // pl.num_programs(0)
    columns = pl.ds(pl.multiple_of(step * depth, 128), depth)
    last = jnp.where(tab[BUSY] == 1, blocks[nodes][:, columns], blocks[nodes - 1][:, columns])
    lhs = jnp.concatenate([b[:, columns] for b in blocks[: nodes - 1]] + [last], 0)
    got = mm(lhs, weight[pl.ds(pl.multiple_of(part * blocks[0].shape[1] + step * depth, 128), depth)])

    @pl.when(step == 0)
    def _():
        acc[...] = got if first else got + before[...]

    @pl.when(step > 0)
    def _():
        acc[...] += got

    @pl.when(step == pl.num_programs(0) - 1)
    def _():
        core = tab[CORE]
        for k in range(nodes):
            at = tab[source + k] * block
            kept[k * half : (k + 1) * half] = acc[pl.ds(pl.multiple_of(at + core * half, half), half)]
            other = acc[pl.ds(pl.multiple_of(at + (1 - core) * half, half), half)]
            given[k * half : (k + 1) * half] = other.astype(bf16)


def project_part_kernel(nodes, part, first, tab, *refs):
    blocks, refs = refs[: nodes + 1], refs[nodes + 1 :]
    weight, out = refs[-2:]
    step = pl.program_id(0)
    depth = blocks[0].shape[1] // pl.num_programs(0)
    columns = pl.ds(pl.multiple_of(step * depth, 128), depth)
    last = jnp.where(tab[BUSY] == 1, blocks[nodes][:, columns], blocks[nodes - 1][:, columns])
    lhs = jnp.concatenate([b[:, columns] for b in blocks[: nodes - 1]] + [last], 0)
    got = mm(lhs, weight[pl.ds(pl.multiple_of(part * blocks[0].shape[1] + step * depth, 128), depth)])

    @pl.when(step == 0)
    def _():
        out[...] = got if first else got + refs[0][...]

    @pl.when(step > 0)
    def _():
        out[...] += got


def project(tab, table, blocks, before, weight, part, parts, cores):
    block, width = blocks[0].shape
    nodes = len(blocks) - 1
    half = block // cores
    features = weight.shape[1]
    depth = width
    steps = width // depth
    total = jax.ShapeDtypeStruct((nodes * block, features), f32)
    final = part == parts - 1
    first = before is None
    ins = [smem()] + [whole()] * (nodes + 2 + (not first))
    args = [tab, *blocks] + ([] if first else [before]) + [weight]
    estimate = cost(
        2 * nodes * block * width * features, 2 * (nodes * block * width + width * features)
    )
    if not final:
        return pl.pallas_call(
            functools.partial(project_part_kernel, nodes, part, first),
            grid=(steps,),
            in_specs=ins,
            out_specs=pl.BlockSpec(total.shape, lambda i: (0, 0)),
            out_shape=total,
            compiler_params=params(16),
            cost_estimate=estimate,
            name="project",
        )(*args)
    return pl.pallas_call(
        functools.partial(project_kernel, table.source, nodes, block, half, part, first),
        grid=(steps,),
        in_specs=ins,
        out_specs=[pl.BlockSpec((nodes * half, features), lambda i: (0, 0))] * 2,
        out_shape=[
            jax.ShapeDtypeStruct((nodes * half, features), f32),
            jax.ShapeDtypeStruct((nodes * half, features), bf16),
        ],
        scratch_shapes=[pltpu.VMEM(total.shape, f32)],
        compiler_params=params(16),
        cost_estimate=estimate,
        name="project",
    )(*args)


def stream_kernel(ranks, half, tab, kept, other, own, shared, *refs):
    pieces, out = refs[:-1], refs[-1]
    rank, core, busy_rank = tab[RANK], tab[CORE], tab[BUSY_RANK]
    count = len(pieces)
    block = own.shape[0] // 2

    def put(slot, extra):
        rows = pl.ds(pl.multiple_of(slot * half, half), half)
        total = kept[rows] + other[rows].astype(f32) + extra.astype(f32)
        out[rows] = total.astype(bf16)

    def put_both(owner, main, extra):
        put(owner, main())

        @pl.when(owner == busy_rank)
        def _():
            put(ranks, extra())

    def owner_of(k, c):
        owner = rank - k - count * c
        return jnp.where(owner < 0, owner + ranks, owner)

    low = pl.ds(pl.multiple_of(core * half, half), half)
    high = pl.ds(pl.multiple_of(block + core * half, half), half)
    for k, piece in enumerate(pieces):

        def received(piece=piece, k=k):
            put_both(owner_of(k, core), lambda: piece[low], lambda: piece[high])

        if k > 0:
            received()
        else:
            pl.when(core == 0)(functools.partial(received, own))
            pl.when(core != 0)(received)
        at = 2 * k * half
        put_both(
            owner_of(k, 1 - core),
            lambda at=at: shared[at : at + half],
            lambda at=at: shared[at + half : at + 2 * half],
        )


def stream_of(tab, kept, other, own, shared, pieces, cores):
    half = own.shape[0] // 2 // cores
    return pl.pallas_call(
        functools.partial(stream_kernel, cores * len(pieces), half),
        in_specs=[smem()] + [whole()] * (4 + len(pieces)),
        out_specs=whole(),
        out_shape=jax.ShapeDtypeStruct(other.shape, bf16),
        compiler_params=params(8),
        cost_estimate=cost(0, 10 * other.size),
        name="stream",
    )(tab, kept, other, own, shared, *pieces)


def expand_kernel(pieces, first, final, width, turned, owners, tab, *refs):
    count = len(pieces)
    blocks = []
    for number in pieces:
        blocks.append(refs[: 2 * number])
        refs = refs[2 * number :]
    gain, gate, up = refs[:3]
    refs = refs[3:]
    if not first:
        before, refs = refs[:3], refs[3:]
    if final:
        hidden, refs = refs[0], refs[1:]
    gates, ups, squares = refs
    step = pl.program_id(0)
    for i in range(count):

        @pl.when(step == i)
        def _(i=i):
            both = jnp.concatenate([x[...] for x in blocks[i]], 0).astype(f32)
            rows_of = both.shape[1]
            scaled = (both * gain[0]).astype(bf16)
            if turned:
                at = pl.ds(pl.multiple_of(tab[owners[i]] * rows_of, 128), rows_of)
                products = mm_nt(scaled, gate[:, at]), mm_nt(scaled, up[:, at])
            else:
                products = mm(scaled, gate[...]), mm(scaled, up[...])
            values = (
                *products,
                jnp.sum(both * both, axis=1, keepdims=True),
            )
            for n, (ref, value) in enumerate(zip((gates, ups, squares), values)):
                if i == 0:
                    ref[...] = value if first else value + before[n][...]
                else:
                    ref[...] += value

    if final:

        @pl.when(step == count - 1)
        def _():
            scale = lax.rsqrt(squares[...] / width + norm_eps)
            g = gates[...] * scale
            hidden[...] = (g / (1.0 + jnp.exp(-g)) * (ups[...] * scale)).astype(bf16)


def expand(tab, mines, theirs, owners, gain, gate, up, before, final):
    count = len(mines)
    pieces = tuple(len(x) for x in mines)
    rows, features = sum(x.shape[0] for x in mines[0]), mines[0][0].shape[1]
    arrays = [x for own, other in zip(mines, theirs) for x in (*own, *other)]
    units = gate.shape[1]
    first = before is None
    width = gate.shape[0]

    def owner(i, tab):
        index = tab[owners[0]]
        for n in range(1, count):
            index = jnp.where(i == n, tab[owners[n]], index)
        return index

    def full(shape):
        return pl.BlockSpec(shape, lambda i, tab: (0,) * len(shape))

    sums = [(2 * rows, units), (2 * rows, units), (2 * rows, 1)]
    ins = [full(x.shape) for x in arrays]
    ins += [pl.BlockSpec((1, 1, features), lambda i, tab: (owner(i, tab), 0, 0))]
    turned = features % 128 == 0
    if turned:
        gate, up = gate.T, up.T
        ins += [pl.BlockSpec(memory_space=pltpu.VMEM)] * 2
    else:
        ins += [pl.BlockSpec((features, units), lambda i, tab: (owner(i, tab), 0))] * 2
    if not first:
        ins += [full(s) for s in sums]
    shapes = [jax.ShapeDtypeStruct(s, f32) for s in sums]
    out_shapes = [jax.ShapeDtypeStruct((2 * rows, units), bf16)] if final else shapes
    return pl.pallas_call(
        functools.partial(expand_kernel, pieces, first, final, width, turned, owners),
        grid_spec=pltpu.PrefetchScalarGridSpec(
            num_scalar_prefetch=1,
            grid=(count,),
            in_specs=ins,
            out_specs=[full(s.shape) for s in out_shapes],
            scratch_shapes=[pltpu.VMEM(s, f32) for s in sums] if final else [],
        ),
        out_shape=out_shapes,
        compiler_params=params(20),
        cost_estimate=cost(
            8 * count * rows * features * units, count * (4 * features * units + 4 * rows * features)
        ),
        name="expand",
    )(tab, *arrays, gain, gate, up, *([] if first else before))


def collect_kernel(owners, tab, *refs):
    out = refs[-1]
    half = out.shape[1] // 2
    for i, at in enumerate(owners):
        out[tab[at], :half] = refs[2 * i][...]
        out[tab[at], half:] = refs[2 * i + 1][...]


def collect(tab, blocks, owners, half):
    ranks = len(blocks)
    features = blocks[0].shape[1]
    ins, args = [], []
    for x in blocks:
        ins += [
            pl.BlockSpec((half, features), lambda i, tab: (tab[RANK], 0)),
            pl.BlockSpec((half, features), lambda i, tab: (ranks, 0)),
        ]
        args += [x, x]
    shape = (ranks, 2 * half, features)
    return pl.pallas_call(
        functools.partial(collect_kernel, owners),
        grid_spec=pltpu.PrefetchScalarGridSpec(
            num_scalar_prefetch=1,
            grid=(1,),
            in_specs=ins,
            out_specs=pl.BlockSpec(shape, lambda i, tab: (0, 0, 0)),
        ),
        out_shape=jax.ShapeDtypeStruct(shape, bf16),
        compiler_params=params(10),
        cost_estimate=cost(0, 8 * ranks * half * features),
        name="collect",
    )(tab, *args)


def contract_kernel(begin, hidden, weight, mine, given):
    rows, wide = mine.shape
    at = pl.ds(pl.multiple_of(begin + pl.program_id(0) * wide, 128), wide)
    got = mm(hidden[...], weight[:, at]).astype(bf16)
    mine[...] = got[:rows]
    given[...] = got[rows:]


def contract(hidden, weight, part, parts):
    rows, units = hidden.shape
    columns = weight.shape[1] // parts
    wide = columns // 2 if columns % 256 == 0 else columns
    steps = columns // wide
    out = jax.ShapeDtypeStruct((rows // 2, columns), bf16)
    return pl.pallas_call(
        functools.partial(contract_kernel, part * columns),
        grid=(steps,),
        in_specs=[
            pl.BlockSpec((rows, units), lambda i: (0, 0)),
            whole(),
        ],
        out_specs=[pl.BlockSpec((rows // 2, wide), lambda i: (0, i))] * 2,
        out_shape=[out, out],
        compiler_params=params(16),
        cost_estimate=cost(2 * rows * units * columns, 2 * (units + rows) * columns),
        name="contract",
    )(hidden, weight)


def pick_kernel(table, half, tab, mine, theirs, *outs):
    busy = tab[BUSY] == 1
    reach = table.reach
    for step in range(1, reach + 1):
        for n, where in enumerate((table.ahead, table.behind)):
            at = pl.multiple_of(tab[where + reach + 1 - step] * half, half)
            total = mine[pl.ds(at, half)].astype(f32) + theirs[pl.ds(at, half)].astype(f32)
            if step == 1 and n == 0:
                total = jnp.where(busy, 0.0, total)
            outs[2 * (step - 1) + n][...] = total


def pick(tab, table, mine, theirs, half):
    columns = mine.shape[1]
    count = 2 * table.reach
    out = jax.ShapeDtypeStruct((half, columns), f32)
    return pl.pallas_call(
        functools.partial(pick_kernel, table, half),
        in_specs=[smem(), whole(), whole()],
        out_specs=[whole()] * count,
        out_shape=[out] * count,
        compiler_params=params(10),
        cost_estimate=cost(0, 8 * count * half * columns),
        name="pick",
    )(tab, mine, theirs)


def close_kernel(begin, tab, mm_, tm, me, te, f_last, f_prev, b_last, b_prev, own, kept, given):
    busy, first = tab[BUSY] == 1, tab[CORE] == 0
    half, columns = kept.shape
    features = own.shape[2]

    def total(*refs):
        out = refs[0][...].astype(f32)
        for r in refs[1:]:
            out = out + r[...].astype(f32)
        return out

    main = total(mm_, tm, f_last) + jnp.where(busy, b_prev[...], b_last[...]).astype(f32)
    extra = total(me, te, f_prev, b_last)
    for c in range(columns // features):
        cols = slice(c * features, (c + 1) * features)
        m = (main[:, cols] + own[begin + c, :half].astype(f32)).astype(bf16)
        e = (extra[:, cols] + own[begin + c, half:].astype(f32)).astype(bf16)
        kept[:, cols] = jnp.where(first, m, e)
        given[:, cols] = jnp.where(first, e, m)


def close(tab, mine, theirs, got_f, got_b, own, begin, half):
    columns = mine.shape[1]
    nodes = mine.shape[0] // half
    own_at = pl.BlockSpec((half, columns), lambda i, tab: (tab[RANK], 0))
    extra_at = pl.BlockSpec((half, columns), lambda i, tab: (nodes - 1, 0))
    full = pl.BlockSpec((half, columns), lambda i, tab: (0, 0))
    out = jax.ShapeDtypeStruct((half, columns), bf16)
    return pl.pallas_call(
        functools.partial(close_kernel, begin),
        grid_spec=pltpu.PrefetchScalarGridSpec(
            num_scalar_prefetch=1,
            grid=(1,),
            in_specs=[own_at, own_at, extra_at, extra_at]
            + [full] * 4
            + [pl.BlockSpec(own.shape, lambda i, tab: (0, 0, 0))],
            out_specs=[full, full],
        ),
        out_shape=[out, out],
        compiler_params=params(12),
        cost_estimate=cost(0, 24 * half * columns),
        name="close",
    )(tab, mine, theirs, mine, theirs, got_f[-1], got_f[-2], got_b[-1], got_b[-2], own)


def finish_kernel(parts, tab, *refs):
    kept, got, out = refs[:parts], refs[parts : 2 * parts], refs[-1]
    half, columns = kept[0].shape
    first = tab[CORE] == 0
    row = tab[CORE] * (2 * half) + lax.broadcasted_iota(i32, (half, 1), 0)
    for p in range(parts):
        cols = slice(p * columns, (p + 1) * columns)
        low = jnp.where(first, kept[p][...], got[p][...])
        high = jnp.where(first, got[p][...], kept[p][...])
        zero = jnp.zeros_like(low)
        out[:half, cols] = jnp.where(row < tab[LIVE], low, zero)
        out[half:, cols] = jnp.where(row + half < tab[LIVE], high, zero)


def finish(tab, kept, got):
    half, columns = kept[0].shape
    return pl.pallas_call(
        functools.partial(finish_kernel, len(kept)),
        in_specs=[smem()] + [whole()] * (2 * len(kept)),
        out_specs=whole(),
        out_shape=jax.ShapeDtypeStruct((2 * half, columns * len(kept)), bf16),
        compiler_params=params(8),
        cost_estimate=cost(0, 8 * half * columns * len(kept)),
        name="finish",
    )(tab, *kept, *got)


contract_parts = 2


def on_device(
    order,
    queries,
    latent_cache,
    new_latent,
    span_len,
    dec_count,
    span_start,
    cache_len,
    value_weight,
    out_weight,
    residual,
    norm_gain,
    gate_weight,
    up_weight,
    down_weight,
):
    ranks = len(order)
    reach = ranks // 2
    cores = lax.axis_size("head")
    rows_dev, width = residual.shape
    half = rows_dev // 2 // cores
    features = out_weight.shape[1]
    table = Table(ranks, cache_len.shape[1])

    forward = [(order[i], order[(i + 1) % ranks]) for i in range(ranks)]
    backward = [(b, a) for a, b in forward]
    exchange = [(c, cores - 1 - c) for c in range(cores)]

    def send_next(x):
        return lax.ppermute(x, "blk", forward)

    def send_prev(x):
        return lax.ppermute(x, "blk", backward)

    def swap(x):
        return lax.ppermute(x, "head", exchange)

    ids = jnp.stack([lax.axis_index("blk"), lax.axis_index("head")]).astype(i32)
    scalars = [ids, span_len, dec_count, span_start, cache_len]
    caches = (queries, latent_cache, new_latent, value_weight)
    tab, *lead, decoded, mask = attend(table, order, scalars, *caches, 0, 2, None)
    here = mask[:1, :1] > 0

    def choose(special, usual):
        return jnp.where(jnp.broadcast_to(here, usual.shape), special, usual)


    packed = list(pack(tab, residual, ranks, cores))
    pieces = [None] * len(packed)

    def send_piece(k):
        pairs = [
            (i * cores + c, (i + k + len(packed) * c) % ranks * cores + c)
            for i in range(ranks)
            for c in range(cores)
            if k + c > 0
        ]
        pieces[k] = lax.ppermute(packed[k], ("blk", "head"), pairs)

    early = len(packed) // 2
    for k in range(early):
        send_piece(k)
    decoded, packed = lax.optimization_barrier((decoded, packed))
    packed = list(packed)
    follow = attend(table, order, [tab], *caches, 1, 2, decoded)
    follow, pieces[:early], out_weight = lax.optimization_barrier(
        (follow, pieces[:early], out_weight)
    )

    total = None
    chains = []
    for head, main, extra in (lead, follow):
        chains.append((head, main, extra, [], []))
    for step in range(reach):
        for part, (head, main, extra, behind, ahead) in enumerate(chains):
            if step == 0:
                out_f, out_b = head, main
            elif step == 1:
                out_f, out_b = choose(main, behind[0]), choose(extra, ahead[0])
            else:
                out_f = choose(behind[step - 2], behind[step - 1])
                out_b = choose(ahead[step - 2], ahead[step - 1])
            piece = early + step - 1 + part * (len(packed) - early) // 2
            if 0 < step <= (len(packed) - early) // 2:
                out_f, out_b, packed[piece] = lax.optimization_barrier((out_f, out_b, packed[piece]))
                send_piece(piece)
            else:
                out_f, out_b = lax.optimization_barrier((out_f, out_b))
            behind.append(send_next(out_f))
            ahead.append(send_prev(out_b))
    gathered = [[main] + behind + ahead + [extra] for _, main, extra, behind, ahead in chains]
    shared = swap(share(tab, packed[0], pieces, cores))
    gathered[0], shared = lax.optimization_barrier((gathered[0], shared))
    for part in range(2):
        total = project(tab, table, gathered[part], total, out_weight, part, 2, cores)
    kept, given = total
    stream = stream_of(tab, kept, swap(given), packed[0], shared, pieces, cores)

    gain = norm_gain.reshape(ranks, 1, features)
    sums = expand(tab, [[stream]], [[swap(stream)]], [RANK], gain, gate_weight, up_weight, None, False)
    blocks, owners = [stream], [RANK]
    fore, back = stream, stream
    cut = -(-stream.shape[0] // 32) * 16
    done = None
    for step in range(1, reach + 1):
        if done is not None:
            back, fore, done = lax.optimization_barrier((back, fore, done))
        done = sums
        if step < reach:
            back, fore = send_next(back), send_prev(fore)
            arrived = [[back], [fore]]
            from_owner = [table.owner_back + step, table.owner_fore + step]
        else:
            arrived = [[send_next(back[:cut]), send_prev(fore[cut:])]]
            from_owner = [table.owner_back + step]
        tied, sums = lax.optimization_barrier((arrived, sums))
        others = [[swap(x) for x in pieces] for pieces in tied]
        sums = expand(
            tab, arrived, others, from_owner, gain, gate_weight, up_weight, sums, step == reach
        )
        blocks += [x[0] if len(x) == 1 else jnp.concatenate(x, 0) for x in arrived]
        owners += from_owner
    (hidden,) = sums
    own = collect(tab, blocks, owners, half)

    parts = contract_parts
    mine, theirs = [], []
    for part in range(parts):
        a, b = contract(hidden, down_weight, part, parts)
        mine.append(a)
        theirs.append(swap(b))
    kept_out, got_out = [], []
    for part in range(parts):
        got_f, got_b = [], []
        owned = pick(tab, table, mine[part], theirs[part], half)
        for step in range(1, reach + 1):
            out_f, out_b = owned[2 * step - 2], owned[2 * step - 1]
            if step == 2:
                out_f = out_f + choose(jnp.zeros_like(out_f), got_f[0].astype(f32))
                out_b = out_b + choose(jnp.zeros_like(out_b), got_b[0].astype(f32))
            elif step > 2:
                out_f = out_f + choose(got_f[step - 3], got_f[step - 2]).astype(f32)
                out_b = out_b + choose(got_b[step - 3], got_b[step - 2]).astype(f32)
            out_f, out_b = lax.optimization_barrier((out_f.astype(bf16), out_b.astype(bf16)))
            got_f.append(send_next(out_f))
            got_b.append(send_prev(out_b))
        a, b = close(
            tab, mine[part], theirs[part], got_f, got_b, own, part * (ranks // parts), half
        )
        kept_out.append(a)
        got_out.append(swap(b))
    return finish(tab, kept_out, got_out)


def solution(mesh):
    placed = (
        P(("groups", "blk"), "head"),
        P(("groups", "blk"), None, None),
        P(None, ("groups", "blk")),
        P("groups"),
        P("groups"),
        P(("groups", "blk")),
        P(("groups", "blk"), None),
        P("head", None, None),
        P("head", "blk"),
        P(("groups", "blk"), None),
        P(),
        P(None, ("blk", "head")),
        P(None, ("blk", "head")),
        P(("blk", "head"), None),
    )
    order = ring_order(mesh)
    return jax.shard_map(
        lambda *args: on_device(order, *args),
        mesh=mesh,
        in_specs=placed,
        out_specs=P(("groups", "blk", "head"), None),
        check_vma=False,
    )
```

```python
import functools

import jax
import jax.numpy as jnp
from jax import lax
from jax.experimental import pallas as pl
from jax.experimental.pallas import tpu as pltpu
from jax.sharding import PartitionSpec as P

score_scale = 192.0 ** (-0.5)
norm_eps = 1e-06
masked_score = -1e30
f32, bf16, i32 = jnp.float32, jnp.bfloat16, jnp.int32
SMEM = pltpu.SMEM
MIB = 1 << 20

RANK, CORE, BUSY, BUSY_RANK, SPAN, DEC, LIVE, START, LENGTHS = range(9)


def mm(a, b):
    return lax.dot_general(a, b, (((1,), (0,)), ((), ())), preferred_element_type=f32)


def mm_nt(a, b):
    return lax.dot_general(a, b, (((1,), (1,)), ((), ())), preferred_element_type=f32)


def in_hbm(x):
    return pltpu.with_memory_space_constraint(x, pltpu.HBM)


def smem():
    return pl.BlockSpec(memory_space=SMEM)


def whole():
    return pl.BlockSpec(memory_space=pltpu.VMEM)


def params(mib=32):
    return pltpu.CompilerParams(vmem_limit_bytes=mib * MIB)


def cost(flops, moved, exps=0):
    return pl.CostEstimate(flops=int(flops), bytes_accessed=int(moved), transcendentals=int(exps))


def ring_order(mesh):
    count = mesh.shape["blk"]
    natural = list(range(count))
    snake = natural[0::2] + natural[1::2][::-1]
    names = list(mesh.axis_names)
    axes = [names.index("blk")] + [a for a, x in enumerate(names) if x != "blk"]
    lane = mesh.devices.transpose(axes)
    firsts = [lane[i].reshape(-1)[0] for i in natural]
    if not all(hasattr(d, "coords") for d in firsts):
        return snake

    def length(order):
        hops = zip(order, order[1:] + order[:1])
        return sum(
            sum(abs(u - v) for u, v in zip(firsts[a].coords, firsts[b].coords)) for a, b in hops
        )

    return natural if length(natural) <= length(snake) else snake


class Table:
    def __init__(self, ranks, slots):
        self.reach = ranks // 2
        self.source = LENGTHS + slots
        self.ahead = self.source + ranks + 1
        self.behind = self.ahead + self.reach + 1
        self.owner_back = self.behind + self.reach + 1
        self.owner_fore = self.owner_back + self.reach + 1
        self.who = self.owner_fore + self.reach + 1
        self.at = self.who + ranks
        self.size = self.at + ranks


def table_kernel(table, order, given, out):
    reach, ranks = table.reach, len(order)
    span = [given[2 + i] for i in range(ranks)]
    dec = [given[2 + ranks + i] for i in range(ranks)]
    lengths = 3 + 2 * ranks
    for i, r in enumerate(order):
        out[table.who + i] = r
        out[table.at + r] = i
    rank, core = given[0], given[1]
    most, busy_rank = span[0] + dec[0], jnp.int32(0)
    for i in range(1, ranks):
        here = span[i] + dec[i]
        busy_rank = jnp.where(here > most, i, busy_rank)
        most = jnp.maximum(here, most)
    busy = rank == busy_rank

    def wrap(x):
        x = jnp.where(x < 0, x + ranks, x)
        return jnp.where(x >= ranks, x - ranks, x)

    place, busy_place = out[table.at + rank], out[table.at + busy_rank]
    to_busy = wrap(busy_place - place)
    from_busy = wrap(place - busy_place)

    def node_ahead(k):
        far = (to_busy > 0) & (k > to_busy + 1)
        slot = out[table.who + wrap(place + k - jnp.where(far, 1, 0))]
        return jnp.where((to_busy > 0) & (k == to_busy + 1), ranks, slot)

    def node_behind(k):
        far = (from_busy > 0) & (k > from_busy)
        slot = out[table.who + wrap(place - k + jnp.where(far, 1, 0))]
        return jnp.where((from_busy > 0) & (k == from_busy), ranks, slot)

    out[RANK] = rank
    out[CORE] = core
    out[BUSY] = jnp.where(busy, 1, 0)
    out[BUSY_RANK] = busy_rank
    out[SPAN] = given[2 + rank]
    out[DEC] = given[2 + ranks + rank]
    out[LIVE] = given[2 + rank] + given[2 + ranks + rank]
    out[START] = given[lengths - 1]
    for j in range(given.shape[0] - lengths):
        out[LENGTHS + j] = given[lengths + j]
    out[table.source + rank] = 0
    for k in range(1, reach + 1):
        out[table.ahead + k] = node_ahead(k)
        out[table.behind + k] = node_behind(k)
        out[table.owner_back + k] = out[table.who + wrap(place - k)]
        out[table.owner_fore + k] = out[table.who + wrap(place + k)]
        out[table.source + node_behind(k)] = k
        last = jnp.where(busy, ranks, node_ahead(k)) if k == reach else node_ahead(k)
        out[table.source + last] = reach + k


def attend_kernel(
    table, order, heads, first, count, group, rows, lat, value, lead, *refs
):
    if lead:
        given, refs = refs[0], refs[1:]
        q_hbm, cache_hbm, fresh, vw_hbm, tab, head, main, extra, later = refs[:9]
        flags, refs = refs[9:12], refs[12:]
        q, keys, vw, latent, fz, q_sem, key_sem, vw_sem, dq = refs
        loaded, base = heads, 0
    else:
        tab, q_hbm, cache_hbm, fresh, vw_hbm, decoded_here, head, main, extra = refs[:9]
        q, keys, vw, latent, fz, q_sem, key_sem, vw_sem = refs[9:]
        loaded, base = count, first
    cached, wide = keys.shape[2], keys.shape[1]
    slots = cache_hbm.shape[0] - 1
    odd_slot = keys.shape[0] - 1
    shift, pair, dr = wide - lat, 2 * lat, 8
    groups, pairs = count // group, group // 2
    loads = loaded // group

    def q_copy(g):
        source = pl.ds((base + g * group) * lat, group * lat)
        return pltpu.make_async_copy(
            q_hbm.at[:, source], q.at[:, pl.ds(g * group * lat, group * lat)], q_sem.at[g]
        )

    def vw_copy(g):
        source = pl.ds(first + g * group, group)
        return pltpu.make_async_copy(vw_hbm.at[source], vw.at[pl.ds(g * group, group)], vw_sem.at[g])

    even_copy = pltpu.make_async_copy(cache_hbm.at[0], keys.at[0, pl.ds(0, lat)], key_sem.at[0])
    odd_copy = pltpu.make_async_copy(
        cache_hbm.at[0], keys.at[odd_slot, pl.ds(shift, lat)], key_sem.at[1]
    )
    waiting = [q_copy(g) for g in range(1, loads)]
    if lead:
        rest_copy = pltpu.make_async_copy(
            cache_hbm.at[pl.ds(1, slots)], keys.at[pl.ds(1, slots), pl.ds(0, lat)], key_sem.at[2]
        )
        waiting.append(rest_copy)
    waiting += [vw_copy(g) for g in range(groups)]

    def start_next(number):
        for _ in range(min(number, len(waiting))):
            waiting.pop(0).start()

    even_copy.start()
    q_copy(0).start()
    odd_copy.start()
    start_next(1)
    if lead:
        table_kernel(table, order, given, tab)
    span, decs = tab[SPAN], tab[DEC]

    def onehot(shape, row_dim, slot_dim):
        r = lax.broadcasted_iota(i32, shape, row_dim)
        j = lax.broadcasted_iota(i32, shape, slot_dim)
        return jnp.where((r == span + j) & (j < decs), 1.0, 0.0).astype(bf16)

    tail = jnp.zeros((shift, cached), bf16)
    for s in range(odd_slot):
        keys[s, lat:] = tail
    keys[odd_slot, :shift] = tail
    fz[...] = jnp.zeros_like(fz)
    fz[:rows, :lat] = fresh[...].astype(f32)
    fresh_even = fz[...].astype(bf16)
    fresh_odd = pltpu.roll(fz[...], shift, 1).astype(bf16)

    m = pairs * rows
    cols = cached + fz.shape[0]
    row = lax.broadcasted_iota(i32, (m, 1), 0) % rows
    col = lax.broadcasted_iota(i32, (m, cols), 1)
    seen = col < jnp.where(col < cached, tab[START], cached + 1 + row)

    def span_latent(lhs, slot, fresh_keys):
        s = jnp.concatenate([mm(lhs, keys[slot]), mm_nt(lhs, fresh_keys)], 1)
        s = jnp.where(seen, s * score_scale, masked_score)
        e = jnp.exp(s - jnp.max(s, axis=1, keepdims=True))
        w = (e * (1.0 / jnp.sum(e, axis=1, keepdims=True))).astype(bf16)
        o = mm_nt(w[:, :cached], keys[0, :value]) + mm(w[:, cached:], fresh_even[:, :value])
        return jnp.where(row < span, o, 0.0).astype(bf16)

    even_copy.wait()
    odd_copy.wait()
    for g in range(groups):
        q_copy(g).wait()
        start_next(2)
        start = g * group * lat
        for odd in range(2):
            off = start + odd * (pair - wide)
            lhs = jnp.concatenate(
                [q[:, off + pair * p : off + pair * p + wide] for p in range(pairs)], 0
            )
            latent[g, odd] = span_latent(lhs, odd_slot * odd, fresh_odd if odd else fresh_even)
    start_next(len(waiting))

    if lead:
        for g in range(groups, loads):
            q_copy(g).wait()
        pick = onehot((16, rows), 1, 0)
        for p in range(heads // 2):
            got = mm(pick, q[:, pair * p : pair * (p + 1)])[:dr]
            dq[2 * p * dr : (2 * p + 1) * dr] = got[:, :wide]
            dq[(2 * p + 1) * dr : (2 * p + 2) * dr] = pltpu.roll(
                got[:, pair - wide :], wide - shift, 1
            )
        n = heads * dr
        queries = dq[...].astype(bf16)
        slot = lax.broadcasted_iota(i32, (n, 1), 0) % dr
        rest_copy.wait()
        length = jnp.zeros((n, 1), i32)
        scores = jnp.zeros((n, cached), f32)
        for s in range(slots):
            scores = jnp.where(slot == s, mm(queries, keys[s + 1]), scores)
            length = jnp.where(slot == s, tab[LENGTHS + s], length)
        unmasked = lax.broadcasted_iota(i32, (n, cached), 1) < length
        scores = jnp.where(unmasked, scores * score_scale, masked_score)
        own = mm_nt(queries, fresh_even)
        column = lax.broadcasted_iota(i32, own.shape, 1)
        own = jnp.sum(jnp.where(column == span + slot, own, 0.0), axis=1, keepdims=True)
        own = own * score_scale
        peak = jnp.maximum(jnp.max(scores, axis=1, keepdims=True), own)
        e = jnp.exp(scores - peak)
        e_own = jnp.exp(own - peak)
        total = jnp.sum(e, axis=1, keepdims=True) + e_own
        w = e / total
        acc = jnp.zeros((n, value), f32)
        for s in range(slots):
            acc = acc + mm_nt(jnp.where(slot == s, w, 0.0).astype(bf16), keys[s + 1, :value])
        own_value = mm(pick, fresh[:, :value])[:dr]
        own_value = jnp.broadcast_to(own_value[None], (heads, dr, value)).reshape(n, value)
        dec = (acc + (e_own / total).astype(bf16).astype(f32) * own_value).astype(bf16)
        later[...] = dec[count * dr :]
        for flag, at in zip(flags, (BUSY, CORE, LIVE)):
            flag[...] = jnp.full(flag.shape, tab[at].astype(f32))
        dec = dec[: count * dr]
    else:
        dec = decoded_here[...]

    place = onehot((rows, 16), 0, 1)
    vh = vw.shape[2]
    block = rows // 2
    for g in range(groups):
        vw_copy(g).wait()
        values, decoded = [], []
        for p in range(pairs):
            h = g * group + 2 * p
            lhs = jnp.concatenate(
                [
                    latent[g, 0, p * rows : (p + 1) * rows],
                    latent[g, 1, p * rows : (p + 1) * rows],
                    dec[h * dr : (h + 2) * dr],
                ],
                0,
            )
            r = mm(lhs, jnp.concatenate([vw[h], vw[h + 1]], 1))
            values += [r[:rows, :vh], r[rows : 2 * rows, vh:]]
            decoded += [r[2 * rows : 2 * rows + dr, :vh], r[2 * rows + dr :, vh:]]
        decoded = jnp.concatenate(decoded, 1)
        decoded = jnp.concatenate([decoded, jnp.zeros_like(decoded)], 0).astype(bf16)
        out = (jnp.concatenate(values, 1) + mm(place, decoded)).astype(bf16)
        at = slice(g * group * vh, (g + 1) * group * vh)
        main[:, at] = out[:block]
        extra[:, at] = out[block:]
        head[:, at] = jnp.where(tab[BUSY] == 1, out[block:], out[:block])


def attend(table, order, numbers, queries, cache, fresh, vw, part, parts, decoded):
    rows, heads = queries.shape[0], vw.shape[0]
    lat = queries.shape[1] // heads
    slots, _, cached = cache.shape
    value, vh = vw.shape[1:]
    count = heads // parts
    group = min(8, count)
    lead = decoded is None
    loaded = heads if lead else count
    wide = -(-lat // 128) * 128
    half = jax.ShapeDtypeStruct((rows // 2, count * vh), bf16)
    hbm = pl.BlockSpec(memory_space=pltpu.HBM)
    scratch = [
        pltpu.VMEM((rows, loaded * lat), bf16),
        pltpu.VMEM((slots + 1 if lead else 2, wide, cached), bf16),
        pltpu.VMEM((count, value, vh), bf16),
        pltpu.VMEM((count // group, 2, group // 2 * rows, value), bf16),
        pltpu.VMEM((-(-rows // 128) * 128, wide), f32),
        pltpu.SemaphoreType.DMA((loaded // group,)),
        pltpu.SemaphoreType.DMA((3,)),
        pltpu.SemaphoreType.DMA((count // group,)),
    ]
    out_shape, out_specs = [half] * 3, [whole()] * 3
    ins = [smem(), hbm, hbm, whole(), hbm]
    args = [numbers, in_hbm(queries), in_hbm(cache), fresh.T, in_hbm(vw)]
    if lead:
        scratch.append(pltpu.VMEM((heads * 8, wide), f32))
        out_shape = [jax.ShapeDtypeStruct((table.size,), i32)] + out_shape
        out_shape += [jax.ShapeDtypeStruct(((heads - count) * 8, value), bf16)]
        out_shape += [jax.ShapeDtypeStruct((1, 1), f32)] * 3
        out_specs = [smem()] + out_specs + [whole()] * 4
    else:
        ins.append(whole())
        args.append(decoded)
    return pl.pallas_call(
        functools.partial(
            attend_kernel, table, order, heads, part * count, count, group, rows, lat, value, lead
        ),
        in_specs=ins,
        out_specs=out_specs,
        out_shape=out_shape,
        scratch_shapes=scratch,
        compiler_params=params(24),
        cost_estimate=cost(
            2 * rows * count * (cached + rows) * (lat + value),
            2 * (queries.size + cache.size + vw.size) // parts,
            rows * count * (cached + rows),
        ),
        name="attend",
    )(*args)


def pack_kernel(ranks, cores, features, tab, res, *outs):
    for k in range(ranks // cores):
        target = tab[RANK] + k + (ranks // cores) * tab[CORE]
        target = jnp.where(target >= ranks, target - ranks, target)

        def put(columns, k=k):
            outs[k][...] = res[:, columns]

        if features % 128 == 0:
            put(pl.ds(pl.multiple_of(target * features, 128), features))
        else:
            for t in range(ranks):
                pl.when(target == t)(functools.partial(put, slice(t * features, (t + 1) * features)))


def pack(tab, residual, ranks, cores):
    rows, width = residual.shape
    features = width // ranks
    count = ranks // cores
    return pl.pallas_call(
        functools.partial(pack_kernel, ranks, cores, features),
        in_specs=[smem(), whole()],
        out_specs=[whole()] * count,
        out_shape=[jax.ShapeDtypeStruct((rows, features), bf16)] * count,
        compiler_params=params(8),
        cost_estimate=cost(0, 4 * residual.size),
        name="pack",
    )(tab, residual)


def share_kernel(half, tab, own, *refs):
    pieces, out = refs[:-1], refs[-1]
    other = 1 - tab[CORE]
    block = own.shape[0] // 2
    low = pl.multiple_of(other * half, half)
    high = pl.multiple_of(block + other * half, half)

    def put(k, piece):
        out[2 * k * half : (2 * k + 1) * half] = piece[pl.ds(low, half)]
        out[(2 * k + 1) * half : (2 * k + 2) * half] = piece[pl.ds(high, half)]

    for k, piece in enumerate(pieces):
        if k > 0:
            put(k, piece)
        else:
            pl.when(tab[CORE] == 0)(functools.partial(put, k, own))
            pl.when(tab[CORE] != 0)(functools.partial(put, k, piece))


def share(tab, own, pieces, cores):
    rows, features = own.shape
    half = rows // 2 // cores
    return pl.pallas_call(
        functools.partial(share_kernel, half),
        in_specs=[smem()] + [whole()] * (1 + len(pieces)),
        out_specs=whole(),
        out_shape=jax.ShapeDtypeStruct((2 * half * len(pieces), features), bf16),
        compiler_params=params(8),
        cost_estimate=cost(0, 4 * own.size * len(pieces)),
        name="share",
    )(tab, own, *pieces)


def project_kernel(source, nodes, block, half, part, first, tab, *refs):
    blocks, refs = refs[: nodes + 1], refs[nodes + 1 :]
    before = None if first else refs[0]
    weight, kept, given, acc = refs[-4:]
    step = pl.program_id(0)
    depth = blocks[0].shape[1] // pl.num_programs(0)
    columns = pl.ds(pl.multiple_of(step * depth, 128), depth)
    last = jnp.where(tab[BUSY] == 1, blocks[nodes][:, columns], blocks[nodes - 1][:, columns])
    lhs = jnp.concatenate([b[:, columns] for b in blocks[: nodes - 1]] + [last], 0)
    got = mm(lhs, weight[pl.ds(pl.multiple_of(part * blocks[0].shape[1] + step * depth, 128), depth)])

    @pl.when(step == 0)
    def _():
        acc[...] = got if first else got + before[...]

    @pl.when(step > 0)
    def _():
        acc[...] += got

    @pl.when(step == pl.num_programs(0) - 1)
    def _():
        core = tab[CORE]
        for k in range(nodes):
            at = tab[source + k] * block
            kept[k * half : (k + 1) * half] = acc[pl.ds(pl.multiple_of(at + core * half, half), half)]
            other = acc[pl.ds(pl.multiple_of(at + (1 - core) * half, half), half)]
            given[k * half : (k + 1) * half] = other.astype(bf16)


def project_part_kernel(nodes, part, first, tab, *refs):
    blocks, refs = refs[: nodes + 1], refs[nodes + 1 :]
    weight, out = refs[-2:]
    step = pl.program_id(0)
    depth = blocks[0].shape[1] // pl.num_programs(0)
    columns = pl.ds(pl.multiple_of(step * depth, 128), depth)
    last = jnp.where(tab[BUSY] == 1, blocks[nodes][:, columns], blocks[nodes - 1][:, columns])
    lhs = jnp.concatenate([b[:, columns] for b in blocks[: nodes - 1]] + [last], 0)
    got = mm(lhs, weight[pl.ds(pl.multiple_of(part * blocks[0].shape[1] + step * depth, 128), depth)])

    @pl.when(step == 0)
    def _():
        out[...] = got if first else got + refs[0][...]

    @pl.when(step > 0)
    def _():
        out[...] += got


def project(tab, table, blocks, before, weight, part, parts, cores):
    block, width = blocks[0].shape
    nodes = len(blocks) - 1
    half = block // cores
    features = weight.shape[1]
    depth = width
    steps = width // depth
    total = jax.ShapeDtypeStruct((nodes * block, features), f32)
    final = part == parts - 1
    first = before is None
    ins = [smem()] + [whole()] * (nodes + 2 + (not first))
    args = [tab, *blocks] + ([] if first else [before]) + [weight]
    estimate = cost(
        2 * nodes * block * width * features, 2 * (nodes * block * width + width * features)
    )
    if not final:
        return pl.pallas_call(
            functools.partial(project_part_kernel, nodes, part, first),
            grid=(steps,),
            in_specs=ins,
            out_specs=pl.BlockSpec(total.shape, lambda i: (0, 0)),
            out_shape=total,
            compiler_params=params(16),
            cost_estimate=estimate,
            name="project",
        )(*args)
    return pl.pallas_call(
        functools.partial(project_kernel, table.source, nodes, block, half, part, first),
        grid=(steps,),
        in_specs=ins,
        out_specs=[pl.BlockSpec((nodes * half, features), lambda i: (0, 0))] * 2,
        out_shape=[
            jax.ShapeDtypeStruct((nodes * half, features), f32),
            jax.ShapeDtypeStruct((nodes * half, features), bf16),
        ],
        scratch_shapes=[pltpu.VMEM(total.shape, f32)],
        compiler_params=params(16),
        cost_estimate=estimate,
        name="project",
    )(*args)


def place_kernel(ranks, half, tab, own, shared, *refs):
    pieces, out = refs[:-1], refs[-1]
    rank, core, busy_rank = tab[RANK], tab[CORE], tab[BUSY_RANK]
    count = len(pieces)
    block = own.shape[0] // 2

    def put(slot, extra):
        out[pl.ds(pl.multiple_of(slot * half, half), half)] = extra

    def put_both(owner, main, extra):
        put(owner, main())

        @pl.when(owner == busy_rank)
        def _():
            put(ranks, extra())

    def owner_of(k, c):
        owner = rank - k - count * c
        return jnp.where(owner < 0, owner + ranks, owner)

    low = pl.ds(pl.multiple_of(core * half, half), half)
    high = pl.ds(pl.multiple_of(block + core * half, half), half)
    for k, piece in enumerate(pieces):

        def received(piece=piece, k=k):
            put_both(owner_of(k, core), lambda: piece[low], lambda: piece[high])

        if k > 0:
            received()
        else:
            pl.when(core == 0)(functools.partial(received, own))
            pl.when(core != 0)(received)
        at = 2 * k * half
        put_both(
            owner_of(k, 1 - core),
            lambda at=at: shared[at : at + half],
            lambda at=at: shared[at + half : at + 2 * half],
        )


def placed_rows(tab, own, shared, pieces, cores):
    rows, features = own.shape
    half = rows // 2 // cores
    ranks = cores * len(pieces)
    return pl.pallas_call(
        functools.partial(place_kernel, ranks, half),
        in_specs=[smem()] + [whole()] * (2 + len(pieces)),
        out_specs=whole(),
        out_shape=jax.ShapeDtypeStruct(((ranks + 1) * half, features), bf16),
        compiler_params=params(8),
        cost_estimate=cost(0, 4 * (ranks + 1) * half * features),
        name="place",
    )(tab, own, shared, *pieces)


def expand_kernel(pieces, others, first, final, width, turned, owners, tab, *refs):
    count = len(pieces)
    blocks = []
    for number in pieces:
        blocks.append(refs[:number])
        refs = refs[number:]
    theirs, refs = refs[:others], refs[others:]
    gain, gate, up = refs[:3]
    refs = refs[3:]
    if not first:
        before, refs = refs[:3], refs[3:]
    if final:
        hidden, refs = refs[0], refs[1:]
    gates, ups, squares = refs
    step = pl.program_id(0)
    for i in range(count):

        @pl.when(step == i)
        def _(i=i):
            both = [x[...] for x in blocks[i]]
            for x in theirs:
                rows = x.shape[0] // count
                both.append(x[i * rows : (i + 1) * rows])
            both = jnp.concatenate(both, 0).astype(f32)
            rows_of = both.shape[1]
            scaled = (both * gain[0]).astype(bf16)
            if turned:
                at = pl.ds(pl.multiple_of(tab[owners[i]] * rows_of, 128), rows_of)
                products = mm_nt(scaled, gate[:, at]), mm_nt(scaled, up[:, at])
            else:
                products = mm(scaled, gate[...]), mm(scaled, up[...])
            values = (
                *products,
                jnp.sum(both * both, axis=1, keepdims=True),
            )
            for n, (ref, value) in enumerate(zip((gates, ups, squares), values)):
                if i == 0:
                    ref[...] = value if first else value + before[n][...]
                else:
                    ref[...] += value

    if final:

        @pl.when(step == count - 1)
        def _():
            scale = lax.rsqrt(squares[...] / width + norm_eps)
            g = gates[...] * scale
            hidden[...] = (g / (1.0 + jnp.exp(-g)) * (ups[...] * scale)).astype(bf16)


def expand(tab, mines, theirs, owners, gain, gate, up, before, final):
    count = len(mines)
    pieces = tuple(len(x) for x in mines)
    rows, features = sum(x.shape[0] for x in mines[0]), mines[0][0].shape[1]
    arrays = [x for own in mines for x in own] + theirs
    units = gate.shape[1]
    first = before is None
    width = gate.shape[0]

    def owner(i, tab):
        index = tab[owners[0]]
        for n in range(1, count):
            index = jnp.where(i == n, tab[owners[n]], index)
        return index

    def full(shape):
        return pl.BlockSpec(shape, lambda i, tab: (0,) * len(shape))

    sums = [(2 * rows, units), (2 * rows, units), (2 * rows, 1)]
    ins = [full(x.shape) for x in arrays]
    ins += [pl.BlockSpec((1, 1, features), lambda i, tab: (owner(i, tab), 0, 0))]
    turned = features % 128 == 0
    if turned:
        gate, up = gate.T, up.T
        ins += [pl.BlockSpec(memory_space=pltpu.VMEM)] * 2
    else:
        ins += [pl.BlockSpec((features, units), lambda i, tab: (owner(i, tab), 0))] * 2
    if not first:
        ins += [full(s) for s in sums]
    shapes = [jax.ShapeDtypeStruct(s, f32) for s in sums]
    out_shapes = [jax.ShapeDtypeStruct((2 * rows, units), bf16)] if final else shapes
    return pl.pallas_call(
        functools.partial(expand_kernel, pieces, len(theirs), first, final, width, turned, owners),
        grid_spec=pltpu.PrefetchScalarGridSpec(
            num_scalar_prefetch=1,
            grid=(count,),
            in_specs=ins,
            out_specs=[full(s.shape) for s in out_shapes],
            scratch_shapes=[pltpu.VMEM(s, f32) for s in sums] if final else [],
        ),
        out_shape=out_shapes,
        compiler_params=params(20),
        cost_estimate=cost(1, 1),
        name="expand",
    )(tab, *arrays, gain, gate, up, *([] if first else before))


def collect_kernel(owners, tab, *refs):
    out = refs[-1]
    if len(out.shape) == 2:
        half, features = out.shape[0] // 2, out.shape[1] // len(owners)
        for i, at in enumerate(owners):
            columns = pl.ds(pl.multiple_of(tab[at] * features, 128), features)
            out[:half, columns] = refs[2 * i][...]
            out[half:, columns] = refs[2 * i + 1][...]
        return
    half = out.shape[1] // 2
    for i, at in enumerate(owners):
        out[tab[at], :half] = refs[2 * i][...]
        out[tab[at], half:] = refs[2 * i + 1][...]


def collect(tab, blocks, owners, half):
    ranks = len(blocks)
    features = blocks[0].shape[1]
    ins, args = [], []
    for x in blocks:
        ins += [
            pl.BlockSpec((half, features), lambda i, tab: (tab[RANK], 0)),
            pl.BlockSpec((half, features), lambda i, tab: (ranks, 0)),
        ]
        args += [x, x]
    aligned = features % 128 == 0
    shape = (2 * half, ranks * features) if aligned else (ranks, 2 * half, features)
    out = pl.pallas_call(
        functools.partial(collect_kernel, owners),
        grid_spec=pltpu.PrefetchScalarGridSpec(
            num_scalar_prefetch=1,
            grid=(1,),
            in_specs=ins,
            out_specs=pl.BlockSpec(shape, lambda i, tab: (0,) * len(shape)),
        ),
        out_shape=jax.ShapeDtypeStruct(shape, bf16),
        compiler_params=params(10),
        cost_estimate=cost(0, 8 * ranks * half * features),
        name="collect",
    )(tab, *args)
    return out if aligned else out.transpose(1, 0, 2).reshape(2 * half, ranks * features)


def contract_kernel(begin, hidden, weight, out):
    wide = out.shape[1]
    at = pl.ds(pl.multiple_of(begin + pl.program_id(0) * wide, 128), wide)
    out[...] = mm(hidden[...], weight[:, at]).astype(bf16)


def contract(hidden, weight, part, parts, which):
    rows, units = hidden.shape[0] // 2, hidden.shape[1]
    columns = weight.shape[1] // parts
    wide = columns // 2 if columns % 256 == 0 else columns
    return pl.pallas_call(
        functools.partial(contract_kernel, part * columns),
        grid=(columns // wide,),
        in_specs=[pl.BlockSpec((rows, units), lambda i: (which, 0)), whole()],
        out_specs=pl.BlockSpec((rows, wide), lambda i: (0, i)),
        out_shape=jax.ShapeDtypeStruct((rows, columns), bf16),
        compiler_params=params(16),
        cost_estimate=cost(2 * rows * units * columns, 2 * (units + rows) * columns),
        name="contract",
    )(hidden, weight)


def pick_kernel(table, half, tab, mine, theirs, *outs):
    busy = tab[BUSY] == 1
    reach = table.reach
    for step in range(1, reach + 1):
        for n, where in enumerate((table.ahead, table.behind)):
            at = pl.multiple_of(tab[where + reach + 1 - step] * half, half)
            total = mine[pl.ds(at, half)].astype(f32) + theirs[pl.ds(at, half)].astype(f32)
            if step == 1 and n == 0:
                total = jnp.where(busy, 0.0, total)
            outs[2 * (step - 1) + n][...] = total
    for n, slot in enumerate((tab[RANK], 2 * reach)):
        at = pl.multiple_of(slot * half, half)
        outs[2 * reach + n][...] = mine[pl.ds(at, half)].astype(f32) + theirs[pl.ds(at, half)].astype(f32)


def pick(tab, table, mine, theirs, half):
    columns = mine.shape[1]
    count = 2 * table.reach + 2
    out = jax.ShapeDtypeStruct((half, columns), f32)
    return pl.pallas_call(
        functools.partial(pick_kernel, table, half),
        in_specs=[smem(), whole(), whole()],
        out_specs=[whole()] * count,
        out_shape=[out] * count,
        compiler_params=params(10),
        cost_estimate=cost(0, 8 * count * half * columns),
        name="pick",
    )(tab, mine, theirs)


contract_parts = 2


def on_device(
    order,
    queries,
    latent_cache,
    new_latent,
    span_len,
    dec_count,
    span_start,
    cache_len,
    value_weight,
    out_weight,
    residual,
    norm_gain,
    gate_weight,
    up_weight,
    down_weight,
):
    ranks = len(order)
    reach = ranks // 2
    cores = lax.axis_size("head")
    rows_dev, width = residual.shape
    half = rows_dev // 2 // cores
    features = out_weight.shape[1]
    table = Table(ranks, cache_len.shape[1])

    forward = [(order[i], order[(i + 1) % ranks]) for i in range(ranks)]
    backward = [(b, a) for a, b in forward]
    exchange = [(c, cores - 1 - c) for c in range(cores)]

    def send_next(x):
        return lax.ppermute(x, "blk", forward)

    def send_prev(x):
        return lax.ppermute(x, "blk", backward)

    def swap(x):
        return lax.ppermute(x, "head", exchange)

    ids = jnp.stack([lax.axis_index("blk"), lax.axis_index("head")]).astype(i32)
    given = jnp.concatenate([ids, span_len, dec_count, span_start, cache_len[0]])
    caches = (queries, latent_cache, new_latent, value_weight)
    tab, *lead, decoded, busy, which, live = attend(table, order, given, *caches, 0, 2, None)

    def choose(special, usual, flag=busy):
        return jnp.where(jnp.broadcast_to(flag > 0, usual.shape), special, usual)


    packed = list(pack(tab, residual, ranks, cores))
    pieces = [None] * len(packed)

    def send_piece(k):
        pairs = [
            (i * cores + c, (i + k + len(packed) * c) % ranks * cores + c)
            for i in range(ranks)
            for c in range(cores)
            if k + c > 0
        ]
        pieces[k] = lax.ppermute(packed[k], ("blk", "head"), pairs)

    early = len(packed) // 2
    for k in range(early):
        send_piece(k)
    decoded, packed = lax.optimization_barrier((decoded, packed))
    packed = list(packed)
    follow = attend(table, order, tab, *caches, 1, 2, decoded)
    follow, pieces[:early], out_weight = lax.optimization_barrier(
        (follow, pieces[:early], out_weight)
    )

    total = None
    chains = []
    for head, main, extra in (lead, follow):
        chains.append((head, main, extra, [], []))
    for step in range(reach):
        for part, (head, main, extra, behind, ahead) in enumerate(chains):
            if step == 0:
                out_f, out_b = head, main
            elif step == 1:
                out_f, out_b = choose(main, behind[0]), choose(extra, ahead[0])
            else:
                out_f = choose(behind[step - 2], behind[step - 1])
                out_b = choose(ahead[step - 2], ahead[step - 1])
            piece = early + step - 1 + part * (len(packed) - early) // 2
            if 0 < step <= (len(packed) - early) // 2:
                out_f, out_b, packed[piece] = lax.optimization_barrier((out_f, out_b, packed[piece]))
                send_piece(piece)
            else:
                out_f, out_b = lax.optimization_barrier((out_f, out_b))
            behind.append(send_next(out_f))
            ahead.append(send_prev(out_b))
    gathered = [[main] + behind + ahead + [extra] for _, main, extra, behind, ahead in chains]
    shared = swap(share(tab, packed[0], pieces, cores))
    gathered[0], shared = lax.optimization_barrier((gathered[0], shared))
    for part in range(2):
        total = project(tab, table, gathered[part], total, out_weight, part, 2, cores)
    kept, other = total
    res_here = placed_rows(tab, packed[0], shared, pieces, cores)
    stream = (kept + swap(other).astype(f32) + res_here.astype(f32)).astype(bf16)

    gain = norm_gain.reshape(ranks, 1, features)
    weights = (gain, gate_weight, up_weight)
    cut = -(-stream.shape[0] // 32) * 16
    backs = [stream[:cut], stream[cut:]]
    fores = list(backs)
    swapped, backs[1], fores[1] = lax.optimization_barrier((swap(stream), backs[1], fores[1]))
    sums = expand(tab, [[stream]], [swapped], [RANK], *weights, None, False)
    blocks, owners = [stream], [RANK]
    done = None
    for step in range(1, reach + 1):
        if done is not None:
            backs[0], fores[0], done = lax.optimization_barrier((backs[0], fores[0], done))
        done = sums
        if step < reach:
            for n in range(2):
                back, fore = lax.optimization_barrier((backs[n], fores[n]))
                backs[n], fores[n] = send_next(back), send_prev(fore)
            arrived = [list(backs), list(fores)]
            from_owner = [table.owner_back + step, table.owner_fore + step]
        else:
            arrived = [[send_next(backs[0]), send_prev(fores[1])]]
            from_owner = [table.owner_back + step]
        others = []
        for chain in zip(*arrived):
            tied, sums = lax.optimization_barrier((chain, sums))
            others.append(swap(jnp.concatenate(tied, 0)))
        sums = expand(tab, arrived, others, from_owner, *weights, sums, step == reach)
        blocks += [jnp.concatenate(x, 0) for x in arrived]
        owners += from_owner
    (hidden,) = sums
    own = collect(tab, blocks, owners, half).astype(f32)

    parts = contract_parts
    theirs = [swap(contract(hidden, down_weight, part, parts, 1)) for part in range(parts)]
    mine = [contract(hidden, down_weight, part, parts, 0) for part in range(parts)]
    columns = width // parts
    lows, highs = [], []
    for part in range(parts):
        got_f, got_b = [], []
        *owned, main, extra = pick(tab, table, mine[part], theirs[part], half)
        for step in range(1, reach + 1):
            out_f, out_b = owned[2 * step - 2], owned[2 * step - 1]
            if step == 2:
                out_f = out_f + choose(jnp.zeros_like(out_f), got_f[0].astype(f32))
                out_b = out_b + choose(jnp.zeros_like(out_b), got_b[0].astype(f32))
            elif step > 2:
                out_f = out_f + choose(got_f[step - 3], got_f[step - 2]).astype(f32)
                out_b = out_b + choose(got_b[step - 3], got_b[step - 2]).astype(f32)
            out_f, out_b = lax.optimization_barrier((out_f.astype(bf16), out_b.astype(bf16)))
            got_f.append(send_next(out_f))
            got_b.append(send_prev(out_b))
        at = slice(part * columns, (part + 1) * columns)
        main = main + own[:half, at] + got_f[-1].astype(f32)
        main = (main + choose(got_b[-2], got_b[-1]).astype(f32)).astype(bf16)
        extra = extra + own[half:, at] + got_f[-2].astype(f32) + got_b[-1].astype(f32)
        extra = extra.astype(bf16)
        received = swap(choose(main, extra, which))
        stays = choose(extra, main, which)
        lows.append(choose(received, stays, which))
        highs.append(choose(stays, received, which))
    result = jnp.concatenate([jnp.concatenate(lows, 1), jnp.concatenate(highs, 1)], 0)
    row = which * (2 * half) + lax.broadcasted_iota(i32, result.shape, 0).astype(f32)
    return jnp.where(row < live, result, jnp.zeros_like(result))


def solution(mesh):
    placed = (
        P(("groups", "blk"), "head"),
        P(("groups", "blk"), None, None),
        P(None, ("groups", "blk")),
        P("groups"),
        P("groups"),
        P(("groups", "blk")),
        P(("groups", "blk"), None),
        P("head", None, None),
        P("head", "blk"),
        P(("groups", "blk"), None),
        P(),
        P(None, ("blk", "head")),
        P(None, ("blk", "head")),
        P(("blk", "head"), None),
    )
    order = ring_order(mesh)
    return jax.shard_map(
        lambda *args: on_device(order, *args),
        mesh=mesh,
        in_specs=placed,
        out_specs=P(("groups", "blk", "head"), None),
        check_vma=False,
    )
```

```python
import functools

import jax
import jax.numpy as jnp
from jax import lax
from jax.experimental import pallas as pl
from jax.experimental.pallas import tpu as pltpu
from jax.sharding import PartitionSpec as P

score_scale = 192.0 ** (-0.5)
norm_eps = 1e-06
masked_score = -1e30
f32, bf16, i32 = jnp.float32, jnp.bfloat16, jnp.int32
SMEM = pltpu.SMEM
MIB = 1 << 20

RANK, CORE, BUSY, BUSY_RANK, SPAN, DEC, LIVE, START, LENGTHS = range(9)


def mm(a, b):
    return lax.dot_general(a, b, (((1,), (0,)), ((), ())), preferred_element_type=f32)


def mm_nt(a, b):
    return lax.dot_general(a, b, (((1,), (1,)), ((), ())), preferred_element_type=f32)


def in_hbm(x):
    return pltpu.with_memory_space_constraint(x, pltpu.HBM)


def smem():
    return pl.BlockSpec(memory_space=SMEM)


def whole():
    return pl.BlockSpec(memory_space=pltpu.VMEM)


def params(mib=32):
    return pltpu.CompilerParams(vmem_limit_bytes=mib * MIB)


def cost(flops, moved, exps=0):
    return pl.CostEstimate(flops=int(flops), bytes_accessed=int(moved), transcendentals=int(exps))


def ring_order(mesh):
    count = mesh.shape["blk"]
    natural = list(range(count))
    snake = natural[0::2] + natural[1::2][::-1]
    names = list(mesh.axis_names)
    axes = [names.index("blk")] + [a for a, x in enumerate(names) if x != "blk"]
    lane = mesh.devices.transpose(axes)
    firsts = [lane[i].reshape(-1)[0] for i in natural]
    if not all(hasattr(d, "coords") for d in firsts):
        return snake

    def length(order):
        hops = zip(order, order[1:] + order[:1])
        return sum(
            sum(abs(u - v) for u, v in zip(firsts[a].coords, firsts[b].coords)) for a, b in hops
        )

    return natural if length(natural) <= length(snake) else snake


class Table:
    def __init__(self, ranks, slots):
        self.reach = ranks // 2
        self.source = LENGTHS + slots
        self.ahead = self.source + ranks + 1
        self.behind = self.ahead + self.reach + 1
        self.owner_back = self.behind + self.reach + 1
        self.owner_fore = self.owner_back + self.reach + 1
        self.who = self.owner_fore + self.reach + 1
        self.at = self.who + ranks
        self.size = self.at + ranks


def table_kernel(table, order, given, out):
    reach, ranks = table.reach, len(order)
    span = [given[2 + i] for i in range(ranks)]
    dec = [given[2 + ranks + i] for i in range(ranks)]
    lengths = 3 + 2 * ranks
    for i, r in enumerate(order):
        out[table.who + i] = r
        out[table.at + r] = i
    rank, core = given[0], given[1]
    most, busy_rank = span[0] + dec[0], jnp.int32(0)
    for i in range(1, ranks):
        here = span[i] + dec[i]
        busy_rank = jnp.where(here > most, i, busy_rank)
        most = jnp.maximum(here, most)
    busy = rank == busy_rank

    def wrap(x):
        x = jnp.where(x < 0, x + ranks, x)
        return jnp.where(x >= ranks, x - ranks, x)

    place, busy_place = out[table.at + rank], out[table.at + busy_rank]
    to_busy = wrap(busy_place - place)
    from_busy = wrap(place - busy_place)

    def node_ahead(k):
        far = (to_busy > 0) & (k > to_busy + 1)
        slot = out[table.who + wrap(place + k - jnp.where(far, 1, 0))]
        return jnp.where((to_busy > 0) & (k == to_busy + 1), ranks, slot)

    def node_behind(k):
        far = (from_busy > 0) & (k > from_busy)
        slot = out[table.who + wrap(place - k + jnp.where(far, 1, 0))]
        return jnp.where((from_busy > 0) & (k == from_busy), ranks, slot)

    out[RANK] = rank
    out[CORE] = core
    out[BUSY] = jnp.where(busy, 1, 0)
    out[BUSY_RANK] = busy_rank
    out[SPAN] = given[2 + rank]
    out[DEC] = given[2 + ranks + rank]
    out[LIVE] = given[2 + rank] + given[2 + ranks + rank]
    out[START] = given[lengths - 1]
    for j in range(given.shape[0] - lengths):
        out[LENGTHS + j] = given[lengths + j]
    out[table.source + rank] = 0
    for k in range(1, reach + 1):
        out[table.ahead + k] = node_ahead(k)
        out[table.behind + k] = node_behind(k)
        out[table.owner_back + k] = out[table.who + wrap(place - k)]
        out[table.owner_fore + k] = out[table.who + wrap(place + k)]
        out[table.source + node_behind(k)] = k
        last = jnp.where(busy, ranks, node_ahead(k)) if k == reach else node_ahead(k)
        out[table.source + last] = reach + k


def attend_kernel(
    table, order, heads, first, count, group, rows, lat, value, lead, *refs
):
    if lead:
        given, refs = refs[0], refs[1:]
        q_hbm, cache_hbm, fresh_hbm, vw_hbm, tab, head, main, extra, later = refs[:9]
        flags, refs = refs[9:12], refs[12:]
        q, keys, vw, latent, fz, fresh, q_sem, key_sem, vw_sem, dq = refs
        loaded, base = heads, 0
    else:
        tab, q_hbm, cache_hbm, fresh_hbm, vw_hbm, decoded_here, head, main, extra = refs[:9]
        q, keys, vw, latent, fz, fresh, q_sem, key_sem, vw_sem = refs[9:]
        loaded, base = count, first
    cached, wide = keys.shape[2], keys.shape[1]
    slots = cache_hbm.shape[0] - 1
    odd_slot = keys.shape[0] - 1
    shift, pair, dr = wide - lat, 2 * lat, 8
    groups, pairs = count // group, group // 2
    loads = loaded // group

    def q_copy(g):
        source = pl.ds((base + g * group) * lat, group * lat)
        return pltpu.make_async_copy(
            q_hbm.at[:, source], q.at[:, pl.ds(g * group * lat, group * lat)], q_sem.at[g]
        )

    def vw_copy(g):
        source = pl.ds(first + g * group, group)
        return pltpu.make_async_copy(vw_hbm.at[source], vw.at[pl.ds(g * group, group)], vw_sem.at[g])

    even_copy = pltpu.make_async_copy(cache_hbm.at[0], keys.at[0, pl.ds(0, lat)], key_sem.at[0])
    odd_copy = pltpu.make_async_copy(
        cache_hbm.at[0], keys.at[odd_slot, pl.ds(shift, lat)], key_sem.at[1]
    )
    waiting = [q_copy(g) for g in range(1, loads)]
    if lead:
        rest_copy = pltpu.make_async_copy(
            cache_hbm.at[pl.ds(1, slots)], keys.at[pl.ds(1, slots), pl.ds(0, lat)], key_sem.at[2]
        )
        waiting.append(rest_copy)
    waiting += [vw_copy(g) for g in range(groups)]

    def start_next(number):
        for _ in range(min(number, len(waiting))):
            waiting.pop(0).start()

    fresh_copy = pltpu.make_async_copy(fresh_hbm, fresh, key_sem.at[3])
    fresh_copy.start()
    even_copy.start()
    q_copy(0).start()
    odd_copy.start()
    start_next(1)
    if lead:
        table_kernel(table, order, given, tab)
    span, decs = tab[SPAN], tab[DEC]

    def onehot(shape, row_dim, slot_dim):
        r = lax.broadcasted_iota(i32, shape, row_dim)
        j = lax.broadcasted_iota(i32, shape, slot_dim)
        return jnp.where((r == span + j) & (j < decs), 1.0, 0.0).astype(bf16)

    tail = jnp.zeros((shift, cached), bf16)
    for s in range(odd_slot):
        keys[s, lat:] = tail
    keys[odd_slot, :shift] = tail
    fz[...] = jnp.zeros_like(fz)
    fresh_copy.wait()
    fz[:rows, :lat] = fresh[...].astype(f32)
    fresh_even = fz[...].astype(bf16)
    fresh_odd = pltpu.roll(fz[...], shift, 1).astype(bf16)

    m = pairs * rows
    cols = cached + fz.shape[0]
    row = lax.broadcasted_iota(i32, (m, 1), 0) % rows
    col = lax.broadcasted_iota(i32, (m, cols), 1)
    seen = col < jnp.where(col < cached, tab[START], cached + 1 + row)

    def span_latent(lhs, slot, fresh_keys):
        s = jnp.concatenate([mm(lhs, keys[slot]), mm_nt(lhs, fresh_keys)], 1)
        s = jnp.where(seen, s * score_scale, masked_score)
        e = jnp.exp(s - jnp.max(s, axis=1, keepdims=True))
        w = (e * (1.0 / jnp.sum(e, axis=1, keepdims=True))).astype(bf16)
        o = mm_nt(w[:, :cached], keys[0, :value]) + mm(w[:, cached:], fresh_even[:, :value])
        return jnp.where(row < span, o, 0.0).astype(bf16)

    even_copy.wait()
    odd_copy.wait()
    for g in range(groups):
        q_copy(g).wait()
        start_next(2)
        start = g * group * lat
        for odd in range(2):
            off = start + odd * (pair - wide)
            lhs = jnp.concatenate(
                [q[:, off + pair * p : off + pair * p + wide] for p in range(pairs)], 0
            )
            latent[g, odd] = span_latent(lhs, odd_slot * odd, fresh_odd if odd else fresh_even)
    start_next(len(waiting))

    if lead:
        for g in range(groups, loads):
            q_copy(g).wait()
        pick = onehot((16, rows), 1, 0)
        for p in range(heads // 2):
            got = mm(pick, q[:, pair * p : pair * (p + 1)])[:dr]
            dq[2 * p * dr : (2 * p + 1) * dr] = got[:, :wide]
            dq[(2 * p + 1) * dr : (2 * p + 2) * dr] = pltpu.roll(
                got[:, pair - wide :], wide - shift, 1
            )
        n = heads * dr
        queries = dq[...].astype(bf16)
        slot = lax.broadcasted_iota(i32, (n, 1), 0) % dr
        rest_copy.wait()
        length = jnp.zeros((n, 1), i32)
        scores = jnp.zeros((n, cached), f32)
        for s in range(slots):
            scores = jnp.where(slot == s, mm(queries, keys[s + 1]), scores)
            length = jnp.where(slot == s, tab[LENGTHS + s], length)
        unmasked = lax.broadcasted_iota(i32, (n, cached), 1) < length
        scores = jnp.where(unmasked, scores * score_scale, masked_score)
        own = mm_nt(queries, fresh_even)
        column = lax.broadcasted_iota(i32, own.shape, 1)
        own = jnp.sum(jnp.where(column == span + slot, own, 0.0), axis=1, keepdims=True)
        own = own * score_scale
        peak = jnp.maximum(jnp.max(scores, axis=1, keepdims=True), own)
        e = jnp.exp(scores - peak)
        e_own = jnp.exp(own - peak)
        total = jnp.sum(e, axis=1, keepdims=True) + e_own
        w = e / total
        acc = jnp.zeros((n, value), f32)
        for s in range(slots):
            acc = acc + mm_nt(jnp.where(slot == s, w, 0.0).astype(bf16), keys[s + 1, :value])
        own_value = mm(pick, fresh[:, :value])[:dr]
        own_value = jnp.broadcast_to(own_value[None], (heads, dr, value)).reshape(n, value)
        dec = (acc + (e_own / total).astype(bf16).astype(f32) * own_value).astype(bf16)
        later[...] = dec[count * dr :]
        for flag, at in zip(flags, (BUSY, CORE, LIVE)):
            flag[...] = jnp.full(flag.shape, tab[at].astype(f32))
        dec = dec[: count * dr]
    else:
        dec = decoded_here[...]

    place = onehot((rows, 16), 0, 1)
    vh = vw.shape[2]
    block = rows // 2
    for g in range(groups):
        vw_copy(g).wait()
        values, decoded = [], []
        for p in range(pairs):
            h = g * group + 2 * p
            lhs = jnp.concatenate(
                [
                    latent[g, 0, p * rows : (p + 1) * rows],
                    latent[g, 1, p * rows : (p + 1) * rows],
                    dec[h * dr : (h + 2) * dr],
                ],
                0,
            )
            r = mm(lhs, jnp.concatenate([vw[h], vw[h + 1]], 1))
            values += [r[:rows, :vh], r[rows : 2 * rows, vh:]]
            decoded += [r[2 * rows : 2 * rows + dr, :vh], r[2 * rows + dr :, vh:]]
        decoded = jnp.concatenate(decoded, 1)
        decoded = jnp.concatenate([decoded, jnp.zeros_like(decoded)], 0).astype(bf16)
        out = (jnp.concatenate(values, 1) + mm(place, decoded)).astype(bf16)
        at = slice(g * group * vh, (g + 1) * group * vh)
        main[:, at] = out[:block]
        extra[:, at] = out[block:]
        head[:, at] = jnp.where(tab[BUSY] == 1, out[block:], out[:block])


def attend(table, order, numbers, queries, cache, fresh, vw, part, parts, decoded):
    rows, heads = queries.shape[0], vw.shape[0]
    lat = queries.shape[1] // heads
    slots, _, cached = cache.shape
    value, vh = vw.shape[1:]
    count = heads // parts
    group = min(8, count)
    lead = decoded is None
    loaded = heads if lead else count
    wide = -(-lat // 128) * 128
    half = jax.ShapeDtypeStruct((rows // 2, count * vh), bf16)
    hbm = pl.BlockSpec(memory_space=pltpu.HBM)
    scratch = [
        pltpu.VMEM((rows, loaded * lat), bf16),
        pltpu.VMEM((slots + 1 if lead else 2, wide, cached), bf16),
        pltpu.VMEM((count, value, vh), bf16),
        pltpu.VMEM((count // group, 2, group // 2 * rows, value), bf16),
        pltpu.VMEM((-(-rows // 128) * 128, wide), f32),
        pltpu.VMEM(fresh.shape[::-1], bf16),
        pltpu.SemaphoreType.DMA((loaded // group,)),
        pltpu.SemaphoreType.DMA((4,)),
        pltpu.SemaphoreType.DMA((count // group,)),
    ]
    out_shape, out_specs = [half] * 3, [whole()] * 3
    ins = [smem()] + [hbm] * 4
    args = [numbers, in_hbm(queries), in_hbm(cache), in_hbm(fresh.T), in_hbm(vw)]
    if lead:
        scratch.append(pltpu.VMEM((heads * 8, wide), f32))
        out_shape = [jax.ShapeDtypeStruct((table.size,), i32)] + out_shape
        out_shape += [jax.ShapeDtypeStruct(((heads - count) * 8, value), bf16)]
        out_shape += [jax.ShapeDtypeStruct((1, 1), f32)] * 3
        out_specs = [smem()] + out_specs + [whole()] * 4
    else:
        ins.append(whole())
        args.append(decoded)
    return pl.pallas_call(
        functools.partial(
            attend_kernel, table, order, heads, part * count, count, group, rows, lat, value, lead
        ),
        in_specs=ins,
        out_specs=out_specs,
        out_shape=out_shape,
        scratch_shapes=scratch,
        compiler_params=params(24),
        cost_estimate=cost(
            2 * rows * count * (cached + rows) * (lat + value),
            2 * (queries.size + cache.size + vw.size) // parts,
            rows * count * (cached + rows),
        ),
        name="attend",
    )(*args)


def pack_kernel(ranks, cores, features, tab, res, *outs):
    for k in range(ranks // cores):
        target = tab[RANK] + k + (ranks // cores) * tab[CORE]
        target = jnp.where(target >= ranks, target - ranks, target)

        def put(columns, k=k):
            outs[k][...] = res[:, columns]

        if features % 128 == 0:
            put(pl.ds(pl.multiple_of(target * features, 128), features))
        else:
            for t in range(ranks):
                pl.when(target == t)(functools.partial(put, slice(t * features, (t + 1) * features)))


def pack(tab, residual, ranks, cores):
    rows, width = residual.shape
    features = width // ranks
    count = ranks // cores
    return pl.pallas_call(
        functools.partial(pack_kernel, ranks, cores, features),
        in_specs=[smem(), whole()],
        out_specs=[whole()] * count,
        out_shape=[jax.ShapeDtypeStruct((rows, features), bf16)] * count,
        compiler_params=params(8),
        cost_estimate=cost(0, 4 * residual.size),
        name="pack",
    )(tab, residual)


def share_kernel(half, tab, own, *refs):
    pieces, out = refs[:-1], refs[-1]
    other = 1 - tab[CORE]
    block = own.shape[0] // 2
    low = pl.multiple_of(other * half, half)
    high = pl.multiple_of(block + other * half, half)

    def put(k, piece):
        out[2 * k * half : (2 * k + 1) * half] = piece[pl.ds(low, half)]
        out[(2 * k + 1) * half : (2 * k + 2) * half] = piece[pl.ds(high, half)]

    for k, piece in enumerate(pieces):
        if k > 0:
            put(k, piece)
        else:
            pl.when(tab[CORE] == 0)(functools.partial(put, k, own))
            pl.when(tab[CORE] != 0)(functools.partial(put, k, piece))


def share(tab, own, pieces, cores):
    rows, features = own.shape
    half = rows // 2 // cores
    return pl.pallas_call(
        functools.partial(share_kernel, half),
        in_specs=[smem()] + [whole()] * (1 + len(pieces)),
        out_specs=whole(),
        out_shape=jax.ShapeDtypeStruct((2 * half * len(pieces), features), bf16),
        compiler_params=params(8),
        cost_estimate=cost(0, 4 * own.size * len(pieces)),
        name="share",
    )(tab, own, *pieces)


def project_kernel(source, nodes, block, half, part, first, tab, *refs):
    blocks, refs = refs[: nodes + 1], refs[nodes + 1 :]
    before = None if first else refs[0]
    weight, kept, given, acc = refs[-4:]
    step = pl.program_id(0)
    depth = blocks[0].shape[1] // pl.num_programs(0)
    columns = pl.ds(pl.multiple_of(step * depth, 128), depth)
    last = jnp.where(tab[BUSY] == 1, blocks[nodes][:, columns], blocks[nodes - 1][:, columns])
    lhs = jnp.concatenate([b[:, columns] for b in blocks[: nodes - 1]] + [last], 0)
    got = mm(lhs, weight[pl.ds(pl.multiple_of(part * blocks[0].shape[1] + step * depth, 128), depth)])

    @pl.when(step == 0)
    def _():
        acc[...] = got if first else got + before[...]

    @pl.when(step > 0)
    def _():
        acc[...] += got

    @pl.when(step == pl.num_programs(0) - 1)
    def _():
        core = tab[CORE]
        for k in range(nodes):
            at = tab[source + k] * block
            kept[k * half : (k + 1) * half] = acc[pl.ds(pl.multiple_of(at + core * half, half), half)]
            other = acc[pl.ds(pl.multiple_of(at + (1 - core) * half, half), half)]
            given[k * half : (k + 1) * half] = other.astype(bf16)


def project_part_kernel(nodes, part, first, tab, *refs):
    blocks, refs = refs[: nodes + 1], refs[nodes + 1 :]
    weight, out = refs[-2:]
    step = pl.program_id(0)
    depth = blocks[0].shape[1] // pl.num_programs(0)
    columns = pl.ds(pl.multiple_of(step * depth, 128), depth)
    last = jnp.where(tab[BUSY] == 1, blocks[nodes][:, columns], blocks[nodes - 1][:, columns])
    lhs = jnp.concatenate([b[:, columns] for b in blocks[: nodes - 1]] + [last], 0)
    got = mm(lhs, weight[pl.ds(pl.multiple_of(part * blocks[0].shape[1] + step * depth, 128), depth)])

    @pl.when(step == 0)
    def _():
        out[...] = got if first else got + refs[0][...]

    @pl.when(step > 0)
    def _():
        out[...] += got


def project(tab, table, blocks, before, weight, part, parts, cores):
    block, width = blocks[0].shape
    nodes = len(blocks) - 1
    half = block // cores
    features = weight.shape[1]
    depth = width
    steps = width // depth
    total = jax.ShapeDtypeStruct((nodes * block, features), f32)
    final = part == parts - 1
    first = before is None
    ins = [smem()] + [whole()] * (nodes + 2 + (not first))
    args = [tab, *blocks] + ([] if first else [before]) + [weight]
    estimate = cost(
        2 * nodes * block * width * features, 2 * (nodes * block * width + width * features)
    )
    if not final:
        return pl.pallas_call(
            functools.partial(project_part_kernel, nodes, part, first),
            grid=(steps,),
            in_specs=ins,
            out_specs=pl.BlockSpec(total.shape, lambda i: (0, 0)),
            out_shape=total,
            compiler_params=params(16),
            cost_estimate=estimate,
            name="project",
        )(*args)
    return pl.pallas_call(
        functools.partial(project_kernel, table.source, nodes, block, half, part, first),
        grid=(steps,),
        in_specs=ins,
        out_specs=[pl.BlockSpec((nodes * half, features), lambda i: (0, 0))] * 2,
        out_shape=[
            jax.ShapeDtypeStruct((nodes * half, features), f32),
            jax.ShapeDtypeStruct((nodes * half, features), bf16),
        ],
        scratch_shapes=[pltpu.VMEM(total.shape, f32)],
        compiler_params=params(16),
        cost_estimate=estimate,
        name="project",
    )(*args)


def place_kernel(ranks, half, tab, own, shared, *refs):
    pieces, out = refs[:-1], refs[-1]
    rank, core, busy_rank = tab[RANK], tab[CORE], tab[BUSY_RANK]
    count = len(pieces)
    block = own.shape[0] // 2

    def put(slot, extra):
        out[pl.ds(pl.multiple_of(slot * half, half), half)] = extra

    def put_both(owner, main, extra):
        put(owner, main())

        @pl.when(owner == busy_rank)
        def _():
            put(ranks, extra())

    def owner_of(k, c):
        owner = rank - k - count * c
        return jnp.where(owner < 0, owner + ranks, owner)

    low = pl.ds(pl.multiple_of(core * half, half), half)
    high = pl.ds(pl.multiple_of(block + core * half, half), half)
    for k, piece in enumerate(pieces):

        def received(piece=piece, k=k):
            put_both(owner_of(k, core), lambda: piece[low], lambda: piece[high])

        if k > 0:
            received()
        else:
            pl.when(core == 0)(functools.partial(received, own))
            pl.when(core != 0)(received)
        at = 2 * k * half
        put_both(
            owner_of(k, 1 - core),
            lambda at=at: shared[at : at + half],
            lambda at=at: shared[at + half : at + 2 * half],
        )


def placed_rows(tab, own, shared, pieces, cores):
    rows, features = own.shape
    half = rows // 2 // cores
    ranks = cores * len(pieces)
    return pl.pallas_call(
        functools.partial(place_kernel, ranks, half),
        in_specs=[smem()] + [whole()] * (2 + len(pieces)),
        out_specs=whole(),
        out_shape=jax.ShapeDtypeStruct(((ranks + 1) * half, features), bf16),
        compiler_params=params(8),
        cost_estimate=cost(0, 4 * (ranks + 1) * half * features),
        name="place",
    )(tab, own, shared, *pieces)


def expand_kernel(pieces, others, first, turned, owners, tab, *refs):
    count = len(pieces)
    blocks = []
    for number in pieces:
        blocks.append(refs[:number])
        refs = refs[number:]
    theirs, refs = refs[:others], refs[others:]
    gain, gate, up = refs[:3]
    refs = refs[3:]
    if not first:
        before, refs = refs[:3], refs[3:]
    gates, ups, squares = refs
    step = pl.program_id(0)
    for i in range(count):

        @pl.when(step == i)
        def _(i=i):
            both = [x[...] for x in blocks[i]]
            for x in theirs:
                rows = x.shape[0] // count
                both.append(x[i * rows : (i + 1) * rows])
            both = jnp.concatenate(both, 0).astype(f32)
            rows_of = both.shape[1]
            scaled = (both * gain[0]).astype(bf16)
            if turned:
                at = pl.ds(pl.multiple_of(tab[owners[i]] * rows_of, 128), rows_of)
                products = mm_nt(scaled, gate[:, at]), mm_nt(scaled, up[:, at])
            else:
                products = mm(scaled, gate[...]), mm(scaled, up[...])
            values = (
                *products,
                jnp.sum(both * both, axis=1, keepdims=True),
            )
            for n, (ref, value) in enumerate(zip((gates, ups, squares), values)):
                if i == 0:
                    ref[...] = value if first else value + before[n][...]
                else:
                    ref[...] += value


def last_kernel(count, width, turned, owner, tab, *refs):
    block = jnp.concatenate([x[...] for x in refs[:count]], 0).astype(f32)
    gain, gate, up, gates, ups, squares, hidden = refs[count:]
    features = block.shape[1]
    scaled = (block * gain[0]).astype(bf16)
    if turned:
        at = pl.ds(pl.multiple_of(tab[owner] * features, 128), features)
        g, u = mm_nt(scaled, gate[:, at]), mm_nt(scaled, up[:, at])
    else:
        g, u = mm(scaled, gate[...]), mm(scaled, up[...])
    total = squares[...] + jnp.sum(block * block, axis=1, keepdims=True)
    scale = lax.rsqrt(total / width + norm_eps)
    g = (g + gates[...]) * scale
    hidden[...] = (g / (1.0 + jnp.exp(-g)) * ((u + ups[...]) * scale)).astype(bf16)


def expand_last(tab, pieces, owner, gain, gate, up, before, which):
    rows, features = sum(x.shape[0] for x in pieces), pieces[0].shape[1]
    units, width = gate.shape[1], gate.shape[0]
    turned = features % 128 == 0

    def full(shape):
        return pl.BlockSpec(shape, lambda i, tab: (0,) * len(shape))

    def half(columns):
        return pl.BlockSpec((rows, columns), lambda i, tab: (which, 0))

    if turned:
        gate, up = gate.T, up.T
        weights = [pl.BlockSpec(memory_space=pltpu.VMEM)] * 2
    else:
        weights = [pl.BlockSpec((features, units), lambda i, tab: (tab[owner], 0))] * 2
    return pl.pallas_call(
        functools.partial(last_kernel, len(pieces), width, turned, owner),
        grid_spec=pltpu.PrefetchScalarGridSpec(
            num_scalar_prefetch=1,
            grid=(1,),
            in_specs=[full(x.shape) for x in pieces]
            + [pl.BlockSpec((1, 1, features), lambda i, tab: (tab[owner], 0, 0))]
            + weights
            + [half(units), half(units), half(1)],
            out_specs=full((rows, units)),
        ),
        out_shape=jax.ShapeDtypeStruct((rows, units), bf16),
        compiler_params=params(20),
        cost_estimate=cost(4 * rows * features * units, 4 * features * units),
        name="last",
    )(tab, *pieces, gain, gate, up, *before)


def expand(tab, mines, theirs, owners, gain, gate, up, before):
    count = len(mines)
    pieces = tuple(len(x) for x in mines)
    rows, features = sum(x.shape[0] for x in mines[0]), mines[0][0].shape[1]
    arrays = [x for own in mines for x in own] + theirs
    units = gate.shape[1]
    first = before is None

    def owner(i, tab):
        index = tab[owners[0]]
        for n in range(1, count):
            index = jnp.where(i == n, tab[owners[n]], index)
        return index

    def full(shape):
        return pl.BlockSpec(shape, lambda i, tab: (0,) * len(shape))

    sums = [(2 * rows, units), (2 * rows, units), (2 * rows, 1)]
    ins = [full(x.shape) for x in arrays]
    ins += [pl.BlockSpec((1, 1, features), lambda i, tab: (owner(i, tab), 0, 0))]
    turned = features % 128 == 0
    if turned:
        gate, up = gate.T, up.T
        ins += [pl.BlockSpec(memory_space=pltpu.VMEM)] * 2
    else:
        ins += [pl.BlockSpec((features, units), lambda i, tab: (owner(i, tab), 0))] * 2
    if not first:
        ins += [full(s) for s in sums]
    shapes = [jax.ShapeDtypeStruct(s, f32) for s in sums]
    return pl.pallas_call(
        functools.partial(expand_kernel, pieces, len(theirs), first, turned, owners),
        grid_spec=pltpu.PrefetchScalarGridSpec(
            num_scalar_prefetch=1,
            grid=(count,),
            in_specs=ins,
            out_specs=[full(s) for s in sums],
        ),
        out_shape=shapes,
        compiler_params=params(20),
        cost_estimate=cost(1, 1),
        name="expand",
    )(tab, *arrays, gain, gate, up, *([] if first else before))


def collect_kernel(owners, tab, *refs):
    out = refs[-1]
    if len(out.shape) == 2:
        half, features = out.shape[0] // 2, out.shape[1] // len(owners)
        for i, at in enumerate(owners):
            columns = pl.ds(pl.multiple_of(tab[at] * features, 128), features)
            out[:half, columns] = refs[2 * i][...]
            out[half:, columns] = refs[2 * i + 1][...]
        return
    half = out.shape[1] // 2
    for i, at in enumerate(owners):
        out[tab[at], :half] = refs[2 * i][...]
        out[tab[at], half:] = refs[2 * i + 1][...]


def collect(tab, blocks, owners, half):
    ranks = len(blocks)
    features = blocks[0].shape[1]
    ins, args = [], []
    for x in blocks:
        ins += [
            pl.BlockSpec((half, features), lambda i, tab: (tab[RANK], 0)),
            pl.BlockSpec((half, features), lambda i, tab: (ranks, 0)),
        ]
        args += [x, x]
    aligned = features % 128 == 0
    shape = (2 * half, ranks * features) if aligned else (ranks, 2 * half, features)
    out = pl.pallas_call(
        functools.partial(collect_kernel, owners),
        grid_spec=pltpu.PrefetchScalarGridSpec(
            num_scalar_prefetch=1,
            grid=(1,),
            in_specs=ins,
            out_specs=pl.BlockSpec(shape, lambda i, tab: (0,) * len(shape)),
        ),
        out_shape=jax.ShapeDtypeStruct(shape, bf16),
        compiler_params=params(10),
        cost_estimate=cost(0, 8 * ranks * half * features),
        name="collect",
    )(tab, *args)
    return out if aligned else out.transpose(1, 0, 2).reshape(2 * half, ranks * features)


def contract_kernel(begin, hidden, weight, out):
    wide = out.shape[1]
    at = pl.ds(pl.multiple_of(begin + pl.program_id(0) * wide, 128), wide)
    out[...] = mm(hidden[...], weight[:, at]).astype(bf16)


def contract(hidden, weight, part, parts):
    rows, units = hidden.shape
    columns = weight.shape[1] // parts
    wide = columns // 2 if columns % 256 == 0 else columns
    return pl.pallas_call(
        functools.partial(contract_kernel, part * columns),
        grid=(columns // wide,),
        in_specs=[pl.BlockSpec((rows, units), lambda i: (0, 0)), whole()],
        out_specs=pl.BlockSpec((rows, wide), lambda i: (0, i)),
        out_shape=jax.ShapeDtypeStruct((rows, columns), bf16),
        compiler_params=params(16),
        cost_estimate=cost(2 * rows * units * columns, 2 * (units + rows) * columns),
        name="contract",
    )(hidden, weight)


def pick_kernel(table, half, tab, mine, theirs, *outs):
    busy = tab[BUSY] == 1
    reach = table.reach
    for step in range(1, reach + 1):
        for n, where in enumerate((table.ahead, table.behind)):
            at = pl.multiple_of(tab[where + reach + 1 - step] * half, half)
            total = mine[pl.ds(at, half)].astype(f32) + theirs[pl.ds(at, half)].astype(f32)
            if step == 1 and n == 0:
                total = jnp.where(busy, 0.0, total)
            outs[2 * (step - 1) + n][...] = total
    for n, slot in enumerate((tab[RANK], 2 * reach)):
        at = pl.multiple_of(slot * half, half)
        outs[2 * reach + n][...] = mine[pl.ds(at, half)].astype(f32) + theirs[pl.ds(at, half)].astype(f32)


def pick(tab, table, mine, theirs, half):
    columns = mine.shape[1]
    count = 2 * table.reach + 2
    out = jax.ShapeDtypeStruct((half, columns), f32)
    return pl.pallas_call(
        functools.partial(pick_kernel, table, half),
        in_specs=[smem(), whole(), whole()],
        out_specs=[whole()] * count,
        out_shape=[out] * count,
        compiler_params=params(10),
        cost_estimate=cost(0, 8 * count * half * columns),
        name="pick",
    )(tab, mine, theirs)


contract_parts = 2


def on_device(
    order,
    queries,
    latent_cache,
    new_latent,
    span_len,
    dec_count,
    span_start,
    cache_len,
    value_weight,
    out_weight,
    residual,
    norm_gain,
    gate_weight,
    up_weight,
    down_weight,
):
    ranks = len(order)
    reach = ranks // 2
    cores = lax.axis_size("head")
    rows_dev, width = residual.shape
    half = rows_dev // 2 // cores
    features = out_weight.shape[1]
    table = Table(ranks, cache_len.shape[1])

    forward = [(order[i], order[(i + 1) % ranks]) for i in range(ranks)]
    backward = [(b, a) for a, b in forward]
    exchange = [(c, cores - 1 - c) for c in range(cores)]

    def send_next(x):
        return lax.ppermute(x, "blk", forward)

    def send_prev(x):
        return lax.ppermute(x, "blk", backward)

    def swap(x):
        return lax.ppermute(x, "head", exchange)

    ids = jnp.stack([lax.axis_index("blk"), lax.axis_index("head")]).astype(i32)
    given = jnp.concatenate([ids, span_len, dec_count, span_start, cache_len[0]])
    caches = (queries, latent_cache, new_latent, value_weight)
    tab, *lead, decoded, busy, which, live = attend(table, order, given, *caches, 0, 2, None)

    def choose(special, usual, flag=busy):
        return jnp.where(jnp.broadcast_to(flag > 0, usual.shape), special, usual)


    packed = list(pack(tab, residual, ranks, cores))
    pieces = [None] * len(packed)

    def send_piece(k):
        pairs = [
            (i * cores + c, (i + k + len(packed) * c) % ranks * cores + c)
            for i in range(ranks)
            for c in range(cores)
            if k + c > 0
        ]
        pieces[k] = lax.ppermute(packed[k], ("blk", "head"), pairs)

    early = len(packed) // 2
    for k in range(early):
        send_piece(k)
    decoded, packed = lax.optimization_barrier((decoded, packed))
    packed = list(packed)
    follow = attend(table, order, tab, *caches, 1, 2, decoded)
    follow, pieces[:early], out_weight = lax.optimization_barrier(
        (follow, pieces[:early], out_weight)
    )

    total = None
    chains = []
    for head, main, extra in (lead, follow):
        chains.append((head, main, extra, [], []))
    for step in range(reach):
        for part, (head, main, extra, behind, ahead) in enumerate(chains):
            if step == 0:
                out_f, out_b = head, main
            elif step == 1:
                out_f, out_b = choose(main, behind[0]), choose(extra, ahead[0])
            else:
                out_f = choose(behind[step - 2], behind[step - 1])
                out_b = choose(ahead[step - 2], ahead[step - 1])
            piece = early + step - 1 + part * (len(packed) - early) // 2
            if 0 < step <= (len(packed) - early) // 2:
                out_f, out_b, packed[piece] = lax.optimization_barrier((out_f, out_b, packed[piece]))
                send_piece(piece)
            else:
                out_f, out_b = lax.optimization_barrier((out_f, out_b))
            behind.append(send_next(out_f))
            ahead.append(send_prev(out_b))
    gathered = [[main] + behind + ahead + [extra] for _, main, extra, behind, ahead in chains]
    chains[0][3][-1], pieces = lax.optimization_barrier((chains[0][3][-1], pieces))
    gathered[0][reach] = chains[0][3][-1]
    shared = swap(share(tab, packed[0], pieces, cores))
    gathered[0], shared = lax.optimization_barrier((gathered[0], shared))
    for part in range(2):
        total = project(tab, table, gathered[part], total, out_weight, part, 2, cores)
    kept, other = total
    res_here = placed_rows(tab, packed[0], shared, pieces, cores)
    stream = (kept + swap(other).astype(f32) + res_here.astype(f32)).astype(bf16)

    gain = norm_gain.reshape(ranks, 1, features)
    weights = (gain, gate_weight, up_weight)
    cut = -(-stream.shape[0] // 32) * 16
    back, fore = stream, stream
    sums = expand(tab, [[stream]], [swap(stream)], [RANK], *weights, None)
    blocks, owners = [stream], [RANK]
    done = None
    for step in range(1, reach):
        if done is not None:
            back, fore, done = lax.optimization_barrier((back, fore, done))
        done = sums
        back, fore = send_next(back), send_prev(fore)
        from_owner = [table.owner_back + step, table.owner_fore + step]
        tied, sums = lax.optimization_barrier(((back, fore), sums))
        others = swap(jnp.concatenate(tied, 0))
        sums = expand(tab, [[back], [fore]], [others], from_owner, *weights, sums)
        blocks += [back, fore]
        owners += from_owner
    back, fore, done = lax.optimization_barrier((back, fore, done))
    last = [send_next(back[:cut]), send_prev(fore[cut:])]
    owner = table.owner_back + reach
    tied, sums = lax.optimization_barrier((last, sums))
    others = [swap(x) for x in tied]
    hidden = [expand_last(tab, x, owner, *weights, sums, n) for n, x in enumerate((last, others))]
    blocks.append(jnp.concatenate(last, 0))
    owners.append(owner)
    own = collect(tab, blocks, owners, half).astype(f32)

    parts = contract_parts
    theirs = [swap(contract(hidden[1], down_weight, part, parts)) for part in range(parts)]
    mine = [contract(hidden[0], down_weight, part, parts) for part in range(parts)]
    columns = width // parts
    lows, highs = [], []
    for part in range(parts):
        got_f, got_b = [], []
        *owned, main, extra = pick(tab, table, mine[part], theirs[part], half)
        for step in range(1, reach + 1):
            out_f, out_b = owned[2 * step - 2], owned[2 * step - 1]
            if step == 2:
                out_f = out_f + choose(jnp.zeros_like(out_f), got_f[0].astype(f32))
                out_b = out_b + choose(jnp.zeros_like(out_b), got_b[0].astype(f32))
            elif step > 2:
                out_f = out_f + choose(got_f[step - 3], got_f[step - 2]).astype(f32)
                out_b = out_b + choose(got_b[step - 3], got_b[step - 2]).astype(f32)
            out_f, out_b = lax.optimization_barrier((out_f.astype(bf16), out_b.astype(bf16)))
            got_f.append(send_next(out_f))
            got_b.append(send_prev(out_b))
        at = slice(part * columns, (part + 1) * columns)
        main = main + own[:half, at] + got_f[-1].astype(f32)
        main = (main + choose(got_b[-2], got_b[-1]).astype(f32)).astype(bf16)
        extra = extra + own[half:, at] + got_f[-2].astype(f32) + got_b[-1].astype(f32)
        extra = extra.astype(bf16)
        received = swap(choose(main, extra, which))
        stays = choose(extra, main, which)
        lows.append(choose(received, stays, which))
        highs.append(choose(stays, received, which))
    result = jnp.concatenate([jnp.concatenate(lows, 1), jnp.concatenate(highs, 1)], 0)
    row = which * (2 * half) + lax.broadcasted_iota(i32, result.shape, 0).astype(f32)
    return jnp.where(row < live, result, jnp.zeros_like(result))


def solution(mesh):
    placed = (
        P(("groups", "blk"), "head"),
        P(("groups", "blk"), None, None),
        P(None, ("groups", "blk")),
        P("groups"),
        P("groups"),
        P(("groups", "blk")),
        P(("groups", "blk"), None),
        P("head", None, None),
        P("head", "blk"),
        P(("groups", "blk"), None),
        P(),
        P(None, ("blk", "head")),
        P(None, ("blk", "head")),
        P(("blk", "head"), None),
    )
    order = ring_order(mesh)
    return jax.shard_map(
        lambda *args: on_device(order, *args),
        mesh=mesh,
        in_specs=placed,
        out_specs=P(("groups", "blk", "head"), None),
        check_vma=False,
    )
```

```python
import functools

import jax
import jax.numpy as jnp
from jax import lax
from jax.experimental import pallas as pl
from jax.experimental.pallas import tpu as pltpu
from jax.sharding import PartitionSpec as P

score_scale = 192.0 ** (-0.5)
norm_eps = 1e-06
masked_score = -1e30
f32, bf16, i32 = jnp.float32, jnp.bfloat16, jnp.int32
SMEM = pltpu.SMEM
MIB = 1 << 20

RANK, CORE, BUSY, BUSY_RANK, SPAN, DEC, LIVE, START, LENGTHS = range(9)


def mm(a, b):
    return lax.dot_general(a, b, (((1,), (0,)), ((), ())), preferred_element_type=f32)


def mm_nt(a, b):
    return lax.dot_general(a, b, (((1,), (1,)), ((), ())), preferred_element_type=f32)


def in_hbm(x):
    return pltpu.with_memory_space_constraint(x, pltpu.HBM)


def smem():
    return pl.BlockSpec(memory_space=SMEM)


def whole():
    return pl.BlockSpec(memory_space=pltpu.VMEM)


def params(mib=32):
    return pltpu.CompilerParams(vmem_limit_bytes=mib * MIB)


def cost(flops, moved, exps=0):
    return pl.CostEstimate(flops=int(flops), bytes_accessed=int(moved), transcendentals=int(exps))


def ring_order(mesh):
    count = mesh.shape["blk"]
    natural = list(range(count))
    snake = natural[0::2] + natural[1::2][::-1]
    names = list(mesh.axis_names)
    axes = [names.index("blk")] + [a for a, x in enumerate(names) if x != "blk"]
    lane = mesh.devices.transpose(axes)
    firsts = [lane[i].reshape(-1)[0] for i in natural]
    if not all(hasattr(d, "coords") for d in firsts):
        return snake

    def length(order):
        hops = zip(order, order[1:] + order[:1])
        return sum(
            sum(abs(u - v) for u, v in zip(firsts[a].coords, firsts[b].coords)) for a, b in hops
        )

    return natural if length(natural) <= length(snake) else snake


class Table:
    def __init__(self, ranks, slots):
        self.reach = ranks // 2
        self.source = LENGTHS + slots
        self.ahead = self.source + ranks + 1
        self.behind = self.ahead + self.reach + 1
        self.owner_back = self.behind + self.reach + 1
        self.owner_fore = self.owner_back + self.reach + 1
        self.who = self.owner_fore + self.reach + 1
        self.at = self.who + ranks
        self.size = self.at + ranks


def table_kernel(table, order, given, out):
    reach, ranks = table.reach, len(order)
    span = [given[2 + i] for i in range(ranks)]
    dec = [given[2 + ranks + i] for i in range(ranks)]
    lengths = 3 + 2 * ranks
    for i, r in enumerate(order):
        out[table.who + i] = r
        out[table.at + r] = i
    rank, core = given[0], given[1]
    most, busy_rank = span[0] + dec[0], jnp.int32(0)
    for i in range(1, ranks):
        here = span[i] + dec[i]
        busy_rank = jnp.where(here > most, i, busy_rank)
        most = jnp.maximum(here, most)
    busy = rank == busy_rank

    def wrap(x):
        x = jnp.where(x < 0, x + ranks, x)
        return jnp.where(x >= ranks, x - ranks, x)

    place, busy_place = out[table.at + rank], out[table.at + busy_rank]
    to_busy = wrap(busy_place - place)
    from_busy = wrap(place - busy_place)

    def node_ahead(k):
        far = (to_busy > 0) & (k > to_busy + 1)
        slot = out[table.who + wrap(place + k - jnp.where(far, 1, 0))]
        return jnp.where((to_busy > 0) & (k == to_busy + 1), ranks, slot)

    def node_behind(k):
        far = (from_busy > 0) & (k > from_busy)
        slot = out[table.who + wrap(place - k + jnp.where(far, 1, 0))]
        return jnp.where((from_busy > 0) & (k == from_busy), ranks, slot)

    out[RANK] = rank
    out[CORE] = core
    out[BUSY] = jnp.where(busy, 1, 0)
    out[BUSY_RANK] = busy_rank
    out[SPAN] = given[2 + rank]
    out[DEC] = given[2 + ranks + rank]
    out[LIVE] = given[2 + rank] + given[2 + ranks + rank]
    out[START] = given[lengths - 1]
    for j in range(given.shape[0] - lengths):
        out[LENGTHS + j] = given[lengths + j]
    out[table.source + rank] = 0
    for k in range(1, reach + 1):
        out[table.ahead + k] = node_ahead(k)
        out[table.behind + k] = node_behind(k)
        out[table.owner_back + k] = out[table.who + wrap(place - k)]
        out[table.owner_fore + k] = out[table.who + wrap(place + k)]
        out[table.source + node_behind(k)] = k
        last = jnp.where(busy, ranks, node_ahead(k)) if k == reach else node_ahead(k)
        out[table.source + last] = reach + k


def attend_kernel(
    table, order, heads, first, count, group, rows, lat, value, lead, *refs
):
    if lead:
        given, refs = refs[0], refs[1:]
        q_hbm, cache_hbm, fresh_hbm, vw_hbm, tab, head, main, extra, later = refs[:9]
        flags, refs = refs[9:12], refs[12:]
        q, keys, vw, latent, fz, fresh, q_sem, key_sem, vw_sem, dq = refs
        loaded, base = heads, 0
    else:
        tab, q_hbm, cache_hbm, fresh_hbm, vw_hbm, decoded_here, head, main, extra = refs[:9]
        q, keys, vw, latent, fz, fresh, q_sem, key_sem, vw_sem = refs[9:]
        loaded, base = count, first
    cached, wide = keys.shape[2], keys.shape[1]
    slots = cache_hbm.shape[0] - 1
    odd_slot = keys.shape[0] - 1
    shift, pair, dr = wide - lat, 2 * lat, 8
    groups, pairs = count // group, group // 2
    loads = loaded // group

    def q_copy(g):
        source = pl.ds((base + g * group) * lat, group * lat)
        return pltpu.make_async_copy(
            q_hbm.at[:, source], q.at[:, pl.ds(g * group * lat, group * lat)], q_sem.at[g]
        )

    def vw_copy(g):
        source = pl.ds(first + g * group, group)
        return pltpu.make_async_copy(vw_hbm.at[source], vw.at[pl.ds(g * group, group)], vw_sem.at[g])

    even_copy = pltpu.make_async_copy(cache_hbm.at[0], keys.at[0, pl.ds(0, lat)], key_sem.at[0])
    odd_copy = pltpu.make_async_copy(
        cache_hbm.at[0], keys.at[odd_slot, pl.ds(shift, lat)], key_sem.at[1]
    )
    waiting = [q_copy(g) for g in range(1, loads)]
    if lead:
        rest_copy = pltpu.make_async_copy(
            cache_hbm.at[pl.ds(1, slots)], keys.at[pl.ds(1, slots), pl.ds(0, lat)], key_sem.at[2]
        )
        waiting.append(rest_copy)
    waiting += [vw_copy(g) for g in range(groups)]

    def start_next(number):
        for _ in range(min(number, len(waiting))):
            waiting.pop(0).start()

    fresh_copy = pltpu.make_async_copy(fresh_hbm, fresh, key_sem.at[3])
    fresh_copy.start()
    even_copy.start()
    q_copy(0).start()
    odd_copy.start()
    start_next(1)
    if lead:
        table_kernel(table, order, given, tab)
    span, decs = tab[SPAN], tab[DEC]

    def onehot(shape, row_dim, slot_dim):
        r = lax.broadcasted_iota(i32, shape, row_dim)
        j = lax.broadcasted_iota(i32, shape, slot_dim)
        return jnp.where((r == span + j) & (j < decs), 1.0, 0.0).astype(bf16)

    tail = jnp.zeros((shift, cached), bf16)
    for s in range(odd_slot):
        keys[s, lat:] = tail
    keys[odd_slot, :shift] = tail
    fz[...] = jnp.zeros_like(fz)
    fresh_copy.wait()
    fz[:rows, :lat] = fresh[...].astype(f32)
    fresh_even = fz[...].astype(bf16)
    fresh_odd = pltpu.roll(fz[...], shift, 1).astype(bf16)

    m = pairs * rows
    cols = cached + fz.shape[0]
    row = lax.broadcasted_iota(i32, (m, 1), 0) % rows
    col = lax.broadcasted_iota(i32, (m, cols), 1)
    seen = col < jnp.where(col < cached, tab[START], cached + 1 + row)

    def span_latent(lhs, slot, fresh_keys):
        s = jnp.concatenate([mm(lhs, keys[slot]), mm_nt(lhs, fresh_keys)], 1)
        s = jnp.where(seen, s * score_scale, masked_score)
        e = jnp.exp(s - jnp.max(s, axis=1, keepdims=True))
        w = (e * (1.0 / jnp.sum(e, axis=1, keepdims=True))).astype(bf16)
        o = mm_nt(w[:, :cached], keys[0, :value]) + mm(w[:, cached:], fresh_even[:, :value])
        return jnp.where(row < span, o, 0.0).astype(bf16)

    even_copy.wait()
    odd_copy.wait()
    for g in range(groups):
        q_copy(g).wait()
        start_next(2)
        start = g * group * lat
        for odd in range(2):
            off = start + odd * (pair - wide)
            lhs = jnp.concatenate(
                [q[:, off + pair * p : off + pair * p + wide] for p in range(pairs)], 0
            )
            latent[g, odd] = span_latent(lhs, odd_slot * odd, fresh_odd if odd else fresh_even)
    start_next(len(waiting))

    if lead:
        for g in range(groups, loads):
            q_copy(g).wait()
        pick = onehot((16, rows), 1, 0)
        for p in range(heads // 2):
            got = mm(pick, q[:, pair * p : pair * (p + 1)])[:dr]
            dq[2 * p * dr : (2 * p + 1) * dr] = got[:, :wide]
            dq[(2 * p + 1) * dr : (2 * p + 2) * dr] = pltpu.roll(
                got[:, pair - wide :], wide - shift, 1
            )
        n = heads * dr
        queries = dq[...].astype(bf16)
        slot = lax.broadcasted_iota(i32, (n, 1), 0) % dr
        rest_copy.wait()
        length = jnp.zeros((n, 1), i32)
        scores = jnp.zeros((n, cached), f32)
        for s in range(slots):
            scores = jnp.where(slot == s, mm(queries, keys[s + 1]), scores)
            length = jnp.where(slot == s, tab[LENGTHS + s], length)
        unmasked = lax.broadcasted_iota(i32, (n, cached), 1) < length
        scores = jnp.where(unmasked, scores * score_scale, masked_score)
        own = mm_nt(queries, fresh_even)
        column = lax.broadcasted_iota(i32, own.shape, 1)
        own = jnp.sum(jnp.where(column == span + slot, own, 0.0), axis=1, keepdims=True)
        own = own * score_scale
        peak = jnp.maximum(jnp.max(scores, axis=1, keepdims=True), own)
        e = jnp.exp(scores - peak)
        e_own = jnp.exp(own - peak)
        total = jnp.sum(e, axis=1, keepdims=True) + e_own
        w = e / total
        acc = jnp.zeros((n, value), f32)
        for s in range(slots):
            acc = acc + mm_nt(jnp.where(slot == s, w, 0.0).astype(bf16), keys[s + 1, :value])
        own_value = mm(pick, fresh[:, :value])[:dr]
        own_value = jnp.broadcast_to(own_value[None], (heads, dr, value)).reshape(n, value)
        dec = (acc + (e_own / total).astype(bf16).astype(f32) * own_value).astype(bf16)
        later[...] = dec[count * dr :]
        for flag, at in zip(flags, (BUSY, CORE, LIVE)):
            flag[...] = jnp.full(flag.shape, tab[at].astype(f32))
        dec = dec[: count * dr]
    else:
        dec = decoded_here[...]

    place = onehot((rows, 16), 0, 1)
    vh = vw.shape[2]
    block = rows // 2
    for g in range(groups):
        vw_copy(g).wait()
        values, decoded = [], []
        for p in range(pairs):
            h = g * group + 2 * p
            lhs = jnp.concatenate(
                [
                    latent[g, 0, p * rows : (p + 1) * rows],
                    latent[g, 1, p * rows : (p + 1) * rows],
                    dec[h * dr : (h + 2) * dr],
                ],
                0,
            )
            r = mm(lhs, jnp.concatenate([vw[h], vw[h + 1]], 1))
            values += [r[:rows, :vh], r[rows : 2 * rows, vh:]]
            decoded += [r[2 * rows : 2 * rows + dr, :vh], r[2 * rows + dr :, vh:]]
        decoded = jnp.concatenate(decoded, 1)
        decoded = jnp.concatenate([decoded, jnp.zeros_like(decoded)], 0).astype(bf16)
        out = (jnp.concatenate(values, 1) + mm(place, decoded)).astype(bf16)
        at = slice(g * group * vh, (g + 1) * group * vh)
        main[:, at] = out[:block]
        extra[:, at] = out[block:]
        head[:, at] = jnp.where(tab[BUSY] == 1, out[block:], out[:block])


def attend(table, order, numbers, queries, cache, fresh, vw, part, parts, decoded):
    rows, heads = queries.shape[0], vw.shape[0]
    lat = queries.shape[1] // heads
    slots, _, cached = cache.shape
    value, vh = vw.shape[1:]
    count = heads // parts
    group = min(8, count)
    lead = decoded is None
    loaded = heads if lead else count
    wide = -(-lat // 128) * 128
    half = jax.ShapeDtypeStruct((rows // 2, count * vh), bf16)
    hbm = pl.BlockSpec(memory_space=pltpu.HBM)
    scratch = [
        pltpu.VMEM((rows, loaded * lat), bf16),
        pltpu.VMEM((slots + 1 if lead else 2, wide, cached), bf16),
        pltpu.VMEM((count, value, vh), bf16),
        pltpu.VMEM((count // group, 2, group // 2 * rows, value), bf16),
        pltpu.VMEM((-(-rows // 128) * 128, wide), f32),
        pltpu.VMEM(fresh.shape[::-1], bf16),
        pltpu.SemaphoreType.DMA((loaded // group,)),
        pltpu.SemaphoreType.DMA((4,)),
        pltpu.SemaphoreType.DMA((count // group,)),
    ]
    out_shape, out_specs = [half] * 3, [whole()] * 3
    ins = [smem()] + [hbm] * 4
    args = [numbers, in_hbm(queries), in_hbm(cache), in_hbm(fresh.T), in_hbm(vw)]
    if lead:
        scratch.append(pltpu.VMEM((heads * 8, wide), f32))
        out_shape = [jax.ShapeDtypeStruct((table.size,), i32)] + out_shape
        out_shape += [jax.ShapeDtypeStruct(((heads - count) * 8, value), bf16)]
        out_shape += [jax.ShapeDtypeStruct((1, 1), f32)] * 3
        out_specs = [smem()] + out_specs + [whole()] * 4
    else:
        ins.append(whole())
        args.append(decoded)
    return pl.pallas_call(
        functools.partial(
            attend_kernel, table, order, heads, part * count, count, group, rows, lat, value, lead
        ),
        in_specs=ins,
        out_specs=out_specs,
        out_shape=out_shape,
        scratch_shapes=scratch,
        compiler_params=params(24),
        cost_estimate=cost(
            2 * rows * count * (cached + rows) * (lat + value),
            2 * (queries.size + cache.size + vw.size) // parts,
            rows * count * (cached + rows),
        ),
        name="attend",
    )(*args)


def pack_kernel(ranks, cores, features, tab, res, *outs):
    for k in range(ranks // cores):
        target = tab[RANK] + k + (ranks // cores) * tab[CORE]
        target = jnp.where(target >= ranks, target - ranks, target)

        def put(columns, k=k):
            outs[k][...] = res[:, columns]

        if features % 128 == 0:
            put(pl.ds(pl.multiple_of(target * features, 128), features))
        else:
            for t in range(ranks):
                pl.when(target == t)(functools.partial(put, slice(t * features, (t + 1) * features)))


def pack(tab, residual, ranks, cores):
    rows, width = residual.shape
    features = width // ranks
    count = ranks // cores
    return pl.pallas_call(
        functools.partial(pack_kernel, ranks, cores, features),
        in_specs=[smem(), whole()],
        out_specs=[whole()] * count,
        out_shape=[jax.ShapeDtypeStruct((rows, features), bf16)] * count,
        compiler_params=params(8),
        cost_estimate=cost(0, 4 * residual.size),
        name="pack",
    )(tab, residual)


def share_kernel(half, tab, own, *refs):
    pieces, out = refs[:-1], refs[-1]
    other = 1 - tab[CORE]
    block = own.shape[0] // 2
    low = pl.multiple_of(other * half, half)
    high = pl.multiple_of(block + other * half, half)

    def put(k, piece):
        out[2 * k * half : (2 * k + 1) * half] = piece[pl.ds(low, half)]
        out[(2 * k + 1) * half : (2 * k + 2) * half] = piece[pl.ds(high, half)]

    for k, piece in enumerate(pieces):
        if k > 0:
            put(k, piece)
        else:
            pl.when(tab[CORE] == 0)(functools.partial(put, k, own))
            pl.when(tab[CORE] != 0)(functools.partial(put, k, piece))


def share(tab, own, pieces, cores):
    rows, features = own.shape
    half = rows // 2 // cores
    return pl.pallas_call(
        functools.partial(share_kernel, half),
        in_specs=[smem()] + [whole()] * (1 + len(pieces)),
        out_specs=whole(),
        out_shape=jax.ShapeDtypeStruct((2 * half * len(pieces), features), bf16),
        compiler_params=params(8),
        cost_estimate=cost(0, 4 * own.size * len(pieces)),
        name="share",
    )(tab, own, *pieces)


def project_kernel(source, nodes, block, half, part, first, tab, *refs):
    blocks, refs = refs[: nodes + 1], refs[nodes + 1 :]
    before = None if first else refs[0]
    weight, kept, given, acc = refs[-4:]
    step = pl.program_id(0)
    depth = blocks[0].shape[1] // pl.num_programs(0)
    columns = pl.ds(pl.multiple_of(step * depth, 128), depth)
    last = jnp.where(tab[BUSY] == 1, blocks[nodes][:, columns], blocks[nodes - 1][:, columns])
    lhs = jnp.concatenate([b[:, columns] for b in blocks[: nodes - 1]] + [last], 0)
    got = mm(lhs, weight[pl.ds(pl.multiple_of(part * blocks[0].shape[1] + step * depth, 128), depth)])

    @pl.when(step == 0)
    def _():
        acc[...] = got if first else got + before[...]

    @pl.when(step > 0)
    def _():
        acc[...] += got

    @pl.when(step == pl.num_programs(0) - 1)
    def _():
        core = tab[CORE]
        for k in range(nodes):
            at = tab[source + k] * block
            kept[k * half : (k + 1) * half] = acc[pl.ds(pl.multiple_of(at + core * half, half), half)]
            other = acc[pl.ds(pl.multiple_of(at + (1 - core) * half, half), half)]
            given[k * half : (k + 1) * half] = other.astype(bf16)


def project_part_kernel(nodes, part, first, tab, *refs):
    blocks, refs = refs[: nodes + 1], refs[nodes + 1 :]
    weight, out = refs[-2:]
    step = pl.program_id(0)
    depth = blocks[0].shape[1] // pl.num_programs(0)
    columns = pl.ds(pl.multiple_of(step * depth, 128), depth)
    last = jnp.where(tab[BUSY] == 1, blocks[nodes][:, columns], blocks[nodes - 1][:, columns])
    lhs = jnp.concatenate([b[:, columns] for b in blocks[: nodes - 1]] + [last], 0)
    got = mm(lhs, weight[pl.ds(pl.multiple_of(part * blocks[0].shape[1] + step * depth, 128), depth)])

    @pl.when(step == 0)
    def _():
        out[...] = got if first else got + refs[0][...]

    @pl.when(step > 0)
    def _():
        out[...] += got


def project(tab, table, blocks, before, weight, part, parts, cores):
    block, width = blocks[0].shape
    nodes = len(blocks) - 1
    half = block // cores
    features = weight.shape[1]
    depth = width
    steps = width // depth
    total = jax.ShapeDtypeStruct((nodes * block, features), f32)
    final = part == parts - 1
    first = before is None
    ins = [smem()] + [whole()] * (nodes + 2 + (not first))
    args = [tab, *blocks] + ([] if first else [before]) + [weight]
    estimate = cost(
        2 * nodes * block * width * features, 2 * (nodes * block * width + width * features)
    )
    if not final:
        return pl.pallas_call(
            functools.partial(project_part_kernel, nodes, part, first),
            grid=(steps,),
            in_specs=ins,
            out_specs=pl.BlockSpec(total.shape, lambda i: (0, 0)),
            out_shape=total,
            compiler_params=params(16),
            cost_estimate=estimate,
            name="project",
        )(*args)
    return pl.pallas_call(
        functools.partial(project_kernel, table.source, nodes, block, half, part, first),
        grid=(steps,),
        in_specs=ins,
        out_specs=[pl.BlockSpec((nodes * half, features), lambda i: (0, 0))] * 2,
        out_shape=[
            jax.ShapeDtypeStruct((nodes * half, features), f32),
            jax.ShapeDtypeStruct((nodes * half, features), bf16),
        ],
        scratch_shapes=[pltpu.VMEM(total.shape, f32)],
        compiler_params=params(16),
        cost_estimate=estimate,
        name="project",
    )(*args)


def place_kernel(ranks, half, tab, own, shared, *refs):
    pieces, out = refs[:-1], refs[-1]
    rank, core, busy_rank = tab[RANK], tab[CORE], tab[BUSY_RANK]
    count = len(pieces)
    block = own.shape[0] // 2

    def put(slot, extra):
        out[pl.ds(pl.multiple_of(slot * half, half), half)] = extra

    def put_both(owner, main, extra):
        put(owner, main())

        @pl.when(owner == busy_rank)
        def _():
            put(ranks, extra())

    def owner_of(k, c):
        owner = rank - k - count * c
        return jnp.where(owner < 0, owner + ranks, owner)

    low = pl.ds(pl.multiple_of(core * half, half), half)
    high = pl.ds(pl.multiple_of(block + core * half, half), half)
    for k, piece in enumerate(pieces):

        def received(piece=piece, k=k):
            put_both(owner_of(k, core), lambda: piece[low], lambda: piece[high])

        if k > 0:
            received()
        else:
            pl.when(core == 0)(functools.partial(received, own))
            pl.when(core != 0)(received)
        at = 2 * k * half
        put_both(
            owner_of(k, 1 - core),
            lambda at=at: shared[at : at + half],
            lambda at=at: shared[at + half : at + 2 * half],
        )


def placed_rows(tab, own, shared, pieces, cores):
    rows, features = own.shape
    half = rows // 2 // cores
    ranks = cores * len(pieces)
    return pl.pallas_call(
        functools.partial(place_kernel, ranks, half),
        in_specs=[smem()] + [whole()] * (2 + len(pieces)),
        out_specs=whole(),
        out_shape=jax.ShapeDtypeStruct(((ranks + 1) * half, features), bf16),
        compiler_params=params(8),
        cost_estimate=cost(0, 4 * (ranks + 1) * half * features),
        name="place",
    )(tab, own, shared, *pieces)


def expand_kernel(pieces, others, first, final, width, turned, owners, tab, *refs):
    count = len(pieces)
    blocks = []
    for number in pieces:
        blocks.append(refs[:number])
        refs = refs[number:]
    theirs, refs = refs[:others], refs[others:]
    gain, gate, up = refs[:3]
    refs = refs[3:]
    if not first:
        before, refs = refs[:3], refs[3:]
    if final:
        hidden, refs = refs[0], refs[1:]
    gates, ups, squares = refs
    step = pl.program_id(0)
    for i in range(count):

        @pl.when(step == i)
        def _(i=i):
            both = [x[...] for x in blocks[i]]
            for x in theirs:
                rows = x.shape[0] // count
                both.append(x[i * rows : (i + 1) * rows])
            both = jnp.concatenate(both, 0).astype(f32)
            rows_of = both.shape[1]
            scaled = (both * gain[0]).astype(bf16)
            if turned:
                at = pl.ds(pl.multiple_of(tab[owners[i]] * rows_of, 128), rows_of)
                products = mm_nt(scaled, gate[:, at]), mm_nt(scaled, up[:, at])
            else:
                products = mm(scaled, gate[...]), mm(scaled, up[...])
            values = (
                *products,
                jnp.sum(both * both, axis=1, keepdims=True),
            )
            for n, (ref, value) in enumerate(zip((gates, ups, squares), values)):
                if i == 0:
                    ref[...] = value if first else value + before[n][...]
                else:
                    ref[...] += value

    if final:

        @pl.when(step == count - 1)
        def _():
            scale = lax.rsqrt(squares[...] / width + norm_eps)
            g = gates[...] * scale
            hidden[...] = (g / (1.0 + jnp.exp(-g)) * (ups[...] * scale)).astype(bf16)


def expand(tab, mines, theirs, owners, gain, gate, up, before, final):
    count = len(mines)
    pieces = tuple(len(x) for x in mines)
    rows, features = sum(x.shape[0] for x in mines[0]), mines[0][0].shape[1]
    arrays = [x for own in mines for x in own] + theirs
    units = gate.shape[1]
    first = before is None
    width = gate.shape[0]

    def owner(i, tab):
        index = tab[owners[0]]
        for n in range(1, count):
            index = jnp.where(i == n, tab[owners[n]], index)
        return index

    def full(shape):
        return pl.BlockSpec(shape, lambda i, tab: (0,) * len(shape))

    sums = [(2 * rows, units), (2 * rows, units), (2 * rows, 1)]
    ins = [full(x.shape) for x in arrays]
    ins += [pl.BlockSpec((1, 1, features), lambda i, tab: (owner(i, tab), 0, 0))]
    turned = features % 128 == 0
    if turned:
        gate, up = gate.T, up.T
        ins += [pl.BlockSpec(memory_space=pltpu.VMEM)] * 2
    else:
        ins += [pl.BlockSpec((features, units), lambda i, tab: (owner(i, tab), 0))] * 2
    if not first:
        ins += [full(s) for s in sums]
    shapes = [jax.ShapeDtypeStruct(s, f32) for s in sums]
    out_shapes = [jax.ShapeDtypeStruct((2 * rows, units), bf16)] if final else shapes
    return pl.pallas_call(
        functools.partial(expand_kernel, pieces, len(theirs), first, final, width, turned, owners),
        grid_spec=pltpu.PrefetchScalarGridSpec(
            num_scalar_prefetch=1,
            grid=(count,),
            in_specs=ins,
            out_specs=[full(s.shape) for s in out_shapes],
            scratch_shapes=[pltpu.VMEM(s, f32) for s in sums] if final else [],
        ),
        out_shape=out_shapes,
        compiler_params=params(20),
        cost_estimate=cost(1, 1),
        name="expand",
    )(tab, *arrays, gain, gate, up, *([] if first else before))


def collect_kernel(owners, tab, *refs):
    out = refs[-1]
    if len(out.shape) == 2:
        half, features = out.shape[0] // 2, out.shape[1] // len(owners)
        for i, at in enumerate(owners):
            columns = pl.ds(pl.multiple_of(tab[at] * features, 128), features)
            out[:half, columns] = refs[2 * i][...]
            out[half:, columns] = refs[2 * i + 1][...]
        return
    half = out.shape[1] // 2
    for i, at in enumerate(owners):
        out[tab[at], :half] = refs[2 * i][...]
        out[tab[at], half:] = refs[2 * i + 1][...]


def collect(tab, blocks, owners, half):
    ranks = len(blocks)
    features = blocks[0].shape[1]
    ins, args = [], []
    for x in blocks:
        ins += [
            pl.BlockSpec((half, features), lambda i, tab: (tab[RANK], 0)),
            pl.BlockSpec((half, features), lambda i, tab: (ranks, 0)),
        ]
        args += [x, x]
    aligned = features % 128 == 0
    shape = (2 * half, ranks * features) if aligned else (ranks, 2 * half, features)
    out = pl.pallas_call(
        functools.partial(collect_kernel, owners),
        grid_spec=pltpu.PrefetchScalarGridSpec(
            num_scalar_prefetch=1,
            grid=(1,),
            in_specs=ins,
            out_specs=pl.BlockSpec(shape, lambda i, tab: (0,) * len(shape)),
        ),
        out_shape=jax.ShapeDtypeStruct(shape, bf16),
        compiler_params=params(10),
        cost_estimate=cost(0, 8 * ranks * half * features),
        name="collect",
    )(tab, *args)
    return out if aligned else out.transpose(1, 0, 2).reshape(2 * half, ranks * features)


def contract_kernel(begin, hidden, weight, out):
    wide = out.shape[1]
    at = pl.ds(pl.multiple_of(begin + pl.program_id(0) * wide, 128), wide)
    out[...] = mm(hidden[...], weight[:, at]).astype(bf16)


def contract(hidden, weight, part, parts, which):
    rows, units = hidden.shape[0] // 2, hidden.shape[1]
    columns = weight.shape[1] // parts
    wide = columns // 2 if columns % 256 == 0 else columns
    return pl.pallas_call(
        functools.partial(contract_kernel, part * columns),
        grid=(columns // wide,),
        in_specs=[pl.BlockSpec((rows, units), lambda i: (which, 0)), whole()],
        out_specs=pl.BlockSpec((rows, wide), lambda i: (0, i)),
        out_shape=jax.ShapeDtypeStruct((rows, columns), bf16),
        compiler_params=params(16),
        cost_estimate=cost(2 * rows * units * columns, 2 * (units + rows) * columns),
        name="contract",
    )(hidden, weight)


def pick_kernel(table, half, tab, mine, theirs, *outs):
    busy = tab[BUSY] == 1
    reach = table.reach
    for step in range(1, reach + 1):
        for n, where in enumerate((table.ahead, table.behind)):
            at = pl.multiple_of(tab[where + reach + 1 - step] * half, half)
            total = mine[pl.ds(at, half)].astype(f32) + theirs[pl.ds(at, half)].astype(f32)
            if step == 1 and n == 0:
                total = jnp.where(busy, 0.0, total)
            outs[2 * (step - 1) + n][...] = total
    for n, slot in enumerate((tab[RANK], 2 * reach)):
        at = pl.multiple_of(slot * half, half)
        outs[2 * reach + n][...] = mine[pl.ds(at, half)].astype(f32) + theirs[pl.ds(at, half)].astype(f32)


def pick(tab, table, mine, theirs, half):
    columns = mine.shape[1]
    count = 2 * table.reach + 2
    out = jax.ShapeDtypeStruct((half, columns), f32)
    return pl.pallas_call(
        functools.partial(pick_kernel, table, half),
        in_specs=[smem(), whole(), whole()],
        out_specs=[whole()] * count,
        out_shape=[out] * count,
        compiler_params=params(10),
        cost_estimate=cost(0, 8 * count * half * columns),
        name="pick",
    )(tab, mine, theirs)


contract_parts = 2


def on_device(
    order,
    queries,
    latent_cache,
    new_latent,
    span_len,
    dec_count,
    span_start,
    cache_len,
    value_weight,
    out_weight,
    residual,
    norm_gain,
    gate_weight,
    up_weight,
    down_weight,
):
    ranks = len(order)
    reach = ranks // 2
    cores = lax.axis_size("head")
    rows_dev, width = residual.shape
    half = rows_dev // 2 // cores
    features = out_weight.shape[1]
    table = Table(ranks, cache_len.shape[1])

    forward = [(order[i], order[(i + 1) % ranks]) for i in range(ranks)]
    backward = [(b, a) for a, b in forward]
    exchange = [(c, cores - 1 - c) for c in range(cores)]

    def send_next(x):
        return lax.ppermute(x, "blk", forward)

    def send_prev(x):
        return lax.ppermute(x, "blk", backward)

    def swap(x):
        return lax.ppermute(x, "head", exchange)

    ids = jnp.stack([lax.axis_index("blk"), lax.axis_index("head")]).astype(i32)
    given = jnp.concatenate([ids, span_len, dec_count, span_start, cache_len[0]])
    caches = (queries, latent_cache, new_latent, value_weight)
    tab, *lead, decoded, busy, which, live = attend(table, order, given, *caches, 0, 2, None)

    def choose(special, usual, flag=busy):
        return jnp.where(jnp.broadcast_to(flag > 0, usual.shape), special, usual)


    packed = list(pack(tab, residual, ranks, cores))
    pieces = [None] * len(packed)

    def send_piece(k):
        pairs = [
            (i * cores + c, (i + k + len(packed) * c) % ranks * cores + c)
            for i in range(ranks)
            for c in range(cores)
            if k + c > 0
        ]
        pieces[k] = lax.ppermute(packed[k], ("blk", "head"), pairs)

    for k in range(1, len(packed)):
        send_piece(k)
    decoded, packed = lax.optimization_barrier((decoded, packed))
    packed = list(packed)
    follow = attend(table, order, tab, *caches, 1, 2, decoded)
    follow, pieces[1:], packed[0], out_weight = lax.optimization_barrier(
        (follow, pieces[1:], packed[0], out_weight)
    )
    send_piece(0)

    total = None
    chains = []
    for head, main, extra in (lead, follow):
        chains.append((head, main, extra, [], []))
    for step in range(reach):
        for part, (head, main, extra, behind, ahead) in enumerate(chains):
            if step == 0:
                out_f, out_b = head, main
            elif step == 1:
                out_f, out_b = choose(main, behind[0]), choose(extra, ahead[0])
            else:
                out_f = choose(behind[step - 2], behind[step - 1])
                out_b = choose(ahead[step - 2], ahead[step - 1])
            out_f, out_b = lax.optimization_barrier((out_f, out_b))
            behind.append(send_next(out_f))
            ahead.append(send_prev(out_b))
    gathered = [[main] + behind + ahead + [extra] for _, main, extra, behind, ahead in chains]
    gathered[0][2], pieces = lax.optimization_barrier((gathered[0][2], pieces))
    shared = swap(share(tab, packed[0], pieces, cores))
    gathered[0], shared = lax.optimization_barrier((gathered[0], shared))
    for part in range(2):
        total = project(tab, table, gathered[part], total, out_weight, part, 2, cores)
    kept, other = total
    res_here = placed_rows(tab, packed[0], shared, pieces, cores)
    stream = (kept + swap(other).astype(f32) + res_here.astype(f32)).astype(bf16)

    gain = norm_gain.reshape(ranks, 1, features)
    weights = (gain, gate_weight, up_weight)
    cut = -(-stream.shape[0] // 32) * 16
    back, fore = stream, stream
    sums = expand(tab, [[stream]], [swap(stream)], [RANK], *weights, None, False)
    blocks, owners = [stream], [RANK]
    done = None
    for step in range(1, reach + 1):
        if done is not None:
            back, fore, done = lax.optimization_barrier((back, fore, done))
        done = sums
        if step < reach:
            back, fore = send_next(back), send_prev(fore)
            arrived = [[back], [fore]]
            from_owner = [table.owner_back + step, table.owner_fore + step]
        else:
            arrived = [[send_next(back[:cut]), send_prev(fore[cut:])]]
            from_owner = [table.owner_back + step]
        tied, sums = lax.optimization_barrier((arrived, sums))
        if step < reach:
            others = [swap(jnp.concatenate([x for (x,) in tied], 0))]
        else:
            others = [swap(x) for x in tied[0]]
        sums = expand(tab, arrived, others, from_owner, *weights, sums, step == reach)
        blocks += [x[0] if len(x) == 1 else jnp.concatenate(x, 0) for x in arrived]
        owners += from_owner
    (hidden,) = sums
    own = collect(tab, blocks, owners, half).astype(f32)

    parts = contract_parts
    theirs = [swap(contract(hidden, down_weight, part, parts, 1)) for part in range(parts)]
    mine = [contract(hidden, down_weight, part, parts, 0) for part in range(parts)]
    columns = width // parts
    lows, highs = [], []
    for part in range(parts):
        got_f, got_b = [], []
        *owned, main, extra = pick(tab, table, mine[part], theirs[part], half)
        for step in range(1, reach + 1):
            out_f, out_b = owned[2 * step - 2], owned[2 * step - 1]
            if step == 2:
                out_f = out_f + choose(jnp.zeros_like(out_f), got_f[0].astype(f32))
                out_b = out_b + choose(jnp.zeros_like(out_b), got_b[0].astype(f32))
            elif step > 2:
                out_f = out_f + choose(got_f[step - 3], got_f[step - 2]).astype(f32)
                out_b = out_b + choose(got_b[step - 3], got_b[step - 2]).astype(f32)
            out_f, out_b = lax.optimization_barrier((out_f.astype(bf16), out_b.astype(bf16)))
            got_f.append(send_next(out_f))
            got_b.append(send_prev(out_b))
        at = slice(part * columns, (part + 1) * columns)
        main = main + own[:half, at] + got_f[-1].astype(f32)
        main = (main + choose(got_b[-2], got_b[-1]).astype(f32)).astype(bf16)
        extra = extra + own[half:, at] + got_f[-2].astype(f32) + got_b[-1].astype(f32)
        extra = extra.astype(bf16)
        received = swap(choose(main, extra, which))
        stays = choose(extra, main, which)
        lows.append(choose(received, stays, which))
        highs.append(choose(stays, received, which))
    result = jnp.concatenate([jnp.concatenate(lows, 1), jnp.concatenate(highs, 1)], 0)
    row = which * (2 * half) + lax.broadcasted_iota(i32, result.shape, 0).astype(f32)
    return jnp.where(row < live, result, jnp.zeros_like(result))


def solution(mesh):
    placed = (
        P(("groups", "blk"), "head"),
        P(("groups", "blk"), None, None),
        P(None, ("groups", "blk")),
        P("groups"),
        P("groups"),
        P(("groups", "blk")),
        P(("groups", "blk"), None),
        P("head", None, None),
        P("head", "blk"),
        P(("groups", "blk"), None),
        P(),
        P(None, ("blk", "head")),
        P(None, ("blk", "head")),
        P(("blk", "head"), None),
    )
    order = ring_order(mesh)
    return jax.shard_map(
        lambda *args: on_device(order, *args),
        mesh=mesh,
        in_specs=placed,
        out_specs=P(("groups", "blk", "head"), None),
        check_vma=False,
    )
```

```python
import functools

import jax
import jax.numpy as jnp
from jax import lax
from jax.experimental import pallas as pl
from jax.experimental.pallas import tpu as pltpu
from jax.sharding import PartitionSpec as P

score_scale = 192.0 ** (-0.5)
norm_eps = 1e-06
masked_score = -1e30
f32, bf16, i32 = jnp.float32, jnp.bfloat16, jnp.int32
SMEM = pltpu.SMEM
MIB = 1 << 20

RANK, CORE, BUSY, BUSY_RANK, SPAN, DEC, LIVE, START, LENGTHS = range(9)


def mm(a, b):
    return lax.dot_general(a, b, (((1,), (0,)), ((), ())), preferred_element_type=f32)


def mm_nt(a, b):
    return lax.dot_general(a, b, (((1,), (1,)), ((), ())), preferred_element_type=f32)


def in_hbm(x):
    return pltpu.with_memory_space_constraint(x, pltpu.HBM)


def smem():
    return pl.BlockSpec(memory_space=SMEM)


def whole():
    return pl.BlockSpec(memory_space=pltpu.VMEM)


def params(mib=32):
    return pltpu.CompilerParams(vmem_limit_bytes=mib * MIB)


def cost(flops, moved, exps=0):
    return pl.CostEstimate(flops=int(flops), bytes_accessed=int(moved), transcendentals=int(exps))


def ring_order(mesh):
    count = mesh.shape["blk"]
    natural = list(range(count))
    snake = natural[0::2] + natural[1::2][::-1]
    names = list(mesh.axis_names)
    axes = [names.index("blk")] + [a for a, x in enumerate(names) if x != "blk"]
    lane = mesh.devices.transpose(axes)
    firsts = [lane[i].reshape(-1)[0] for i in natural]
    if not all(hasattr(d, "coords") for d in firsts):
        return snake

    def length(order):
        hops = zip(order, order[1:] + order[:1])
        return sum(
            sum(abs(u - v) for u, v in zip(firsts[a].coords, firsts[b].coords)) for a, b in hops
        )

    return natural if length(natural) <= length(snake) else snake


class Table:
    def __init__(self, ranks, slots):
        self.reach = ranks // 2
        self.source = LENGTHS + slots
        self.ahead = self.source + ranks + 1
        self.behind = self.ahead + self.reach + 1
        self.owner_back = self.behind + self.reach + 1
        self.owner_fore = self.owner_back + self.reach + 1
        self.who = self.owner_fore + self.reach + 1
        self.at = self.who + ranks
        self.size = self.at + ranks


def table_kernel(table, order, given, out):
    reach, ranks = table.reach, len(order)
    span = [given[2 + i] for i in range(ranks)]
    dec = [given[2 + ranks + i] for i in range(ranks)]
    lengths = 3 + 2 * ranks
    for i, r in enumerate(order):
        out[table.who + i] = r
        out[table.at + r] = i
    rank, core = given[0], given[1]
    most, busy_rank = span[0] + dec[0], jnp.int32(0)
    for i in range(1, ranks):
        here = span[i] + dec[i]
        busy_rank = jnp.where(here > most, i, busy_rank)
        most = jnp.maximum(here, most)
    busy = rank == busy_rank

    def wrap(x):
        x = jnp.where(x < 0, x + ranks, x)
        return jnp.where(x >= ranks, x - ranks, x)

    place, busy_place = out[table.at + rank], out[table.at + busy_rank]
    to_busy = wrap(busy_place - place)
    from_busy = wrap(place - busy_place)

    def node_ahead(k):
        far = (to_busy > 0) & (k > to_busy + 1)
        slot = out[table.who + wrap(place + k - jnp.where(far, 1, 0))]
        return jnp.where((to_busy > 0) & (k == to_busy + 1), ranks, slot)

    def node_behind(k):
        far = (from_busy > 0) & (k > from_busy)
        slot = out[table.who + wrap(place - k + jnp.where(far, 1, 0))]
        return jnp.where((from_busy > 0) & (k == from_busy), ranks, slot)

    out[RANK] = rank
    out[CORE] = core
    out[BUSY] = jnp.where(busy, 1, 0)
    out[BUSY_RANK] = busy_rank
    out[SPAN] = given[2 + rank]
    out[DEC] = given[2 + ranks + rank]
    out[LIVE] = given[2 + rank] + given[2 + ranks + rank]
    out[START] = given[lengths - 1]
    for j in range(given.shape[0] - lengths):
        out[LENGTHS + j] = given[lengths + j]
    out[table.source + rank] = 0
    for k in range(1, reach + 1):
        out[table.ahead + k] = node_ahead(k)
        out[table.behind + k] = node_behind(k)
        out[table.owner_back + k] = out[table.who + wrap(place - k)]
        out[table.owner_fore + k] = out[table.who + wrap(place + k)]
        out[table.source + node_behind(k)] = k
        last = jnp.where(busy, ranks, node_ahead(k)) if k == reach else node_ahead(k)
        out[table.source + last] = reach + k


def attend_kernel(
    table, order, heads, first, count, group, rows, lat, value, lead, *refs
):
    if lead:
        given, refs = refs[0], refs[1:]
        q_hbm, cache_hbm, fresh_hbm, vw_hbm, tab, head, main, extra, later = refs[:9]
        flags, refs = refs[9:12], refs[12:]
        q, keys, vw, latent, fz, fresh, q_sem, key_sem, vw_sem, dq = refs
        loaded, base = heads, 0
    else:
        tab, q_hbm, cache_hbm, fresh_hbm, vw_hbm, decoded_here, head, main, extra = refs[:9]
        q, keys, vw, latent, fz, fresh, q_sem, key_sem, vw_sem = refs[9:]
        loaded, base = count, first
    cached, wide = keys.shape[2], keys.shape[1]
    slots = cache_hbm.shape[0] - 1
    odd_slot = keys.shape[0] - 1
    shift, pair, dr = wide - lat, 2 * lat, 8
    groups, pairs = count // group, group // 2
    loads = loaded // group

    def q_copy(g):
        source = pl.ds((base + g * group) * lat, group * lat)
        return pltpu.make_async_copy(
            q_hbm.at[:, source], q.at[:, pl.ds(g * group * lat, group * lat)], q_sem.at[g]
        )

    def vw_copy(g):
        source = pl.ds(first + g * group, group)
        return pltpu.make_async_copy(vw_hbm.at[source], vw.at[pl.ds(g * group, group)], vw_sem.at[g])

    even_copy = pltpu.make_async_copy(cache_hbm.at[0], keys.at[0, pl.ds(0, lat)], key_sem.at[0])
    odd_copy = pltpu.make_async_copy(
        cache_hbm.at[0], keys.at[odd_slot, pl.ds(shift, lat)], key_sem.at[1]
    )
    waiting = [q_copy(g) for g in range(1, loads)]
    if lead:
        rest_copy = pltpu.make_async_copy(
            cache_hbm.at[pl.ds(1, slots)], keys.at[pl.ds(1, slots), pl.ds(0, lat)], key_sem.at[2]
        )
        waiting.append(rest_copy)
    waiting += [vw_copy(g) for g in range(groups)]

    def start_next(number):
        for _ in range(min(number, len(waiting))):
            waiting.pop(0).start()

    fresh_copy = pltpu.make_async_copy(fresh_hbm, fresh, key_sem.at[3])
    fresh_copy.start()
    even_copy.start()
    q_copy(0).start()
    odd_copy.start()
    start_next(1)
    if lead:
        table_kernel(table, order, given, tab)
    span, decs = tab[SPAN], tab[DEC]

    def onehot(shape, row_dim, slot_dim):
        r = lax.broadcasted_iota(i32, shape, row_dim)
        j = lax.broadcasted_iota(i32, shape, slot_dim)
        return jnp.where((r == span + j) & (j < decs), 1.0, 0.0).astype(bf16)

    tail = jnp.zeros((shift, cached), bf16)
    for s in range(odd_slot):
        keys[s, lat:] = tail
    keys[odd_slot, :shift] = tail
    fz[...] = jnp.zeros_like(fz)
    fresh_copy.wait()
    fz[:rows, :lat] = fresh[...].astype(f32)
    fresh_even = fz[...].astype(bf16)
    fresh_odd = pltpu.roll(fz[...], shift, 1).astype(bf16)

    m = pairs * rows
    cols = cached + fz.shape[0]
    row = lax.broadcasted_iota(i32, (m, 1), 0) % rows
    col = lax.broadcasted_iota(i32, (m, cols), 1)
    seen = col < jnp.where(col < cached, tab[START], cached + 1 + row)

    def span_latent(lhs, slot, fresh_keys):
        s = jnp.concatenate([mm(lhs, keys[slot]), mm_nt(lhs, fresh_keys)], 1)
        s = jnp.where(seen, s * score_scale, masked_score)
        e = jnp.exp(s - jnp.max(s, axis=1, keepdims=True))
        w = (e * (1.0 / jnp.sum(e, axis=1, keepdims=True))).astype(bf16)
        o = mm_nt(w[:, :cached], keys[0, :value]) + mm(w[:, cached:], fresh_even[:, :value])
        return jnp.where(row < span, o, 0.0).astype(bf16)

    even_copy.wait()
    odd_copy.wait()
    for g in range(groups):
        q_copy(g).wait()
        start_next(2)
        start = g * group * lat
        for odd in range(2):
            off = start + odd * (pair - wide)
            lhs = jnp.concatenate(
                [q[:, off + pair * p : off + pair * p + wide] for p in range(pairs)], 0
            )
            latent[g, odd] = span_latent(lhs, odd_slot * odd, fresh_odd if odd else fresh_even)
    start_next(len(waiting))

    if lead:
        for g in range(groups, loads):
            q_copy(g).wait()
        pick = onehot((16, rows), 1, 0)
        for p in range(heads // 2):
            got = mm(pick, q[:, pair * p : pair * (p + 1)])[:dr]
            dq[2 * p * dr : (2 * p + 1) * dr] = got[:, :wide]
            dq[(2 * p + 1) * dr : (2 * p + 2) * dr] = pltpu.roll(
                got[:, pair - wide :], wide - shift, 1
            )
        n = heads * dr
        queries = dq[...].astype(bf16)
        slot = lax.broadcasted_iota(i32, (n, 1), 0) % dr
        rest_copy.wait()
        length = jnp.zeros((n, 1), i32)
        scores = jnp.zeros((n, cached), f32)
        for s in range(slots):
            scores = jnp.where(slot == s, mm(queries, keys[s + 1]), scores)
            length = jnp.where(slot == s, tab[LENGTHS + s], length)
        unmasked = lax.broadcasted_iota(i32, (n, cached), 1) < length
        scores = jnp.where(unmasked, scores * score_scale, masked_score)
        own = mm_nt(queries, fresh_even)
        column = lax.broadcasted_iota(i32, own.shape, 1)
        own = jnp.sum(jnp.where(column == span + slot, own, 0.0), axis=1, keepdims=True)
        own = own * score_scale
        peak = jnp.maximum(jnp.max(scores, axis=1, keepdims=True), own)
        e = jnp.exp(scores - peak)
        e_own = jnp.exp(own - peak)
        total = jnp.sum(e, axis=1, keepdims=True) + e_own
        w = e / total
        acc = jnp.zeros((n, value), f32)
        for s in range(slots):
            acc = acc + mm_nt(jnp.where(slot == s, w, 0.0).astype(bf16), keys[s + 1, :value])
        own_value = mm(pick, fresh[:, :value])[:dr]
        own_value = jnp.broadcast_to(own_value[None], (heads, dr, value)).reshape(n, value)
        dec = (acc + (e_own / total).astype(bf16).astype(f32) * own_value).astype(bf16)
        later[...] = dec[count * dr :]
        for flag, at in zip(flags, (BUSY, CORE)):
            flag[...] = jnp.full(flag.shape, tab[at].astype(f32))
        block = rows // 2
        slot_row = tab[CORE] * block + lax.broadcasted_iota(i32, (block, 1), 0)
        flags[2][...] = jnp.where(slot_row < tab[LIVE], 1.0, 0.0)
        dec = dec[: count * dr]
    else:
        dec = decoded_here[...]

    place = onehot((rows, 16), 0, 1)
    vh = vw.shape[2]
    block = rows // 2
    for g in range(groups):
        vw_copy(g).wait()
        values, decoded = [], []
        for p in range(pairs):
            h = g * group + 2 * p
            lhs = jnp.concatenate(
                [
                    latent[g, 0, p * rows : (p + 1) * rows],
                    latent[g, 1, p * rows : (p + 1) * rows],
                    dec[h * dr : (h + 2) * dr],
                ],
                0,
            )
            r = mm(lhs, jnp.concatenate([vw[h], vw[h + 1]], 1))
            values += [r[:rows, :vh], r[rows : 2 * rows, vh:]]
            decoded += [r[2 * rows : 2 * rows + dr, :vh], r[2 * rows + dr :, vh:]]
        decoded = jnp.concatenate(decoded, 1)
        decoded = jnp.concatenate([decoded, jnp.zeros_like(decoded)], 0).astype(bf16)
        out = (jnp.concatenate(values, 1) + mm(place, decoded)).astype(bf16)
        at = slice(g * group * vh, (g + 1) * group * vh)
        main[:, at] = out[:block]
        extra[:, at] = out[block:]
        head[:, at] = jnp.where(tab[BUSY] == 1, out[block:], out[:block])


def attend(table, order, numbers, queries, cache, fresh, vw, part, parts, decoded):
    rows, heads = queries.shape[0], vw.shape[0]
    lat = queries.shape[1] // heads
    slots, _, cached = cache.shape
    value, vh = vw.shape[1:]
    count = heads // parts
    group = min(8, count)
    lead = decoded is None
    loaded = heads if lead else count
    wide = -(-lat // 128) * 128
    half = jax.ShapeDtypeStruct((rows // 2, count * vh), bf16)
    hbm = pl.BlockSpec(memory_space=pltpu.HBM)
    scratch = [
        pltpu.VMEM((rows, loaded * lat), bf16),
        pltpu.VMEM((slots + 1 if lead else 2, wide, cached), bf16),
        pltpu.VMEM((count, value, vh), bf16),
        pltpu.VMEM((count // group, 2, group // 2 * rows, value), bf16),
        pltpu.VMEM((-(-rows // 128) * 128, wide), f32),
        pltpu.VMEM(fresh.shape[::-1], bf16),
        pltpu.SemaphoreType.DMA((loaded // group,)),
        pltpu.SemaphoreType.DMA((4,)),
        pltpu.SemaphoreType.DMA((count // group,)),
    ]
    out_shape, out_specs = [half] * 3, [whole()] * 3
    ins = [smem()] + [hbm] * 4
    args = [numbers, in_hbm(queries), in_hbm(cache), in_hbm(fresh.T), in_hbm(vw)]
    if lead:
        scratch.append(pltpu.VMEM((heads * 8, wide), f32))
        out_shape = [jax.ShapeDtypeStruct((table.size,), i32)] + out_shape
        out_shape += [jax.ShapeDtypeStruct(((heads - count) * 8, value), bf16)]
        out_shape += [jax.ShapeDtypeStruct((n, 1), f32) for n in (1, 1, rows // 2)]
        out_specs = [smem()] + out_specs + [whole()] * 4
    else:
        ins.append(whole())
        args.append(decoded)
    return pl.pallas_call(
        functools.partial(
            attend_kernel, table, order, heads, part * count, count, group, rows, lat, value, lead
        ),
        in_specs=ins,
        out_specs=out_specs,
        out_shape=out_shape,
        scratch_shapes=scratch,
        compiler_params=params(24),
        cost_estimate=cost(
            2 * rows * count * (cached + rows) * (lat + value),
            2 * (queries.size + cache.size + vw.size) // parts,
            rows * count * (cached + rows),
        ),
        name="attend",
    )(*args)


def pack_kernel(ranks, cores, features, tab, res, *outs):
    for k in range(ranks // cores):
        target = tab[RANK] + k + (ranks // cores) * tab[CORE]
        target = jnp.where(target >= ranks, target - ranks, target)

        def put(columns, k=k):
            outs[k][...] = res[:, columns]

        if features % 128 == 0:
            put(pl.ds(pl.multiple_of(target * features, 128), features))
        else:
            for t in range(ranks):
                pl.when(target == t)(functools.partial(put, slice(t * features, (t + 1) * features)))


def pack(tab, residual, ranks, cores):
    rows, width = residual.shape
    features = width // ranks
    count = ranks // cores
    return pl.pallas_call(
        functools.partial(pack_kernel, ranks, cores, features),
        in_specs=[smem(), whole()],
        out_specs=[whole()] * count,
        out_shape=[jax.ShapeDtypeStruct((rows, features), bf16)] * count,
        compiler_params=params(8),
        cost_estimate=cost(0, 4 * residual.size),
        name="pack",
    )(tab, residual)


def share_kernel(half, tab, own, *refs):
    pieces, out = refs[:-1], refs[-1]
    other = 1 - tab[CORE]
    block = own.shape[0] // 2
    low = pl.multiple_of(other * half, half)
    high = pl.multiple_of(block + other * half, half)

    def put(k, piece):
        out[2 * k * half : (2 * k + 1) * half] = piece[pl.ds(low, half)]
        out[(2 * k + 1) * half : (2 * k + 2) * half] = piece[pl.ds(high, half)]

    for k, piece in enumerate(pieces):
        if k > 0:
            put(k, piece)
        else:
            pl.when(tab[CORE] == 0)(functools.partial(put, k, own))
            pl.when(tab[CORE] != 0)(functools.partial(put, k, piece))


def share(tab, own, pieces, cores):
    rows, features = own.shape
    half = rows // 2 // cores
    return pl.pallas_call(
        functools.partial(share_kernel, half),
        in_specs=[smem()] + [whole()] * (1 + len(pieces)),
        out_specs=whole(),
        out_shape=jax.ShapeDtypeStruct((2 * half * len(pieces), features), bf16),
        compiler_params=params(8),
        cost_estimate=cost(0, 4 * own.size * len(pieces)),
        name="share",
    )(tab, own, *pieces)


def project_kernel(source, nodes, block, half, part, first, tab, *refs):
    blocks, refs = refs[: nodes + 1], refs[nodes + 1 :]
    before = None if first else refs[0]
    weight, kept, given, acc = refs[-4:]
    step = pl.program_id(0)
    depth = blocks[0].shape[1] // pl.num_programs(0)
    columns = pl.ds(pl.multiple_of(step * depth, 128), depth)
    last = jnp.where(tab[BUSY] == 1, blocks[nodes][:, columns], blocks[nodes - 1][:, columns])
    lhs = jnp.concatenate([b[:, columns] for b in blocks[: nodes - 1]] + [last], 0)
    got = mm(lhs, weight[pl.ds(pl.multiple_of(part * blocks[0].shape[1] + step * depth, 128), depth)])

    @pl.when(step == 0)
    def _():
        acc[...] = got if first else got + before[...]

    @pl.when(step > 0)
    def _():
        acc[...] += got

    @pl.when(step == pl.num_programs(0) - 1)
    def _():
        core = tab[CORE]
        for k in range(nodes):
            at = tab[source + k] * block
            kept[k * half : (k + 1) * half] = acc[pl.ds(pl.multiple_of(at + core * half, half), half)]
            other = acc[pl.ds(pl.multiple_of(at + (1 - core) * half, half), half)]
            given[k * half : (k + 1) * half] = other.astype(bf16)


def project_part_kernel(nodes, part, first, tab, *refs):
    blocks, refs = refs[: nodes + 1], refs[nodes + 1 :]
    weight, out = refs[-2:]
    step = pl.program_id(0)
    depth = blocks[0].shape[1] // pl.num_programs(0)
    columns = pl.ds(pl.multiple_of(step * depth, 128), depth)
    last = jnp.where(tab[BUSY] == 1, blocks[nodes][:, columns], blocks[nodes - 1][:, columns])
    lhs = jnp.concatenate([b[:, columns] for b in blocks[: nodes - 1]] + [last], 0)
    got = mm(lhs, weight[pl.ds(pl.multiple_of(part * blocks[0].shape[1] + step * depth, 128), depth)])

    @pl.when(step == 0)
    def _():
        out[...] = got if first else got + refs[0][...]

    @pl.when(step > 0)
    def _():
        out[...] += got


def project(tab, table, blocks, before, weight, part, parts, cores):
    block, width = blocks[0].shape
    nodes = len(blocks) - 1
    half = block // cores
    features = weight.shape[1]
    depth = width
    steps = width // depth
    total = jax.ShapeDtypeStruct((nodes * block, features), f32)
    final = part == parts - 1
    first = before is None
    ins = [smem()] + [whole()] * (nodes + 2 + (not first))
    args = [tab, *blocks] + ([] if first else [before]) + [weight]
    estimate = cost(
        2 * nodes * block * width * features, 2 * (nodes * block * width + width * features)
    )
    if not final:
        return pl.pallas_call(
            functools.partial(project_part_kernel, nodes, part, first),
            grid=(steps,),
            in_specs=ins,
            out_specs=pl.BlockSpec(total.shape, lambda i: (0, 0)),
            out_shape=total,
            compiler_params=params(16),
            cost_estimate=estimate,
            name="project",
        )(*args)
    return pl.pallas_call(
        functools.partial(project_kernel, table.source, nodes, block, half, part, first),
        grid=(steps,),
        in_specs=ins,
        out_specs=[pl.BlockSpec((nodes * half, features), lambda i: (0, 0))] * 2,
        out_shape=[
            jax.ShapeDtypeStruct((nodes * half, features), f32),
            jax.ShapeDtypeStruct((nodes * half, features), bf16),
        ],
        scratch_shapes=[pltpu.VMEM(total.shape, f32)],
        compiler_params=params(16),
        cost_estimate=estimate,
        name="project",
    )(*args)


def place_kernel(ranks, half, tab, own, shared, *refs):
    pieces, out = refs[:-1], refs[-1]
    rank, core, busy_rank = tab[RANK], tab[CORE], tab[BUSY_RANK]
    count = len(pieces)
    block = own.shape[0] // 2

    def put(slot, extra):
        out[pl.ds(pl.multiple_of(slot * half, half), half)] = extra

    def put_both(owner, main, extra):
        put(owner, main())

        @pl.when(owner == busy_rank)
        def _():
            put(ranks, extra())

    def owner_of(k, c):
        owner = rank - k - count * c
        return jnp.where(owner < 0, owner + ranks, owner)

    low = pl.ds(pl.multiple_of(core * half, half), half)
    high = pl.ds(pl.multiple_of(block + core * half, half), half)
    for k, piece in enumerate(pieces):

        def received(piece=piece, k=k):
            put_both(owner_of(k, core), lambda: piece[low], lambda: piece[high])

        if k > 0:
            received()
        else:
            pl.when(core == 0)(functools.partial(received, own))
            pl.when(core != 0)(received)
        at = 2 * k * half
        put_both(
            owner_of(k, 1 - core),
            lambda at=at: shared[at : at + half],
            lambda at=at: shared[at + half : at + 2 * half],
        )


def placed_rows(tab, own, shared, pieces, cores):
    rows, features = own.shape
    half = rows // 2 // cores
    ranks = cores * len(pieces)
    return pl.pallas_call(
        functools.partial(place_kernel, ranks, half),
        in_specs=[smem()] + [whole()] * (2 + len(pieces)),
        out_specs=whole(),
        out_shape=jax.ShapeDtypeStruct(((ranks + 1) * half, features), bf16),
        compiler_params=params(8),
        cost_estimate=cost(0, 4 * (ranks + 1) * half * features),
        name="place",
    )(tab, own, shared, *pieces)


def expand_kernel(pieces, others, first, final, width, turned, owners, tab, *refs):
    count = len(pieces)
    blocks = []
    for number in pieces:
        blocks.append(refs[:number])
        refs = refs[number:]
    theirs, refs = refs[:others], refs[others:]
    gain, gate, up = refs[:3]
    refs = refs[3:]
    if not first:
        before, refs = refs[:3], refs[3:]
    if final:
        hidden, refs = refs[0], refs[1:]
    gates, ups, squares = refs
    step = pl.program_id(0)
    for i in range(count):

        @pl.when(step == i)
        def _(i=i):
            both = [x[...] for x in blocks[i]]
            for x in theirs:
                rows = x.shape[0] // count
                both.append(x[i * rows : (i + 1) * rows])
            both = jnp.concatenate(both, 0).astype(f32)
            rows_of = both.shape[1]
            scaled = (both * gain[0]).astype(bf16)
            if turned:
                at = pl.ds(pl.multiple_of(tab[owners[i]] * rows_of, 128), rows_of)
                products = mm_nt(scaled, gate[:, at]), mm_nt(scaled, up[:, at])
            else:
                products = mm(scaled, gate[...]), mm(scaled, up[...])
            values = (
                *products,
                jnp.sum(both * both, axis=1, keepdims=True),
            )
            for n, (ref, value) in enumerate(zip((gates, ups, squares), values)):
                if i == 0:
                    ref[...] = value if first else value + before[n][...]
                else:
                    ref[...] += value

    if final:

        @pl.when(step == count - 1)
        def _():
            scale = lax.rsqrt(squares[...] / width + norm_eps)
            g = gates[...] * scale
            hidden[...] = (g / (1.0 + jnp.exp(-g)) * (ups[...] * scale)).astype(bf16)


def expand(tab, mines, theirs, owners, gain, gate, up, before, final):
    count = len(mines)
    pieces = tuple(len(x) for x in mines)
    rows, features = sum(x.shape[0] for x in mines[0]), mines[0][0].shape[1]
    arrays = [x for own in mines for x in own] + theirs
    units = gate.shape[1]
    first = before is None
    width = gate.shape[0]

    def owner(i, tab):
        index = tab[owners[0]]
        for n in range(1, count):
            index = jnp.where(i == n, tab[owners[n]], index)
        return index

    def full(shape):
        return pl.BlockSpec(shape, lambda i, tab: (0,) * len(shape))

    sums = [(2 * rows, units), (2 * rows, units), (2 * rows, 1)]
    ins = [full(x.shape) for x in arrays]
    ins += [pl.BlockSpec((1, 1, features), lambda i, tab: (owner(i, tab), 0, 0))]
    turned = features % 128 == 0
    if turned:
        gate, up = gate.T, up.T
        ins += [pl.BlockSpec(memory_space=pltpu.VMEM)] * 2
    else:
        ins += [pl.BlockSpec((features, units), lambda i, tab: (owner(i, tab), 0))] * 2
    if not first:
        ins += [full(s) for s in sums]
    shapes = [jax.ShapeDtypeStruct(s, f32) for s in sums]
    out_shapes = [jax.ShapeDtypeStruct((2 * rows, units), bf16)] if final else shapes
    return pl.pallas_call(
        functools.partial(expand_kernel, pieces, len(theirs), first, final, width, turned, owners),
        grid_spec=pltpu.PrefetchScalarGridSpec(
            num_scalar_prefetch=1,
            grid=(count,),
            in_specs=ins,
            out_specs=[full(s.shape) for s in out_shapes],
            scratch_shapes=[pltpu.VMEM(s, f32) for s in sums] if final else [],
        ),
        out_shape=out_shapes,
        compiler_params=params(20),
        cost_estimate=cost(1, 1),
        name="expand",
    )(tab, *arrays, gain, gate, up, *([] if first else before))


def collect_kernel(owners, tab, *refs):
    out = refs[-1]
    if len(out.shape) == 2:
        half, features = out.shape[0] // 2, out.shape[1] // len(owners)
        for i, at in enumerate(owners):
            columns = pl.ds(pl.multiple_of(tab[at] * features, 128), features)
            out[:half, columns] = refs[2 * i][...]
            out[half:, columns] = refs[2 * i + 1][...]
        return
    half = out.shape[1] // 2
    for i, at in enumerate(owners):
        out[tab[at], :half] = refs[2 * i][...]
        out[tab[at], half:] = refs[2 * i + 1][...]


def collect(tab, blocks, owners, half):
    ranks = len(blocks)
    features = blocks[0].shape[1]
    ins, args = [], []
    for x in blocks:
        ins += [
            pl.BlockSpec((half, features), lambda i, tab: (tab[RANK], 0)),
            pl.BlockSpec((half, features), lambda i, tab: (ranks, 0)),
        ]
        args += [x, x]
    aligned = features % 128 == 0
    shape = (2 * half, ranks * features) if aligned else (ranks, 2 * half, features)
    out = pl.pallas_call(
        functools.partial(collect_kernel, owners),
        grid_spec=pltpu.PrefetchScalarGridSpec(
            num_scalar_prefetch=1,
            grid=(1,),
            in_specs=ins,
            out_specs=pl.BlockSpec(shape, lambda i, tab: (0,) * len(shape)),
        ),
        out_shape=jax.ShapeDtypeStruct(shape, bf16),
        compiler_params=params(10),
        cost_estimate=cost(0, 8 * ranks * half * features),
        name="collect",
    )(tab, *args)
    return out if aligned else out.transpose(1, 0, 2).reshape(2 * half, ranks * features)


def contract_kernel(begin, hidden, weight, out):
    wide = out.shape[1]
    at = pl.ds(pl.multiple_of(begin + pl.program_id(0) * wide, 128), wide)
    out[...] = mm(hidden[...], weight[:, at]).astype(bf16)


def contract(hidden, weight, part, parts, which):
    rows, units = hidden.shape[0] // 2, hidden.shape[1]
    columns = weight.shape[1] // parts
    wide = columns // 2 if columns % 256 == 0 else columns
    return pl.pallas_call(
        functools.partial(contract_kernel, part * columns),
        grid=(columns // wide,),
        in_specs=[pl.BlockSpec((rows, units), lambda i: (which, 0)), whole()],
        out_specs=pl.BlockSpec((rows, wide), lambda i: (0, i)),
        out_shape=jax.ShapeDtypeStruct((rows, columns), bf16),
        compiler_params=params(16),
        cost_estimate=cost(2 * rows * units * columns, 2 * (units + rows) * columns),
        name="contract",
    )(hidden, weight)


def pick_kernel(table, half, tab, mine, theirs, *outs):
    busy = tab[BUSY] == 1
    reach = table.reach
    for step in range(1, reach + 1):
        for n, where in enumerate((table.ahead, table.behind)):
            at = pl.multiple_of(tab[where + reach + 1 - step] * half, half)
            total = mine[pl.ds(at, half)].astype(f32) + theirs[pl.ds(at, half)].astype(f32)
            if step == 1 and n == 0:
                total = jnp.where(busy, 0.0, total)
            outs[2 * (step - 1) + n][...] = total
    for n, slot in enumerate((tab[RANK], 2 * reach)):
        at = pl.multiple_of(slot * half, half)
        outs[2 * reach + n][...] = mine[pl.ds(at, half)].astype(f32) + theirs[pl.ds(at, half)].astype(f32)


def pick(tab, table, mine, theirs, half):
    columns = mine.shape[1]
    count = 2 * table.reach + 2
    out = jax.ShapeDtypeStruct((half, columns), f32)
    return pl.pallas_call(
        functools.partial(pick_kernel, table, half),
        in_specs=[smem(), whole(), whole()],
        out_specs=[whole()] * count,
        out_shape=[out] * count,
        compiler_params=params(10),
        cost_estimate=cost(0, 8 * count * half * columns),
        name="pick",
    )(tab, mine, theirs)


contract_parts = 2


def on_device(
    order,
    queries,
    latent_cache,
    new_latent,
    span_len,
    dec_count,
    span_start,
    cache_len,
    value_weight,
    out_weight,
    residual,
    norm_gain,
    gate_weight,
    up_weight,
    down_weight,
):
    ranks = len(order)
    reach = ranks // 2
    cores = lax.axis_size("head")
    rows_dev, width = residual.shape
    half = rows_dev // 2 // cores
    features = out_weight.shape[1]
    table = Table(ranks, cache_len.shape[1])

    forward = [(order[i], order[(i + 1) % ranks]) for i in range(ranks)]
    backward = [(b, a) for a, b in forward]
    exchange = [(c, cores - 1 - c) for c in range(cores)]

    def send_next(x):
        return lax.ppermute(x, "blk", forward)

    def send_prev(x):
        return lax.ppermute(x, "blk", backward)

    def swap(x):
        return lax.ppermute(x, "head", exchange)

    ids = jnp.stack([lax.axis_index("blk"), lax.axis_index("head")]).astype(i32)
    given = jnp.concatenate([ids, span_len, dec_count, span_start, cache_len[0]])
    caches = (queries, latent_cache, new_latent, value_weight)
    tab, *lead, decoded, busy, which, alive = attend(table, order, given, *caches, 0, 2, None)

    def choose(special, usual, flag=busy):
        return jnp.where(jnp.broadcast_to(flag > 0, usual.shape), special, usual)


    packed = list(pack(tab, residual, ranks, cores))
    pieces = [None] * len(packed)

    def send_piece(k):
        pairs = [
            (i * cores + c, (i + k + len(packed) * c) % ranks * cores + c)
            for i in range(ranks)
            for c in range(cores)
            if k + c > 0
        ]
        pieces[k] = lax.ppermute(packed[k], ("blk", "head"), pairs)

    for k in range(1, len(packed)):
        send_piece(k)
    decoded, packed = lax.optimization_barrier((decoded, packed))
    packed = list(packed)
    follow = attend(table, order, tab, *caches, 1, 2, decoded)
    follow, pieces[1:], packed[0], out_weight = lax.optimization_barrier(
        (follow, pieces[1:], packed[0], out_weight)
    )
    send_piece(0)

    total = None
    chains = []
    for head, main, extra in (lead, follow):
        chains.append((head, main, extra, [], []))
    for step in range(reach):
        for part, (head, main, extra, behind, ahead) in enumerate(chains):
            if step == 0:
                out_f, out_b = head, main
            elif step == 1:
                out_f, out_b = choose(main, behind[0]), choose(extra, ahead[0])
            else:
                out_f = choose(behind[step - 2], behind[step - 1])
                out_b = choose(ahead[step - 2], ahead[step - 1])
            out_f, out_b = lax.optimization_barrier((out_f, out_b))
            behind.append(send_next(out_f))
            ahead.append(send_prev(out_b))
    gathered = [[main] + behind + ahead + [extra] for _, main, extra, behind, ahead in chains]
    gathered[0][2], pieces = lax.optimization_barrier((gathered[0][2], pieces))
    shared = swap(share(tab, packed[0], pieces, cores))
    gathered[0], shared = lax.optimization_barrier((gathered[0], shared))
    for part in range(2):
        total = project(tab, table, gathered[part], total, out_weight, part, 2, cores)
    kept, other = total
    res_here = placed_rows(tab, packed[0], shared, pieces, cores)
    stream = (kept + swap(other).astype(f32) + res_here.astype(f32)).astype(bf16)

    gain = norm_gain.reshape(ranks, 1, features)
    weights = (gain, gate_weight, up_weight)
    cut = -(-stream.shape[0] // 32) * 16
    back, fore = stream, stream
    sums = expand(tab, [[stream]], [swap(stream)], [RANK], *weights, None, False)
    blocks, owners = [stream], [RANK]
    done = None
    for step in range(1, reach + 1):
        if done is not None:
            back, fore, done = lax.optimization_barrier((back, fore, done))
        done = sums
        if step < reach:
            back, fore = send_next(back), send_prev(fore)
            arrived = [[back], [fore]]
            from_owner = [table.owner_back + step, table.owner_fore + step]
        else:
            arrived = [[send_next(back[:cut]), send_prev(fore[cut:])]]
            from_owner = [table.owner_back + step]
        tied, sums = lax.optimization_barrier((arrived, sums))
        if step < reach:
            others = [swap(jnp.concatenate([x for (x,) in tied], 0))]
        else:
            others = [swap(x) for x in tied[0]]
        sums = expand(tab, arrived, others, from_owner, *weights, sums, step == reach)
        blocks += [x[0] if len(x) == 1 else jnp.concatenate(x, 0) for x in arrived]
        owners += from_owner
    (hidden,) = sums
    own = collect(tab, blocks, owners, half).astype(f32)

    parts = contract_parts
    theirs = [swap(contract(hidden, down_weight, part, parts, 1)) for part in range(parts)]
    mine = [contract(hidden, down_weight, part, parts, 0) for part in range(parts)]
    mine = lax.optimization_barrier(mine)
    columns = width // parts
    lows, highs = [], []
    for part in range(parts):
        got_f, got_b = [], []
        *owned, main, extra = pick(tab, table, mine[part], theirs[part], half)
        for step in range(1, reach + 1):
            out_f, out_b = owned[2 * step - 2], owned[2 * step - 1]
            if step == 2:
                out_f = out_f + choose(jnp.zeros_like(out_f), got_f[0].astype(f32))
                out_b = out_b + choose(jnp.zeros_like(out_b), got_b[0].astype(f32))
            elif step > 2:
                out_f = out_f + choose(got_f[step - 3], got_f[step - 2]).astype(f32)
                out_b = out_b + choose(got_b[step - 3], got_b[step - 2]).astype(f32)
            out_f, out_b = lax.optimization_barrier((out_f.astype(bf16), out_b.astype(bf16)))
            got_f.append(send_next(out_f))
            got_b.append(send_prev(out_b))
        if part > 0:
            lows, highs, got_f[-1] = lax.optimization_barrier((lows, highs, got_f[-1]))
        at = slice(part * columns, (part + 1) * columns)
        main = main + own[:half, at] + got_f[-1].astype(f32)
        main = (main + choose(got_b[-2], got_b[-1]).astype(f32)).astype(bf16)
        extra = extra + own[half:, at] + got_f[-2].astype(f32) + got_b[-1].astype(f32)
        extra = extra.astype(bf16)
        received = swap(choose(main, extra, which))
        stays = choose(extra, main, which)
        lows.append(choose(received, stays, which))
        highs.append(choose(stays, received, which))
    result = jnp.concatenate([jnp.concatenate(lows, 1), jnp.concatenate(highs, 1)], 0)
    return choose(result, jnp.zeros_like(result), alive)


def solution(mesh):
    placed = (
        P(("groups", "blk"), "head"),
        P(("groups", "blk"), None, None),
        P(None, ("groups", "blk")),
        P("groups"),
        P("groups"),
        P(("groups", "blk")),
        P(("groups", "blk"), None),
        P("head", None, None),
        P("head", "blk"),
        P(("groups", "blk"), None),
        P(),
        P(None, ("blk", "head")),
        P(None, ("blk", "head")),
        P(("blk", "head"), None),
    )
    order = ring_order(mesh)
    return jax.shard_map(
        lambda *args: on_device(order, *args),
        mesh=mesh,
        in_specs=placed,
        out_specs=P(("groups", "blk", "head"), None),
        check_vma=False,
    )
```

```python
import functools

import jax
import jax.numpy as jnp
from jax import lax
from jax.experimental import pallas as pl
from jax.experimental.pallas import tpu as pltpu
from jax.sharding import PartitionSpec as P

score_scale = 192.0 ** (-0.5)
norm_eps = 1e-06
masked_score = -1e30
f32, bf16, i32 = jnp.float32, jnp.bfloat16, jnp.int32
SMEM = pltpu.SMEM
MIB = 1 << 20

RANK, CORE, BUSY, BUSY_RANK, SPAN, DEC, LIVE, START, LENGTHS = range(9)


def mm(a, b):
    return lax.dot_general(a, b, (((1,), (0,)), ((), ())), preferred_element_type=f32)


def mm_nt(a, b):
    return lax.dot_general(a, b, (((1,), (1,)), ((), ())), preferred_element_type=f32)


def in_hbm(x):
    return pltpu.with_memory_space_constraint(x, pltpu.HBM)


def smem():
    return pl.BlockSpec(memory_space=SMEM)


def whole():
    return pl.BlockSpec(memory_space=pltpu.VMEM)


def params(mib=32):
    return pltpu.CompilerParams(vmem_limit_bytes=mib * MIB)


def cost(flops, moved, exps=0):
    return pl.CostEstimate(flops=int(flops), bytes_accessed=int(moved), transcendentals=int(exps))


def ring_order(mesh):
    count = mesh.shape["blk"]
    natural = list(range(count))
    snake = natural[0::2] + natural[1::2][::-1]
    names = list(mesh.axis_names)
    axes = [names.index("blk")] + [a for a, x in enumerate(names) if x != "blk"]
    lane = mesh.devices.transpose(axes)
    firsts = [lane[i].reshape(-1)[0] for i in natural]
    if not all(hasattr(d, "coords") for d in firsts):
        return snake

    def length(order):
        hops = zip(order, order[1:] + order[:1])
        return sum(
            sum(abs(u - v) for u, v in zip(firsts[a].coords, firsts[b].coords)) for a, b in hops
        )

    return natural if length(natural) <= length(snake) else snake


class Table:
    def __init__(self, ranks, slots):
        self.reach = ranks // 2
        self.source = LENGTHS + slots
        self.ahead = self.source + ranks + 1
        self.behind = self.ahead + self.reach + 1
        self.owner_back = self.behind + self.reach + 1
        self.owner_fore = self.owner_back + self.reach + 1
        self.who = self.owner_fore + self.reach + 1
        self.at = self.who + ranks
        self.size = self.at + ranks


def table_kernel(table, order, given, out):
    reach, ranks = table.reach, len(order)
    span = [given[2 + i] for i in range(ranks)]
    dec = [given[2 + ranks + i] for i in range(ranks)]
    lengths = 3 + 2 * ranks
    for i, r in enumerate(order):
        out[table.who + i] = r
        out[table.at + r] = i
    rank, core = given[0], given[1]
    most, busy_rank = span[0] + dec[0], jnp.int32(0)
    for i in range(1, ranks):
        here = span[i] + dec[i]
        busy_rank = jnp.where(here > most, i, busy_rank)
        most = jnp.maximum(here, most)
    busy = rank == busy_rank

    def wrap(x):
        x = jnp.where(x < 0, x + ranks, x)
        return jnp.where(x >= ranks, x - ranks, x)

    place, busy_place = out[table.at + rank], out[table.at + busy_rank]
    to_busy = wrap(busy_place - place)
    from_busy = wrap(place - busy_place)

    def node_ahead(k):
        far = (to_busy > 0) & (k > to_busy + 1)
        slot = out[table.who + wrap(place + k - jnp.where(far, 1, 0))]
        return jnp.where((to_busy > 0) & (k == to_busy + 1), ranks, slot)

    def node_behind(k):
        far = (from_busy > 0) & (k > from_busy)
        slot = out[table.who + wrap(place - k + jnp.where(far, 1, 0))]
        return jnp.where((from_busy > 0) & (k == from_busy), ranks, slot)

    out[RANK] = rank
    out[CORE] = core
    out[BUSY] = jnp.where(busy, 1, 0)
    out[BUSY_RANK] = busy_rank
    out[SPAN] = given[2 + rank]
    out[DEC] = given[2 + ranks + rank]
    out[LIVE] = given[2 + rank] + given[2 + ranks + rank]
    out[START] = given[lengths - 1]
    for j in range(given.shape[0] - lengths):
        out[LENGTHS + j] = given[lengths + j]
    out[table.source + rank] = 0
    for k in range(1, reach + 1):
        out[table.ahead + k] = node_ahead(k)
        out[table.behind + k] = node_behind(k)
        out[table.owner_back + k] = out[table.who + wrap(place - k)]
        out[table.owner_fore + k] = out[table.who + wrap(place + k)]
        out[table.source + node_behind(k)] = k
        last = jnp.where(busy, ranks, node_ahead(k)) if k == reach else node_ahead(k)
        out[table.source + last] = reach + k


def attend_kernel(
    table, order, heads, first, count, group, rows, lat, value, lead, *refs
):
    if lead:
        given, refs = refs[0], refs[1:]
        q_hbm, cache_hbm, fresh_hbm, vw_hbm, tab, head, main, extra, later = refs[:9]
        flags, refs = refs[9:12], refs[12:]
        q, keys, vw, latent, fz, fresh, q_sem, key_sem, vw_sem, dq = refs
        loaded, base = heads, 0
    else:
        tab, q_hbm, cache_hbm, fresh_hbm, vw_hbm, decoded_here, head, main, extra = refs[:9]
        q, keys, vw, latent, fz, fresh, q_sem, key_sem, vw_sem = refs[9:]
        loaded, base = count, first
    cached, wide = keys.shape[2], keys.shape[1]
    slots = cache_hbm.shape[0] - 1
    odd_slot = keys.shape[0] - 1
    shift, pair, dr = wide - lat, 2 * lat, 8
    groups, pairs = count // group, group // 2
    loads = loaded // group

    def q_copy(g):
        source = pl.ds((base + g * group) * lat, group * lat)
        return pltpu.make_async_copy(
            q_hbm.at[:, source], q.at[:, pl.ds(g * group * lat, group * lat)], q_sem.at[g]
        )

    def vw_copy(g):
        source = pl.ds(first + g * group, group)
        return pltpu.make_async_copy(vw_hbm.at[source], vw.at[pl.ds(g * group, group)], vw_sem.at[g])

    even_copy = pltpu.make_async_copy(cache_hbm.at[0], keys.at[0, pl.ds(0, lat)], key_sem.at[0])
    odd_copy = pltpu.make_async_copy(
        cache_hbm.at[0], keys.at[odd_slot, pl.ds(shift, lat)], key_sem.at[1]
    )
    waiting = [q_copy(g) for g in range(1, loads)]
    if lead:
        rest_copy = pltpu.make_async_copy(
            cache_hbm.at[pl.ds(1, slots)], keys.at[pl.ds(1, slots), pl.ds(0, lat)], key_sem.at[2]
        )
        waiting.append(rest_copy)
    waiting += [vw_copy(g) for g in range(groups)]

    def start_next(number):
        for _ in range(min(number, len(waiting))):
            waiting.pop(0).start()

    fresh_copy = pltpu.make_async_copy(fresh_hbm, fresh, key_sem.at[3])
    fresh_copy.start()
    even_copy.start()
    q_copy(0).start()
    odd_copy.start()
    start_next(1)
    if lead:
        table_kernel(table, order, given, tab)
    span, decs = tab[SPAN], tab[DEC]

    def onehot(shape, row_dim, slot_dim):
        r = lax.broadcasted_iota(i32, shape, row_dim)
        j = lax.broadcasted_iota(i32, shape, slot_dim)
        return jnp.where((r == span + j) & (j < decs), 1.0, 0.0).astype(bf16)

    tail = jnp.zeros((shift, cached), bf16)
    for s in range(odd_slot):
        keys[s, lat:] = tail
    keys[odd_slot, :shift] = tail
    fz[...] = jnp.zeros_like(fz)
    fresh_copy.wait()
    fz[:rows, :lat] = fresh[...].astype(f32)
    fresh_even = fz[...].astype(bf16)
    fresh_odd = pltpu.roll(fz[...], shift, 1).astype(bf16)

    m = pairs * rows
    cols = cached + fz.shape[0]
    row = lax.broadcasted_iota(i32, (m, 1), 0) % rows
    col = lax.broadcasted_iota(i32, (m, cols), 1)
    seen = col < jnp.where(col < cached, tab[START], cached + 1 + row)

    def span_latent(lhs, slot, fresh_keys):
        s = jnp.concatenate([mm(lhs, keys[slot]), mm_nt(lhs, fresh_keys)], 1)
        s = jnp.where(seen, s * score_scale, masked_score)
        e = jnp.exp(s - jnp.max(s, axis=1, keepdims=True))
        w = (e * (1.0 / jnp.sum(e, axis=1, keepdims=True))).astype(bf16)
        o = mm_nt(w[:, :cached], keys[0, :value]) + mm(w[:, cached:], fresh_even[:, :value])
        return jnp.where(row < span, o, 0.0).astype(bf16)

    even_copy.wait()
    odd_copy.wait()
    for g in range(groups):
        q_copy(g).wait()
        start_next(2)
        start = g * group * lat
        for odd in range(2):
            off = start + odd * (pair - wide)
            lhs = jnp.concatenate(
                [q[:, off + pair * p : off + pair * p + wide] for p in range(pairs)], 0
            )
            latent[g, odd] = span_latent(lhs, odd_slot * odd, fresh_odd if odd else fresh_even)
    start_next(len(waiting))

    if lead:
        for g in range(groups, loads):
            q_copy(g).wait()
        pick = onehot((16, rows), 1, 0)
        for p in range(heads // 2):
            got = mm(pick, q[:, pair * p : pair * (p + 1)])[:dr]
            dq[2 * p * dr : (2 * p + 1) * dr] = got[:, :wide]
            dq[(2 * p + 1) * dr : (2 * p + 2) * dr] = pltpu.roll(
                got[:, pair - wide :], wide - shift, 1
            )
        n = heads * dr
        queries = dq[...].astype(bf16)
        slot = lax.broadcasted_iota(i32, (n, 1), 0) % dr
        rest_copy.wait()
        length = jnp.zeros((n, 1), i32)
        scores = jnp.zeros((n, cached), f32)
        for s in range(slots):
            scores = jnp.where(slot == s, mm(queries, keys[s + 1]), scores)
            length = jnp.where(slot == s, tab[LENGTHS + s], length)
        unmasked = lax.broadcasted_iota(i32, (n, cached), 1) < length
        scores = jnp.where(unmasked, scores * score_scale, masked_score)
        own = mm_nt(queries, fresh_even)
        column = lax.broadcasted_iota(i32, own.shape, 1)
        own = jnp.sum(jnp.where(column == span + slot, own, 0.0), axis=1, keepdims=True)
        own = own * score_scale
        peak = jnp.maximum(jnp.max(scores, axis=1, keepdims=True), own)
        e = jnp.exp(scores - peak)
        e_own = jnp.exp(own - peak)
        total = jnp.sum(e, axis=1, keepdims=True) + e_own
        w = e / total
        acc = jnp.zeros((n, value), f32)
        for s in range(slots):
            acc = acc + mm_nt(jnp.where(slot == s, w, 0.0).astype(bf16), keys[s + 1, :value])
        own_value = mm(pick, fresh[:, :value])[:dr]
        own_value = jnp.broadcast_to(own_value[None], (heads, dr, value)).reshape(n, value)
        dec = (acc + (e_own / total).astype(bf16).astype(f32) * own_value).astype(bf16)
        later[...] = dec[count * dr :]
        for flag, at in zip(flags, (BUSY, CORE)):
            flag[...] = jnp.full(flag.shape, tab[at].astype(f32))
        block = rows // 2
        slot_row = tab[CORE] * block + lax.broadcasted_iota(i32, (block, 1), 0)
        flags[2][...] = jnp.where(slot_row < tab[LIVE], 1.0, 0.0)
        dec = dec[: count * dr]
    else:
        dec = decoded_here[...]

    place = onehot((rows, 16), 0, 1)
    vh = vw.shape[2]
    block = rows // 2
    for g in range(groups):
        vw_copy(g).wait()
        values, decoded = [], []
        for p in range(pairs):
            h = g * group + 2 * p
            lhs = jnp.concatenate(
                [
                    latent[g, 0, p * rows : (p + 1) * rows],
                    latent[g, 1, p * rows : (p + 1) * rows],
                    dec[h * dr : (h + 2) * dr],
                ],
                0,
            )
            r = mm(lhs, jnp.concatenate([vw[h], vw[h + 1]], 1))
            values += [r[:rows, :vh], r[rows : 2 * rows, vh:]]
            decoded += [r[2 * rows : 2 * rows + dr, :vh], r[2 * rows + dr :, vh:]]
        decoded = jnp.concatenate(decoded, 1)
        decoded = jnp.concatenate([decoded, jnp.zeros_like(decoded)], 0).astype(bf16)
        out = (jnp.concatenate(values, 1) + mm(place, decoded)).astype(bf16)
        at = slice(g * group * vh, (g + 1) * group * vh)
        main[:, at] = out[:block]
        extra[:, at] = out[block:]
        head[:, at] = jnp.where(tab[BUSY] == 1, out[block:], out[:block])


def attend(table, order, numbers, queries, cache, fresh, vw, part, parts, decoded):
    rows, heads = queries.shape[0], vw.shape[0]
    lat = queries.shape[1] // heads
    slots, _, cached = cache.shape
    value, vh = vw.shape[1:]
    count = heads // parts
    group = min(8, count)
    lead = decoded is None
    loaded = heads if lead else count
    wide = -(-lat // 128) * 128
    half = jax.ShapeDtypeStruct((rows // 2, count * vh), bf16)
    hbm = pl.BlockSpec(memory_space=pltpu.HBM)
    scratch = [
        pltpu.VMEM((rows, loaded * lat), bf16),
        pltpu.VMEM((slots + 1 if lead else 2, wide, cached), bf16),
        pltpu.VMEM((count, value, vh), bf16),
        pltpu.VMEM((count // group, 2, group // 2 * rows, value), bf16),
        pltpu.VMEM((-(-rows // 128) * 128, wide), f32),
        pltpu.VMEM(fresh.shape[::-1], bf16),
        pltpu.SemaphoreType.DMA((loaded // group,)),
        pltpu.SemaphoreType.DMA((4,)),
        pltpu.SemaphoreType.DMA((count // group,)),
    ]
    out_shape, out_specs = [half] * 3, [whole()] * 3
    ins = [smem()] + [hbm] * 4
    args = [numbers, in_hbm(queries), in_hbm(cache), in_hbm(fresh.T), in_hbm(vw)]
    if lead:
        scratch.append(pltpu.VMEM((heads * 8, wide), f32))
        out_shape = [jax.ShapeDtypeStruct((table.size,), i32)] + out_shape
        out_shape += [jax.ShapeDtypeStruct(((heads - count) * 8, value), bf16)]
        out_shape += [jax.ShapeDtypeStruct((n, 1), f32) for n in (1, 1, rows // 2)]
        out_specs = [smem()] + out_specs + [whole()] * 4
    else:
        ins.append(whole())
        args.append(decoded)
    return pl.pallas_call(
        functools.partial(
            attend_kernel, table, order, heads, part * count, count, group, rows, lat, value, lead
        ),
        in_specs=ins,
        out_specs=out_specs,
        out_shape=out_shape,
        scratch_shapes=scratch,
        compiler_params=params(24),
        cost_estimate=cost(
            2 * rows * count * (cached + rows) * (lat + value),
            2 * (queries.size + cache.size + vw.size) // parts,
            rows * count * (cached + rows),
        ),
        name="attend",
    )(*args)


def pack_kernel(ranks, cores, features, tab, res, *outs):
    for k in range(ranks // cores):
        target = tab[RANK] + k + (ranks // cores) * tab[CORE]
        target = jnp.where(target >= ranks, target - ranks, target)

        def put(columns, k=k):
            outs[k][...] = res[:, columns]

        if features % 128 == 0:
            put(pl.ds(pl.multiple_of(target * features, 128), features))
        else:
            for t in range(ranks):
                pl.when(target == t)(functools.partial(put, slice(t * features, (t + 1) * features)))


def pack(tab, residual, ranks, cores):
    rows, width = residual.shape
    features = width // ranks
    count = ranks // cores
    return pl.pallas_call(
        functools.partial(pack_kernel, ranks, cores, features),
        in_specs=[smem(), whole()],
        out_specs=[whole()] * count,
        out_shape=[jax.ShapeDtypeStruct((rows, features), bf16)] * count,
        compiler_params=params(8),
        cost_estimate=cost(0, 4 * residual.size),
        name="pack",
    )(tab, residual)


def share_kernel(half, tab, own, *refs):
    pieces, out = refs[:-1], refs[-1]
    other = 1 - tab[CORE]
    block = own.shape[0] // 2
    low = pl.multiple_of(other * half, half)
    high = pl.multiple_of(block + other * half, half)

    def put(k, piece):
        out[2 * k * half : (2 * k + 1) * half] = piece[pl.ds(low, half)]
        out[(2 * k + 1) * half : (2 * k + 2) * half] = piece[pl.ds(high, half)]

    for k, piece in enumerate(pieces):
        if k > 0:
            put(k, piece)
        else:
            pl.when(tab[CORE] == 0)(functools.partial(put, k, own))
            pl.when(tab[CORE] != 0)(functools.partial(put, k, piece))


def share(tab, own, pieces, cores):
    rows, features = own.shape
    half = rows // 2 // cores
    return pl.pallas_call(
        functools.partial(share_kernel, half),
        in_specs=[smem()] + [whole()] * (1 + len(pieces)),
        out_specs=whole(),
        out_shape=jax.ShapeDtypeStruct((2 * half * len(pieces), features), bf16),
        compiler_params=params(8),
        cost_estimate=cost(0, 4 * own.size * len(pieces)),
        name="share",
    )(tab, own, *pieces)


def project_kernel(source, nodes, block, half, part, first, tab, *refs):
    blocks, refs = refs[: nodes + 1], refs[nodes + 1 :]
    before = None if first else refs[0]
    weight, kept, given, acc = refs[-4:]
    step = pl.program_id(0)
    depth = blocks[0].shape[1] // pl.num_programs(0)
    columns = pl.ds(pl.multiple_of(step * depth, 128), depth)
    last = jnp.where(tab[BUSY] == 1, blocks[nodes][:, columns], blocks[nodes - 1][:, columns])
    lhs = jnp.concatenate([b[:, columns] for b in blocks[: nodes - 1]] + [last], 0)
    got = mm(lhs, weight[pl.ds(pl.multiple_of(part * blocks[0].shape[1] + step * depth, 128), depth)])

    @pl.when(step == 0)
    def _():
        acc[...] = got if first else got + before[...]

    @pl.when(step > 0)
    def _():
        acc[...] += got

    @pl.when(step == pl.num_programs(0) - 1)
    def _():
        core = tab[CORE]
        for k in range(nodes):
            at = tab[source + k] * block
            kept[k * half : (k + 1) * half] = acc[pl.ds(pl.multiple_of(at + core * half, half), half)]
            other = acc[pl.ds(pl.multiple_of(at + (1 - core) * half, half), half)]
            given[k * half : (k + 1) * half] = other.astype(bf16)


def project_part_kernel(nodes, part, first, tab, *refs):
    blocks, refs = refs[: nodes + 1], refs[nodes + 1 :]
    weight, out = refs[-2:]
    step = pl.program_id(0)
    depth = blocks[0].shape[1] // pl.num_programs(0)
    columns = pl.ds(pl.multiple_of(step * depth, 128), depth)
    last = jnp.where(tab[BUSY] == 1, blocks[nodes][:, columns], blocks[nodes - 1][:, columns])
    lhs = jnp.concatenate([b[:, columns] for b in blocks[: nodes - 1]] + [last], 0)
    got = mm(lhs, weight[pl.ds(pl.multiple_of(part * blocks[0].shape[1] + step * depth, 128), depth)])

    @pl.when(step == 0)
    def _():
        out[...] = got if first else got + refs[0][...]

    @pl.when(step > 0)
    def _():
        out[...] += got


def project(tab, table, blocks, before, weight, part, parts, cores):
    block, width = blocks[0].shape
    nodes = len(blocks) - 1
    half = block // cores
    features = weight.shape[1]
    depth = width
    steps = width // depth
    total = jax.ShapeDtypeStruct((nodes * block, features), f32)
    final = part == parts - 1
    first = before is None
    ins = [smem()] + [whole()] * (nodes + 2 + (not first))
    args = [tab, *blocks] + ([] if first else [before]) + [weight]
    estimate = cost(
        2 * nodes * block * width * features, 2 * (nodes * block * width + width * features)
    )
    if not final:
        return pl.pallas_call(
            functools.partial(project_part_kernel, nodes, part, first),
            grid=(steps,),
            in_specs=ins,
            out_specs=pl.BlockSpec(total.shape, lambda i: (0, 0)),
            out_shape=total,
            compiler_params=params(16),
            cost_estimate=estimate,
            name="project",
        )(*args)
    return pl.pallas_call(
        functools.partial(project_kernel, table.source, nodes, block, half, part, first),
        grid=(steps,),
        in_specs=ins,
        out_specs=[pl.BlockSpec((nodes * half, features), lambda i: (0, 0))] * 2,
        out_shape=[
            jax.ShapeDtypeStruct((nodes * half, features), f32),
            jax.ShapeDtypeStruct((nodes * half, features), bf16),
        ],
        scratch_shapes=[pltpu.VMEM(total.shape, f32)],
        compiler_params=params(16),
        cost_estimate=estimate,
        name="project",
    )(*args)


def place_kernel(ranks, half, tab, own, shared, *refs):
    pieces, out = refs[:-1], refs[-1]
    rank, core, busy_rank = tab[RANK], tab[CORE], tab[BUSY_RANK]
    count = len(pieces)
    block = own.shape[0] // 2

    def put(slot, extra):
        out[pl.ds(pl.multiple_of(slot * half, half), half)] = extra

    def put_both(owner, main, extra):
        put(owner, main())

        @pl.when(owner == busy_rank)
        def _():
            put(ranks, extra())

    def owner_of(k, c):
        owner = rank - k - count * c
        return jnp.where(owner < 0, owner + ranks, owner)

    low = pl.ds(pl.multiple_of(core * half, half), half)
    high = pl.ds(pl.multiple_of(block + core * half, half), half)
    for k, piece in enumerate(pieces):

        def received(piece=piece, k=k):
            put_both(owner_of(k, core), lambda: piece[low], lambda: piece[high])

        if k > 0:
            received()
        else:
            pl.when(core == 0)(functools.partial(received, own))
            pl.when(core != 0)(received)
        at = 2 * k * half
        put_both(
            owner_of(k, 1 - core),
            lambda at=at: shared[at : at + half],
            lambda at=at: shared[at + half : at + 2 * half],
        )


def placed_rows(tab, own, shared, pieces, cores):
    rows, features = own.shape
    half = rows // 2 // cores
    ranks = cores * len(pieces)
    return pl.pallas_call(
        functools.partial(place_kernel, ranks, half),
        in_specs=[smem()] + [whole()] * (2 + len(pieces)),
        out_specs=whole(),
        out_shape=jax.ShapeDtypeStruct(((ranks + 1) * half, features), bf16),
        compiler_params=params(8),
        cost_estimate=cost(0, 4 * (ranks + 1) * half * features),
        name="place",
    )(tab, own, shared, *pieces)


def expand_kernel(pieces, others, first, final, width, turned, owners, tab, *refs):
    count = len(pieces)
    blocks = []
    for number in pieces:
        blocks.append(refs[:number])
        refs = refs[number:]
    theirs, refs = refs[:others], refs[others:]
    gain, gate, up = refs[:3]
    refs = refs[3:]
    if not first:
        before, refs = refs[:3], refs[3:]
    if final:
        hidden, refs = refs[0], refs[1:]
    gates, ups, squares = refs
    step = pl.program_id(0)
    for i in range(count):

        @pl.when(step == i)
        def _(i=i):
            both = [x[...] for x in blocks[i]]
            for x in theirs:
                rows = x.shape[0] // count
                both.append(x[i * rows : (i + 1) * rows])
            both = jnp.concatenate(both, 0).astype(f32)
            rows_of = both.shape[1]
            scaled = (both * gain[0]).astype(bf16)
            if turned:
                at = pl.ds(pl.multiple_of(tab[owners[i]] * rows_of, 128), rows_of)
                products = mm_nt(scaled, gate[:, at]), mm_nt(scaled, up[:, at])
            else:
                products = mm(scaled, gate[...]), mm(scaled, up[...])
            values = (
                *products,
                jnp.sum(both * both, axis=1, keepdims=True),
            )
            for n, (ref, value) in enumerate(zip((gates, ups, squares), values)):
                if i == 0:
                    ref[...] = value if first else value + before[n][...]
                else:
                    ref[...] += value

    if final:

        @pl.when(step == count - 1)
        def _():
            scale = lax.rsqrt(squares[...] / width + norm_eps)
            g = gates[...] * scale
            hidden[...] = (g / (1.0 + jnp.exp(-g)) * (ups[...] * scale)).astype(bf16)


def expand(tab, mines, theirs, owners, gain, gate, up, before, final):
    count = len(mines)
    pieces = tuple(len(x) for x in mines)
    rows, features = sum(x.shape[0] for x in mines[0]), mines[0][0].shape[1]
    arrays = [x for own in mines for x in own] + theirs
    units = gate.shape[1]
    first = before is None
    width = gate.shape[0]

    def owner(i, tab):
        index = tab[owners[0]]
        for n in range(1, count):
            index = jnp.where(i == n, tab[owners[n]], index)
        return index

    def full(shape):
        return pl.BlockSpec(shape, lambda i, tab: (0,) * len(shape))

    sums = [(2 * rows, units), (2 * rows, units), (2 * rows, 1)]
    ins = [full(x.shape) for x in arrays]
    ins += [pl.BlockSpec((1, 1, features), lambda i, tab: (owner(i, tab), 0, 0))]
    turned = features % 128 == 0
    if turned:
        gate, up = gate.T, up.T
        ins += [pl.BlockSpec(memory_space=pltpu.VMEM)] * 2
    else:
        ins += [pl.BlockSpec((features, units), lambda i, tab: (owner(i, tab), 0))] * 2
    if not first:
        ins += [full(s) for s in sums]
    shapes = [jax.ShapeDtypeStruct(s, f32) for s in sums]
    out_shapes = [jax.ShapeDtypeStruct((2 * rows, units), bf16)] if final else shapes
    return pl.pallas_call(
        functools.partial(expand_kernel, pieces, len(theirs), first, final, width, turned, owners),
        grid_spec=pltpu.PrefetchScalarGridSpec(
            num_scalar_prefetch=1,
            grid=(count,),
            in_specs=ins,
            out_specs=[full(s.shape) for s in out_shapes],
            scratch_shapes=[pltpu.VMEM(s, f32) for s in sums] if final else [],
        ),
        out_shape=out_shapes,
        compiler_params=params(20),
        cost_estimate=cost(1, 1),
        name="expand",
    )(tab, *arrays, gain, gate, up, *([] if first else before))


def collect_kernel(owners, tab, *refs):
    out = refs[-1]
    if len(out.shape) == 2:
        half, features = out.shape[0] // 2, out.shape[1] // len(owners)
        for i, at in enumerate(owners):
            columns = pl.ds(pl.multiple_of(tab[at] * features, 128), features)
            out[:half, columns] = refs[2 * i][...]
            out[half:, columns] = refs[2 * i + 1][...]
        return
    half = out.shape[1] // 2
    for i, at in enumerate(owners):
        out[tab[at], :half] = refs[2 * i][...]
        out[tab[at], half:] = refs[2 * i + 1][...]


def collect(tab, blocks, owners, half):
    ranks = len(blocks)
    features = blocks[0].shape[1]
    ins, args = [], []
    for x in blocks:
        ins += [
            pl.BlockSpec((half, features), lambda i, tab: (tab[RANK], 0)),
            pl.BlockSpec((half, features), lambda i, tab: (ranks, 0)),
        ]
        args += [x, x]
    aligned = features % 128 == 0
    shape = (2 * half, ranks * features) if aligned else (ranks, 2 * half, features)
    out = pl.pallas_call(
        functools.partial(collect_kernel, owners),
        grid_spec=pltpu.PrefetchScalarGridSpec(
            num_scalar_prefetch=1,
            grid=(1,),
            in_specs=ins,
            out_specs=pl.BlockSpec(shape, lambda i, tab: (0,) * len(shape)),
        ),
        out_shape=jax.ShapeDtypeStruct(shape, bf16),
        compiler_params=params(10),
        cost_estimate=cost(0, 8 * ranks * half * features),
        name="collect",
    )(tab, *args)
    return out if aligned else out.transpose(1, 0, 2).reshape(2 * half, ranks * features)


def contract_kernel(begin, hidden, weight, out):
    wide = out.shape[1]
    at = pl.ds(pl.multiple_of(begin + pl.program_id(0) * wide, 128), wide)
    out[...] = mm(hidden[...], weight[:, at]).astype(bf16)


def contract(hidden, weight, part, parts, which):
    rows, units = hidden.shape[0] // 2, hidden.shape[1]
    columns = weight.shape[1] // parts
    wide = columns // 2 if columns % 256 == 0 else columns
    return pl.pallas_call(
        functools.partial(contract_kernel, part * columns),
        grid=(columns // wide,),
        in_specs=[pl.BlockSpec((rows, units), lambda i: (which, 0)), whole()],
        out_specs=pl.BlockSpec((rows, wide), lambda i: (0, i)),
        out_shape=jax.ShapeDtypeStruct((rows, columns), bf16),
        compiler_params=params(16),
        cost_estimate=cost(2 * rows * units * columns, 2 * (units + rows) * columns),
        name="contract",
    )(hidden, weight)


def pick_kernel(table, half, tab, mine, theirs, *outs):
    busy = tab[BUSY] == 1
    reach = table.reach
    for step in range(1, reach + 1):
        for n, where in enumerate((table.ahead, table.behind)):
            at = pl.multiple_of(tab[where + reach + 1 - step] * half, half)
            total = mine[pl.ds(at, half)].astype(f32) + theirs[pl.ds(at, half)].astype(f32)
            if step == 1 and n == 0:
                total = jnp.where(busy, 0.0, total)
            outs[2 * (step - 1) + n][...] = total
    for n, slot in enumerate((tab[RANK], 2 * reach)):
        at = pl.multiple_of(slot * half, half)
        outs[2 * reach + n][...] = mine[pl.ds(at, half)].astype(f32) + theirs[pl.ds(at, half)].astype(f32)


def pick(tab, table, mine, theirs, half):
    columns = mine.shape[1]
    count = 2 * table.reach + 2
    out = jax.ShapeDtypeStruct((half, columns), f32)
    return pl.pallas_call(
        functools.partial(pick_kernel, table, half),
        in_specs=[smem(), whole(), whole()],
        out_specs=[whole()] * count,
        out_shape=[out] * count,
        compiler_params=params(10),
        cost_estimate=cost(0, 8 * count * half * columns),
        name="pick",
    )(tab, mine, theirs)


contract_parts = 2


def on_device(
    order,
    queries,
    latent_cache,
    new_latent,
    span_len,
    dec_count,
    span_start,
    cache_len,
    value_weight,
    out_weight,
    residual,
    norm_gain,
    gate_weight,
    up_weight,
    down_weight,
):
    ranks = len(order)
    reach = ranks // 2
    cores = lax.axis_size("head")
    rows_dev, width = residual.shape
    half = rows_dev // 2 // cores
    features = out_weight.shape[1]
    table = Table(ranks, cache_len.shape[1])

    forward = [(order[i], order[(i + 1) % ranks]) for i in range(ranks)]
    backward = [(b, a) for a, b in forward]
    exchange = [(c, cores - 1 - c) for c in range(cores)]

    def send_next(x):
        return lax.ppermute(x, "blk", forward)

    def send_prev(x):
        return lax.ppermute(x, "blk", backward)

    def swap(x):
        return lax.ppermute(x, "head", exchange)

    ids = jnp.stack([lax.axis_index("blk"), lax.axis_index("head")]).astype(i32)
    given = jnp.concatenate([ids, span_len, dec_count, span_start, cache_len[0]])
    caches = (queries, latent_cache, new_latent, value_weight)
    tab, *lead, decoded, busy, which, alive = attend(table, order, given, *caches, 0, 2, None)

    def choose(special, usual, flag=busy):
        return jnp.where(jnp.broadcast_to(flag > 0, usual.shape), special, usual)


    packed = list(pack(tab, residual, ranks, cores))
    pieces = [None] * len(packed)

    def send_piece(k):
        pairs = [
            (i * cores + c, (i + k + len(packed) * c) % ranks * cores + c)
            for i in range(ranks)
            for c in range(cores)
            if k + c > 0
        ]
        pieces[k] = lax.ppermute(packed[k], ("blk", "head"), pairs)

    for k in range(1, len(packed)):
        send_piece(k)
    decoded, packed = lax.optimization_barrier((decoded, packed))
    packed = list(packed)
    follow = attend(table, order, tab, *caches, 1, 2, decoded)
    follow, pieces[1:], packed[0], out_weight = lax.optimization_barrier(
        (follow, pieces[1:], packed[0], out_weight)
    )
    send_piece(0)

    total = None
    chains = []
    for head, main, extra in (lead, follow):
        chains.append((head, main, extra, [], []))
    for step in range(reach):
        for part, (head, main, extra, behind, ahead) in enumerate(chains):
            if step == 0:
                out_f, out_b = head, main
            elif step == 1:
                out_f, out_b = choose(main, behind[0]), choose(extra, ahead[0])
            else:
                out_f = choose(behind[step - 2], behind[step - 1])
                out_b = choose(ahead[step - 2], ahead[step - 1])
            out_f, out_b = lax.optimization_barrier((out_f, out_b))
            behind.append(send_next(out_f))
            ahead.append(send_prev(out_b))
    gathered = [[main] + behind + ahead + [extra] for _, main, extra, behind, ahead in chains]
    gathered[0][2], pieces = lax.optimization_barrier((gathered[0][2], pieces))
    shared = swap(share(tab, packed[0], pieces, cores))
    gathered[0], shared = lax.optimization_barrier((gathered[0], shared))
    for part in range(2):
        total = project(tab, table, gathered[part], total, out_weight, part, 2, cores)
    kept, other = total
    res_here = placed_rows(tab, packed[0], shared, pieces, cores)
    stream = (kept + swap(other).astype(f32) + res_here.astype(f32)).astype(bf16)

    gain = norm_gain.reshape(ranks, 1, features)
    weights = (gain, gate_weight, up_weight)
    cut = -(-stream.shape[0] // 32) * 16
    back, fore = stream, stream
    sums = expand(tab, [[stream]], [swap(stream)], [RANK], *weights, None, False)
    blocks, owners = [stream], [RANK]
    done = None
    for step in range(1, reach + 1):
        if done is not None:
            back, fore, done = lax.optimization_barrier((back, fore, done))
        done = sums
        if step < reach:
            back, fore = send_next(back), send_prev(fore)
            arrived = [[back], [fore]]
            from_owner = [table.owner_back + step, table.owner_fore + step]
        else:
            arrived = [[send_next(back[:cut]), send_prev(fore[cut:])]]
            from_owner = [table.owner_back + step]
        tied, sums = lax.optimization_barrier((arrived, sums))
        if step < reach:
            others = [swap(jnp.concatenate([x for (x,) in tied], 0))]
        else:
            others = [swap(x) for x in tied[0]]
        sums = expand(tab, arrived, others, from_owner, *weights, sums, step == reach)
        blocks += [x[0] if len(x) == 1 else jnp.concatenate(x, 0) for x in arrived]
        owners += from_owner
    (hidden,) = sums

    parts = contract_parts
    theirs = [swap(contract(hidden, down_weight, part, parts, 1)) for part in range(parts)]
    mine = [contract(hidden, down_weight, part, parts, 0) for part in range(parts)]
    mine = lax.optimization_barrier(mine)
    columns = width // parts
    lows, highs = [], []
    for part in range(parts):
        got_f, got_b = [], []
        *owned, main, extra = pick(tab, table, mine[part], theirs[part], half)
        for step in range(1, reach + 1):
            out_f, out_b = owned[2 * step - 2], owned[2 * step - 1]
            if step == 2:
                out_f = out_f + choose(jnp.zeros_like(out_f), got_f[0].astype(f32))
                out_b = out_b + choose(jnp.zeros_like(out_b), got_b[0].astype(f32))
            elif step > 2:
                out_f = out_f + choose(got_f[step - 3], got_f[step - 2]).astype(f32)
                out_b = out_b + choose(got_b[step - 3], got_b[step - 2]).astype(f32)
            out_f, out_b = lax.optimization_barrier((out_f.astype(bf16), out_b.astype(bf16)))
            got_f.append(send_next(out_f))
            got_b.append(send_prev(out_b))
        if part == 0:
            blocks[-1], got_f[1] = lax.optimization_barrier((blocks[-1], got_f[1]))
            own = collect(tab, blocks, owners, half).astype(f32)
        at = slice(part * columns, (part + 1) * columns)
        main = main + own[:half, at] + got_f[-1].astype(f32)
        main = (main + choose(got_b[-2], got_b[-1]).astype(f32)).astype(bf16)
        extra = extra + own[half:, at] + got_f[-2].astype(f32) + got_b[-1].astype(f32)
        extra = extra.astype(bf16)
        received = swap(choose(main, extra, which))
        stays = choose(extra, main, which)
        lows.append(choose(received, stays, which))
        highs.append(choose(stays, received, which))
    result = jnp.concatenate([jnp.concatenate(lows, 1), jnp.concatenate(highs, 1)], 0)
    return choose(result, jnp.zeros_like(result), alive)


def solution(mesh):
    placed = (
        P(("groups", "blk"), "head"),
        P(("groups", "blk"), None, None),
        P(None, ("groups", "blk")),
        P("groups"),
        P("groups"),
        P(("groups", "blk")),
        P(("groups", "blk"), None),
        P("head", None, None),
        P("head", "blk"),
        P(("groups", "blk"), None),
        P(),
        P(None, ("blk", "head")),
        P(None, ("blk", "head")),
        P(("blk", "head"), None),
    )
    order = ring_order(mesh)
    return jax.shard_map(
        lambda *args: on_device(order, *args),
        mesh=mesh,
        in_specs=placed,
        out_specs=P(("groups", "blk", "head"), None),
        check_vma=False,
    )
```

```python
import functools

import jax
import jax.numpy as jnp
from jax import lax
from jax.experimental import pallas as pl
from jax.experimental.pallas import tpu as pltpu
from jax.sharding import PartitionSpec as P

score_scale = 192.0 ** (-0.5)
norm_eps = 1e-06
masked_score = -1e30
f32, bf16, i32 = jnp.float32, jnp.bfloat16, jnp.int32
SMEM = pltpu.SMEM
MIB = 1 << 20

RANK, CORE, BUSY, BUSY_RANK, SPAN, DEC, LIVE, START, LENGTHS = range(9)


def mm(a, b):
    return lax.dot_general(a, b, (((1,), (0,)), ((), ())), preferred_element_type=f32)


def mm_nt(a, b):
    return lax.dot_general(a, b, (((1,), (1,)), ((), ())), preferred_element_type=f32)


def in_hbm(x):
    return pltpu.with_memory_space_constraint(x, pltpu.HBM)


def smem():
    return pl.BlockSpec(memory_space=SMEM)


def whole():
    return pl.BlockSpec(memory_space=pltpu.VMEM)


def params(mib=32):
    return pltpu.CompilerParams(vmem_limit_bytes=mib * MIB)


def cost(flops, moved, exps=0):
    return pl.CostEstimate(flops=int(flops), bytes_accessed=int(moved), transcendentals=int(exps))


def ring_order(mesh):
    count = mesh.shape["blk"]
    natural = list(range(count))
    snake = natural[0::2] + natural[1::2][::-1]
    names = list(mesh.axis_names)
    axes = [names.index("blk")] + [a for a, x in enumerate(names) if x != "blk"]
    lane = mesh.devices.transpose(axes)
    firsts = [lane[i].reshape(-1)[0] for i in natural]
    if not all(hasattr(d, "coords") for d in firsts):
        return snake

    def length(order):
        hops = zip(order, order[1:] + order[:1])
        return sum(
            sum(abs(u - v) for u, v in zip(firsts[a].coords, firsts[b].coords)) for a, b in hops
        )

    return natural if length(natural) <= length(snake) else snake


class Table:
    def __init__(self, ranks, slots):
        self.reach = ranks // 2
        self.source = LENGTHS + slots
        self.ahead = self.source + ranks + 1
        self.behind = self.ahead + self.reach + 1
        self.owner_back = self.behind + self.reach + 1
        self.owner_fore = self.owner_back + self.reach + 1
        self.who = self.owner_fore + self.reach + 1
        self.at = self.who + ranks
        self.size = self.at + ranks


def table_kernel(table, order, given, out):
    reach, ranks = table.reach, len(order)
    span = [given[2 + i] for i in range(ranks)]
    dec = [given[2 + ranks + i] for i in range(ranks)]
    lengths = 3 + 2 * ranks
    for i, r in enumerate(order):
        out[table.who + i] = r
        out[table.at + r] = i
    rank, core = given[0], given[1]
    most, busy_rank = span[0] + dec[0], jnp.int32(0)
    for i in range(1, ranks):
        here = span[i] + dec[i]
        busy_rank = jnp.where(here > most, i, busy_rank)
        most = jnp.maximum(here, most)
    busy = rank == busy_rank

    def wrap(x):
        x = jnp.where(x < 0, x + ranks, x)
        return jnp.where(x >= ranks, x - ranks, x)

    place, busy_place = out[table.at + rank], out[table.at + busy_rank]
    to_busy = wrap(busy_place - place)
    from_busy = wrap(place - busy_place)

    def node_ahead(k):
        far = (to_busy > 0) & (k > to_busy + 1)
        slot = out[table.who + wrap(place + k - jnp.where(far, 1, 0))]
        return jnp.where((to_busy > 0) & (k == to_busy + 1), ranks, slot)

    def node_behind(k):
        far = (from_busy > 0) & (k > from_busy)
        slot = out[table.who + wrap(place - k + jnp.where(far, 1, 0))]
        return jnp.where((from_busy > 0) & (k == from_busy), ranks, slot)

    out[RANK] = rank
    out[CORE] = core
    out[BUSY] = jnp.where(busy, 1, 0)
    out[BUSY_RANK] = busy_rank
    out[SPAN] = given[2 + rank]
    out[DEC] = given[2 + ranks + rank]
    out[LIVE] = given[2 + rank] + given[2 + ranks + rank]
    out[START] = given[lengths - 1]
    for j in range(given.shape[0] - lengths):
        out[LENGTHS + j] = given[lengths + j]
    out[table.source + rank] = 0
    for k in range(1, reach + 1):
        out[table.ahead + k] = node_ahead(k)
        out[table.behind + k] = node_behind(k)
        out[table.owner_back + k] = out[table.who + wrap(place - k)]
        out[table.owner_fore + k] = out[table.who + wrap(place + k)]
        out[table.source + node_behind(k)] = k
        last = jnp.where(busy, ranks, node_ahead(k)) if k == reach else node_ahead(k)
        out[table.source + last] = reach + k


def attend_kernel(
    table, order, heads, first, count, group, rows, lat, value, lead, *refs
):
    if lead:
        given, refs = refs[0], refs[1:]
        q_hbm, cache_hbm, fresh_hbm, vw_hbm, tab, head, main, extra, later = refs[:9]
        flags, refs = refs[9:12], refs[12:]
        q, keys, vw, latent, fz, fresh, q_sem, key_sem, vw_sem, dq = refs
        loaded, base = heads, 0
    else:
        tab, q_hbm, cache_hbm, fresh_hbm, vw_hbm, decoded_here, head, main, extra = refs[:9]
        q, keys, vw, latent, fz, fresh, q_sem, key_sem, vw_sem = refs[9:]
        loaded, base = count, first
    cached, wide = keys.shape[2], keys.shape[1]
    slots = cache_hbm.shape[0] - 1
    odd_slot = keys.shape[0] - 1
    shift, pair, dr = wide - lat, 2 * lat, 8
    groups, pairs = count // group, group // 2
    loads = loaded // group

    def q_copy(g):
        source = pl.ds((base + g * group) * lat, group * lat)
        return pltpu.make_async_copy(
            q_hbm.at[:, source], q.at[:, pl.ds(g * group * lat, group * lat)], q_sem.at[g]
        )

    def vw_copy(g):
        source = pl.ds(first + g * group, group)
        return pltpu.make_async_copy(vw_hbm.at[source], vw.at[pl.ds(g * group, group)], vw_sem.at[g])

    even_copy = pltpu.make_async_copy(cache_hbm.at[0], keys.at[0, pl.ds(0, lat)], key_sem.at[0])
    odd_copy = pltpu.make_async_copy(
        cache_hbm.at[0], keys.at[odd_slot, pl.ds(shift, lat)], key_sem.at[1]
    )
    waiting = [q_copy(g) for g in range(1, loads)]
    if lead:
        rest_copy = pltpu.make_async_copy(
            cache_hbm.at[pl.ds(1, slots)], keys.at[pl.ds(1, slots), pl.ds(0, lat)], key_sem.at[2]
        )
        waiting.append(rest_copy)
    waiting += [vw_copy(g) for g in range(groups)]

    def start_next(number):
        for _ in range(min(number, len(waiting))):
            waiting.pop(0).start()

    fresh_copy = pltpu.make_async_copy(fresh_hbm, fresh, key_sem.at[3])
    fresh_copy.start()
    even_copy.start()
    q_copy(0).start()
    odd_copy.start()
    start_next(1)
    if lead:
        table_kernel(table, order, given, tab)
    span, decs = tab[SPAN], tab[DEC]

    def onehot(shape, row_dim, slot_dim):
        r = lax.broadcasted_iota(i32, shape, row_dim)
        j = lax.broadcasted_iota(i32, shape, slot_dim)
        return jnp.where((r == span + j) & (j < decs), 1.0, 0.0).astype(bf16)

    tail = jnp.zeros((shift, cached), bf16)
    for s in range(odd_slot):
        keys[s, lat:] = tail
    keys[odd_slot, :shift] = tail
    fz[...] = jnp.zeros_like(fz)
    fresh_copy.wait()
    fz[:rows, :lat] = fresh[...].astype(f32)
    fresh_even = fz[...].astype(bf16)
    fresh_odd = pltpu.roll(fz[...], shift, 1).astype(bf16)

    m = pairs * rows
    cols = cached + fz.shape[0]
    row = lax.broadcasted_iota(i32, (m, 1), 0) % rows
    col = lax.broadcasted_iota(i32, (m, cols), 1)
    seen = col < jnp.where(col < cached, tab[START], cached + 1 + row)

    def span_latent(lhs, slot, fresh_keys):
        s = jnp.concatenate([mm(lhs, keys[slot]), mm_nt(lhs, fresh_keys)], 1)
        s = jnp.where(seen, s * score_scale, masked_score)
        e = jnp.exp(s - jnp.max(s, axis=1, keepdims=True))
        w = (e * (1.0 / jnp.sum(e, axis=1, keepdims=True))).astype(bf16)
        o = mm_nt(w[:, :cached], keys[0, :value]) + mm(w[:, cached:], fresh_even[:, :value])
        return jnp.where(row < span, o, 0.0).astype(bf16)

    even_copy.wait()
    odd_copy.wait()
    for g in range(groups):
        q_copy(g).wait()
        start_next(2)
        start = g * group * lat
        for odd in range(2):
            off = start + odd * (pair - wide)
            lhs = jnp.concatenate(
                [q[:, off + pair * p : off + pair * p + wide] for p in range(pairs)], 0
            )
            latent[g, odd] = span_latent(lhs, odd_slot * odd, fresh_odd if odd else fresh_even)
    start_next(len(waiting))

    if lead:
        for g in range(groups, loads):
            q_copy(g).wait()
        pick = onehot((16, rows), 1, 0)
        for p in range(heads // 2):
            got = mm(pick, q[:, pair * p : pair * (p + 1)])[:dr]
            dq[2 * p * dr : (2 * p + 1) * dr] = got[:, :wide]
            dq[(2 * p + 1) * dr : (2 * p + 2) * dr] = pltpu.roll(
                got[:, pair - wide :], wide - shift, 1
            )
        n = heads * dr
        queries = dq[...].astype(bf16)
        slot = lax.broadcasted_iota(i32, (n, 1), 0) % dr
        rest_copy.wait()
        length = jnp.zeros((n, 1), i32)
        scores = jnp.zeros((n, cached), f32)
        for s in range(slots):
            scores = jnp.where(slot == s, mm(queries, keys[s + 1]), scores)
            length = jnp.where(slot == s, tab[LENGTHS + s], length)
        unmasked = lax.broadcasted_iota(i32, (n, cached), 1) < length
        scores = jnp.where(unmasked, scores * score_scale, masked_score)
        own = mm_nt(queries, fresh_even)
        column = lax.broadcasted_iota(i32, own.shape, 1)
        own = jnp.sum(jnp.where(column == span + slot, own, 0.0), axis=1, keepdims=True)
        own = own * score_scale
        peak = jnp.maximum(jnp.max(scores, axis=1, keepdims=True), own)
        e = jnp.exp(scores - peak)
        e_own = jnp.exp(own - peak)
        total = jnp.sum(e, axis=1, keepdims=True) + e_own
        w = e / total
        acc = jnp.zeros((n, value), f32)
        for s in range(slots):
            acc = acc + mm_nt(jnp.where(slot == s, w, 0.0).astype(bf16), keys[s + 1, :value])
        own_value = mm(pick, fresh[:, :value])[:dr]
        own_value = jnp.broadcast_to(own_value[None], (heads, dr, value)).reshape(n, value)
        dec = (acc + (e_own / total).astype(bf16).astype(f32) * own_value).astype(bf16)
        later[...] = dec[count * dr :]
        for flag, at in zip(flags, (BUSY, CORE)):
            flag[...] = jnp.full(flag.shape, tab[at].astype(f32))
        block = rows // 2
        slot_row = tab[CORE] * block + lax.broadcasted_iota(i32, (block, 1), 0)
        flags[2][...] = jnp.where(slot_row < tab[LIVE], 1.0, 0.0)
        dec = dec[: count * dr]
    else:
        dec = decoded_here[...]

    place = onehot((rows, 16), 0, 1)
    vh = vw.shape[2]
    block = rows // 2
    for g in range(groups):
        vw_copy(g).wait()
        values, decoded = [], []
        for p in range(pairs):
            h = g * group + 2 * p
            lhs = jnp.concatenate(
                [
                    latent[g, 0, p * rows : (p + 1) * rows],
                    latent[g, 1, p * rows : (p + 1) * rows],
                    dec[h * dr : (h + 2) * dr],
                ],
                0,
            )
            r = mm(lhs, jnp.concatenate([vw[h], vw[h + 1]], 1))
            values += [r[:rows, :vh], r[rows : 2 * rows, vh:]]
            decoded += [r[2 * rows : 2 * rows + dr, :vh], r[2 * rows + dr :, vh:]]
        decoded = jnp.concatenate(decoded, 1)
        decoded = jnp.concatenate([decoded, jnp.zeros_like(decoded)], 0).astype(bf16)
        out = (jnp.concatenate(values, 1) + mm(place, decoded)).astype(bf16)
        at = slice(g * group * vh, (g + 1) * group * vh)
        main[:, at] = out[:block]
        extra[:, at] = out[block:]
        head[:, at] = jnp.where(tab[BUSY] == 1, out[block:], out[:block])


def attend(table, order, numbers, queries, cache, fresh, vw, part, parts, decoded):
    rows, heads = queries.shape[0], vw.shape[0]
    lat = queries.shape[1] // heads
    slots, _, cached = cache.shape
    value, vh = vw.shape[1:]
    count = heads // parts
    group = min(8, count)
    lead = decoded is None
    loaded = heads if lead else count
    wide = -(-lat // 128) * 128
    half = jax.ShapeDtypeStruct((rows // 2, count * vh), bf16)
    hbm = pl.BlockSpec(memory_space=pltpu.HBM)
    scratch = [
        pltpu.VMEM((rows, loaded * lat), bf16),
        pltpu.VMEM((slots + 1 if lead else 2, wide, cached), bf16),
        pltpu.VMEM((count, value, vh), bf16),
        pltpu.VMEM((count // group, 2, group // 2 * rows, value), bf16),
        pltpu.VMEM((-(-rows // 128) * 128, wide), f32),
        pltpu.VMEM(fresh.shape[::-1], bf16),
        pltpu.SemaphoreType.DMA((loaded // group,)),
        pltpu.SemaphoreType.DMA((4,)),
        pltpu.SemaphoreType.DMA((count // group,)),
    ]
    out_shape, out_specs = [half] * 3, [whole()] * 3
    ins = [smem()] + [hbm] * 4
    args = [numbers, in_hbm(queries), in_hbm(cache), in_hbm(fresh.T), in_hbm(vw)]
    if lead:
        scratch.append(pltpu.VMEM((heads * 8, wide), f32))
        out_shape = [jax.ShapeDtypeStruct((table.size,), i32)] + out_shape
        out_shape += [jax.ShapeDtypeStruct(((heads - count) * 8, value), bf16)]
        out_shape += [jax.ShapeDtypeStruct((n, 1), f32) for n in (1, 1, rows // 2)]
        out_specs = [smem()] + out_specs + [whole()] * 4
    else:
        ins.append(whole())
        args.append(decoded)
    return pl.pallas_call(
        functools.partial(
            attend_kernel, table, order, heads, part * count, count, group, rows, lat, value, lead
        ),
        in_specs=ins,
        out_specs=out_specs,
        out_shape=out_shape,
        scratch_shapes=scratch,
        compiler_params=params(24),
        cost_estimate=cost(
            2 * rows * count * (cached + rows) * (lat + value),
            2 * (queries.size + cache.size + vw.size) // parts,
            rows * count * (cached + rows),
        ),
        name="attend",
    )(*args)


def partner(rank, j, ranks, back=False):
    if ranks & (ranks - 1) == 0:
        return rank ^ j
    if isinstance(rank, int):
        return (rank - j if back else rank + j) % ranks
    other = rank - j if back else rank + j
    return jnp.where(other < 0, other + ranks, jnp.where(other >= ranks, other - ranks, other))


def pack_kernel(ranks, cores, features, tab, res, *outs):
    for k in range(ranks // cores):
        target = partner(tab[RANK], k + (ranks // cores) * tab[CORE], ranks)

        def put(columns, k=k):
            outs[k][...] = res[:, columns]

        if features % 128 == 0:
            put(pl.ds(pl.multiple_of(target * features, 128), features))
        else:
            for t in range(ranks):
                pl.when(target == t)(functools.partial(put, slice(t * features, (t + 1) * features)))


def pack(tab, residual, ranks, cores):
    rows, width = residual.shape
    features = width // ranks
    count = ranks // cores
    return pl.pallas_call(
        functools.partial(pack_kernel, ranks, cores, features),
        in_specs=[smem(), whole()],
        out_specs=[whole()] * count,
        out_shape=[jax.ShapeDtypeStruct((rows, features), bf16)] * count,
        compiler_params=params(8),
        cost_estimate=cost(0, 4 * residual.size),
        name="pack",
    )(tab, residual)


def share_kernel(half, tab, own, *refs):
    pieces, out = refs[:-1], refs[-1]
    other = 1 - tab[CORE]
    block = own.shape[0] // 2
    low = pl.multiple_of(other * half, half)
    high = pl.multiple_of(block + other * half, half)

    def put(k, piece):
        out[2 * k * half : (2 * k + 1) * half] = piece[pl.ds(low, half)]
        out[(2 * k + 1) * half : (2 * k + 2) * half] = piece[pl.ds(high, half)]

    for k, piece in enumerate(pieces):
        if k > 0:
            put(k, piece)
        else:
            pl.when(tab[CORE] == 0)(functools.partial(put, k, own))
            pl.when(tab[CORE] != 0)(functools.partial(put, k, piece))


def share(tab, own, pieces, cores):
    rows, features = own.shape
    half = rows // 2 // cores
    return pl.pallas_call(
        functools.partial(share_kernel, half),
        in_specs=[smem()] + [whole()] * (1 + len(pieces)),
        out_specs=whole(),
        out_shape=jax.ShapeDtypeStruct((2 * half * len(pieces), features), bf16),
        compiler_params=params(8),
        cost_estimate=cost(0, 4 * own.size * len(pieces)),
        name="share",
    )(tab, own, *pieces)


def project_kernel(source, nodes, block, half, part, first, tab, *refs):
    blocks, refs = refs[: nodes + 1], refs[nodes + 1 :]
    before = None if first else refs[0]
    weight, kept, given, acc = refs[-4:]
    step = pl.program_id(0)
    depth = blocks[0].shape[1] // pl.num_programs(0)
    columns = pl.ds(pl.multiple_of(step * depth, 128), depth)
    last = jnp.where(tab[BUSY] == 1, blocks[nodes][:, columns], blocks[nodes - 1][:, columns])
    lhs = jnp.concatenate([b[:, columns] for b in blocks[: nodes - 1]] + [last], 0)
    got = mm(lhs, weight[pl.ds(pl.multiple_of(part * blocks[0].shape[1] + step * depth, 128), depth)])

    @pl.when(step == 0)
    def _():
        acc[...] = got if first else got + before[...]

    @pl.when(step > 0)
    def _():
        acc[...] += got

    @pl.when(step == pl.num_programs(0) - 1)
    def _():
        core = tab[CORE]
        for k in range(nodes):
            at = tab[source + k] * block
            kept[k * half : (k + 1) * half] = acc[pl.ds(pl.multiple_of(at + core * half, half), half)]
            other = acc[pl.ds(pl.multiple_of(at + (1 - core) * half, half), half)]
            given[k * half : (k + 1) * half] = other.astype(bf16)


def project_part_kernel(nodes, part, first, tab, *refs):
    blocks, refs = refs[: nodes + 1], refs[nodes + 1 :]
    weight, out = refs[-2:]
    step = pl.program_id(0)
    depth = blocks[0].shape[1] // pl.num_programs(0)
    columns = pl.ds(pl.multiple_of(step * depth, 128), depth)
    last = jnp.where(tab[BUSY] == 1, blocks[nodes][:, columns], blocks[nodes - 1][:, columns])
    lhs = jnp.concatenate([b[:, columns] for b in blocks[: nodes - 1]] + [last], 0)
    got = mm(lhs, weight[pl.ds(pl.multiple_of(part * blocks[0].shape[1] + step * depth, 128), depth)])

    @pl.when(step == 0)
    def _():
        out[...] = got if first else got + refs[0][...]

    @pl.when(step > 0)
    def _():
        out[...] += got


def project(tab, table, blocks, before, weight, part, parts, cores):
    block, width = blocks[0].shape
    nodes = len(blocks) - 1
    half = block // cores
    features = weight.shape[1]
    depth = width
    steps = width // depth
    total = jax.ShapeDtypeStruct((nodes * block, features), f32)
    final = part == parts - 1
    first = before is None
    ins = [smem()] + [whole()] * (nodes + 2 + (not first))
    args = [tab, *blocks] + ([] if first else [before]) + [weight]
    estimate = cost(
        2 * nodes * block * width * features, 2 * (nodes * block * width + width * features)
    )
    if not final:
        return pl.pallas_call(
            functools.partial(project_part_kernel, nodes, part, first),
            grid=(steps,),
            in_specs=ins,
            out_specs=pl.BlockSpec(total.shape, lambda i: (0, 0)),
            out_shape=total,
            compiler_params=params(16),
            cost_estimate=estimate,
            name="project",
        )(*args)
    return pl.pallas_call(
        functools.partial(project_kernel, table.source, nodes, block, half, part, first),
        grid=(steps,),
        in_specs=ins,
        out_specs=[pl.BlockSpec((nodes * half, features), lambda i: (0, 0))] * 2,
        out_shape=[
            jax.ShapeDtypeStruct((nodes * half, features), f32),
            jax.ShapeDtypeStruct((nodes * half, features), bf16),
        ],
        scratch_shapes=[pltpu.VMEM(total.shape, f32)],
        compiler_params=params(16),
        cost_estimate=estimate,
        name="project",
    )(*args)


def place_kernel(ranks, half, tab, own, shared, *refs):
    pieces, out = refs[:-1], refs[-1]
    rank, core, busy_rank = tab[RANK], tab[CORE], tab[BUSY_RANK]
    count = len(pieces)
    block = own.shape[0] // 2

    def put(slot, extra):
        out[pl.ds(pl.multiple_of(slot * half, half), half)] = extra

    def put_both(owner, main, extra):
        put(owner, main())

        @pl.when(owner == busy_rank)
        def _():
            put(ranks, extra())

    def owner_of(k, c):
        return partner(rank, k + count * c, ranks, True)

    low = pl.ds(pl.multiple_of(core * half, half), half)
    high = pl.ds(pl.multiple_of(block + core * half, half), half)
    for k, piece in enumerate(pieces):

        def received(piece=piece, k=k):
            put_both(owner_of(k, core), lambda: piece[low], lambda: piece[high])

        if k > 0:
            received()
        else:
            pl.when(core == 0)(functools.partial(received, own))
            pl.when(core != 0)(received)
        at = 2 * k * half
        put_both(
            owner_of(k, 1 - core),
            lambda at=at: shared[at : at + half],
            lambda at=at: shared[at + half : at + 2 * half],
        )


def placed_rows(tab, own, shared, pieces, cores):
    rows, features = own.shape
    half = rows // 2 // cores
    ranks = cores * len(pieces)
    return pl.pallas_call(
        functools.partial(place_kernel, ranks, half),
        in_specs=[smem()] + [whole()] * (2 + len(pieces)),
        out_specs=whole(),
        out_shape=jax.ShapeDtypeStruct(((ranks + 1) * half, features), bf16),
        compiler_params=params(8),
        cost_estimate=cost(0, 4 * (ranks + 1) * half * features),
        name="place",
    )(tab, own, shared, *pieces)


def expand_kernel(pieces, others, first, final, width, turned, owners, tab, *refs):
    count = len(pieces)
    blocks = []
    for number in pieces:
        blocks.append(refs[:number])
        refs = refs[number:]
    theirs, refs = refs[:others], refs[others:]
    gain, gate, up = refs[:3]
    refs = refs[3:]
    if not first:
        before, refs = refs[:3], refs[3:]
    if final:
        hidden, refs = refs[0], refs[1:]
    gates, ups, squares = refs
    step = pl.program_id(0)
    for i in range(count):

        @pl.when(step == i)
        def _(i=i):
            both = [x[...] for x in blocks[i]]
            for x in theirs:
                rows = x.shape[0] // count
                both.append(x[i * rows : (i + 1) * rows])
            both = jnp.concatenate(both, 0).astype(f32)
            rows_of = both.shape[1]
            scaled = (both * gain[0]).astype(bf16)
            if turned:
                at = pl.ds(pl.multiple_of(tab[owners[i]] * rows_of, 128), rows_of)
                products = mm_nt(scaled, gate[:, at]), mm_nt(scaled, up[:, at])
            else:
                products = mm(scaled, gate[...]), mm(scaled, up[...])
            values = (
                *products,
                jnp.sum(both * both, axis=1, keepdims=True),
            )
            for n, (ref, value) in enumerate(zip((gates, ups, squares), values)):
                if i == 0:
                    ref[...] = value if first else value + before[n][...]
                else:
                    ref[...] += value

    if final:

        @pl.when(step == count - 1)
        def _():
            scale = lax.rsqrt(squares[...] / width + norm_eps)
            g = gates[...] * scale
            hidden[...] = (g / (1.0 + jnp.exp(-g)) * (ups[...] * scale)).astype(bf16)


def expand(tab, mines, theirs, owners, gain, gate, up, before, final):
    count = len(mines)
    pieces = tuple(len(x) for x in mines)
    rows, features = sum(x.shape[0] for x in mines[0]), mines[0][0].shape[1]
    arrays = [x for own in mines for x in own] + theirs
    units = gate.shape[1]
    first = before is None
    width = gate.shape[0]

    def owner(i, tab):
        index = tab[owners[0]]
        for n in range(1, count):
            index = jnp.where(i == n, tab[owners[n]], index)
        return index

    def full(shape):
        return pl.BlockSpec(shape, lambda i, tab: (0,) * len(shape))

    sums = [(2 * rows, units), (2 * rows, units), (2 * rows, 1)]
    ins = [full(x.shape) for x in arrays]
    ins += [pl.BlockSpec((1, 1, features), lambda i, tab: (owner(i, tab), 0, 0))]
    turned = features % 128 == 0
    if turned:
        gate, up = gate.T, up.T
        ins += [pl.BlockSpec(memory_space=pltpu.VMEM)] * 2
    else:
        ins += [pl.BlockSpec((features, units), lambda i, tab: (owner(i, tab), 0))] * 2
    if not first:
        ins += [full(s) for s in sums]
    shapes = [jax.ShapeDtypeStruct(s, f32) for s in sums]
    out_shapes = [jax.ShapeDtypeStruct((2 * rows, units), bf16)] if final else shapes
    return pl.pallas_call(
        functools.partial(expand_kernel, pieces, len(theirs), first, final, width, turned, owners),
        grid_spec=pltpu.PrefetchScalarGridSpec(
            num_scalar_prefetch=1,
            grid=(count,),
            in_specs=ins,
            out_specs=[full(s.shape) for s in out_shapes],
            scratch_shapes=[pltpu.VMEM(s, f32) for s in sums] if final else [],
        ),
        out_shape=out_shapes,
        compiler_params=params(20),
        cost_estimate=cost(1, 1),
        name="expand",
    )(tab, *arrays, gain, gate, up, *([] if first else before))


def collect_kernel(owners, tab, *refs):
    out = refs[-1]
    if len(out.shape) == 2:
        half, features = out.shape[0] // 2, out.shape[1] // len(owners)
        for i, at in enumerate(owners):
            columns = pl.ds(pl.multiple_of(tab[at] * features, 128), features)
            out[:half, columns] = refs[2 * i][...]
            out[half:, columns] = refs[2 * i + 1][...]
        return
    half = out.shape[1] // 2
    for i, at in enumerate(owners):
        out[tab[at], :half] = refs[2 * i][...]
        out[tab[at], half:] = refs[2 * i + 1][...]


def collect(tab, blocks, owners, half):
    ranks = len(blocks)
    features = blocks[0].shape[1]
    ins, args = [], []
    for x in blocks:
        ins += [
            pl.BlockSpec((half, features), lambda i, tab: (tab[RANK], 0)),
            pl.BlockSpec((half, features), lambda i, tab: (ranks, 0)),
        ]
        args += [x, x]
    aligned = features % 128 == 0
    shape = (2 * half, ranks * features) if aligned else (ranks, 2 * half, features)
    out = pl.pallas_call(
        functools.partial(collect_kernel, owners),
        grid_spec=pltpu.PrefetchScalarGridSpec(
            num_scalar_prefetch=1,
            grid=(1,),
            in_specs=ins,
            out_specs=pl.BlockSpec(shape, lambda i, tab: (0,) * len(shape)),
        ),
        out_shape=jax.ShapeDtypeStruct(shape, bf16),
        compiler_params=params(10),
        cost_estimate=cost(0, 8 * ranks * half * features),
        name="collect",
    )(tab, *args)
    return out if aligned else out.transpose(1, 0, 2).reshape(2 * half, ranks * features)


def contract_kernel(begin, hidden, weight, out):
    wide = out.shape[1]
    at = pl.ds(pl.multiple_of(begin + pl.program_id(0) * wide, 128), wide)
    out[...] = mm(hidden[...], weight[:, at]).astype(bf16)


def contract(hidden, weight, part, parts, which):
    rows, units = hidden.shape[0] // 2, hidden.shape[1]
    columns = weight.shape[1] // parts
    wide = columns // 2 if columns % 256 == 0 else columns
    return pl.pallas_call(
        functools.partial(contract_kernel, part * columns),
        grid=(columns // wide,),
        in_specs=[pl.BlockSpec((rows, units), lambda i: (which, 0)), whole()],
        out_specs=pl.BlockSpec((rows, wide), lambda i: (0, i)),
        out_shape=jax.ShapeDtypeStruct((rows, columns), bf16),
        compiler_params=params(16),
        cost_estimate=cost(2 * rows * units * columns, 2 * (units + rows) * columns),
        name="contract",
    )(hidden, weight)


def pick_kernel(table, half, tab, mine, theirs, *outs):
    busy = tab[BUSY] == 1
    reach = table.reach
    for step in range(1, reach + 1):
        for n, where in enumerate((table.ahead, table.behind)):
            at = pl.multiple_of(tab[where + reach + 1 - step] * half, half)
            total = mine[pl.ds(at, half)].astype(f32) + theirs[pl.ds(at, half)].astype(f32)
            if step == 1 and n == 0:
                total = jnp.where(busy, 0.0, total)
            outs[2 * (step - 1) + n][...] = total
    for n, slot in enumerate((tab[RANK], 2 * reach)):
        at = pl.multiple_of(slot * half, half)
        outs[2 * reach + n][...] = mine[pl.ds(at, half)].astype(f32) + theirs[pl.ds(at, half)].astype(f32)


def pick(tab, table, mine, theirs, half):
    columns = mine.shape[1]
    count = 2 * table.reach + 2
    out = jax.ShapeDtypeStruct((half, columns), f32)
    return pl.pallas_call(
        functools.partial(pick_kernel, table, half),
        in_specs=[smem(), whole(), whole()],
        out_specs=[whole()] * count,
        out_shape=[out] * count,
        compiler_params=params(10),
        cost_estimate=cost(0, 8 * count * half * columns),
        name="pick",
    )(tab, mine, theirs)


contract_parts = 2


def on_device(
    order,
    queries,
    latent_cache,
    new_latent,
    span_len,
    dec_count,
    span_start,
    cache_len,
    value_weight,
    out_weight,
    residual,
    norm_gain,
    gate_weight,
    up_weight,
    down_weight,
):
    ranks = len(order)
    reach = ranks // 2
    cores = lax.axis_size("head")
    rows_dev, width = residual.shape
    half = rows_dev // 2 // cores
    features = out_weight.shape[1]
    table = Table(ranks, cache_len.shape[1])

    forward = [(order[i], order[(i + 1) % ranks]) for i in range(ranks)]
    backward = [(b, a) for a, b in forward]
    exchange = [(c, cores - 1 - c) for c in range(cores)]

    def send_next(x):
        return lax.ppermute(x, "blk", forward)

    def send_prev(x):
        return lax.ppermute(x, "blk", backward)

    def swap(x):
        return lax.ppermute(x, "head", exchange)

    ids = jnp.stack([lax.axis_index("blk"), lax.axis_index("head")]).astype(i32)
    given = jnp.concatenate([ids, span_len, dec_count, span_start, cache_len[0]])
    caches = (queries, latent_cache, new_latent, value_weight)
    tab, *lead, decoded, busy, which, alive = attend(table, order, given, *caches, 0, 2, None)

    def choose(special, usual, flag=busy):
        return jnp.where(jnp.broadcast_to(flag > 0, usual.shape), special, usual)


    packed = list(pack(tab, residual, ranks, cores))
    pieces = [None] * len(packed)

    def send_piece(k):
        pairs = [
            (i * cores + c, partner(i, k + len(packed) * c, ranks) * cores + c)
            for i in range(ranks)
            for c in range(cores)
            if k + c > 0
        ]
        pieces[k] = lax.ppermute(packed[k], ("blk", "head"), pairs)

    for k in range(1, len(packed)):
        send_piece(k)
    decoded, packed = lax.optimization_barrier((decoded, packed))
    packed = list(packed)
    follow = attend(table, order, tab, *caches, 1, 2, decoded)
    follow, pieces[1:], packed[0], out_weight = lax.optimization_barrier(
        (follow, pieces[1:], packed[0], out_weight)
    )
    send_piece(0)

    total = None
    chains = []
    for head, main, extra in (lead, follow):
        chains.append((head, main, extra, [], []))
    for step in range(reach):
        for part, (head, main, extra, behind, ahead) in enumerate(chains):
            if step == 0:
                out_f, out_b = head, main
            elif step == 1:
                out_f, out_b = choose(main, behind[0]), choose(extra, ahead[0])
            else:
                out_f = choose(behind[step - 2], behind[step - 1])
                out_b = choose(ahead[step - 2], ahead[step - 1])
            out_f, out_b = lax.optimization_barrier((out_f, out_b))
            behind.append(send_next(out_f))
            ahead.append(send_prev(out_b))
    gathered = [[main] + behind + ahead + [extra] for _, main, extra, behind, ahead in chains]
    gathered[0][reach], pieces = lax.optimization_barrier((gathered[0][reach], pieces))
    shared = swap(share(tab, packed[0], pieces, cores))
    gathered[0], shared = lax.optimization_barrier((gathered[0], shared))
    for part in range(2):
        total = project(tab, table, gathered[part], total, out_weight, part, 2, cores)
    kept, other = total
    res_here = placed_rows(tab, packed[0], shared, pieces, cores)
    stream = (kept + swap(other).astype(f32) + res_here.astype(f32)).astype(bf16)

    gain = norm_gain.reshape(ranks, 1, features)
    weights = (gain, gate_weight, up_weight)
    cut = -(-stream.shape[0] // 32) * 16
    back, fore = stream, stream
    sums = expand(tab, [[stream]], [swap(stream)], [RANK], *weights, None, False)
    blocks, owners = [stream], [RANK]
    done = None
    for step in range(1, reach + 1):
        if done is not None:
            back, fore, done = lax.optimization_barrier((back, fore, done))
        done = sums
        if step < reach:
            back, fore = send_next(back), send_prev(fore)
            arrived = [[back], [fore]]
            from_owner = [table.owner_back + step, table.owner_fore + step]
        else:
            arrived = [[send_next(back[:cut]), send_prev(fore[cut:])]]
            from_owner = [table.owner_back + step]
        tied, sums = lax.optimization_barrier((arrived, sums))
        if step < reach:
            others = [swap(jnp.concatenate([x for (x,) in tied], 0))]
        else:
            others = [swap(x) for x in tied[0]]
        sums = expand(tab, arrived, others, from_owner, *weights, sums, step == reach)
        blocks += [x[0] if len(x) == 1 else jnp.concatenate(x, 0) for x in arrived]
        owners += from_owner
    (hidden,) = sums

    parts = contract_parts
    theirs = [swap(contract(hidden, down_weight, part, parts, 1)) for part in range(parts)]
    mine = [contract(hidden, down_weight, part, parts, 0) for part in range(parts)]
    mine = lax.optimization_barrier(mine)
    columns = width // parts
    lows, highs = [], []
    for part in range(parts):
        got_f, got_b = [], []
        *owned, main, extra = pick(tab, table, mine[part], theirs[part], half)
        for step in range(1, reach + 1):
            out_f, out_b = owned[2 * step - 2], owned[2 * step - 1]
            if step == 2:
                out_f = out_f + choose(jnp.zeros_like(out_f), got_f[0].astype(f32))
                out_b = out_b + choose(jnp.zeros_like(out_b), got_b[0].astype(f32))
            elif step > 2:
                out_f = out_f + choose(got_f[step - 3], got_f[step - 2]).astype(f32)
                out_b = out_b + choose(got_b[step - 3], got_b[step - 2]).astype(f32)
            out_f, out_b = lax.optimization_barrier((out_f.astype(bf16), out_b.astype(bf16)))
            got_f.append(send_next(out_f))
            got_b.append(send_prev(out_b))
        if part == 0:
            blocks[-1], got_f[1] = lax.optimization_barrier((blocks[-1], got_f[1]))
            own = collect(tab, blocks, owners, half).astype(f32)
        at = slice(part * columns, (part + 1) * columns)
        main = main + own[:half, at] + got_f[-1].astype(f32)
        main = (main + choose(got_b[-2], got_b[-1]).astype(f32)).astype(bf16)
        extra = extra + own[half:, at] + got_f[-2].astype(f32) + got_b[-1].astype(f32)
        extra = extra.astype(bf16)
        received = swap(choose(main, extra, which))
        stays = choose(extra, main, which)
        lows.append(choose(received, stays, which))
        highs.append(choose(stays, received, which))
    result = jnp.concatenate([jnp.concatenate(lows, 1), jnp.concatenate(highs, 1)], 0)
    return choose(result, jnp.zeros_like(result), alive)


def solution(mesh):
    placed = (
        P(("groups", "blk"), "head"),
        P(("groups", "blk"), None, None),
        P(None, ("groups", "blk")),
        P("groups"),
        P("groups"),
        P(("groups", "blk")),
        P(("groups", "blk"), None),
        P("head", None, None),
        P("head", "blk"),
        P(("groups", "blk"), None),
        P(),
        P(None, ("blk", "head")),
        P(None, ("blk", "head")),
        P(("blk", "head"), None),
    )
    order = ring_order(mesh)
    return jax.shard_map(
        lambda *args: on_device(order, *args),
        mesh=mesh,
        in_specs=placed,
        out_specs=P(("groups", "blk", "head"), None),
        check_vma=False,
    )
```

```python
import functools

import jax
import jax.numpy as jnp
from jax import lax
from jax.experimental import pallas as pl
from jax.experimental.pallas import tpu as pltpu
from jax.sharding import PartitionSpec as P

score_scale = 192.0 ** (-0.5)
norm_eps = 1e-06
masked_score = -1e30
f32, bf16, i32 = jnp.float32, jnp.bfloat16, jnp.int32
SMEM = pltpu.SMEM
MIB = 1 << 20

RANK, CORE, BUSY, BUSY_RANK, SPAN, DEC, LIVE, START, LENGTHS = range(9)


def mm(a, b):
    return lax.dot_general(a, b, (((1,), (0,)), ((), ())), preferred_element_type=f32)


def mm_nt(a, b):
    return lax.dot_general(a, b, (((1,), (1,)), ((), ())), preferred_element_type=f32)


def in_hbm(x):
    return pltpu.with_memory_space_constraint(x, pltpu.HBM)


def smem():
    return pl.BlockSpec(memory_space=SMEM)


def whole():
    return pl.BlockSpec(memory_space=pltpu.VMEM)


def params(mib=32):
    return pltpu.CompilerParams(vmem_limit_bytes=mib * MIB)


def cost(flops, moved, exps=0):
    return pl.CostEstimate(flops=int(flops), bytes_accessed=int(moved), transcendentals=int(exps))


def ring_order(mesh):
    count = mesh.shape["blk"]
    natural = list(range(count))
    snake = natural[0::2] + natural[1::2][::-1]
    names = list(mesh.axis_names)
    axes = [names.index("blk")] + [a for a, x in enumerate(names) if x != "blk"]
    lane = mesh.devices.transpose(axes)
    firsts = [lane[i].reshape(-1)[0] for i in natural]
    if not all(hasattr(d, "coords") for d in firsts):
        return snake

    def length(order):
        hops = zip(order, order[1:] + order[:1])
        return sum(
            sum(abs(u - v) for u, v in zip(firsts[a].coords, firsts[b].coords)) for a, b in hops
        )

    return natural if length(natural) <= length(snake) else snake


class Table:
    def __init__(self, ranks, slots):
        self.reach = ranks // 2
        self.source = LENGTHS + slots
        self.ahead = self.source + ranks + 1
        self.behind = self.ahead + self.reach + 1
        self.owner_back = self.behind + self.reach + 1
        self.owner_fore = self.owner_back + self.reach + 1
        self.who = self.owner_fore + self.reach + 1
        self.at = self.who + ranks
        self.size = self.at + ranks


def table_kernel(table, order, given, out):
    reach, ranks = table.reach, len(order)
    span = [given[2 + i] for i in range(ranks)]
    dec = [given[2 + ranks + i] for i in range(ranks)]
    lengths = 3 + 2 * ranks
    for i, r in enumerate(order):
        out[table.who + i] = r
        out[table.at + r] = i
    rank, core = given[0], given[1]
    most, busy_rank = span[0] + dec[0], jnp.int32(0)
    for i in range(1, ranks):
        here = span[i] + dec[i]
        busy_rank = jnp.where(here > most, i, busy_rank)
        most = jnp.maximum(here, most)
    busy = rank == busy_rank

    def wrap(x):
        x = jnp.where(x < 0, x + ranks, x)
        return jnp.where(x >= ranks, x - ranks, x)

    place, busy_place = out[table.at + rank], out[table.at + busy_rank]
    to_busy = wrap(busy_place - place)
    from_busy = wrap(place - busy_place)

    def node_ahead(k):
        far = (to_busy > 0) & (k > to_busy + 1)
        slot = out[table.who + wrap(place + k - jnp.where(far, 1, 0))]
        return jnp.where((to_busy > 0) & (k == to_busy + 1), ranks, slot)

    def node_behind(k):
        far = (from_busy > 0) & (k > from_busy)
        slot = out[table.who + wrap(place - k + jnp.where(far, 1, 0))]
        return jnp.where((from_busy > 0) & (k == from_busy), ranks, slot)

    out[RANK] = rank
    out[CORE] = core
    out[BUSY] = jnp.where(busy, 1, 0)
    out[BUSY_RANK] = busy_rank
    out[SPAN] = given[2 + rank]
    out[DEC] = given[2 + ranks + rank]
    out[LIVE] = given[2 + rank] + given[2 + ranks + rank]
    out[START] = given[lengths - 1]
    for j in range(given.shape[0] - lengths):
        out[LENGTHS + j] = given[lengths + j]
    out[table.source + rank] = 0
    for k in range(1, reach + 1):
        out[table.ahead + k] = node_ahead(k)
        out[table.behind + k] = node_behind(k)
        out[table.owner_back + k] = out[table.who + wrap(place - k)]
        out[table.owner_fore + k] = out[table.who + wrap(place + k)]
        out[table.source + node_behind(k)] = k
        last = jnp.where(busy, ranks, node_ahead(k)) if k == reach else node_ahead(k)
        out[table.source + last] = reach + k


def attend_kernel(
    table, order, heads, first, count, group, rows, lat, value, lead, *refs
):
    if lead:
        given, refs = refs[0], refs[1:]
        q_hbm, cache_hbm, fresh_hbm, vw_hbm, tab, head, main, extra, later = refs[:9]
        flags, refs = refs[9:12], refs[12:]
        q, keys, vw, latent, fz, fresh, q_sem, key_sem, vw_sem, dq = refs
        loaded, base = heads, 0
    else:
        tab, q_hbm, cache_hbm, fresh_hbm, vw_hbm, decoded_here, head, main, extra = refs[:9]
        q, keys, vw, latent, fz, fresh, q_sem, key_sem, vw_sem = refs[9:]
        loaded, base = count, first
    cached, wide = keys.shape[2], keys.shape[1]
    slots = cache_hbm.shape[0] - 1
    odd_slot = keys.shape[0] - 1
    shift, pair, dr = wide - lat, 2 * lat, 8
    groups, pairs = count // group, group // 2
    loads = loaded // group

    def q_copy(g):
        source = pl.ds((base + g * group) * lat, group * lat)
        return pltpu.make_async_copy(
            q_hbm.at[:, source], q.at[:, pl.ds(g * group * lat, group * lat)], q_sem.at[g]
        )

    def vw_copy(g):
        source = pl.ds(first + g * group, group)
        return pltpu.make_async_copy(vw_hbm.at[source], vw.at[pl.ds(g * group, group)], vw_sem.at[g])

    even_copy = pltpu.make_async_copy(cache_hbm.at[0], keys.at[0, pl.ds(0, lat)], key_sem.at[0])
    odd_copy = pltpu.make_async_copy(
        cache_hbm.at[0], keys.at[odd_slot, pl.ds(shift, lat)], key_sem.at[1]
    )
    waiting = [q_copy(g) for g in range(1, loads)]
    if lead:
        rest_copy = pltpu.make_async_copy(
            cache_hbm.at[pl.ds(1, slots)], keys.at[pl.ds(1, slots), pl.ds(0, lat)], key_sem.at[2]
        )
        waiting.append(rest_copy)
    waiting += [vw_copy(g) for g in range(groups)]

    def start_next(number):
        for _ in range(min(number, len(waiting))):
            waiting.pop(0).start()

    fresh_copy = pltpu.make_async_copy(fresh_hbm, fresh, key_sem.at[3])
    fresh_copy.start()
    even_copy.start()
    q_copy(0).start()
    odd_copy.start()
    start_next(1)
    if lead:
        table_kernel(table, order, given, tab)
    span, decs = tab[SPAN], tab[DEC]

    def onehot(shape, row_dim, slot_dim):
        r = lax.broadcasted_iota(i32, shape, row_dim)
        j = lax.broadcasted_iota(i32, shape, slot_dim)
        return jnp.where((r == span + j) & (j < decs), 1.0, 0.0).astype(bf16)

    tail = jnp.zeros((shift, cached), bf16)
    for s in range(odd_slot):
        keys[s, lat:] = tail
    keys[odd_slot, :shift] = tail
    fz[...] = jnp.zeros_like(fz)
    fresh_copy.wait()
    fz[:rows, :lat] = fresh[...].astype(f32)
    fresh_even = fz[...].astype(bf16)
    fresh_odd = pltpu.roll(fz[...], shift, 1).astype(bf16)

    m = pairs * rows
    cols = cached + fz.shape[0]
    row = lax.broadcasted_iota(i32, (m, 1), 0) % rows
    col = lax.broadcasted_iota(i32, (m, cols), 1)
    seen = col < jnp.where(col < cached, tab[START], cached + 1 + row)

    def span_latent(lhs, slot, fresh_keys):
        s = jnp.concatenate([mm(lhs, keys[slot]), mm_nt(lhs, fresh_keys)], 1)
        s = jnp.where(seen, s * score_scale, masked_score)
        e = jnp.exp(s - jnp.max(s, axis=1, keepdims=True))
        w = (e * (1.0 / jnp.sum(e, axis=1, keepdims=True))).astype(bf16)
        o = mm_nt(w[:, :cached], keys[0, :value]) + mm(w[:, cached:], fresh_even[:, :value])
        return jnp.where(row < span, o, 0.0).astype(bf16)

    even_copy.wait()
    odd_copy.wait()
    for g in range(groups):
        q_copy(g).wait()
        start_next(2)
        start = g * group * lat
        for odd in range(2):
            off = start + odd * (pair - wide)
            lhs = jnp.concatenate(
                [q[:, off + pair * p : off + pair * p + wide] for p in range(pairs)], 0
            )
            latent[g, odd] = span_latent(lhs, odd_slot * odd, fresh_odd if odd else fresh_even)
    start_next(len(waiting))

    if lead:
        for g in range(groups, loads):
            q_copy(g).wait()
        pick = onehot((16, rows), 1, 0)
        for p in range(heads // 2):
            got = mm(pick, q[:, pair * p : pair * (p + 1)])[:dr]
            dq[2 * p * dr : (2 * p + 1) * dr] = got[:, :wide]
            dq[(2 * p + 1) * dr : (2 * p + 2) * dr] = pltpu.roll(
                got[:, pair - wide :], wide - shift, 1
            )
        n = heads * dr
        queries = dq[...].astype(bf16)
        slot = lax.broadcasted_iota(i32, (n, 1), 0) % dr
        rest_copy.wait()
        length = jnp.zeros((n, 1), i32)
        scores = jnp.zeros((n, cached), f32)
        for s in range(slots):
            scores = jnp.where(slot == s, mm(queries, keys[s + 1]), scores)
            length = jnp.where(slot == s, tab[LENGTHS + s], length)
        unmasked = lax.broadcasted_iota(i32, (n, cached), 1) < length
        scores = jnp.where(unmasked, scores * score_scale, masked_score)
        own = mm_nt(queries, fresh_even)
        column = lax.broadcasted_iota(i32, own.shape, 1)
        own = jnp.sum(jnp.where(column == span + slot, own, 0.0), axis=1, keepdims=True)
        own = own * score_scale
        peak = jnp.maximum(jnp.max(scores, axis=1, keepdims=True), own)
        e = jnp.exp(scores - peak)
        e_own = jnp.exp(own - peak)
        total = jnp.sum(e, axis=1, keepdims=True) + e_own
        w = e / total
        acc = jnp.zeros((n, value), f32)
        for s in range(slots):
            acc = acc + mm_nt(jnp.where(slot == s, w, 0.0).astype(bf16), keys[s + 1, :value])
        own_value = mm(pick, fresh[:, :value])[:dr]
        own_value = jnp.broadcast_to(own_value[None], (heads, dr, value)).reshape(n, value)
        dec = (acc + (e_own / total).astype(bf16).astype(f32) * own_value).astype(bf16)
        later[...] = dec[count * dr :]
        for flag, at in zip(flags, (BUSY, CORE)):
            flag[...] = jnp.full(flag.shape, tab[at].astype(f32))
        block = rows // 2
        slot_row = tab[CORE] * block + lax.broadcasted_iota(i32, (block, 1), 0)
        flags[2][...] = jnp.where(slot_row < tab[LIVE], 1.0, 0.0)
        dec = dec[: count * dr]
    else:
        dec = decoded_here[...]

    place = onehot((rows, 16), 0, 1)
    vh = vw.shape[2]
    block = rows // 2
    for g in range(groups):
        vw_copy(g).wait()
        values, decoded = [], []
        for p in range(pairs):
            h = g * group + 2 * p
            lhs = jnp.concatenate(
                [
                    latent[g, 0, p * rows : (p + 1) * rows],
                    latent[g, 1, p * rows : (p + 1) * rows],
                    dec[h * dr : (h + 2) * dr],
                ],
                0,
            )
            r = mm(lhs, jnp.concatenate([vw[h], vw[h + 1]], 1))
            values += [r[:rows, :vh], r[rows : 2 * rows, vh:]]
            decoded += [r[2 * rows : 2 * rows + dr, :vh], r[2 * rows + dr :, vh:]]
        decoded = jnp.concatenate(decoded, 1)
        decoded = jnp.concatenate([decoded, jnp.zeros_like(decoded)], 0).astype(bf16)
        out = (jnp.concatenate(values, 1) + mm(place, decoded)).astype(bf16)
        at = slice(g * group * vh, (g + 1) * group * vh)
        main[:, at] = out[:block]
        extra[:, at] = out[block:]
        head[:, at] = jnp.where(tab[BUSY] == 1, out[block:], out[:block])


def attend(table, order, numbers, queries, cache, fresh, vw, part, parts, decoded):
    rows, heads = queries.shape[0], vw.shape[0]
    lat = queries.shape[1] // heads
    slots, _, cached = cache.shape
    value, vh = vw.shape[1:]
    count = heads // parts
    group = min(8, count)
    lead = decoded is None
    loaded = heads if lead else count
    wide = -(-lat // 128) * 128
    half = jax.ShapeDtypeStruct((rows // 2, count * vh), bf16)
    hbm = pl.BlockSpec(memory_space=pltpu.HBM)
    scratch = [
        pltpu.VMEM((rows, loaded * lat), bf16),
        pltpu.VMEM((slots + 1 if lead else 2, wide, cached), bf16),
        pltpu.VMEM((count, value, vh), bf16),
        pltpu.VMEM((count // group, 2, group // 2 * rows, value), bf16),
        pltpu.VMEM((-(-rows // 128) * 128, wide), f32),
        pltpu.VMEM(fresh.shape[::-1], bf16),
        pltpu.SemaphoreType.DMA((loaded // group,)),
        pltpu.SemaphoreType.DMA((4,)),
        pltpu.SemaphoreType.DMA((count // group,)),
    ]
    out_shape, out_specs = [half] * 3, [whole()] * 3
    ins = [smem()] + [hbm] * 4
    args = [numbers, in_hbm(queries), in_hbm(cache), in_hbm(fresh.T), in_hbm(vw)]
    if lead:
        scratch.append(pltpu.VMEM((heads * 8, wide), f32))
        out_shape = [jax.ShapeDtypeStruct((table.size,), i32)] + out_shape
        out_shape += [jax.ShapeDtypeStruct(((heads - count) * 8, value), bf16)]
        out_shape += [jax.ShapeDtypeStruct((n, 1), f32) for n in (1, 1, rows // 2)]
        out_specs = [smem()] + out_specs + [whole()] * 4
    else:
        ins.append(whole())
        args.append(decoded)
    return pl.pallas_call(
        functools.partial(
            attend_kernel, table, order, heads, part * count, count, group, rows, lat, value, lead
        ),
        in_specs=ins,
        out_specs=out_specs,
        out_shape=out_shape,
        scratch_shapes=scratch,
        compiler_params=params(24),
        cost_estimate=cost(
            2 * rows * count * (cached + rows) * (lat + value),
            2 * (queries.size + cache.size + vw.size) // parts,
            rows * count * (cached + rows),
        ),
        name="attend",
    )(*args)


def partner(rank, j, ranks, back=False):
    if ranks & (ranks - 1) == 0:
        return rank ^ j
    if isinstance(rank, int):
        return (rank - j if back else rank + j) % ranks
    other = rank - j if back else rank + j
    return jnp.where(other < 0, other + ranks, jnp.where(other >= ranks, other - ranks, other))


def pack_kernel(ranks, cores, features, tab, res, *outs):
    for k in range(ranks // cores):
        target = partner(tab[RANK], k + (ranks // cores) * tab[CORE], ranks)

        def put(columns, k=k):
            outs[k][...] = res[:, columns]

        if features % 128 == 0:
            put(pl.ds(pl.multiple_of(target * features, 128), features))
        else:
            for t in range(ranks):
                pl.when(target == t)(functools.partial(put, slice(t * features, (t + 1) * features)))


def pack(tab, residual, ranks, cores):
    rows, width = residual.shape
    features = width // ranks
    count = ranks // cores
    return pl.pallas_call(
        functools.partial(pack_kernel, ranks, cores, features),
        in_specs=[smem(), whole()],
        out_specs=[whole()] * count,
        out_shape=[jax.ShapeDtypeStruct((rows, features), bf16)] * count,
        compiler_params=params(8),
        cost_estimate=cost(0, 4 * residual.size),
        name="pack",
    )(tab, residual)


def share_kernel(half, tab, own, *refs):
    pieces, out = refs[:-1], refs[-1]
    other = 1 - tab[CORE]
    block = own.shape[0] // 2
    low = pl.multiple_of(other * half, half)
    high = pl.multiple_of(block + other * half, half)

    def put(k, piece):
        out[2 * k * half : (2 * k + 1) * half] = piece[pl.ds(low, half)]
        out[(2 * k + 1) * half : (2 * k + 2) * half] = piece[pl.ds(high, half)]

    for k, piece in enumerate(pieces):
        if k > 0:
            put(k, piece)
        else:
            pl.when(tab[CORE] == 0)(functools.partial(put, k, own))
            pl.when(tab[CORE] != 0)(functools.partial(put, k, piece))


def share(tab, own, pieces, cores):
    rows, features = own.shape
    half = rows // 2 // cores
    return pl.pallas_call(
        functools.partial(share_kernel, half),
        in_specs=[smem()] + [whole()] * (1 + len(pieces)),
        out_specs=whole(),
        out_shape=jax.ShapeDtypeStruct((2 * half * len(pieces), features), bf16),
        compiler_params=params(8),
        cost_estimate=cost(0, 4 * own.size * len(pieces)),
        name="share",
    )(tab, own, *pieces)


def project_kernel(source, nodes, block, half, part, first, tab, *refs):
    blocks, refs = refs[: nodes + 1], refs[nodes + 1 :]
    before = None if first else refs[0]
    weight, kept, given, acc = refs[-4:]
    step = pl.program_id(0)
    depth = blocks[0].shape[1] // pl.num_programs(0)
    columns = pl.ds(pl.multiple_of(step * depth, 128), depth)
    last = jnp.where(tab[BUSY] == 1, blocks[nodes][:, columns], blocks[nodes - 1][:, columns])
    lhs = jnp.concatenate([b[:, columns] for b in blocks[: nodes - 1]] + [last], 0)
    got = mm(lhs, weight[pl.ds(pl.multiple_of(part * blocks[0].shape[1] + step * depth, 128), depth)])

    @pl.when(step == 0)
    def _():
        acc[...] = got if first else got + before[...]

    @pl.when(step > 0)
    def _():
        acc[...] += got

    @pl.when(step == pl.num_programs(0) - 1)
    def _():
        core = tab[CORE]
        for k in range(nodes):
            at = tab[source + k] * block
            kept[k * half : (k + 1) * half] = acc[pl.ds(pl.multiple_of(at + core * half, half), half)]
            other = acc[pl.ds(pl.multiple_of(at + (1 - core) * half, half), half)]
            given[k * half : (k + 1) * half] = other.astype(bf16)


def project_part_kernel(nodes, part, first, tab, *refs):
    blocks, refs = refs[: nodes + 1], refs[nodes + 1 :]
    weight, out = refs[-2:]
    step = pl.program_id(0)
    depth = blocks[0].shape[1] // pl.num_programs(0)
    columns = pl.ds(pl.multiple_of(step * depth, 128), depth)
    last = jnp.where(tab[BUSY] == 1, blocks[nodes][:, columns], blocks[nodes - 1][:, columns])
    lhs = jnp.concatenate([b[:, columns] for b in blocks[: nodes - 1]] + [last], 0)
    got = mm(lhs, weight[pl.ds(pl.multiple_of(part * blocks[0].shape[1] + step * depth, 128), depth)])

    @pl.when(step == 0)
    def _():
        out[...] = got if first else got + refs[0][...]

    @pl.when(step > 0)
    def _():
        out[...] += got


def project(tab, table, blocks, before, weight, part, parts, cores):
    block, width = blocks[0].shape
    nodes = len(blocks) - 1
    half = block // cores
    features = weight.shape[1]
    depth = width
    steps = width // depth
    total = jax.ShapeDtypeStruct((nodes * block, features), f32)
    final = part == parts - 1
    first = before is None
    ins = [smem()] + [whole()] * (nodes + 2 + (not first))
    args = [tab, *blocks] + ([] if first else [before]) + [weight]
    estimate = cost(
        2 * nodes * block * width * features, 2 * (nodes * block * width + width * features)
    )
    if not final:
        return pl.pallas_call(
            functools.partial(project_part_kernel, nodes, part, first),
            grid=(steps,),
            in_specs=ins,
            out_specs=pl.BlockSpec(total.shape, lambda i: (0, 0)),
            out_shape=total,
            compiler_params=params(16),
            cost_estimate=estimate,
            name="project",
        )(*args)
    return pl.pallas_call(
        functools.partial(project_kernel, table.source, nodes, block, half, part, first),
        grid=(steps,),
        in_specs=ins,
        out_specs=[pl.BlockSpec((nodes * half, features), lambda i: (0, 0))] * 2,
        out_shape=[
            jax.ShapeDtypeStruct((nodes * half, features), f32),
            jax.ShapeDtypeStruct((nodes * half, features), bf16),
        ],
        scratch_shapes=[pltpu.VMEM(total.shape, f32)],
        compiler_params=params(16),
        cost_estimate=estimate,
        name="project",
    )(*args)


def place_kernel(ranks, half, tab, own, shared, *refs):
    pieces, out = refs[:-1], refs[-1]
    rank, core, busy_rank = tab[RANK], tab[CORE], tab[BUSY_RANK]
    count = len(pieces)
    block = own.shape[0] // 2

    def put(slot, extra):
        out[pl.ds(pl.multiple_of(slot * half, half), half)] = extra

    def put_both(owner, main, extra):
        put(owner, main())

        @pl.when(owner == busy_rank)
        def _():
            put(ranks, extra())

    def owner_of(k, c):
        return partner(rank, k + count * c, ranks, True)

    low = pl.ds(pl.multiple_of(core * half, half), half)
    high = pl.ds(pl.multiple_of(block + core * half, half), half)
    for k, piece in enumerate(pieces):

        def received(piece=piece, k=k):
            put_both(owner_of(k, core), lambda: piece[low], lambda: piece[high])

        if k > 0:
            received()
        else:
            pl.when(core == 0)(functools.partial(received, own))
            pl.when(core != 0)(received)
        at = 2 * k * half
        put_both(
            owner_of(k, 1 - core),
            lambda at=at: shared[at : at + half],
            lambda at=at: shared[at + half : at + 2 * half],
        )


def placed_rows(tab, own, shared, pieces, cores):
    rows, features = own.shape
    half = rows // 2 // cores
    ranks = cores * len(pieces)
    return pl.pallas_call(
        functools.partial(place_kernel, ranks, half),
        in_specs=[smem()] + [whole()] * (2 + len(pieces)),
        out_specs=whole(),
        out_shape=jax.ShapeDtypeStruct(((ranks + 1) * half, features), bf16),
        compiler_params=params(8),
        cost_estimate=cost(0, 4 * (ranks + 1) * half * features),
        name="place",
    )(tab, own, shared, *pieces)


def expand_kernel(pieces, others, first, final, width, turned, owners, tab, *refs):
    count = len(pieces)
    blocks = []
    for number in pieces:
        blocks.append(refs[:number])
        refs = refs[number:]
    theirs, refs = refs[:others], refs[others:]
    gain, gate, up = refs[:3]
    refs = refs[3:]
    if not first:
        before, refs = refs[:3], refs[3:]
    if final:
        hidden, refs = refs[0], refs[1:]
    gates, ups, squares = refs
    step = pl.program_id(0)
    for i in range(count):

        @pl.when(step == i)
        def _(i=i):
            both = [x[...] for x in blocks[i]]
            for x in theirs:
                rows = x.shape[0] // count
                both.append(x[i * rows : (i + 1) * rows])
            both = jnp.concatenate(both, 0).astype(f32)
            rows_of = both.shape[1]
            scaled = (both * gain[0]).astype(bf16)
            if turned:
                at = pl.ds(pl.multiple_of(tab[owners[i]] * rows_of, 128), rows_of)
                products = mm_nt(scaled, gate[:, at]), mm_nt(scaled, up[:, at])
            else:
                products = mm(scaled, gate[...]), mm(scaled, up[...])
            values = (
                *products,
                jnp.sum(both * both, axis=1, keepdims=True),
            )
            for n, (ref, value) in enumerate(zip((gates, ups, squares), values)):
                if i == 0:
                    ref[...] = value if first else value + before[n][...]
                else:
                    ref[...] += value

    if final:

        @pl.when(step == count - 1)
        def _():
            scale = lax.rsqrt(squares[...] / width + norm_eps)
            g = gates[...] * scale
            hidden[...] = (g / (1.0 + jnp.exp(-g)) * (ups[...] * scale)).astype(bf16)


def expand(tab, mines, theirs, owners, gain, gate, up, before, final):
    count = len(mines)
    pieces = tuple(len(x) for x in mines)
    rows, features = sum(x.shape[0] for x in mines[0]), mines[0][0].shape[1]
    arrays = [x for own in mines for x in own] + theirs
    units = gate.shape[1]
    first = before is None
    width = gate.shape[0]

    def owner(i, tab):
        index = tab[owners[0]]
        for n in range(1, count):
            index = jnp.where(i == n, tab[owners[n]], index)
        return index

    def full(shape):
        return pl.BlockSpec(shape, lambda i, tab: (0,) * len(shape))

    sums = [(2 * rows, units), (2 * rows, units), (2 * rows, 1)]
    ins = [full(x.shape) for x in arrays]
    ins += [pl.BlockSpec((1, 1, features), lambda i, tab: (owner(i, tab), 0, 0))]
    turned = features % 128 == 0
    if turned:
        gate, up = gate.T, up.T
        ins += [pl.BlockSpec(memory_space=pltpu.VMEM)] * 2
    else:
        ins += [pl.BlockSpec((features, units), lambda i, tab: (owner(i, tab), 0))] * 2
    if not first:
        ins += [full(s) for s in sums]
    shapes = [jax.ShapeDtypeStruct(s, f32) for s in sums]
    out_shapes = [jax.ShapeDtypeStruct((2 * rows, units), bf16)] if final else shapes
    return pl.pallas_call(
        functools.partial(expand_kernel, pieces, len(theirs), first, final, width, turned, owners),
        grid_spec=pltpu.PrefetchScalarGridSpec(
            num_scalar_prefetch=1,
            grid=(count,),
            in_specs=ins,
            out_specs=[full(s.shape) for s in out_shapes],
            scratch_shapes=[pltpu.VMEM(s, f32) for s in sums] if final else [],
        ),
        out_shape=out_shapes,
        compiler_params=params(20),
        cost_estimate=cost(1, 1),
        name="expand",
    )(tab, *arrays, gain, gate, up, *([] if first else before))


def collect_kernel(owners, tab, *refs):
    out = refs[-1]
    if len(out.shape) == 2:
        half, features = out.shape[0] // 2, out.shape[1] // len(owners)
        for i, at in enumerate(owners):
            columns = pl.ds(pl.multiple_of(tab[at] * features, 128), features)
            out[:half, columns] = refs[2 * i][...]
            out[half:, columns] = refs[2 * i + 1][...]
        return
    half = out.shape[1] // 2
    for i, at in enumerate(owners):
        out[tab[at], :half] = refs[2 * i][...]
        out[tab[at], half:] = refs[2 * i + 1][...]


def collect(tab, blocks, owners, half):
    ranks = len(blocks)
    features = blocks[0].shape[1]
    ins, args = [], []
    for x in blocks:
        ins += [
            pl.BlockSpec((half, features), lambda i, tab: (tab[RANK], 0)),
            pl.BlockSpec((half, features), lambda i, tab: (ranks, 0)),
        ]
        args += [x, x]
    aligned = features % 128 == 0
    shape = (2 * half, ranks * features) if aligned else (ranks, 2 * half, features)
    out = pl.pallas_call(
        functools.partial(collect_kernel, owners),
        grid_spec=pltpu.PrefetchScalarGridSpec(
            num_scalar_prefetch=1,
            grid=(1,),
            in_specs=ins,
            out_specs=pl.BlockSpec(shape, lambda i, tab: (0,) * len(shape)),
        ),
        out_shape=jax.ShapeDtypeStruct(shape, bf16),
        compiler_params=params(10),
        cost_estimate=cost(0, 8 * ranks * half * features),
        name="collect",
    )(tab, *args)
    return out if aligned else out.transpose(1, 0, 2).reshape(2 * half, ranks * features)


def contract_kernel(begin, hidden, weight, out):
    wide = out.shape[1]
    at = pl.ds(pl.multiple_of(begin + pl.program_id(0) * wide, 128), wide)
    out[...] = mm(hidden[...], weight[:, at]).astype(bf16)


def contract(hidden, weight, part, parts, which):
    rows, units = hidden.shape[0] // 2, hidden.shape[1]
    columns = weight.shape[1] // parts
    wide = columns // 2 if columns % 256 == 0 else columns
    return pl.pallas_call(
        functools.partial(contract_kernel, part * columns),
        grid=(columns // wide,),
        in_specs=[pl.BlockSpec((rows, units), lambda i: (which, 0)), whole()],
        out_specs=pl.BlockSpec((rows, wide), lambda i: (0, i)),
        out_shape=jax.ShapeDtypeStruct((rows, columns), bf16),
        compiler_params=params(16),
        cost_estimate=cost(2 * rows * units * columns, 2 * (units + rows) * columns),
        name="contract",
    )(hidden, weight)


def pick_kernel(table, half, tab, mine, theirs, *outs):
    busy = tab[BUSY] == 1
    reach = table.reach
    for step in range(1, reach + 1):
        for n, where in enumerate((table.ahead, table.behind)):
            at = pl.multiple_of(tab[where + reach + 1 - step] * half, half)
            total = mine[pl.ds(at, half)].astype(f32) + theirs[pl.ds(at, half)].astype(f32)
            if step == 1 and n == 0:
                total = jnp.where(busy, 0.0, total)
            outs[2 * (step - 1) + n][...] = total
    for n, slot in enumerate((tab[RANK], 2 * reach)):
        at = pl.multiple_of(slot * half, half)
        outs[2 * reach + n][...] = mine[pl.ds(at, half)].astype(f32) + theirs[pl.ds(at, half)].astype(f32)


def pick(tab, table, mine, theirs, half):
    columns = mine.shape[1]
    count = 2 * table.reach + 2
    out = jax.ShapeDtypeStruct((half, columns), f32)
    return pl.pallas_call(
        functools.partial(pick_kernel, table, half),
        in_specs=[smem(), whole(), whole()],
        out_specs=[whole()] * count,
        out_shape=[out] * count,
        compiler_params=params(10),
        cost_estimate=cost(0, 8 * count * half * columns),
        name="pick",
    )(tab, mine, theirs)


contract_parts = 2


def on_device(
    order,
    queries,
    latent_cache,
    new_latent,
    span_len,
    dec_count,
    span_start,
    cache_len,
    value_weight,
    out_weight,
    residual,
    norm_gain,
    gate_weight,
    up_weight,
    down_weight,
):
    ranks = len(order)
    reach = ranks // 2
    cores = lax.axis_size("head")
    rows_dev, width = residual.shape
    half = rows_dev // 2 // cores
    features = out_weight.shape[1]
    table = Table(ranks, cache_len.shape[1])

    forward = [(order[i], order[(i + 1) % ranks]) for i in range(ranks)]
    backward = [(b, a) for a, b in forward]
    exchange = [(c, cores - 1 - c) for c in range(cores)]

    def send_next(x):
        return lax.ppermute(x, "blk", forward)

    def send_prev(x):
        return lax.ppermute(x, "blk", backward)

    def swap(x):
        return lax.ppermute(x, "head", exchange)

    ids = jnp.stack([lax.axis_index("blk"), lax.axis_index("head")]).astype(i32)
    given = jnp.concatenate([ids, span_len, dec_count, span_start, cache_len[0]])
    caches = (queries, latent_cache, new_latent, value_weight)
    tab, *lead, decoded, busy, which, alive = attend(table, order, given, *caches, 0, 2, None)

    def choose(special, usual, flag=busy):
        return jnp.where(jnp.broadcast_to(flag > 0, usual.shape), special, usual)


    packed = list(pack(tab, residual, ranks, cores))
    pieces = [None] * len(packed)

    def send_piece(k):
        pairs = [
            (i * cores + c, partner(i, k + len(packed) * c, ranks) * cores + c)
            for i in range(ranks)
            for c in range(cores)
            if k + c > 0
        ]
        pieces[k] = lax.ppermute(packed[k], ("blk", "head"), pairs)

    for k in range(1, len(packed)):
        send_piece(k)
    decoded, packed = lax.optimization_barrier((decoded, packed))
    packed = list(packed)
    follow = attend(table, order, tab, *caches, 1, 2, decoded)
    follow, pieces[1:], packed[0], out_weight = lax.optimization_barrier(
        (follow, pieces[1:], packed[0], out_weight)
    )
    send_piece(0)

    total = None
    chains = []
    for head, main, extra in (lead, follow):
        chains.append((head, main, extra, [], []))
    for step in range(reach):
        for part, (head, main, extra, behind, ahead) in enumerate(chains):
            if step == 0:
                out_f, out_b = head, main
            elif step == 1:
                out_f, out_b = choose(main, behind[0]), choose(extra, ahead[0])
            else:
                out_f = choose(behind[step - 2], behind[step - 1])
                out_b = choose(ahead[step - 2], ahead[step - 1])
            out_f, out_b = lax.optimization_barrier((out_f, out_b))
            behind.append(send_next(out_f))
            ahead.append(send_prev(out_b))
    gathered = [[main] + behind + ahead + [extra] for _, main, extra, behind, ahead in chains]
    gathered[0][2], pieces = lax.optimization_barrier((gathered[0][2], pieces))
    shared = swap(share(tab, packed[0], pieces, cores))
    gathered[0], shared = lax.optimization_barrier((gathered[0], shared))
    for part in range(2):
        total = project(tab, table, gathered[part], total, out_weight, part, 2, cores)
    kept, other = total
    res_here = placed_rows(tab, packed[0], shared, pieces, cores)
    stream = (kept + swap(other).astype(f32) + res_here.astype(f32)).astype(bf16)

    gain = norm_gain.reshape(ranks, 1, features)
    weights = (gain, gate_weight, up_weight)
    cut = -(-stream.shape[0] // 32) * 16
    back, fore = stream, stream
    sums = expand(tab, [[stream]], [swap(stream)], [RANK], *weights, None, False)
    blocks, owners = [stream], [RANK]
    done = None
    for step in range(1, reach + 1):
        if done is not None:
            back, fore, done = lax.optimization_barrier((back, fore, done))
        done = sums
        if step < reach:
            back, fore = send_next(back), send_prev(fore)
            arrived = [[back], [fore]]
            from_owner = [table.owner_back + step, table.owner_fore + step]
        else:
            arrived = [[send_next(back[:cut]), send_prev(fore[cut:])]]
            from_owner = [table.owner_back + step]
        tied, sums = lax.optimization_barrier((arrived, sums))
        if step < reach:
            others = [swap(jnp.concatenate([x for (x,) in tied], 0))]
        else:
            others = [swap(x) for x in tied[0]]
        sums = expand(tab, arrived, others, from_owner, *weights, sums, step == reach)
        blocks += [x[0] if len(x) == 1 else jnp.concatenate(x, 0) for x in arrived]
        owners += from_owner
    (hidden,) = sums

    parts = contract_parts
    theirs = [swap(contract(hidden, down_weight, part, parts, 1)) for part in range(parts)]
    mine = [contract(hidden, down_weight, part, parts, 0) for part in range(parts)]
    mine = lax.optimization_barrier(mine)
    columns = width // parts
    lows, highs = [], []
    for part in range(parts):
        got_f, got_b = [], []
        *owned, main, extra = pick(tab, table, mine[part], theirs[part], half)
        for step in range(1, reach + 1):
            out_f, out_b = owned[2 * step - 2], owned[2 * step - 1]
            if step == 2:
                out_f = out_f + choose(jnp.zeros_like(out_f), got_f[0].astype(f32))
                out_b = out_b + choose(jnp.zeros_like(out_b), got_b[0].astype(f32))
            elif step > 2:
                out_f = out_f + choose(got_f[step - 3], got_f[step - 2]).astype(f32)
                out_b = out_b + choose(got_b[step - 3], got_b[step - 2]).astype(f32)
            out_f, out_b = lax.optimization_barrier((out_f.astype(bf16), out_b.astype(bf16)))
            got_f.append(send_next(out_f))
            got_b.append(send_prev(out_b))
        if part == 0:
            blocks[-1], got_f[1] = lax.optimization_barrier((blocks[-1], got_f[1]))
            own = collect(tab, blocks, owners, half).astype(f32)
        at = slice(part * columns, (part + 1) * columns)
        main = main + own[:half, at] + got_f[-1].astype(f32)
        main = (main + choose(got_b[-2], got_b[-1]).astype(f32)).astype(bf16)
        extra = extra + own[half:, at] + got_f[-2].astype(f32) + got_b[-1].astype(f32)
        extra = extra.astype(bf16)
        received = swap(choose(main, extra, which))
        stays = choose(extra, main, which)
        lows.append(choose(received, stays, which))
        highs.append(choose(stays, received, which))
    result = jnp.concatenate([jnp.concatenate(lows, 1), jnp.concatenate(highs, 1)], 0)
    return choose(result, jnp.zeros_like(result), alive)


def solution(mesh):
    placed = (
        P(("groups", "blk"), "head"),
        P(("groups", "blk"), None, None),
        P(None, ("groups", "blk")),
        P("groups"),
        P("groups"),
        P(("groups", "blk")),
        P(("groups", "blk"), None),
        P("head", None, None),
        P("head", "blk"),
        P(("groups", "blk"), None),
        P(),
        P(None, ("blk", "head")),
        P(None, ("blk", "head")),
        P(("blk", "head"), None),
    )
    order = ring_order(mesh)
    return jax.shard_map(
        lambda *args: on_device(order, *args),
        mesh=mesh,
        in_specs=placed,
        out_specs=P(("groups", "blk", "head"), None),
        check_vma=False,
    )
```

```python
import functools

import jax
import jax.numpy as jnp
from jax import lax
from jax.experimental import pallas as pl
from jax.experimental.pallas import tpu as pltpu
from jax.sharding import PartitionSpec as P

score_scale = 192.0 ** (-0.5)
norm_eps = 1e-06
masked_score = -1e30
f32, bf16, i32 = jnp.float32, jnp.bfloat16, jnp.int32
SMEM = pltpu.SMEM
MIB = 1 << 20

RANK, CORE, BUSY, BUSY_RANK, SPAN, DEC, LIVE, START, LENGTHS = range(9)


def mm(a, b):
    return lax.dot_general(a, b, (((1,), (0,)), ((), ())), preferred_element_type=f32)


def mm_nt(a, b):
    return lax.dot_general(a, b, (((1,), (1,)), ((), ())), preferred_element_type=f32)


def in_hbm(x):
    return pltpu.with_memory_space_constraint(x, pltpu.HBM)


def smem():
    return pl.BlockSpec(memory_space=SMEM)


def whole():
    return pl.BlockSpec(memory_space=pltpu.VMEM)


def params(mib=32):
    return pltpu.CompilerParams(vmem_limit_bytes=mib * MIB)


def cost(flops, moved, exps=0):
    return pl.CostEstimate(flops=int(flops), bytes_accessed=int(moved), transcendentals=int(exps))


def ring_order(mesh):
    count = mesh.shape["blk"]
    natural = list(range(count))
    snake = natural[0::2] + natural[1::2][::-1]
    names = list(mesh.axis_names)
    axes = [names.index("blk")] + [a for a, x in enumerate(names) if x != "blk"]
    lane = mesh.devices.transpose(axes)
    firsts = [lane[i].reshape(-1)[0] for i in natural]
    if not all(hasattr(d, "coords") for d in firsts):
        return snake

    def length(order):
        hops = zip(order, order[1:] + order[:1])
        return sum(
            sum(abs(u - v) for u, v in zip(firsts[a].coords, firsts[b].coords)) for a, b in hops
        )

    return natural if length(natural) <= length(snake) else snake


class Table:
    def __init__(self, ranks, slots):
        self.reach = ranks // 2
        self.source = LENGTHS + slots
        self.ahead = self.source + ranks + 1
        self.behind = self.ahead + self.reach + 1
        self.owner_back = self.behind + self.reach + 1
        self.owner_fore = self.owner_back + self.reach + 1
        self.who = self.owner_fore + self.reach + 1
        self.at = self.who + ranks
        self.size = self.at + ranks


def table_kernel(table, order, given, out):
    reach, ranks = table.reach, len(order)
    span = [given[2 + i] for i in range(ranks)]
    dec = [given[2 + ranks + i] for i in range(ranks)]
    lengths = 3 + 2 * ranks
    for i, r in enumerate(order):
        out[table.who + i] = r
        out[table.at + r] = i
    rank, core = given[0], given[1]
    most, busy_rank = span[0] + dec[0], jnp.int32(0)
    for i in range(1, ranks):
        here = span[i] + dec[i]
        busy_rank = jnp.where(here > most, i, busy_rank)
        most = jnp.maximum(here, most)
    busy = rank == busy_rank

    def wrap(x):
        x = jnp.where(x < 0, x + ranks, x)
        return jnp.where(x >= ranks, x - ranks, x)

    place, busy_place = out[table.at + rank], out[table.at + busy_rank]
    to_busy = wrap(busy_place - place)
    from_busy = wrap(place - busy_place)

    def node_ahead(k):
        far = (to_busy > 0) & (k > to_busy + 1)
        slot = out[table.who + wrap(place + k - jnp.where(far, 1, 0))]
        return jnp.where((to_busy > 0) & (k == to_busy + 1), ranks, slot)

    def node_behind(k):
        far = (from_busy > 0) & (k > from_busy)
        slot = out[table.who + wrap(place - k + jnp.where(far, 1, 0))]
        return jnp.where((from_busy > 0) & (k == from_busy), ranks, slot)

    out[RANK] = rank
    out[CORE] = core
    out[BUSY] = jnp.where(busy, 1, 0)
    out[BUSY_RANK] = busy_rank
    out[SPAN] = given[2 + rank]
    out[DEC] = given[2 + ranks + rank]
    out[LIVE] = given[2 + rank] + given[2 + ranks + rank]
    out[START] = given[lengths - 1]
    for j in range(given.shape[0] - lengths):
        out[LENGTHS + j] = given[lengths + j]
    out[table.source + rank] = 0
    for k in range(1, reach + 1):
        out[table.ahead + k] = node_ahead(k)
        out[table.behind + k] = node_behind(k)
        out[table.owner_back + k] = out[table.who + wrap(place - k)]
        out[table.owner_fore + k] = out[table.who + wrap(place + k)]
        out[table.source + node_behind(k)] = k
        last = jnp.where(busy, ranks, node_ahead(k)) if k == reach else node_ahead(k)
        out[table.source + last] = reach + k


def attend_kernel(
    table, order, heads, first, count, group, rows, lat, value, lead, *refs
):
    if lead:
        given, q_hbm, cache_hbm, fresh_hbm, vw_hbm, tab, head, main, extra, later = refs[:10]
        flags, refs = refs[10:13], refs[13:]
        q, keys, fresh, vw, latent, fz, vw_sem, q_sem, key_sem, dq = refs
    else:
        tab, vw_hbm, decoded_here, q, keys, fresh, head, main, extra = refs[:9]
        vw, latent, fz, vw_sem = refs[9:]
    cached, wide = keys.shape[2], keys.shape[1]
    odd_slot = keys.shape[0] - 1
    slots = odd_slot - 1
    shift, pair, dr = wide - lat, 2 * lat, 8
    groups, pairs = count // group, group // 2
    loads = heads // group

    def q_copy(g):
        at = pl.ds(g * group * lat, group * lat)
        return pltpu.make_async_copy(q_hbm.at[:, at], q.at[:, at], q_sem.at[g])

    def vw_copy(g):
        source = pl.ds(first + g * group, group)
        return pltpu.make_async_copy(vw_hbm.at[source], vw.at[pl.ds(g * group, group)], vw_sem.at[g])

    waiting = []
    if lead:
        first_copies = [
            pltpu.make_async_copy(fresh_hbm, fresh, key_sem.at[3]),
            pltpu.make_async_copy(cache_hbm.at[0], keys.at[0, pl.ds(0, lat)], key_sem.at[0]),
            q_copy(0),
            pltpu.make_async_copy(
                cache_hbm.at[0], keys.at[odd_slot, pl.ds(shift, lat)], key_sem.at[1]
            ),
        ]
        rest_copy = pltpu.make_async_copy(
            cache_hbm.at[pl.ds(1, slots)], keys.at[pl.ds(1, slots), pl.ds(0, lat)], key_sem.at[2]
        )
        waiting += [q_copy(1), rest_copy] + [q_copy(g) for g in range(2, loads)]
    waiting += [vw_copy(g) for g in range(groups)]

    def start_next(number):
        for _ in range(min(number, len(waiting))):
            waiting.pop(0).start()

    if lead:
        for copy in first_copies:
            copy.start()
        start_next(1)
        table_kernel(table, order, given, tab)
    else:
        start_next(len(waiting))
    span, decs = tab[SPAN], tab[DEC]

    def onehot(shape, row_dim, slot_dim):
        r = lax.broadcasted_iota(i32, shape, row_dim)
        j = lax.broadcasted_iota(i32, shape, slot_dim)
        return jnp.where((r == span + j) & (j < decs), 1.0, 0.0).astype(bf16)

    if lead:
        tail = jnp.zeros((shift, cached), bf16)
        for s in range(odd_slot):
            keys[s, lat:] = tail
        keys[odd_slot, :shift] = tail
    fz[...] = jnp.zeros_like(fz)
    if lead:
        first_copies[0].wait()
    fz[:rows, :lat] = fresh[...].astype(f32)
    fresh_even = fz[...].astype(bf16)
    fresh_odd = pltpu.roll(fz[...], shift, 1).astype(bf16)

    m = pairs * rows
    cols = cached + fz.shape[0]
    row = lax.broadcasted_iota(i32, (m, 1), 0) % rows
    col = lax.broadcasted_iota(i32, (m, cols), 1)
    seen = col < jnp.where(col < cached, tab[START], cached + 1 + row)

    def span_latent(lhs, slot, fresh_keys):
        s = jnp.concatenate([mm(lhs, keys[slot]), mm_nt(lhs, fresh_keys)], 1)
        s = jnp.where(seen, s * score_scale, masked_score)
        e = jnp.exp(s - jnp.max(s, axis=1, keepdims=True))
        w = (e * (1.0 / jnp.sum(e, axis=1, keepdims=True))).astype(bf16)
        o = mm_nt(w[:, :cached], keys[0, :value]) + mm(w[:, cached:], fresh_even[:, :value])
        return jnp.where(row < span, o, 0.0).astype(bf16)

    if lead:
        first_copies[1].wait()
        first_copies[3].wait()
    for g in range(groups):
        if lead:
            q_copy(g).wait()
            start_next(3)
        start = (first + g * group) * lat
        for odd in range(2):
            off = start + odd * (pair - wide)
            lhs = jnp.concatenate(
                [q[:, off + pair * p : off + pair * p + wide] for p in range(pairs)], 0
            )
            latent[g, odd] = span_latent(lhs, odd_slot * odd, fresh_odd if odd else fresh_even)
    start_next(len(waiting))

    if lead:
        for g in range(groups, loads):
            q_copy(g).wait()
        pick = onehot((16, rows), 1, 0)
        for p in range(heads // 2):
            got = mm(pick, q[:, pair * p : pair * (p + 1)])[:dr]
            dq[2 * p * dr : (2 * p + 1) * dr] = got[:, :wide]
            dq[(2 * p + 1) * dr : (2 * p + 2) * dr] = pltpu.roll(
                got[:, pair - wide :], wide - shift, 1
            )
        n = heads * dr
        queries = dq[...].astype(bf16)
        slot = lax.broadcasted_iota(i32, (n, 1), 0) % dr
        rest_copy.wait()
        length = jnp.zeros((n, 1), i32)
        scores = jnp.zeros((n, cached), f32)
        for s in range(slots):
            scores = jnp.where(slot == s, mm(queries, keys[s + 1]), scores)
            length = jnp.where(slot == s, tab[LENGTHS + s], length)
        unmasked = lax.broadcasted_iota(i32, (n, cached), 1) < length
        scores = jnp.where(unmasked, scores * score_scale, masked_score)
        own = mm_nt(queries, fresh_even)
        column = lax.broadcasted_iota(i32, own.shape, 1)
        own = jnp.sum(jnp.where(column == span + slot, own, 0.0), axis=1, keepdims=True)
        own = own * score_scale
        peak = jnp.maximum(jnp.max(scores, axis=1, keepdims=True), own)
        e = jnp.exp(scores - peak)
        e_own = jnp.exp(own - peak)
        total = jnp.sum(e, axis=1, keepdims=True) + e_own
        w = e / total
        acc = jnp.zeros((n, value), f32)
        for s in range(slots):
            acc = acc + mm_nt(jnp.where(slot == s, w, 0.0).astype(bf16), keys[s + 1, :value])
        own_value = mm(pick, fresh[:, :value])[:dr]
        own_value = jnp.broadcast_to(own_value[None], (heads, dr, value)).reshape(n, value)
        dec = (acc + (e_own / total).astype(bf16).astype(f32) * own_value).astype(bf16)
        later[...] = dec[count * dr :]
        for flag, at in zip(flags, (BUSY, CORE)):
            flag[...] = jnp.full(flag.shape, tab[at].astype(f32))
        block = rows // 2
        slot_row = tab[CORE] * block + lax.broadcasted_iota(i32, (block, 1), 0)
        flags[2][...] = jnp.where(slot_row < tab[LIVE], 1.0, 0.0)
        dec = dec[: count * dr]
    else:
        dec = decoded_here[...]

    place = onehot((rows, 16), 0, 1)
    vh = vw.shape[2]
    block = rows // 2
    for g in range(groups):
        vw_copy(g).wait()
        values, decoded = [], []
        for p in range(pairs):
            h = g * group + 2 * p
            lhs = jnp.concatenate(
                [
                    latent[g, 0, p * rows : (p + 1) * rows],
                    latent[g, 1, p * rows : (p + 1) * rows],
                    dec[h * dr : (h + 2) * dr],
                ],
                0,
            )
            r = mm(lhs, jnp.concatenate([vw[h], vw[h + 1]], 1))
            values += [r[:rows, :vh], r[rows : 2 * rows, vh:]]
            decoded += [r[2 * rows : 2 * rows + dr, :vh], r[2 * rows + dr :, vh:]]
        decoded = jnp.concatenate(decoded, 1)
        decoded = jnp.concatenate([decoded, jnp.zeros_like(decoded)], 0).astype(bf16)
        out = (jnp.concatenate(values, 1) + mm(place, decoded)).astype(bf16)
        at = slice(g * group * vh, (g + 1) * group * vh)
        main[:, at] = out[:block]
        extra[:, at] = out[block:]
        head[:, at] = jnp.where(tab[BUSY] == 1, out[block:], out[:block])


def attend(table, order, queries, cache, fresh, vw, numbers):
    rows, heads = queries.shape[0], vw.shape[0]
    lat = queries.shape[1] // heads
    slots, _, cached = cache.shape
    value, vh = vw.shape[1:]
    count = heads // 2
    group = min(8, count)
    wide = -(-lat // 128) * 128
    hbm = pl.BlockSpec(memory_space=pltpu.HBM)
    half = jax.ShapeDtypeStruct((rows // 2, count * vh), bf16)
    out_shape = [jax.ShapeDtypeStruct((table.size,), i32)] + [half] * 3
    out_shape += [jax.ShapeDtypeStruct(((heads - count) * 8, value), bf16)]
    out_shape += [jax.ShapeDtypeStruct((n, 1), f32) for n in (1, 1, rows // 2)]
    out_shape += [
        jax.ShapeDtypeStruct(queries.shape, bf16),
        jax.ShapeDtypeStruct((slots + 1, wide, cached), bf16),
        jax.ShapeDtypeStruct(fresh.shape[::-1], bf16),
    ]
    return pl.pallas_call(
        functools.partial(
            attend_kernel, table, order, heads, 0, count, group, rows, lat, value, True
        ),
        in_specs=[smem()] + [hbm] * 4,
        out_specs=[smem()] + [whole()] * (len(out_shape) - 1),
        out_shape=out_shape,
        scratch_shapes=attend_scratch(rows, count, group, value, vh, wide)
        + [
            pltpu.SemaphoreType.DMA((heads // group,)),
            pltpu.SemaphoreType.DMA((4,)),
            pltpu.VMEM((heads * 8, wide), f32),
        ],
        compiler_params=params(24),
        cost_estimate=cost(
            2 * rows * count * (cached + rows) * (lat + value),
            2 * (queries.size + cache.size + vw.size // 2),
            rows * count * (cached + rows),
        ),
        name="attend",
    )(numbers, in_hbm(queries), in_hbm(cache), in_hbm(fresh.T), in_hbm(vw))


def attend_scratch(rows, count, group, value, vh, wide):
    return [
        pltpu.VMEM((count, value, vh), bf16),
        pltpu.VMEM((count // group, 2, group // 2 * rows, value), bf16),
        pltpu.VMEM((-(-rows // 128) * 128, wide), f32),
        pltpu.SemaphoreType.DMA((count // group,)),
    ]


def attend_more(table, order, tab, vw, decoded, queries, keys, fresh):
    rows, heads = queries.shape[0], vw.shape[0]
    lat = queries.shape[1] // heads
    value, vh = vw.shape[1:]
    count = heads - heads // 2
    group = min(8, count)
    _, wide, cached = keys.shape
    half = jax.ShapeDtypeStruct((rows // 2, count * vh), bf16)
    return pl.pallas_call(
        functools.partial(
            attend_kernel, table, order, heads, heads - count, count, group, rows, lat, value, False
        ),
        in_specs=[smem(), pl.BlockSpec(memory_space=pltpu.HBM)] + [whole()] * 4,
        out_specs=[whole()] * 3,
        out_shape=[half] * 3,
        scratch_shapes=attend_scratch(rows, count, group, value, vh, wide),
        compiler_params=params(20),
        cost_estimate=cost(
            2 * rows * count * (cached + rows) * (lat + value),
            vw.size,
            rows * count * (cached + rows),
        ),
        name="attend",
    )(tab, in_hbm(vw), decoded, queries, keys, fresh)


def pack_kernel(ranks, cores, features, tab, res, *outs):
    for k in range(ranks // cores):
        target = tab[RANK] + k + (ranks // cores) * tab[CORE]
        target = jnp.where(target >= ranks, target - ranks, target)

        def put(columns, k=k):
            outs[k][...] = res[:, columns]

        if features % 128 == 0:
            put(pl.ds(pl.multiple_of(target * features, 128), features))
        else:
            for t in range(ranks):
                pl.when(target == t)(functools.partial(put, slice(t * features, (t + 1) * features)))


def pack(tab, residual, ranks, cores):
    rows, width = residual.shape
    features = width // ranks
    count = ranks // cores
    return pl.pallas_call(
        functools.partial(pack_kernel, ranks, cores, features),
        in_specs=[smem(), whole()],
        out_specs=[whole()] * count,
        out_shape=[jax.ShapeDtypeStruct((rows, features), bf16)] * count,
        compiler_params=params(8),
        cost_estimate=cost(0, 4 * residual.size),
        name="pack",
    )(tab, residual)


def share_kernel(half, tab, own, *refs):
    pieces, out = refs[:-1], refs[-1]
    other = 1 - tab[CORE]
    block = own.shape[0] // 2
    low = pl.multiple_of(other * half, half)
    high = pl.multiple_of(block + other * half, half)

    def put(k, piece):
        out[2 * k * half : (2 * k + 1) * half] = piece[pl.ds(low, half)]
        out[(2 * k + 1) * half : (2 * k + 2) * half] = piece[pl.ds(high, half)]

    for k, piece in enumerate(pieces):
        if k > 0:
            put(k, piece)
        else:
            pl.when(tab[CORE] == 0)(functools.partial(put, k, own))
            pl.when(tab[CORE] != 0)(functools.partial(put, k, piece))


def share(tab, own, pieces, cores):
    rows, features = own.shape
    half = rows // 2 // cores
    return pl.pallas_call(
        functools.partial(share_kernel, half),
        in_specs=[smem()] + [whole()] * (1 + len(pieces)),
        out_specs=whole(),
        out_shape=jax.ShapeDtypeStruct((2 * half * len(pieces), features), bf16),
        compiler_params=params(8),
        cost_estimate=cost(0, 4 * own.size * len(pieces)),
        name="share",
    )(tab, own, *pieces)


def project_kernel(source, nodes, block, half, part, first, tab, *refs):
    blocks, refs = refs[: nodes + 1], refs[nodes + 1 :]
    before = None if first else refs[0]
    weight, kept, given, acc = refs[-4:]
    step = pl.program_id(0)
    depth = blocks[0].shape[1] // pl.num_programs(0)
    columns = pl.ds(pl.multiple_of(step * depth, 128), depth)
    last = jnp.where(tab[BUSY] == 1, blocks[nodes][:, columns], blocks[nodes - 1][:, columns])
    lhs = jnp.concatenate([b[:, columns] for b in blocks[: nodes - 1]] + [last], 0)
    got = mm(lhs, weight[pl.ds(pl.multiple_of(part * blocks[0].shape[1] + step * depth, 128), depth)])

    @pl.when(step == 0)
    def _():
        acc[...] = got if first else got + before[...]

    @pl.when(step > 0)
    def _():
        acc[...] += got

    @pl.when(step == pl.num_programs(0) - 1)
    def _():
        core = tab[CORE]
        for k in range(nodes):
            at = tab[source + k] * block
            kept[k * half : (k + 1) * half] = acc[pl.ds(pl.multiple_of(at + core * half, half), half)]
            other = acc[pl.ds(pl.multiple_of(at + (1 - core) * half, half), half)]
            given[k * half : (k + 1) * half] = other.astype(bf16)


def project_part_kernel(nodes, part, first, tab, *refs):
    blocks, refs = refs[: nodes + 1], refs[nodes + 1 :]
    weight, out = refs[-2:]
    step = pl.program_id(0)
    depth = blocks[0].shape[1] // pl.num_programs(0)
    columns = pl.ds(pl.multiple_of(step * depth, 128), depth)
    last = jnp.where(tab[BUSY] == 1, blocks[nodes][:, columns], blocks[nodes - 1][:, columns])
    lhs = jnp.concatenate([b[:, columns] for b in blocks[: nodes - 1]] + [last], 0)
    got = mm(lhs, weight[pl.ds(pl.multiple_of(part * blocks[0].shape[1] + step * depth, 128), depth)])

    @pl.when(step == 0)
    def _():
        out[...] = got if first else got + refs[0][...]

    @pl.when(step > 0)
    def _():
        out[...] += got


def project(tab, table, blocks, before, weight, part, parts, cores):
    block, width = blocks[0].shape
    nodes = len(blocks) - 1
    half = block // cores
    features = weight.shape[1]
    depth = width
    steps = width // depth
    total = jax.ShapeDtypeStruct((nodes * block, features), f32)
    final = part == parts - 1
    first = before is None
    ins = [smem()] + [whole()] * (nodes + 2 + (not first))
    args = [tab, *blocks] + ([] if first else [before]) + [weight]
    estimate = cost(
        2 * nodes * block * width * features, 2 * (nodes * block * width + width * features)
    )
    if not final:
        return pl.pallas_call(
            functools.partial(project_part_kernel, nodes, part, first),
            grid=(steps,),
            in_specs=ins,
            out_specs=pl.BlockSpec(total.shape, lambda i: (0, 0)),
            out_shape=total,
            compiler_params=params(16),
            cost_estimate=estimate,
            name="project",
        )(*args)
    return pl.pallas_call(
        functools.partial(project_kernel, table.source, nodes, block, half, part, first),
        grid=(steps,),
        in_specs=ins,
        out_specs=[pl.BlockSpec((nodes * half, features), lambda i: (0, 0))] * 2,
        out_shape=[
            jax.ShapeDtypeStruct((nodes * half, features), f32),
            jax.ShapeDtypeStruct((nodes * half, features), bf16),
        ],
        scratch_shapes=[pltpu.VMEM(total.shape, f32)],
        compiler_params=params(16),
        cost_estimate=estimate,
        name="project",
    )(*args)


def place_kernel(ranks, half, tab, own, shared, *refs):
    pieces, out = refs[:-1], refs[-1]
    rank, core, busy_rank = tab[RANK], tab[CORE], tab[BUSY_RANK]
    count = len(pieces)
    block = own.shape[0] // 2

    def put(slot, extra):
        out[pl.ds(pl.multiple_of(slot * half, half), half)] = extra

    def put_both(owner, main, extra):
        put(owner, main())

        @pl.when(owner == busy_rank)
        def _():
            put(ranks, extra())

    def owner_of(k, c):
        owner = rank - k - count * c
        return jnp.where(owner < 0, owner + ranks, owner)

    low = pl.ds(pl.multiple_of(core * half, half), half)
    high = pl.ds(pl.multiple_of(block + core * half, half), half)
    for k, piece in enumerate(pieces):

        def received(piece=piece, k=k):
            put_both(owner_of(k, core), lambda: piece[low], lambda: piece[high])

        if k > 0:
            received()
        else:
            pl.when(core == 0)(functools.partial(received, own))
            pl.when(core != 0)(received)
        at = 2 * k * half
        put_both(
            owner_of(k, 1 - core),
            lambda at=at: shared[at : at + half],
            lambda at=at: shared[at + half : at + 2 * half],
        )


def placed_rows(tab, own, shared, pieces, cores):
    rows, features = own.shape
    half = rows // 2 // cores
    ranks = cores * len(pieces)
    return pl.pallas_call(
        functools.partial(place_kernel, ranks, half),
        in_specs=[smem()] + [whole()] * (2 + len(pieces)),
        out_specs=whole(),
        out_shape=jax.ShapeDtypeStruct(((ranks + 1) * half, features), bf16),
        compiler_params=params(8),
        cost_estimate=cost(0, 4 * (ranks + 1) * half * features),
        name="place",
    )(tab, own, shared, *pieces)


def expand_kernel(pieces, others, first, final, width, turned, owners, tab, *refs):
    count = len(pieces)
    blocks = []
    for number in pieces:
        blocks.append(refs[:number])
        refs = refs[number:]
    theirs, refs = refs[:others], refs[others:]
    gain, gate, up = refs[:3]
    refs = refs[3:]
    if not first:
        before, refs = refs[:3], refs[3:]
    if final:
        hidden, refs = refs[0], refs[1:]
    gates, ups, squares = refs
    step = pl.program_id(0)
    for i in range(count):

        @pl.when(step == i)
        def _(i=i):
            both = [x[...] for x in blocks[i]]
            for x in theirs:
                rows = x.shape[0] // count
                both.append(x[i * rows : (i + 1) * rows])
            both = jnp.concatenate(both, 0).astype(f32)
            rows_of = both.shape[1]
            scaled = (both * gain[0]).astype(bf16)
            if turned:
                at = pl.ds(pl.multiple_of(tab[owners[i]] * rows_of, 128), rows_of)
                products = mm_nt(scaled, gate[:, at]), mm_nt(scaled, up[:, at])
            else:
                products = mm(scaled, gate[...]), mm(scaled, up[...])
            values = (
                *products,
                jnp.sum(both * both, axis=1, keepdims=True),
            )
            for n, (ref, value) in enumerate(zip((gates, ups, squares), values)):
                if i == 0:
                    ref[...] = value if first else value + before[n][...]
                else:
                    ref[...] += value

    if final:

        @pl.when(step == count - 1)
        def _():
            scale = lax.rsqrt(squares[...] / width + norm_eps)
            g = gates[...] * scale
            hidden[...] = (g / (1.0 + jnp.exp(-g)) * (ups[...] * scale)).astype(bf16)


def expand(tab, mines, theirs, owners, gain, gate, up, before, final):
    count = len(mines)
    pieces = tuple(len(x) for x in mines)
    rows, features = sum(x.shape[0] for x in mines[0]), mines[0][0].shape[1]
    arrays = [x for own in mines for x in own] + theirs
    units = gate.shape[1]
    first = before is None
    width = gate.shape[0]

    def owner(i, tab):
        index = tab[owners[0]]
        for n in range(1, count):
            index = jnp.where(i == n, tab[owners[n]], index)
        return index

    def full(shape):
        return pl.BlockSpec(shape, lambda i, tab: (0,) * len(shape))

    sums = [(2 * rows, units), (2 * rows, units), (2 * rows, 1)]
    ins = [full(x.shape) for x in arrays]
    ins += [pl.BlockSpec((1, 1, features), lambda i, tab: (owner(i, tab), 0, 0))]
    turned = features % 128 == 0
    if turned:
        gate, up = gate.T, up.T
        ins += [pl.BlockSpec(memory_space=pltpu.VMEM)] * 2
    else:
        ins += [pl.BlockSpec((features, units), lambda i, tab: (owner(i, tab), 0))] * 2
    if not first:
        ins += [full(s) for s in sums]
    shapes = [jax.ShapeDtypeStruct(s, f32) for s in sums]
    out_shapes = [jax.ShapeDtypeStruct((2 * rows, units), bf16)] if final else shapes
    return pl.pallas_call(
        functools.partial(expand_kernel, pieces, len(theirs), first, final, width, turned, owners),
        grid_spec=pltpu.PrefetchScalarGridSpec(
            num_scalar_prefetch=1,
            grid=(count,),
            in_specs=ins,
            out_specs=[full(s.shape) for s in out_shapes],
            scratch_shapes=[pltpu.VMEM(s, f32) for s in sums] if final else [],
        ),
        out_shape=out_shapes,
        compiler_params=params(20),
        cost_estimate=cost(1, 1),
        name="expand",
    )(tab, *arrays, gain, gate, up, *([] if first else before))


def collect_kernel(owners, tab, *refs):
    out = refs[-1]
    if len(out.shape) == 2:
        half, features = out.shape[0] // 2, out.shape[1] // len(owners)
        for i, at in enumerate(owners):
            columns = pl.ds(pl.multiple_of(tab[at] * features, 128), features)
            out[:half, columns] = refs[2 * i][...]
            out[half:, columns] = refs[2 * i + 1][...]
        return
    half = out.shape[1] // 2
    for i, at in enumerate(owners):
        out[tab[at], :half] = refs[2 * i][...]
        out[tab[at], half:] = refs[2 * i + 1][...]


def collect(tab, blocks, owners, half):
    ranks = len(blocks)
    features = blocks[0].shape[1]
    ins, args = [], []
    for x in blocks:
        ins += [
            pl.BlockSpec((half, features), lambda i, tab: (tab[RANK], 0)),
            pl.BlockSpec((half, features), lambda i, tab: (ranks, 0)),
        ]
        args += [x, x]
    aligned = features % 128 == 0
    shape = (2 * half, ranks * features) if aligned else (ranks, 2 * half, features)
    out = pl.pallas_call(
        functools.partial(collect_kernel, owners),
        grid_spec=pltpu.PrefetchScalarGridSpec(
            num_scalar_prefetch=1,
            grid=(1,),
            in_specs=ins,
            out_specs=pl.BlockSpec(shape, lambda i, tab: (0,) * len(shape)),
        ),
        out_shape=jax.ShapeDtypeStruct(shape, bf16),
        compiler_params=params(10),
        cost_estimate=cost(0, 8 * ranks * half * features),
        name="collect",
    )(tab, *args)
    return out if aligned else out.transpose(1, 0, 2).reshape(2 * half, ranks * features)


def contract_kernel(begin, hidden, weight, out):
    wide = out.shape[1]
    at = pl.ds(pl.multiple_of(begin + pl.program_id(0) * wide, 128), wide)
    out[...] = mm(hidden[...], weight[:, at]).astype(bf16)


def contract(hidden, weight, part, parts, which):
    rows, units = hidden.shape[0] // 2, hidden.shape[1]
    columns = weight.shape[1] // parts
    wide = columns // 2 if columns % 256 == 0 else columns
    return pl.pallas_call(
        functools.partial(contract_kernel, part * columns),
        grid=(columns // wide,),
        in_specs=[pl.BlockSpec((rows, units), lambda i: (which, 0)), whole()],
        out_specs=pl.BlockSpec((rows, wide), lambda i: (0, i)),
        out_shape=jax.ShapeDtypeStruct((rows, columns), bf16),
        compiler_params=params(16),
        cost_estimate=cost(2 * rows * units * columns, 2 * (units + rows) * columns),
        name="contract",
    )(hidden, weight)


def pick_kernel(table, half, tab, mine, theirs, *outs):
    busy = tab[BUSY] == 1
    reach = table.reach
    for step in range(1, reach + 1):
        for n, where in enumerate((table.ahead, table.behind)):
            at = pl.multiple_of(tab[where + reach + 1 - step] * half, half)
            total = mine[pl.ds(at, half)].astype(f32) + theirs[pl.ds(at, half)].astype(f32)
            if step == 1 and n == 0:
                total = jnp.where(busy, 0.0, total)
            outs[2 * (step - 1) + n][...] = total
    for n, slot in enumerate((tab[RANK], 2 * reach)):
        at = pl.multiple_of(slot * half, half)
        outs[2 * reach + n][...] = mine[pl.ds(at, half)].astype(f32) + theirs[pl.ds(at, half)].astype(f32)


def pick(tab, table, mine, theirs, half):
    columns = mine.shape[1]
    count = 2 * table.reach + 2
    out = jax.ShapeDtypeStruct((half, columns), f32)
    return pl.pallas_call(
        functools.partial(pick_kernel, table, half),
        in_specs=[smem(), whole(), whole()],
        out_specs=[whole()] * count,
        out_shape=[out] * count,
        compiler_params=params(10),
        cost_estimate=cost(0, 8 * count * half * columns),
        name="pick",
    )(tab, mine, theirs)


contract_parts = 2


def on_device(
    order,
    queries,
    latent_cache,
    new_latent,
    span_len,
    dec_count,
    span_start,
    cache_len,
    value_weight,
    out_weight,
    residual,
    norm_gain,
    gate_weight,
    up_weight,
    down_weight,
):
    ranks = len(order)
    reach = ranks // 2
    cores = lax.axis_size("head")
    rows_dev, width = residual.shape
    half = rows_dev // 2 // cores
    features = out_weight.shape[1]
    table = Table(ranks, cache_len.shape[1])

    forward = [(order[i], order[(i + 1) % ranks]) for i in range(ranks)]
    backward = [(b, a) for a, b in forward]
    exchange = [(c, cores - 1 - c) for c in range(cores)]

    def send_next(x):
        return lax.ppermute(x, "blk", forward)

    def send_prev(x):
        return lax.ppermute(x, "blk", backward)

    def swap(x):
        return lax.ppermute(x, "head", exchange)

    ids = jnp.stack([lax.axis_index("blk"), lax.axis_index("head")]).astype(i32)
    given = jnp.concatenate([ids, span_len, dec_count, span_start, cache_len[0]])
    tab, *lead, decoded, busy, which, alive, held, keys, fresh = attend(
        table, order, queries, latent_cache, new_latent, value_weight, given
    )

    def choose(special, usual, flag=busy):
        return jnp.where(jnp.broadcast_to(flag > 0, usual.shape), special, usual)


    packed = list(pack(tab, residual, ranks, cores))
    pieces = [None] * len(packed)

    def send_piece(k):
        pairs = [
            (i * cores + c, (i + k + len(packed) * c) % ranks * cores + c)
            for i in range(ranks)
            for c in range(cores)
            if k + c > 0
        ]
        pieces[k] = lax.ppermute(packed[k], ("blk", "head"), pairs)

    for k in range(1, len(packed)):
        send_piece(k)
    decoded, packed = lax.optimization_barrier((decoded, packed))
    packed = list(packed)
    follow = attend_more(table, order, tab, value_weight, decoded, held, keys, fresh)
    follow, pieces[1:], packed[0], out_weight = lax.optimization_barrier(
        (follow, pieces[1:], packed[0], out_weight)
    )
    send_piece(0)

    total = None
    chains = []
    for head, main, extra in (lead, follow):
        chains.append((head, main, extra, [], []))
    for step in range(reach):
        for part, (head, main, extra, behind, ahead) in enumerate(chains):
            if step == 0:
                out_f, out_b = head, main
            elif step == 1:
                out_f, out_b = choose(main, behind[0]), choose(extra, ahead[0])
            else:
                out_f = choose(behind[step - 2], behind[step - 1])
                out_b = choose(ahead[step - 2], ahead[step - 1])
            out_f, out_b = lax.optimization_barrier((out_f, out_b))
            behind.append(send_next(out_f))
            ahead.append(send_prev(out_b))
    gathered = [[main] + behind + ahead + [extra] for _, main, extra, behind, ahead in chains]
    gathered[0][2], pieces = lax.optimization_barrier((gathered[0][2], pieces))
    shared = swap(share(tab, packed[0], pieces, cores))
    gathered[0], shared = lax.optimization_barrier((gathered[0], shared))
    for part in range(2):
        total = project(tab, table, gathered[part], total, out_weight, part, 2, cores)
    kept, other = total
    res_here = placed_rows(tab, packed[0], shared, pieces, cores)
    stream = (kept + swap(other).astype(f32) + res_here.astype(f32)).astype(bf16)

    gain = norm_gain.reshape(ranks, 1, features)
    weights = (gain, gate_weight, up_weight)
    cut = -(-stream.shape[0] // 32) * 16
    back, fore = stream, stream
    sums = expand(tab, [[stream]], [swap(stream)], [RANK], *weights, None, False)
    blocks, owners = [stream], [RANK]
    done = None
    for step in range(1, reach + 1):
        if done is not None:
            back, fore, done = lax.optimization_barrier((back, fore, done))
        done = sums
        if step < reach:
            back, fore = send_next(back), send_prev(fore)
            arrived = [[back], [fore]]
            from_owner = [table.owner_back + step, table.owner_fore + step]
        else:
            arrived = [[send_next(back[:cut]), send_prev(fore[cut:])]]
            from_owner = [table.owner_back + step]
        tied, sums = lax.optimization_barrier((arrived, sums))
        if step < reach:
            others = [swap(jnp.concatenate([x for (x,) in tied], 0))]
        else:
            others = [swap(x) for x in tied[0]]
        sums = expand(tab, arrived, others, from_owner, *weights, sums, step == reach)
        blocks += [x[0] if len(x) == 1 else jnp.concatenate(x, 0) for x in arrived]
        owners += from_owner
    (hidden,) = sums

    parts = contract_parts
    theirs = [swap(contract(hidden, down_weight, part, parts, 1)) for part in range(parts)]
    mine = [contract(hidden, down_weight, part, parts, 0) for part in range(parts)]
    mine = lax.optimization_barrier(mine)
    columns = width // parts
    lows, highs = [], []
    for part in range(parts):
        got_f, got_b = [], []
        *owned, main, extra = pick(tab, table, mine[part], theirs[part], half)
        for step in range(1, reach + 1):
            out_f, out_b = owned[2 * step - 2], owned[2 * step - 1]
            if step == 2:
                out_f = out_f + choose(jnp.zeros_like(out_f), got_f[0].astype(f32))
                out_b = out_b + choose(jnp.zeros_like(out_b), got_b[0].astype(f32))
            elif step > 2:
                out_f = out_f + choose(got_f[step - 3], got_f[step - 2]).astype(f32)
                out_b = out_b + choose(got_b[step - 3], got_b[step - 2]).astype(f32)
            out_f, out_b = lax.optimization_barrier((out_f.astype(bf16), out_b.astype(bf16)))
            got_f.append(send_next(out_f))
            got_b.append(send_prev(out_b))
        if part == 0:
            blocks[-1], got_f[1] = lax.optimization_barrier((blocks[-1], got_f[1]))
            own = collect(tab, blocks, owners, half).astype(f32)
        at = slice(part * columns, (part + 1) * columns)
        main = main + own[:half, at] + got_f[-1].astype(f32)
        main = (main + choose(got_b[-2], got_b[-1]).astype(f32)).astype(bf16)
        extra = extra + own[half:, at] + got_f[-2].astype(f32) + got_b[-1].astype(f32)
        extra = extra.astype(bf16)
        received = swap(choose(main, extra, which))
        stays = choose(extra, main, which)
        lows.append(choose(received, stays, which))
        highs.append(choose(stays, received, which))
    result = jnp.concatenate([jnp.concatenate(lows, 1), jnp.concatenate(highs, 1)], 0)
    return choose(result, jnp.zeros_like(result), alive)


def solution(mesh):
    placed = (
        P(("groups", "blk"), "head"),
        P(("groups", "blk"), None, None),
        P(None, ("groups", "blk")),
        P("groups"),
        P("groups"),
        P(("groups", "blk")),
        P(("groups", "blk"), None),
        P("head", None, None),
        P("head", "blk"),
        P(("groups", "blk"), None),
        P(),
        P(None, ("blk", "head")),
        P(None, ("blk", "head")),
        P(("blk", "head"), None),
    )
    order = ring_order(mesh)
    return jax.shard_map(
        lambda *args: on_device(order, *args),
        mesh=mesh,
        in_specs=placed,
        out_specs=P(("groups", "blk", "head"), None),
        check_vma=False,
    )
```

```python
import functools

import jax
import jax.numpy as jnp
from jax import lax
from jax.experimental import pallas as pl
from jax.experimental.pallas import tpu as pltpu
from jax.sharding import PartitionSpec as P

score_scale = 192.0 ** (-0.5)
norm_eps = 1e-06
masked_score = -1e30
f32, bf16, i32 = jnp.float32, jnp.bfloat16, jnp.int32
SMEM = pltpu.SMEM
MIB = 1 << 20

RANK, CORE, BUSY, BUSY_RANK, SPAN, DEC, LIVE, START, LENGTHS = range(9)


def mm(a, b):
    return lax.dot_general(a, b, (((1,), (0,)), ((), ())), preferred_element_type=f32)


def mm_nt(a, b):
    return lax.dot_general(a, b, (((1,), (1,)), ((), ())), preferred_element_type=f32)


def in_hbm(x):
    return pltpu.with_memory_space_constraint(x, pltpu.HBM)


def smem():
    return pl.BlockSpec(memory_space=SMEM)


def whole():
    return pl.BlockSpec(memory_space=pltpu.VMEM)


def params(mib=32):
    return pltpu.CompilerParams(vmem_limit_bytes=mib * MIB)


def cost(flops, moved, exps=0):
    return pl.CostEstimate(flops=int(flops), bytes_accessed=int(moved), transcendentals=int(exps))


def ring_order(mesh):
    count = mesh.shape["blk"]
    natural = list(range(count))
    snake = natural[0::2] + natural[1::2][::-1]
    names = list(mesh.axis_names)
    axes = [names.index("blk")] + [a for a, x in enumerate(names) if x != "blk"]
    lane = mesh.devices.transpose(axes)
    firsts = [lane[i].reshape(-1)[0] for i in natural]
    if not all(hasattr(d, "coords") for d in firsts):
        return snake

    def length(order):
        hops = zip(order, order[1:] + order[:1])
        return sum(
            sum(abs(u - v) for u, v in zip(firsts[a].coords, firsts[b].coords)) for a, b in hops
        )

    return natural if length(natural) <= length(snake) else snake


class Table:
    def __init__(self, ranks, slots):
        self.reach = ranks // 2
        self.source = LENGTHS + slots
        self.ahead = self.source + ranks + 1
        self.behind = self.ahead + self.reach + 1
        self.owner_back = self.behind + self.reach + 1
        self.owner_fore = self.owner_back + self.reach + 1
        self.who = self.owner_fore + self.reach + 1
        self.at = self.who + ranks
        self.size = self.at + ranks


def table_kernel(table, order, given, out):
    reach, ranks = table.reach, len(order)
    span = [given[2 + i] for i in range(ranks)]
    dec = [given[2 + ranks + i] for i in range(ranks)]
    lengths = 3 + 2 * ranks
    for i, r in enumerate(order):
        out[table.who + i] = r
        out[table.at + r] = i
    rank, core = given[0], given[1]
    most, busy_rank = span[0] + dec[0], jnp.int32(0)
    for i in range(1, ranks):
        here = span[i] + dec[i]
        busy_rank = jnp.where(here > most, i, busy_rank)
        most = jnp.maximum(here, most)
    busy = rank == busy_rank

    def wrap(x):
        x = jnp.where(x < 0, x + ranks, x)
        return jnp.where(x >= ranks, x - ranks, x)

    place, busy_place = out[table.at + rank], out[table.at + busy_rank]
    to_busy = wrap(busy_place - place)
    from_busy = wrap(place - busy_place)

    def node_ahead(k):
        far = (to_busy > 0) & (k > to_busy + 1)
        slot = out[table.who + wrap(place + k - jnp.where(far, 1, 0))]
        return jnp.where((to_busy > 0) & (k == to_busy + 1), ranks, slot)

    def node_behind(k):
        far = (from_busy > 0) & (k > from_busy)
        slot = out[table.who + wrap(place - k + jnp.where(far, 1, 0))]
        return jnp.where((from_busy > 0) & (k == from_busy), ranks, slot)

    out[RANK] = rank
    out[CORE] = core
    out[BUSY] = jnp.where(busy, 1, 0)
    out[BUSY_RANK] = busy_rank
    out[SPAN] = given[2 + rank]
    out[DEC] = given[2 + ranks + rank]
    out[LIVE] = given[2 + rank] + given[2 + ranks + rank]
    out[START] = given[lengths - 1]
    for j in range(given.shape[0] - lengths):
        out[LENGTHS + j] = given[lengths + j]
    out[table.source + rank] = 0
    for k in range(1, reach + 1):
        out[table.ahead + k] = node_ahead(k)
        out[table.behind + k] = node_behind(k)
        out[table.owner_back + k] = out[table.who + wrap(place - k)]
        out[table.owner_fore + k] = out[table.who + wrap(place + k)]
        out[table.source + node_behind(k)] = k
        last = jnp.where(busy, ranks, node_ahead(k)) if k == reach else node_ahead(k)
        out[table.source + last] = reach + k


def attend_kernel(
    table, order, heads, first, count, group, rows, lat, value, lead, *refs
):
    if lead:
        given, q_hbm, cache_hbm, fresh_hbm, vw_hbm, tab, head, main, extra, later = refs[:10]
        flags, refs = refs[10:13], refs[13:]
        q, keys, fresh, vw, latent, fz, vw_sem, q_sem, key_sem, dq = refs
    else:
        tab, vw_hbm, decoded_here, q, keys, fresh, head, main, extra = refs[:9]
        vw, latent, fz, vw_sem = refs[9:]
    cached, wide = keys.shape[2], keys.shape[1]
    odd_slot = keys.shape[0] - 1
    slots = odd_slot - 1
    shift, pair, dr = wide - lat, 2 * lat, 8
    groups, pairs = count // group, group // 2
    loads = heads // group

    def q_copy(g):
        at = pl.ds(g * group * lat, group * lat)
        return pltpu.make_async_copy(q_hbm.at[:, at], q.at[:, at], q_sem.at[g])

    def vw_copy(g):
        source = pl.ds(first + g * group, group)
        return pltpu.make_async_copy(vw_hbm.at[source], vw.at[pl.ds(g * group, group)], vw_sem.at[g])

    waiting = []
    if lead:
        first_copies = [
            pltpu.make_async_copy(fresh_hbm, fresh, key_sem.at[3]),
            pltpu.make_async_copy(cache_hbm.at[0], keys.at[0, pl.ds(0, lat)], key_sem.at[0]),
            q_copy(0),
            pltpu.make_async_copy(
                cache_hbm.at[0], keys.at[odd_slot, pl.ds(shift, lat)], key_sem.at[1]
            ),
        ]
        rest_copy = pltpu.make_async_copy(
            cache_hbm.at[pl.ds(1, slots)], keys.at[pl.ds(1, slots), pl.ds(0, lat)], key_sem.at[2]
        )
        waiting += [q_copy(1), rest_copy] + [q_copy(g) for g in range(2, loads)]
    waiting += [vw_copy(g) for g in range(groups)]

    def start_next(number):
        for _ in range(min(number, len(waiting))):
            waiting.pop(0).start()

    if lead:
        for copy in first_copies:
            copy.start()
        start_next(1)
        table_kernel(table, order, given, tab)
    else:
        start_next(len(waiting))
    span, decs = tab[SPAN], tab[DEC]

    def onehot(shape, row_dim, slot_dim):
        r = lax.broadcasted_iota(i32, shape, row_dim)
        j = lax.broadcasted_iota(i32, shape, slot_dim)
        return jnp.where((r == span + j) & (j < decs), 1.0, 0.0).astype(bf16)

    if lead:
        tail = jnp.zeros((shift, cached), bf16)
        for s in range(odd_slot):
            keys[s, lat:] = tail
        keys[odd_slot, :shift] = tail
    fz[...] = jnp.zeros_like(fz)
    if lead:
        first_copies[0].wait()
    fz[:rows, :lat] = fresh[...].astype(f32)
    fresh_even = fz[...].astype(bf16)
    fresh_odd = pltpu.roll(fz[...], shift, 1).astype(bf16)

    m = pairs * rows
    cols = cached + fz.shape[0]
    row = lax.broadcasted_iota(i32, (m, 1), 0) % rows
    col = lax.broadcasted_iota(i32, (m, cols), 1)
    seen = col < jnp.where(col < cached, tab[START], cached + 1 + row)

    def span_latent(lhs, slot, fresh_keys):
        s = jnp.concatenate([mm(lhs, keys[slot]), mm_nt(lhs, fresh_keys)], 1)
        s = jnp.where(seen, s * score_scale, masked_score)
        e = jnp.exp(s - jnp.max(s, axis=1, keepdims=True))
        w = (e * (1.0 / jnp.sum(e, axis=1, keepdims=True))).astype(bf16)
        o = mm_nt(w[:, :cached], keys[0, :value]) + mm(w[:, cached:], fresh_even[:, :value])
        return jnp.where(row < span, o, 0.0).astype(bf16)

    if lead:
        first_copies[1].wait()
        first_copies[3].wait()
    for g in range(groups):
        if lead:
            q_copy(g).wait()
            start_next(3)
        start = (first + g * group) * lat
        for odd in range(2):
            off = start + odd * (pair - wide)
            lhs = jnp.concatenate(
                [q[:, off + pair * p : off + pair * p + wide] for p in range(pairs)], 0
            )
            latent[g, odd] = span_latent(lhs, odd_slot * odd, fresh_odd if odd else fresh_even)
    start_next(len(waiting))

    if lead:
        for g in range(groups, loads):
            q_copy(g).wait()
        pick = onehot((16, rows), 1, 0)
        for p in range(heads // 2):
            got = mm(pick, q[:, pair * p : pair * (p + 1)])[:dr]
            dq[2 * p * dr : (2 * p + 1) * dr] = got[:, :wide]
            dq[(2 * p + 1) * dr : (2 * p + 2) * dr] = pltpu.roll(
                got[:, pair - wide :], wide - shift, 1
            )
        n = heads * dr
        queries = dq[...].astype(bf16)
        slot = lax.broadcasted_iota(i32, (n, 1), 0) % dr
        rest_copy.wait()
        length = jnp.zeros((n, 1), i32)
        scores = jnp.zeros((n, cached), f32)
        for s in range(slots):
            scores = jnp.where(slot == s, mm(queries, keys[s + 1]), scores)
            length = jnp.where(slot == s, tab[LENGTHS + s], length)
        unmasked = lax.broadcasted_iota(i32, (n, cached), 1) < length
        scores = jnp.where(unmasked, scores * score_scale, masked_score)
        own = mm_nt(queries, fresh_even)
        column = lax.broadcasted_iota(i32, own.shape, 1)
        own = jnp.sum(jnp.where(column == span + slot, own, 0.0), axis=1, keepdims=True)
        own = own * score_scale
        peak = jnp.maximum(jnp.max(scores, axis=1, keepdims=True), own)
        e = jnp.exp(scores - peak)
        e_own = jnp.exp(own - peak)
        total = jnp.sum(e, axis=1, keepdims=True) + e_own
        w = e / total
        acc = jnp.zeros((n, value), f32)
        for s in range(slots):
            acc = acc + mm_nt(jnp.where(slot == s, w, 0.0).astype(bf16), keys[s + 1, :value])
        own_value = mm(pick, fresh[:, :value])[:dr]
        own_value = jnp.broadcast_to(own_value[None], (heads, dr, value)).reshape(n, value)
        dec = (acc + (e_own / total).astype(bf16).astype(f32) * own_value).astype(bf16)
        later[...] = dec[count * dr :]
        for flag, at in zip(flags, (BUSY, CORE)):
            flag[...] = jnp.full(flag.shape, tab[at].astype(f32))
        block = rows // 2
        slot_row = tab[CORE] * block + lax.broadcasted_iota(i32, (block, 1), 0)
        flags[2][...] = jnp.where(slot_row < tab[LIVE], 1.0, 0.0)
        dec = dec[: count * dr]
    else:
        dec = decoded_here[...]

    place = onehot((rows, 16), 0, 1)
    vh = vw.shape[2]
    block = rows // 2
    for g in range(groups):
        vw_copy(g).wait()
        values, decoded = [], []
        for p in range(pairs):
            h = g * group + 2 * p
            lhs = jnp.concatenate(
                [
                    latent[g, 0, p * rows : (p + 1) * rows],
                    latent[g, 1, p * rows : (p + 1) * rows],
                    dec[h * dr : (h + 2) * dr],
                ],
                0,
            )
            r = mm(lhs, jnp.concatenate([vw[h], vw[h + 1]], 1))
            values += [r[:rows, :vh], r[rows : 2 * rows, vh:]]
            decoded += [r[2 * rows : 2 * rows + dr, :vh], r[2 * rows + dr :, vh:]]
        decoded = jnp.concatenate(decoded, 1)
        decoded = jnp.concatenate([decoded, jnp.zeros_like(decoded)], 0).astype(bf16)
        out = (jnp.concatenate(values, 1) + mm(place, decoded)).astype(bf16)
        at = slice(g * group * vh, (g + 1) * group * vh)
        main[:, at] = out[:block]
        extra[:, at] = out[block:]
        head[:, at] = jnp.where(tab[BUSY] == 1, out[block:], out[:block])


def attend(table, order, queries, cache, fresh, vw, numbers):
    rows, heads = queries.shape[0], vw.shape[0]
    lat = queries.shape[1] // heads
    slots, _, cached = cache.shape
    value, vh = vw.shape[1:]
    count = heads // 2
    group = min(8, count)
    wide = -(-lat // 128) * 128
    hbm = pl.BlockSpec(memory_space=pltpu.HBM)
    half = jax.ShapeDtypeStruct((rows // 2, count * vh), bf16)
    out_shape = [jax.ShapeDtypeStruct((table.size,), i32)] + [half] * 3
    out_shape += [jax.ShapeDtypeStruct(((heads - count) * 8, value), bf16)]
    out_shape += [jax.ShapeDtypeStruct((n, 1), f32) for n in (1, 1, rows // 2)]
    out_shape += [
        jax.ShapeDtypeStruct(queries.shape, bf16),
        jax.ShapeDtypeStruct((slots + 1, wide, cached), bf16),
        jax.ShapeDtypeStruct(fresh.shape[::-1], bf16),
    ]
    return pl.pallas_call(
        functools.partial(
            attend_kernel, table, order, heads, 0, count, group, rows, lat, value, True
        ),
        in_specs=[smem()] + [hbm] * 4,
        out_specs=[smem()] + [whole()] * (len(out_shape) - 1),
        out_shape=out_shape,
        scratch_shapes=attend_scratch(rows, count, group, value, vh, wide)
        + [
            pltpu.SemaphoreType.DMA((heads // group,)),
            pltpu.SemaphoreType.DMA((4,)),
            pltpu.VMEM((heads * 8, wide), f32),
        ],
        compiler_params=params(24),
        cost_estimate=cost(
            2 * rows * count * (cached + rows) * (lat + value),
            2 * (queries.size + cache.size + vw.size // 2),
            rows * count * (cached + rows),
        ),
        name="attend",
    )(numbers, in_hbm(queries), in_hbm(cache), in_hbm(fresh.T), in_hbm(vw))


def attend_scratch(rows, count, group, value, vh, wide):
    return [
        pltpu.VMEM((count, value, vh), bf16),
        pltpu.VMEM((count // group, 2, group // 2 * rows, value), bf16),
        pltpu.VMEM((-(-rows // 128) * 128, wide), f32),
        pltpu.SemaphoreType.DMA((count // group,)),
    ]


def attend_more(table, order, tab, vw, decoded, queries, keys, fresh):
    rows, heads = queries.shape[0], vw.shape[0]
    lat = queries.shape[1] // heads
    value, vh = vw.shape[1:]
    count = heads - heads // 2
    group = min(8, count)
    _, wide, cached = keys.shape
    half = jax.ShapeDtypeStruct((rows // 2, count * vh), bf16)
    return pl.pallas_call(
        functools.partial(
            attend_kernel, table, order, heads, heads - count, count, group, rows, lat, value, False
        ),
        in_specs=[smem(), pl.BlockSpec(memory_space=pltpu.HBM)] + [whole()] * 4,
        out_specs=[whole()] * 3,
        out_shape=[half] * 3,
        scratch_shapes=attend_scratch(rows, count, group, value, vh, wide),
        compiler_params=params(20),
        cost_estimate=cost(
            2 * rows * count * (cached + rows) * (lat + value),
            vw.size,
            rows * count * (cached + rows),
        ),
        name="attend",
    )(tab, in_hbm(vw), decoded, queries, keys, fresh)


def partner(rank, j, ranks, back=False):
    if ranks & (ranks - 1) == 0:
        return rank ^ j
    if isinstance(rank, int):
        return (rank - j if back else rank + j) % ranks
    other = rank - j if back else rank + j
    return jnp.where(other < 0, other + ranks, jnp.where(other >= ranks, other - ranks, other))


def pack_kernel(ranks, cores, features, tab, res, *outs):
    for k in range(ranks // cores):
        target = partner(tab[RANK], k + (ranks // cores) * tab[CORE], ranks)

        def put(columns, k=k):
            outs[k][...] = res[:, columns]

        if features % 128 == 0:
            put(pl.ds(pl.multiple_of(target * features, 128), features))
        else:
            for t in range(ranks):
                pl.when(target == t)(functools.partial(put, slice(t * features, (t + 1) * features)))


def pack(tab, residual, ranks, cores):
    rows, width = residual.shape
    features = width // ranks
    count = ranks // cores
    return pl.pallas_call(
        functools.partial(pack_kernel, ranks, cores, features),
        in_specs=[smem(), whole()],
        out_specs=[whole()] * count,
        out_shape=[jax.ShapeDtypeStruct((rows, features), bf16)] * count,
        compiler_params=params(8),
        cost_estimate=cost(0, 4 * residual.size),
        name="pack",
    )(tab, residual)


def share_kernel(half, tab, own, *refs):
    pieces, out = refs[:-1], refs[-1]
    other = 1 - tab[CORE]
    block = own.shape[0] // 2
    low = pl.multiple_of(other * half, half)
    high = pl.multiple_of(block + other * half, half)

    def put(k, piece):
        out[2 * k * half : (2 * k + 1) * half] = piece[pl.ds(low, half)]
        out[(2 * k + 1) * half : (2 * k + 2) * half] = piece[pl.ds(high, half)]

    for k, piece in enumerate(pieces):
        if k > 0:
            put(k, piece)
        else:
            pl.when(tab[CORE] == 0)(functools.partial(put, k, own))
            pl.when(tab[CORE] != 0)(functools.partial(put, k, piece))


def share(tab, own, pieces, cores):
    rows, features = own.shape
    half = rows // 2 // cores
    return pl.pallas_call(
        functools.partial(share_kernel, half),
        in_specs=[smem()] + [whole()] * (1 + len(pieces)),
        out_specs=whole(),
        out_shape=jax.ShapeDtypeStruct((2 * half * len(pieces), features), bf16),
        compiler_params=params(8),
        cost_estimate=cost(0, 4 * own.size * len(pieces)),
        name="share",
    )(tab, own, *pieces)


def project_kernel(source, nodes, block, half, part, first, tab, *refs):
    blocks, refs = refs[: nodes + 1], refs[nodes + 1 :]
    before = None if first else refs[0]
    weight, kept, given, acc = refs[-4:]
    step = pl.program_id(0)
    depth = blocks[0].shape[1] // pl.num_programs(0)
    columns = pl.ds(pl.multiple_of(step * depth, 128), depth)
    last = jnp.where(tab[BUSY] == 1, blocks[nodes][:, columns], blocks[nodes - 1][:, columns])
    lhs = jnp.concatenate([b[:, columns] for b in blocks[: nodes - 1]] + [last], 0)
    got = mm(lhs, weight[pl.ds(pl.multiple_of(part * blocks[0].shape[1] + step * depth, 128), depth)])

    @pl.when(step == 0)
    def _():
        acc[...] = got if first else got + before[...]

    @pl.when(step > 0)
    def _():
        acc[...] += got

    @pl.when(step == pl.num_programs(0) - 1)
    def _():
        core = tab[CORE]
        for k in range(nodes):
            at = tab[source + k] * block
            kept[k * half : (k + 1) * half] = acc[pl.ds(pl.multiple_of(at + core * half, half), half)]
            other = acc[pl.ds(pl.multiple_of(at + (1 - core) * half, half), half)]
            given[k * half : (k + 1) * half] = other.astype(bf16)


def project_part_kernel(nodes, part, first, tab, *refs):
    blocks, refs = refs[: nodes + 1], refs[nodes + 1 :]
    weight, out = refs[-2:]
    step = pl.program_id(0)
    depth = blocks[0].shape[1] // pl.num_programs(0)
    columns = pl.ds(pl.multiple_of(step * depth, 128), depth)
    last = jnp.where(tab[BUSY] == 1, blocks[nodes][:, columns], blocks[nodes - 1][:, columns])
    lhs = jnp.concatenate([b[:, columns] for b in blocks[: nodes - 1]] + [last], 0)
    got = mm(lhs, weight[pl.ds(pl.multiple_of(part * blocks[0].shape[1] + step * depth, 128), depth)])

    @pl.when(step == 0)
    def _():
        out[...] = got if first else got + refs[0][...]

    @pl.when(step > 0)
    def _():
        out[...] += got


def project(tab, table, blocks, before, weight, part, parts, cores):
    block, width = blocks[0].shape
    nodes = len(blocks) - 1
    half = block // cores
    features = weight.shape[1]
    depth = width
    steps = width // depth
    total = jax.ShapeDtypeStruct((nodes * block, features), f32)
    final = part == parts - 1
    first = before is None
    ins = [smem()] + [whole()] * (nodes + 2 + (not first))
    args = [tab, *blocks] + ([] if first else [before]) + [weight]
    estimate = cost(
        2 * nodes * block * width * features, 2 * (nodes * block * width + width * features)
    )
    if not final:
        return pl.pallas_call(
            functools.partial(project_part_kernel, nodes, part, first),
            grid=(steps,),
            in_specs=ins,
            out_specs=pl.BlockSpec(total.shape, lambda i: (0, 0)),
            out_shape=total,
            compiler_params=params(16),
            cost_estimate=estimate,
            name="project",
        )(*args)
    return pl.pallas_call(
        functools.partial(project_kernel, table.source, nodes, block, half, part, first),
        grid=(steps,),
        in_specs=ins,
        out_specs=[pl.BlockSpec((nodes * half, features), lambda i: (0, 0))] * 2,
        out_shape=[
            jax.ShapeDtypeStruct((nodes * half, features), f32),
            jax.ShapeDtypeStruct((nodes * half, features), bf16),
        ],
        scratch_shapes=[pltpu.VMEM(total.shape, f32)],
        compiler_params=params(16),
        cost_estimate=estimate,
        name="project",
    )(*args)


def place_kernel(ranks, half, tab, own, shared, *refs):
    pieces, out = refs[:-1], refs[-1]
    rank, core, busy_rank = tab[RANK], tab[CORE], tab[BUSY_RANK]
    count = len(pieces)
    block = own.shape[0] // 2

    def put(slot, extra):
        out[pl.ds(pl.multiple_of(slot * half, half), half)] = extra

    def put_both(owner, main, extra):
        put(owner, main())

        @pl.when(owner == busy_rank)
        def _():
            put(ranks, extra())

    def owner_of(k, c):
        return partner(rank, k + count * c, ranks, True)

    low = pl.ds(pl.multiple_of(core * half, half), half)
    high = pl.ds(pl.multiple_of(block + core * half, half), half)
    for k, piece in enumerate(pieces):

        def received(piece=piece, k=k):
            put_both(owner_of(k, core), lambda: piece[low], lambda: piece[high])

        if k > 0:
            received()
        else:
            pl.when(core == 0)(functools.partial(received, own))
            pl.when(core != 0)(received)
        at = 2 * k * half
        put_both(
            owner_of(k, 1 - core),
            lambda at=at: shared[at : at + half],
            lambda at=at: shared[at + half : at + 2 * half],
        )


def placed_rows(tab, own, shared, pieces, cores):
    rows, features = own.shape
    half = rows // 2 // cores
    ranks = cores * len(pieces)
    return pl.pallas_call(
        functools.partial(place_kernel, ranks, half),
        in_specs=[smem()] + [whole()] * (2 + len(pieces)),
        out_specs=whole(),
        out_shape=jax.ShapeDtypeStruct(((ranks + 1) * half, features), bf16),
        compiler_params=params(8),
        cost_estimate=cost(0, 4 * (ranks + 1) * half * features),
        name="place",
    )(tab, own, shared, *pieces)


def expand_kernel(pieces, others, first, final, width, turned, owners, tab, *refs):
    count = len(pieces)
    blocks = []
    for number in pieces:
        blocks.append(refs[:number])
        refs = refs[number:]
    theirs, refs = refs[:others], refs[others:]
    gain, gate, up = refs[:3]
    refs = refs[3:]
    if not first:
        before, refs = refs[:3], refs[3:]
    if final:
        hidden, refs = refs[0], refs[1:]
    gates, ups, squares = refs
    step = pl.program_id(0)
    for i in range(count):

        @pl.when(step == i)
        def _(i=i):
            both = [x[...] for x in blocks[i]]
            for x in theirs:
                rows = x.shape[0] // count
                both.append(x[i * rows : (i + 1) * rows])
            both = jnp.concatenate(both, 0).astype(f32)
            rows_of = both.shape[1]
            scaled = (both * gain[0]).astype(bf16)
            if turned:
                at = pl.ds(pl.multiple_of(tab[owners[i]] * rows_of, 128), rows_of)
                products = mm_nt(scaled, gate[:, at]), mm_nt(scaled, up[:, at])
            else:
                products = mm(scaled, gate[...]), mm(scaled, up[...])
            values = (
                *products,
                jnp.sum(both * both, axis=1, keepdims=True),
            )
            for n, (ref, value) in enumerate(zip((gates, ups, squares), values)):
                if i == 0:
                    ref[...] = value if first else value + before[n][...]
                else:
                    ref[...] += value

    if final:

        @pl.when(step == count - 1)
        def _():
            scale = lax.rsqrt(squares[...] / width + norm_eps)
            g = gates[...] * scale
            hidden[...] = (g / (1.0 + jnp.exp(-g)) * (ups[...] * scale)).astype(bf16)


def expand(tab, mines, theirs, owners, gain, gate, up, before, final):
    count = len(mines)
    pieces = tuple(len(x) for x in mines)
    rows, features = sum(x.shape[0] for x in mines[0]), mines[0][0].shape[1]
    arrays = [x for own in mines for x in own] + theirs
    units = gate.shape[1]
    first = before is None
    width = gate.shape[0]

    def owner(i, tab):
        index = tab[owners[0]]
        for n in range(1, count):
            index = jnp.where(i == n, tab[owners[n]], index)
        return index

    def full(shape):
        return pl.BlockSpec(shape, lambda i, tab: (0,) * len(shape))

    sums = [(2 * rows, units), (2 * rows, units), (2 * rows, 1)]
    ins = [full(x.shape) for x in arrays]
    ins += [pl.BlockSpec((1, 1, features), lambda i, tab: (owner(i, tab), 0, 0))]
    turned = features % 128 == 0
    if turned:
        gate, up = gate.T, up.T
        ins += [pl.BlockSpec(memory_space=pltpu.VMEM)] * 2
    else:
        ins += [pl.BlockSpec((features, units), lambda i, tab: (owner(i, tab), 0))] * 2
    if not first:
        ins += [full(s) for s in sums]
    shapes = [jax.ShapeDtypeStruct(s, f32) for s in sums]
    out_shapes = [jax.ShapeDtypeStruct((2 * rows, units), bf16)] if final else shapes
    return pl.pallas_call(
        functools.partial(expand_kernel, pieces, len(theirs), first, final, width, turned, owners),
        grid_spec=pltpu.PrefetchScalarGridSpec(
            num_scalar_prefetch=1,
            grid=(count,),
            in_specs=ins,
            out_specs=[full(s.shape) for s in out_shapes],
            scratch_shapes=[pltpu.VMEM(s, f32) for s in sums] if final else [],
        ),
        out_shape=out_shapes,
        compiler_params=params(20),
        cost_estimate=cost(1, 1),
        name="expand",
    )(tab, *arrays, gain, gate, up, *([] if first else before))


def collect_kernel(owners, tab, *refs):
    out = refs[-1]
    if len(out.shape) == 2:
        half, features = out.shape[0] // 2, out.shape[1] // len(owners)
        for i, at in enumerate(owners):
            columns = pl.ds(pl.multiple_of(tab[at] * features, 128), features)
            out[:half, columns] = refs[2 * i][...]
            out[half:, columns] = refs[2 * i + 1][...]
        return
    half = out.shape[1] // 2
    for i, at in enumerate(owners):
        out[tab[at], :half] = refs[2 * i][...]
        out[tab[at], half:] = refs[2 * i + 1][...]


def collect(tab, blocks, owners, half):
    ranks = len(blocks)
    features = blocks[0].shape[1]
    ins, args = [], []
    for x in blocks:
        ins += [
            pl.BlockSpec((half, features), lambda i, tab: (tab[RANK], 0)),
            pl.BlockSpec((half, features), lambda i, tab: (ranks, 0)),
        ]
        args += [x, x]
    aligned = features % 128 == 0
    shape = (2 * half, ranks * features) if aligned else (ranks, 2 * half, features)
    out = pl.pallas_call(
        functools.partial(collect_kernel, owners),
        grid_spec=pltpu.PrefetchScalarGridSpec(
            num_scalar_prefetch=1,
            grid=(1,),
            in_specs=ins,
            out_specs=pl.BlockSpec(shape, lambda i, tab: (0,) * len(shape)),
        ),
        out_shape=jax.ShapeDtypeStruct(shape, bf16),
        compiler_params=params(10),
        cost_estimate=cost(0, 8 * ranks * half * features),
        name="collect",
    )(tab, *args)
    return out if aligned else out.transpose(1, 0, 2).reshape(2 * half, ranks * features)


def contract_kernel(begin, hidden, weight, out):
    wide = out.shape[1]
    at = pl.ds(pl.multiple_of(begin + pl.program_id(0) * wide, 128), wide)
    out[...] = mm(hidden[...], weight[:, at]).astype(bf16)


def contract(hidden, weight, part, parts, which):
    rows, units = hidden.shape[0] // 2, hidden.shape[1]
    columns = weight.shape[1] // parts
    wide = columns // 2 if columns % 256 == 0 else columns
    return pl.pallas_call(
        functools.partial(contract_kernel, part * columns),
        grid=(columns // wide,),
        in_specs=[pl.BlockSpec((rows, units), lambda i: (which, 0)), whole()],
        out_specs=pl.BlockSpec((rows, wide), lambda i: (0, i)),
        out_shape=jax.ShapeDtypeStruct((rows, columns), bf16),
        compiler_params=params(16),
        cost_estimate=cost(2 * rows * units * columns, 2 * (units + rows) * columns),
        name="contract",
    )(hidden, weight)


def pick_kernel(table, half, tab, mine, theirs, *outs):
    busy = tab[BUSY] == 1
    reach = table.reach
    for step in range(1, reach + 1):
        for n, where in enumerate((table.ahead, table.behind)):
            at = pl.multiple_of(tab[where + reach + 1 - step] * half, half)
            total = mine[pl.ds(at, half)].astype(f32) + theirs[pl.ds(at, half)].astype(f32)
            if step == 1 and n == 0:
                total = jnp.where(busy, 0.0, total)
            outs[2 * (step - 1) + n][...] = total
    for n, slot in enumerate((tab[RANK], 2 * reach)):
        at = pl.multiple_of(slot * half, half)
        outs[2 * reach + n][...] = mine[pl.ds(at, half)].astype(f32) + theirs[pl.ds(at, half)].astype(f32)


def pick(tab, table, mine, theirs, half):
    columns = mine.shape[1]
    count = 2 * table.reach + 2
    out = jax.ShapeDtypeStruct((half, columns), f32)
    return pl.pallas_call(
        functools.partial(pick_kernel, table, half),
        in_specs=[smem(), whole(), whole()],
        out_specs=[whole()] * count,
        out_shape=[out] * count,
        compiler_params=params(10),
        cost_estimate=cost(0, 8 * count * half * columns),
        name="pick",
    )(tab, mine, theirs)


contract_parts = 2


def on_device(
    order,
    queries,
    latent_cache,
    new_latent,
    span_len,
    dec_count,
    span_start,
    cache_len,
    value_weight,
    out_weight,
    residual,
    norm_gain,
    gate_weight,
    up_weight,
    down_weight,
):
    ranks = len(order)
    reach = ranks // 2
    cores = lax.axis_size("head")
    rows_dev, width = residual.shape
    half = rows_dev // 2 // cores
    features = out_weight.shape[1]
    table = Table(ranks, cache_len.shape[1])

    forward = [(order[i], order[(i + 1) % ranks]) for i in range(ranks)]
    backward = [(b, a) for a, b in forward]
    exchange = [(c, cores - 1 - c) for c in range(cores)]

    def send_next(x):
        return lax.ppermute(x, "blk", forward)

    def send_prev(x):
        return lax.ppermute(x, "blk", backward)

    def swap(x):
        return lax.ppermute(x, "head", exchange)

    ids = jnp.stack([lax.axis_index("blk"), lax.axis_index("head")]).astype(i32)
    given = jnp.concatenate([ids, span_len, dec_count, span_start, cache_len[0]])
    tab, *lead, decoded, busy, which, alive, held, keys, fresh = attend(
        table, order, queries, latent_cache, new_latent, value_weight, given
    )

    def choose(special, usual, flag=busy):
        return jnp.where(jnp.broadcast_to(flag > 0, usual.shape), special, usual)


    packed = list(pack(tab, residual, ranks, cores))
    pieces = [None] * len(packed)

    def send_piece(k):
        pairs = [
            (i * cores + c, partner(i, k + len(packed) * c, ranks) * cores + c)
            for i in range(ranks)
            for c in range(cores)
            if k + c > 0
        ]
        pieces[k] = lax.ppermute(packed[k], ("blk", "head"), pairs)

    for k in range(1, len(packed)):
        send_piece(k)
    decoded, packed = lax.optimization_barrier((decoded, packed))
    packed = list(packed)
    follow = attend_more(table, order, tab, value_weight, decoded, held, keys, fresh)
    follow, pieces[1:], packed[0], out_weight = lax.optimization_barrier(
        (follow, pieces[1:], packed[0], out_weight)
    )
    send_piece(0)

    total = None
    chains = []
    for head, main, extra in (lead, follow):
        chains.append((head, main, extra, [], []))
    for step in range(reach):
        for part, (head, main, extra, behind, ahead) in enumerate(chains):
            if step == 0:
                out_f, out_b = head, main
            elif step == 1:
                out_f, out_b = choose(main, behind[0]), choose(extra, ahead[0])
            else:
                out_f = choose(behind[step - 2], behind[step - 1])
                out_b = choose(ahead[step - 2], ahead[step - 1])
            out_f, out_b = lax.optimization_barrier((out_f, out_b))
            behind.append(send_next(out_f))
            ahead.append(send_prev(out_b))
    gathered = [[main] + behind + ahead + [extra] for _, main, extra, behind, ahead in chains]
    gathered[0][2], pieces = lax.optimization_barrier((gathered[0][2], pieces))
    shared = swap(share(tab, packed[0], pieces, cores))
    gathered[0], shared = lax.optimization_barrier((gathered[0], shared))
    for part in range(2):
        total = project(tab, table, gathered[part], total, out_weight, part, 2, cores)
    kept, other = total
    res_here = placed_rows(tab, packed[0], shared, pieces, cores)
    stream = (kept + swap(other).astype(f32) + res_here.astype(f32)).astype(bf16)

    gain = norm_gain.reshape(ranks, 1, features)
    weights = (gain, gate_weight, up_weight)
    cut = -(-stream.shape[0] // 32) * 16
    back, fore = stream, stream
    sums = expand(tab, [[stream]], [swap(stream)], [RANK], *weights, None, False)
    blocks, owners = [stream], [RANK]
    done = None
    for step in range(1, reach + 1):
        if done is not None:
            back, fore, done = lax.optimization_barrier((back, fore, done))
        done = sums
        if step < reach:
            back, fore = send_next(back), send_prev(fore)
            arrived = [[back], [fore]]
            from_owner = [table.owner_back + step, table.owner_fore + step]
        else:
            arrived = [[send_next(back[:cut]), send_prev(fore[cut:])]]
            from_owner = [table.owner_back + step]
        tied, sums = lax.optimization_barrier((arrived, sums))
        if step < reach:
            others = [swap(jnp.concatenate([x for (x,) in tied], 0))]
        else:
            others = [swap(x) for x in tied[0]]
        sums = expand(tab, arrived, others, from_owner, *weights, sums, step == reach)
        blocks += [x[0] if len(x) == 1 else jnp.concatenate(x, 0) for x in arrived]
        owners += from_owner
    (hidden,) = sums

    parts = contract_parts
    theirs = [swap(contract(hidden, down_weight, part, parts, 1)) for part in range(parts)]
    mine = [contract(hidden, down_weight, part, parts, 0) for part in range(parts)]
    mine = lax.optimization_barrier(mine)
    columns = width // parts
    lows, highs = [], []
    for part in range(parts):
        got_f, got_b = [], []
        *owned, main, extra = pick(tab, table, mine[part], theirs[part], half)
        for step in range(1, reach + 1):
            out_f, out_b = owned[2 * step - 2], owned[2 * step - 1]
            if step == 2:
                out_f = out_f + choose(jnp.zeros_like(out_f), got_f[0].astype(f32))
                out_b = out_b + choose(jnp.zeros_like(out_b), got_b[0].astype(f32))
            elif step > 2:
                out_f = out_f + choose(got_f[step - 3], got_f[step - 2]).astype(f32)
                out_b = out_b + choose(got_b[step - 3], got_b[step - 2]).astype(f32)
            out_f, out_b = lax.optimization_barrier((out_f.astype(bf16), out_b.astype(bf16)))
            got_f.append(send_next(out_f))
            got_b.append(send_prev(out_b))
        if part == 0:
            blocks[-1], got_f[1] = lax.optimization_barrier((blocks[-1], got_f[1]))
            own = collect(tab, blocks, owners, half).astype(f32)
        at = slice(part * columns, (part + 1) * columns)
        main = main + own[:half, at] + got_f[-1].astype(f32)
        main = (main + choose(got_b[-2], got_b[-1]).astype(f32)).astype(bf16)
        extra = extra + own[half:, at] + got_f[-2].astype(f32) + got_b[-1].astype(f32)
        extra = extra.astype(bf16)
        received = swap(choose(main, extra, which))
        stays = choose(extra, main, which)
        lows.append(choose(received, stays, which))
        highs.append(choose(stays, received, which))
    result = jnp.concatenate([jnp.concatenate(lows, 1), jnp.concatenate(highs, 1)], 0)
    return choose(result, jnp.zeros_like(result), alive)


def solution(mesh):
    placed = (
        P(("groups", "blk"), "head"),
        P(("groups", "blk"), None, None),
        P(None, ("groups", "blk")),
        P("groups"),
        P("groups"),
        P(("groups", "blk")),
        P(("groups", "blk"), None),
        P("head", None, None),
        P("head", "blk"),
        P(("groups", "blk"), None),
        P(),
        P(None, ("blk", "head")),
        P(None, ("blk", "head")),
        P(("blk", "head"), None),
    )
    order = ring_order(mesh)
    return jax.shard_map(
        lambda *args: on_device(order, *args),
        mesh=mesh,
        in_specs=placed,
        out_specs=P(("groups", "blk", "head"), None),
        check_vma=False,
    )
```
